32 devices in a mesh: rep: 8 (over z, y), grp: 4 (over x, core).
Axes of the slice: x: 2, y: 2, z: 4, core: 2. Of those that a mesh axis runs over, the one named last changes fastest.
Arguments:
- params: float32 [14115072], P(('rep', 'grp'))
- first_moment: float32 [14115072], P(('rep', 'grp')), may hold values from -1.9073486e-05 to 1.9073486e-05
- second_moment: float32 [14115072], P(('rep', 'grp')), may hold values from 1.5420462e-13 to 6.168185e-13
- teacher: float32 [14115072], P(('rep', 'grp'))
- protos: float32 [256, 8192], P('rep', 'grp'), may hold values from -6 to 6
- proto_first: float32 [256, 8192], P('rep', 'grp'), may hold values from -1.9073486e-05 to 1.9073486e-05
- proto_second: float32 [256, 8192], P('rep', 'grp'), may hold values from 1.5420462e-13 to 6.168185e-13
- teacher_protos: float32 [256, 8192], P('rep', 'grp'), may hold values from -6 to 6
- center: float32 [8192], P('grp'), may hold values from -0.3125 to 0.3125
- patches: bfloat16 [128, 196, 768], P(('rep', 'grp')), may hold values from -6 to 6
- partner: int32 [128], P(('rep', 'grp')), may hold values from 0 to 3, as said below
Outputs:
- new_params: float32 [14115072], P(('rep', 'grp'))
- new_first: float32 [14115072], P(('rep', 'grp'))
- new_second: float32 [14115072], P(('rep', 'grp'))
- new_teacher: float32 [14115072], P(('rep', 'grp'))
- new_protos: float32 [256, 8192], P('rep', 'grp')
- new_proto_first: float32 [256, 8192], P('rep', 'grp')
- new_proto_second: float32 [256, 8192], P('rep', 'grp')
- new_teacher_protos: float32 [256, 8192], P('rep', 'grp')
- new_center: float32 [8192], P('grp')
- loss: float32 [], replicated
- grad_norm: float32 [], replicated
The draws below stay inside these ranges and needn't reach their ends.
Inputs may be any that keep to these rules, and one draw needn't show every extreme that they name: In each aligned block of 4 views (the views of one device) partner pairs the views: partner[i] is the place in the block of another view of the block, whose partner is view i.
All inputs are finite; a program needn't handle non-finite values.
Results may differ from the reference program's by a relative error of at most 0.0071.
The reference program's roundings to bfloat16 on the way count: a program that leaves them out, or rounds other values in their place, can miss the bound.
Values may be sent and summed in bfloat16 or wider, within the bound.
No kernel may reach another device: no remote copies, remote signals or barrier semaphores. Data moves between devices by JAX's collectives and lax.ppermute only.
A program may use at most 320 MiB of HBM per device.

```python
import math
import jax
import jax.numpy as jnp
from jax import lax

D = 768
HEADS = 12
HDIM = 64
F = 3072
PD = 768
NTOK = 197
H = 2048
B = 256
K = 8192
LAYERS = 1
STEP = 10
VD = 4
VIEWS = 128
PFLAT = 14115072
NPARAMS = 16212224


def norm_rows(repeats):
    scales = jnp.repeat(jnp.array([0.25, 0.1] * repeats, jnp.float32), D)
    offsets = jnp.repeat(jnp.array([1.0, 0.0] * repeats, jnp.float32), D)
    return (scales, offsets)


def scale_table():
    scales = [jnp.full((PD * D,), PD ** (-0.5), jnp.float32), jnp.full((NTOK * D,), 0.3, jnp.float32)]
    offsets = [jnp.zeros((PD * D + NTOK * D,), jnp.float32)]
    for level_index in range(LAYERS):
        gains, shifts = norm_rows(2)
        scales = scales + [gains, jnp.full((3 * D * D,), D ** (-0.5), jnp.float32), jnp.full((D * D,), NTOK ** 0.25 * D ** (-0.5), jnp.float32), jnp.full((D * F,), D ** (-0.5), jnp.float32), jnp.full((F * D,), F ** (-0.5), jnp.float32)]
        offsets = offsets + [shifts, jnp.zeros((4 * D * D + 2 * D * F,), jnp.float32)]
    gains, shifts = norm_rows(1)
    scales = scales + [gains, jnp.full((D * H,), D ** (-0.5), jnp.float32), jnp.full((H * H + H * B,), H ** (-0.5), jnp.float32)]
    offsets = offsets + [shifts, jnp.zeros((D * H + H * H + H * B,), jnp.float32)]
    return (jnp.concatenate(scales), jnp.concatenate(offsets))


def draw_params(key, part):
    key = jax.random.fold_in(key, 11)
    scales, offsets = scale_table()
    noise = jax.random.normal(key, scales.shape, jnp.float32)
    return noise * scales + offsets


def draw_teacher(key, part):
    key = jax.random.fold_in(key, 12)
    scales, offsets = scale_table()
    noise = jax.random.normal(key, scales.shape, jnp.float32)
    return noise * scales + offsets


def draw_partner(key, part):
    key = jax.random.fold_in(key, 13)
    blocks = VIEWS // VD
    orders = jax.vmap(lambda single: jax.random.permutation(single, VD))(jax.random.split(key, blocks)).astype(jnp.int32)
    evens = orders[:, 0::2]
    odds = orders[:, 1::2]
    places = jnp.arange(blocks, dtype=jnp.int32)[:, None]
    table = jnp.zeros((blocks, VD), jnp.int32).at[places, evens].set(odds).at[places, odds].set(evens)
    return table.reshape(-1).astype(jnp.int32)


def block_scale(rng, dims, cuts, least, high):
    factor_of, own = 1.0, jax.random.fold_in(rng, 6)
    for dim, blocks in cuts:
        draws = jnp.exp(jax.random.uniform(jax.random.fold_in(own, dim), (blocks,), jnp.float32, least / len(cuts), high / len(cuts)))
        factor_of = factor_of * jnp.repeat(draws, dims[dim] // blocks).reshape([-1 if axis == dim else 1 for axis in range(len(dims))])
    return factor_of


def gaussian(rng, shape, width, bound, cuts=(), held_as=jnp.bfloat16):
    result = jax.random.normal(rng, shape, jnp.float32) * width
    if len(cuts) > 0:
        result = block_scale(rng, shape, cuts, -0.22, 0.18) * result
    return jnp.clip(result, min=-bound, max=bound).astype(held_as)


def setup_inputs(seed: int = 0) -> dict:
    key_list = jax.random.split(jax.random.key(seed), 12)
    return {
        "params": draw_params(jax.random.fold_in(key_list[11], 71), 0),
        "first_moment": gaussian(key_list[1], (PFLAT,), (0.0055 * NPARAMS ** -0.5), 1.9073486328125e-05, ((0, 32),), jnp.float32),
        "second_moment": jnp.clip(jnp.exp(math.log(6.168184994888304e-13) - 1.3862944 * jax.random.uniform(key_list[2], (PFLAT,), jnp.float32) ** block_scale(key_list[2], (PFLAT,), ((0, 32),), -0.2, 0.2)), 1.542046248722076e-13, 6.168184994888304e-13),
        "teacher": draw_teacher(jax.random.fold_in(key_list[11], 71), 0),
        "protos": gaussian(key_list[4], (B, K), 1.0, 6.0, ((0, 8), (1, 4)), jnp.float32),
        "proto_first": gaussian(key_list[5], (B, K), (0.0055 * NPARAMS ** -0.5), 1.9073486328125e-05, ((0, 8), (1, 4)), jnp.float32),
        "proto_second": jnp.clip(jnp.exp(math.log(6.168184994888304e-13) - 1.3862944 * jax.random.uniform(key_list[6], (B, K), jnp.float32) ** block_scale(key_list[6], (B, K), ((0, 8), (1, 4)), -0.2, 0.2)), 1.542046248722076e-13, 6.168184994888304e-13),
        "teacher_protos": gaussian(key_list[7], (B, K), 1.0, 6.0, ((0, 8), (1, 4)), jnp.float32),
        "center": gaussian(key_list[8], (K,), 0.02, 0.3125, ((0, 4),), jnp.float32),
        "patches": gaussian(key_list[9], (VIEWS, NTOK - 1, PD), 1.0, 6.0, ((0, 32),)),
        "partner": draw_partner(jax.random.fold_in(key_list[11], 71), 0),
    }


PRECISE = lax.Precision.HIGHEST
STUDENT_TEMP = 0.1
TEACHER_TEMP = 0.04
CENTER_MOMENTUM = 0.9
TEACHER_MOMENTUM = 0.8
CLIP_NORM = 0.05
LEARNING_RATE = 0.03
PROTO_RATE = 0.6
BETA_FIRST = 0.9
BETA_SECOND = 0.999
ADAM_EPSILON = 1e-08
WEIGHT_DECAY = 0.04

@jax.custom_vjp
def low(v):
    return lax.optimization_barrier(v.astype(jnp.bfloat16)).astype(jnp.float32)

@jax.custom_vjp
def low_back(v):
    return v

def low_keep(v):
    return (low(v), None)

def low_pass(kept, grad):
    return (grad,)

def back_keep(v):
    return (v, None)

def back_low(kept, grad):
    return (low(grad),)
low.defvjp(low_keep, low_pass)
low_back.defvjp(back_keep, back_low)

def shape_list():
    shapes = [(PD, D), (NTOK, D)]
    for level_index in range(LAYERS):
        shapes = shapes + [(4, D), (D, 3 * D), (D, D), (D, F), (F, D)]
    return shapes + [(2, D), (D, H), (H, H), (H, B)]

def unpack(flat_params):
    pieces = []
    offset = 0
    for dims_pair in shape_list():
        entries = dims_pair[0] * dims_pair[1]
        pieces.append(flat_params[offset:offset + entries].reshape(dims_pair))
        offset = offset + entries
    return pieces

def product(left, right):
    return jnp.matmul(left, right, precision=PRECISE)

def layer_norm(stream, gain_row, shift_row):
    middle_mean = lax.optimization_barrier(jnp.mean(stream, -1, keepdims=True))
    centred = stream - middle_mean
    spread = lax.optimization_barrier(jnp.mean(centred * centred, -1, keepdims=True))
    return centred * lax.rsqrt(spread + 1e-06) * gain_row + shift_row

def activate(values):
    return jax.nn.gelu(values, approximate=False)

def block(stream, norms, qkv_w, out_w, up_w, down_w):
    view_count = stream.shape[0]
    normed = low(layer_norm(stream, norms[0], norms[1]))
    qkv = low(low_back(product(normed, qkv_w))).reshape(view_count, NTOK, 3, HEADS, HDIM)
    scores = low_back(jnp.einsum('vqhd,vkhd->vhqk', qkv[:, :, 0], qkv[:, :, 1], precision=PRECISE) * HDIM ** (-0.5))
    probs = low(jax.nn.softmax(scores, -1))
    attended = jnp.einsum('vhqk,vkhd->vqhd', probs, qkv[:, :, 2], precision=PRECISE).reshape(view_count, NTOK, D)
    middle = stream + low_back(product(low(low_back(attended)), out_w))
    normed_two = low(layer_norm(middle, norms[2], norms[3]))
    act = low(activate(low_back(product(normed_two, up_w))))
    return middle + low_back(product(act, down_w))

def trunk(pieces, patches):
    view_count = patches.shape[0]
    embedded = low_back(product(patches, pieces[0]))
    stream = jnp.concatenate([jnp.zeros((view_count, 1, D), jnp.float32), embedded], 1) + pieces[1]
    for level_index in range(LAYERS):
        stream = block(stream, *pieces[2 + 5 * level_index:7 + 5 * level_index])
    final = pieces[2 + 5 * LAYERS]
    cls = low(layer_norm(stream[:, 0], final[0], final[1]))
    first = low(activate(low_back(product(cls, pieces[3 + 5 * LAYERS]))))
    second = low(activate(low_back(product(first, pieces[4 + 5 * LAYERS]))))
    bottle = low_back(product(second, pieces[5 + 5 * LAYERS]))
    unit = bottle * lax.rsqrt(lax.optimization_barrier(jnp.sum(bottle * bottle, -1, keepdims=True)) + 1e-06)
    return low(low_back(unit))

def class_rows(pieces, patches):
    group_size = math.gcd(VIEWS, 8)
    blocks = patches.reshape(VIEWS // group_size, group_size, NTOK - 1, PD)
    rows = lax.map(jax.checkpoint(lambda piece: trunk(pieces, piece)), blocks)
    return rows.reshape(VIEWS, B)

def prototypes(table):
    return low(table * lax.rsqrt(lax.optimization_barrier(jnp.sum(table * table, 0, keepdims=True)) + 1e-06))

def adam_update(weight, grad, first, second, rate):
    first = BETA_FIRST * first + (1.0 - BETA_FIRST) * grad
    second = BETA_SECOND * second + (1.0 - BETA_SECOND) * grad * grad
    stepped = first / (1.0 - BETA_FIRST ** STEP) / (jnp.sqrt(second / (1.0 - BETA_SECOND ** STEP)) + ADAM_EPSILON)
    return (weight - rate * (stepped + WEIGHT_DECAY * weight), first, second)

def reference(params, first_moment, second_moment, teacher, protos, proto_first, proto_second, teacher_protos, center, patches, partner):
    patches = patches.astype(jnp.float32)
    owners = jnp.arange(VIEWS, dtype=jnp.int32) // VD * VD + partner.astype(jnp.int32)
    teacher_rows = class_rows(unpack(low(teacher)), patches)
    teacher_logits = product(teacher_rows, prototypes(low(teacher_protos)))
    new_center = CENTER_MOMENTUM * center + (1.0 - CENTER_MOMENTUM) * lax.optimization_barrier(jnp.mean(teacher_logits, 0))
    targets = jax.nn.softmax((teacher_logits - center) / TEACHER_TEMP, -1)[owners]

    def loss_of(flat_params, table):
        rows = class_rows(unpack(low(flat_params)), patches)
        logits = product(rows, prototypes(low(table))) / STUDENT_TEMP
        return -jnp.sum(targets * jax.nn.log_softmax(logits, -1))
    loss, pullback = jax.vjp(loss_of, params, protos)
    grad_flat, grad_table = pullback(jnp.ones((), jnp.float32))
    grad_norm = jnp.sqrt(jnp.sum(grad_flat * grad_flat) + jnp.sum(grad_table * grad_table))
    factor = jnp.minimum(1.0, CLIP_NORM / (grad_norm + 1e-06))
    new_params, new_first, new_second = adam_update(params, grad_flat * factor, first_moment, second_moment, LEARNING_RATE)
    new_protos, new_proto_first, new_proto_second = adam_update(protos, grad_table * factor, proto_first, proto_second, PROTO_RATE)
    new_teacher = TEACHER_MOMENTUM * teacher + (1.0 - TEACHER_MOMENTUM) * new_params
    new_teacher_protos = TEACHER_MOMENTUM * teacher_protos + (1.0 - TEACHER_MOMENTUM) * new_protos
    return (new_params, new_first, new_second, new_teacher, new_protos, new_proto_first, new_proto_second, new_teacher_protos, new_center, loss, grad_norm)
```

```python
import functools
import math

import jax
import jax.numpy as jnp
import numpy as np
from jax import lax
from jax.experimental import pallas as pl
from jax.experimental.pallas import tpu as pltpu
from jax.sharding import PartitionSpec as P

D = 768
HEADS = 12
HDIM = 64
F = 3072
PD = 768
NTOK = 197
H = 2048
B = 256
STEP = 10
NPATCH = NTOK - 1

PRECISE = lax.Precision.HIGHEST
STUDENT_TEMP = 0.1
TEACHER_TEMP = 0.04
CENTER_MOMENTUM = 0.9
TEACHER_MOMENTUM = 0.8
CLIP_NORM = 0.05
LEARNING_RATE = 0.03
PROTO_RATE = 0.6
BETA_FIRST = 0.9
BETA_SECOND = 0.999
ADAM_EPSILON = 1e-08
WEIGHT_DECAY = 0.04
BOTH = ("rep", "grp")
LANES = 128
F32 = jnp.float32
BF16 = jnp.bfloat16

SEGMENTS = []
_offset = 0
for _rows, _cols in ((PD + NTOK + 4, D), (D, 3 * D), (D, D), (D, F), (F + 2, D), (D + H, H), (H, B)):
    SEGMENTS.append((_offset, _rows, _cols))
    _offset += _rows * _cols
PFLAT = _offset
WIDTHS = sorted({cols // LANES for _, _, cols in SEGMENTS})

PIECES = []
_offset = 0
for _rows, _cols in (
    (PD + NTOK + 4, D),
    (D, 3 * D),
    (D, D),
    (D, F),
    (F, D),
    (2, D),
    (D, H),
    (H, H),
    (H, B),
):
    PIECES.append((_offset, _rows, _cols))
    _offset += _rows * _cols

FRONT = 24
GRAD_FRONT = 8 * FRONT
CHUNK = 64


def round_up(value, step):
    return -(-value // step) * step


def shard_parts(start, stop, table):
    parts = []
    line0 = start // LANES
    for index, (offset, rows, cols) in enumerate(table):
        low, high = max(start, offset), min(stop, offset + rows * cols)
        if low >= high:
            continue
        row0 = (low - offset) // cols
        row1 = -(-(high - offset) // cols)
        parts.append((index, row0, row1 - row0, (offset + row0 * cols) // LANES - line0))
    return parts


FINAL_ROW = round_up(PD + NTOK + 4, 8)


class Plan:
    def __init__(self, count):
        self.count = count
        self.size = PFLAT // count
        self.lines = round_up(-(-self.size // LANES) + 1, CHUNK)
        self.scratch = FRONT + self.lines + 8 * max(WIDTHS) + 16
        table = []
        self.blocks = [[] for _ in SEGMENTS]
        longest = 0
        for device in range(count):
            start = device * self.size
            entry = [start % LANES]
            target = 0
            parts = shard_parts(start, start + self.size, SEGMENTS)
            for index, row0, rows, line in parts:
                width = SEGMENTS[index][2] // LANES
                tiles = round_up(rows, 8) // 8
                self.blocks[index].append((device, target, row0, tiles * 8))
                entry += [WIDTHS.index(width), FRONT + line, tiles, target]
                target += tiles * 8 * width
            longest = max(longest, target)
            entry += [-1, 0, 0, 0] * (2 - len(parts))
            table.append(entry)
        self.buffer = round_up(longest, 16)
        self.lay_table = np.array(table, np.int32)
        table = []
        self.most = max(
            len(shard_parts(d * self.size, (d + 1) * self.size, PIECES)) for d in range(count)
        )
        for device in range(count):
            start = device * self.size
            entry = [start % LANES]
            parts = shard_parts(start, start + self.size, PIECES)
            for index, row0, rows, line in parts:
                skew = row0 % 8
                line -= skew * (PIECES[index][2] // LANES)
                entry += [index, GRAD_FRONT + line, -(-(rows + skew) // CHUNK), row0 - skew]
            entry += [-1, 0, 0, 0] * (self.most - len(parts))
            table.append(entry)
        self.grad_table = np.array(table, np.int32)
        self.grad_scratch = GRAD_FRONT + self.lines + CHUNK * max(WIDTHS) + 16


def lay_kernel(plan, tab_ref, x_ref, out_ref, line_ref):
    shift = tab_ref[0]
    lane = lax.broadcasted_iota(jnp.int32, (CHUNK + 8, LANES), 1)
    line_ref[pl.ds(0, FRONT), :] = jnp.zeros((FRONT, LANES), F32)
    tail = plan.scratch - FRONT - plan.lines
    line_ref[pl.ds(FRONT + plan.lines, tail), :] = jnp.zeros((tail, LANES), F32)

    def align(step, carry):
        base = pl.multiple_of(step * CHUNK, 8)
        here = pltpu.roll(x_ref[pl.ds(base, CHUNK + 8), :], shift, 1)
        above = pltpu.roll(here, 1, 0)
        both = jnp.where(lane >= shift, here, above)
        line_ref[pl.ds(pl.multiple_of(FRONT + base, 8), CHUNK), :] = both[8:]
        return carry

    lax.fori_loop(0, plan.lines // CHUNK, align, 0)
    for part in range(2):
        kind, base, tiles, target = (tab_ref[1 + 4 * part + i] for i in range(4))
        for index, width in enumerate(WIDTHS):

            @pl.when(kind == index)
            def _():
                def move(tile, carry):
                    row = base + tile * (8 * width)
                    goal = target + tile * (8 * width)
                    for pair in range(0, width, 2):
                        two = jnp.concatenate(
                            [
                                line_ref[pl.ds(row + pair, 8, stride=width), :],
                                line_ref[pl.ds(row + pair + 1, 8, stride=width), :],
                            ],
                            0,
                        )
                        out_ref[pl.ds(pl.multiple_of(goal + 8 * pair, 16), 16), :] = two.astype(BF16)
                    return carry

                lax.fori_loop(0, tiles, move, 0)


def lay_out(plan, table, flat):
    padded = jnp.pad(flat, (8 * LANES, plan.lines * LANES - plan.size))
    lines = padded.reshape(8 + plan.lines, LANES)
    return pl.pallas_call(
        functools.partial(lay_kernel, plan),
        out_shape=jax.ShapeDtypeStruct((plan.buffer, LANES), BF16),
        in_specs=[
            pl.BlockSpec(memory_space=pltpu.SMEM),
            pl.BlockSpec(memory_space=pltpu.VMEM),
        ],
        out_specs=pl.BlockSpec(memory_space=pltpu.VMEM),
        scratch_shapes=[pltpu.VMEM((plan.scratch, LANES), F32)],
        compiler_params=pltpu.CompilerParams(vmem_limit_bytes=24 * 1024 * 1024),
    )(table, lines)


def blocks_of(plan, index, first, count):
    return [
        (device, target, row0 - first, rows)
        for device, target, row0, rows in plan.blocks[index]
        if row0 < first + count and row0 + rows > first
    ]


class Rows:
    def __init__(self, plan, gathered, index, first, count):
        width = SEGMENTS[index][2] // LANES
        half = plan.count // 2
        self.count = count
        self.blocks = [block[2:] for block in blocks_of(plan, index, first, count)]
        pieces = [
            gathered[device % half, device // half, target : target + rows * width]
            for device, target, _, rows in blocks_of(plan, index, first, count)
        ]
        tiles = jnp.concatenate(pieces, 0).reshape(-1, width, 8, LANES)
        self.matrix = tiles.transpose(0, 2, 1, 3).reshape(-1, width * LANES)

    def spread(self, values):
        before = max(0, -min(row0 for row0, _ in self.blocks))
        after = max(0, max(row0 + rows for row0, rows in self.blocks) - self.count)
        padded = jnp.pad(values, ((0, 0), (before, after)))
        return jnp.concatenate(
            [padded[:, before + row0 : before + row0 + rows] for row0, rows in self.blocks], 1
        )

    def times(self, values):
        return product(self.spread(values), self.matrix)

    def back(self, values):
        wide = product_t(values, self.matrix)
        total, place = 0.0, 0
        for row0, rows in self.blocks:
            low, high = max(0, row0), min(self.count, row0 + rows)
            piece = wide[:, place + low - row0 : place + high - row0]
            total = total + jnp.pad(piece, ((0, 0), (low, self.count - high)))
            place += rows
        return total

    def folded(self):
        total, place = 0.0, 0
        for row0, rows in self.blocks:
            low, high = max(0, row0), min(self.count, row0 + rows)
            piece = self.matrix[place + low - row0 : place + high - row0]
            total = total + jnp.pad(piece, ((low, self.count - high), (0, 0)))
            place += rows
        return total


def product(left, right):
    return jnp.dot(left, right, preferred_element_type=F32)


def product_t(left, right):
    return lax.dot_general(
        left, right, (((left.ndim - 1,), (1,)), ((), ())), preferred_element_type=F32
    )


def activate(values):
    return jax.nn.gelu(values, approximate=False)


def gelu_back(values, grad):
    return jax.vjp(activate, values)[1](grad)[0]


def normalised(values):
    centred = values - jnp.mean(values, -1, keepdims=True)
    scale = lax.rsqrt(jnp.mean(centred * centred, -1, keepdims=True) + 1e-06)
    return centred * scale, scale


def norm_back(grad, gain, unit, scale):
    inner = grad * gain
    return scale * (
        inner
        - jnp.mean(inner, -1, keepdims=True)
        - unit * jnp.mean(inner * unit, -1, keepdims=True)
    )


def head_mask():
    return jnp.arange(HEADS)[:, None] == jnp.arange(D)[None, :] // HDIM


def trunk_forward(patches, wide, qkv_w):
    views = patches.shape[0]
    position = wide[PD : PD + NTOK].astype(F32)
    norms = wide[PD + NTOK :].astype(F32)
    embedded = product(patches, wide[:PD])
    unit, scale = normalised(embedded + position[1:])
    normed = (unit * norms[0] + norms[1]).astype(BF16)
    class_unit, class_scale = normalised(position[:1])
    class_normed = (class_unit * norms[0] + norms[1]).astype(BF16)
    query = product(class_normed, qkv_w[:, :D]).astype(BF16)
    by_head = jnp.where(head_mask(), query, 0).astype(BF16)
    looked = product_t(by_head, qkv_w[:, D : 2 * D]).astype(BF16)
    temper = HDIM ** (-0.5)
    scores = jnp.einsum("hd,vkd->vhk", looked, normed, preferred_element_type=F32) * temper
    class_score = product_t(looked, class_normed)[None] * temper
    top = jnp.maximum(jnp.max(scores, -1, keepdims=True), class_score)
    total = jnp.sum(jnp.exp(scores - top), -1, keepdims=True) + jnp.exp(class_score - top)
    row_top = top + jnp.log(total)
    probs = jnp.exp(scores - row_top)
    class_probs = jnp.exp(class_score - row_top)
    mixed = jnp.einsum("vhk,vkd->vhd", probs.astype(BF16), normed, preferred_element_type=F32)
    mixed = mixed + class_probs.astype(BF16).astype(F32) * class_normed.astype(F32)
    mixed = mixed.astype(BF16)
    valued = product(mixed.reshape(-1, D), qkv_w[:, 2 * D :]).reshape(views, HEADS, D)
    attended = jnp.sum(jnp.where(head_mask(), valued, 0.0), 1).astype(BF16)
    kept = (unit, scale, normed, class_unit, class_scale, class_normed, query, looked)
    return position[0], attended, mixed, kept + (probs, class_probs)


def trunk_backward(patches, wide, qkv_w, grad_att, grad_class, kept):
    unit, scale, normed, class_unit, class_scale, class_normed, query, looked = kept[:8]
    probs, class_probs = kept[8:]
    views = patches.shape[0]
    norms = wide[PD + NTOK :].astype(F32)
    temper = HDIM ** (-0.5)
    spread = jnp.where(head_mask(), grad_att[:, None], 0).astype(BF16).reshape(-1, D)
    back = product_t(spread, qkv_w[:, 2 * D :]).astype(BF16).reshape(views, HEADS, D)
    grad_probs = jnp.einsum("vhd,vkd->vhk", back, normed, preferred_element_type=F32)
    class_grad = jnp.sum(
        back.astype(F32) * class_normed.astype(F32), -1, keepdims=True
    )
    delta = jnp.sum(probs * grad_probs, -1, keepdims=True) + class_probs * class_grad
    grad_scores = (probs * (grad_probs - delta)).astype(BF16)
    class_scores = (class_probs * (class_grad - delta)).astype(BF16)
    reach = jnp.einsum("vhk,vkd->vhd", grad_scores, normed, preferred_element_type=F32)
    reach = (reach + class_scores.astype(F32) * class_normed.astype(F32)) * temper
    keyed = product(reach.astype(BF16).reshape(-1, D), qkv_w[:, D : 2 * D])
    keyed = keyed.reshape(views, HEADS, D)
    grad_query = jnp.sum(jnp.where(head_mask(), keyed, 0.0), 1).astype(BF16)
    left = jnp.concatenate([grad_scores, probs.astype(BF16)], 1)
    right = jnp.concatenate(
        [jnp.broadcast_to((looked.astype(F32) * temper).astype(BF16), back.shape), back], 1
    )
    grad_normed = jnp.einsum("vhk,vhd->vkd", left, right, preferred_element_type=F32)
    class_left = jnp.concatenate([class_scores, class_probs.astype(BF16)], 1).astype(F32)
    class_row = jnp.sum(class_left * right.astype(F32), 1) + product_t(grad_query, qkv_w[:, :D])
    gain = jnp.sum(grad_normed * unit, (0, 1)) + jnp.sum(class_row * class_unit, 0)
    offset = jnp.sum(grad_normed, (0, 1)) + jnp.sum(class_row, 0)
    grad_stream = norm_back(grad_normed, norms[0], unit, scale)
    class_stream = norm_back(class_row, norms[0], class_unit, class_scale) + grad_class
    grad_patch = lax.dot_general(
        patches.reshape(-1, PD),
        grad_stream.astype(BF16).reshape(-1, D),
        (((0,), (0,)), ((), ())),
        preferred_element_type=F32,
    )
    return (
        grad_patch,
        jnp.sum(class_stream, 0, keepdims=True),
        jnp.sum(grad_stream, 0),
        gain[None],
        offset[None],
        jnp.sum(grad_query.astype(F32), 0, keepdims=True),
        jnp.sum(reach, 0),
    )


def grad_kernel(plan, spans, tab_ref, rows_ref, cols_ref, wide_ref, qkv_ref, out_ref, line_ref):
    for part in range(plan.most):
        kind, base, chunks, row0 = (tab_ref[1 + 4 * part + i] for i in range(4))
        for index, (_, _, cols) in enumerate(PIECES):
            width = cols // LANES

            @pl.when(kind == index)
            def _():
                def move(step, carry):
                    row = pl.multiple_of(row0 + step * CHUNK, 8)
                    goal = base + step * (CHUNK * width)
                    if spans[index] is None:
                        source = qkv_ref if index == 1 else wide_ref
                        first = row if index == 0 else row + FINAL_ROW
                        if index == 1:
                            first = step * CHUNK
                        block = source[pl.ds(pl.multiple_of(first, 8), CHUNK), :]
                    else:
                        first, column = spans[index]
                        left = rows_ref[pl.ds(pl.multiple_of(first + row, 8), CHUNK), :].astype(BF16)
                        block = product(left, cols_ref[:, column : column + cols])
                    for tile in range(width):
                        line_ref[pl.ds(goal + tile, CHUNK, stride=width), :] = block[
                            :, tile * LANES : (tile + 1) * LANES
                        ]
                    return carry

                lax.fori_loop(0, chunks, move, 0)

    shift = tab_ref[0]
    turn = lax.rem(LANES - shift, LANES)
    lane = lax.broadcasted_iota(jnp.int32, (CHUNK + 8, LANES), 1)

    def align(step, carry):
        start = pl.multiple_of(step * CHUNK, 8)
        here = pltpu.roll(line_ref[pl.ds(pl.multiple_of(GRAD_FRONT + start, 8), CHUNK + 8), :], turn, 1)
        below = pltpu.roll(here, CHUNK + 7, 0)
        both = jnp.where(lane < LANES - shift, here, below)
        out_ref[pl.ds(start, CHUNK), :] = both[:CHUNK]
        return carry

    lax.fori_loop(0, plan.lines // CHUNK, align, 0)


def adam_update(weight, grad, first, second, rate):
    first = BETA_FIRST * first + (1.0 - BETA_FIRST) * grad
    second = BETA_SECOND * second + (1.0 - BETA_SECOND) * grad * grad
    stepped = (
        first
        / (1.0 - BETA_FIRST**STEP)
        / (jnp.sqrt(second / (1.0 - BETA_SECOND**STEP)) + ADAM_EPSILON)
    )
    return (weight - rate * (stepped + WEIGHT_DECAY * weight), first, second)


def per_device(
    plan,
    params,
    first_moment,
    second_moment,
    teacher,
    protos,
    proto_first,
    proto_second,
    teacher_protos,
    center,
    patches,
    partner,
):
    reps, groups = lax.axis_size("rep"), lax.axis_size("grp")
    count, half = reps * groups, reps * groups // 2
    rep, grp = lax.axis_index("rep"), lax.axis_index("grp")
    device = rep * groups + grp
    low = rep < reps // 2
    halves = [list(range(half)), list(range(half, count))]
    swap = [(r, (r + reps // 2) % reps) for r in range(reps)]
    own_views = patches.shape[0]
    views = 2 * own_views

    def trade(values):
        return lax.ppermute(values, "rep", swap)

    def in_order(values):
        other = trade(values)
        return jnp.where(low, values, other), jnp.where(low, other, values)

    table = jnp.asarray(plan.lay_table)[device]
    kept = lay_out(plan, table, jnp.where(low, params, teacher))
    given = trade(lay_out(plan, table, jnp.where(low, teacher, params)))
    shards = jnp.stack([jnp.where(low, kept, given), jnp.where(low, given, kept)])
    gathered = lax.all_gather(shards, BOTH, axis=0, axis_index_groups=halves)
    pixels = jnp.concatenate(in_order(patches), 0)
    places = in_order(partner.astype(F32))
    tables = lax.all_gather(
        jnp.stack([protos, teacher_protos]).astype(BF16), "rep", axis=1, tiled=True
    ).astype(F32)

    def columns_of(values):
        scale = lax.rsqrt(jnp.sum(values * values, 0, keepdims=True) + 1e-06)
        return (values * scale).astype(BF16), scale

    columns, column_scale = columns_of(tables[0])
    teacher_columns = columns_of(tables[1])[0]

    wide = Rows(plan, gathered, 0, 0, PD + NTOK + 4).folded()
    qkv_w = Rows(plan, gathered, 1, 0, D).folded()
    out_w = Rows(plan, gathered, 2, 0, D)
    up_w = Rows(plan, gathered, 3, 0, D)
    down_w = Rows(plan, gathered, 4, 0, F)
    final = Rows(plan, gathered, 4, F, 2).folded().astype(F32)
    head_one = Rows(plan, gathered, 5, 0, D)
    head_two = Rows(plan, gathered, 5, D, H)
    head_three = Rows(plan, gathered, 6, 0, H)
    norms = wide[PD + NTOK :].astype(F32)

    class_row, attended, mixed, trunk_kept = trunk_forward(pixels, wide, qkv_w)
    middle = class_row + out_w.times(attended)
    unit_two, scale_two = normalised(middle)
    normed_two = (unit_two * norms[2] + norms[3]).astype(BF16)
    hidden = up_w.times(normed_two)
    act = activate(hidden).astype(BF16)
    stream = middle + down_w.times(act)
    unit_three, scale_three = normalised(stream)
    cls = (unit_three * final[0] + final[1]).astype(BF16)
    pre_one = head_one.times(cls)
    first = activate(pre_one).astype(BF16)
    pre_two = head_two.times(first)
    second = activate(pre_two).astype(BF16)
    bottle = head_three.times(second)
    bottle_scale = lax.rsqrt(jnp.sum(bottle * bottle, -1, keepdims=True) + 1e-06)
    rows = (bottle * bottle_scale).astype(BF16)

    here = jnp.arange(views)
    place = jnp.concatenate([places[0], places[1] + own_views]).astype(jnp.int32)
    place = jnp.where(low, here, place)
    rows = product((place[:, None] == here[None, :]).astype(BF16), rows).astype(BF16)
    all_rows = lax.all_to_all(
        jnp.broadcast_to(rows[None], (count, views, B)), BOTH, 0, 0
    )
    student_rows = all_rows[:half].reshape(-1, B)
    teacher_rows = all_rows[half:].reshape(-1, B)

    teacher_logits = product(teacher_rows, teacher_columns)
    new_center = CENTER_MOMENTUM * center + (1.0 - CENTER_MOMENTUM) * jnp.mean(teacher_logits, 0)
    exp_teacher = jnp.exp((teacher_logits - center) / TEACHER_TEMP)
    scaled = product(student_rows, columns) / STUDENT_TEMP
    exp_student = jnp.exp(scaled)
    sums = jnp.stack(
        [jnp.sum(exp_student, 1), jnp.sum(exp_teacher, 1), jnp.sum(exp_teacher * scaled, 1)]
    )
    band = groups * views
    start = lax.rem(rep, reps // 2) * band
    pulls = jnp.concatenate(
        [
            lax.dynamic_slice_in_dim(exp_student, start, band, 0),
            lax.dynamic_slice_in_dim(exp_teacher, start, band, 0),
        ],
        0,
    )
    pulls = lax.dot_general(
        pulls, columns.astype(F32), (((1,), (1,)), ((), ())), precision=PRECISE
    ).reshape(2, groups, views * B)
    note = jnp.concatenate(
        [
            pulls.transpose(1, 0, 2).reshape(groups, -1),
            jnp.broadcast_to(sums.reshape(1, -1), (groups, sums.size)),
        ],
        1,
    ).reshape(groups, -1, LANES)
    note = jnp.sum(lax.all_to_all(note, "grp", 0, 0), 0).reshape(-1)
    pulls = note[: 2 * views * B].reshape(2, views, B)
    sum_student, sum_teacher, crossed = note[2 * views * B :].reshape(3, -1)
    loss_value = jnp.sum(jnp.log(sum_student) - crossed / sum_teacher)
    own = lax.rem(device, half) * views
    own_student = lax.dynamic_slice_in_dim(sum_student, own, views)[:, None]
    own_teacher = lax.dynamic_slice_in_dim(sum_teacher, own, views)[:, None]
    grad_rows = (pulls[0] / own_student - pulls[1] / own_teacher) / STUDENT_TEMP
    grad_rows = jnp.where(low, grad_rows, 0.0).astype(BF16).astype(F32)

    grad_logits = (
        exp_student / sum_student[:, None] - exp_teacher / sum_teacher[:, None]
    ) / STUDENT_TEMP
    grad_columns = lax.dot_general(
        student_rows.astype(F32), grad_logits, (((0,), (0,)), ((), ())), precision=PRECISE
    )
    inner = jnp.sum(grad_columns * tables[0], 0, keepdims=True)
    depth = protos.shape[0]
    grad_protos = (
        lax.dynamic_slice_in_dim(grad_columns, rep * depth, depth, 0) * column_scale
        - protos.astype(BF16).astype(F32) * column_scale**3 * inner
    )

    grad_bottle = (
        grad_rows * bottle_scale
        - bottle * bottle_scale**3 * jnp.sum(grad_rows * bottle, -1, keepdims=True)
    ).astype(BF16)
    grad_two = gelu_back(pre_two, head_three.back(grad_bottle)).astype(BF16)
    grad_one = gelu_back(pre_one, head_two.back(grad_two)).astype(BF16)
    grad_cls = head_one.back(grad_one)
    head_pack = jnp.concatenate([cls, first, second, grad_bottle, grad_two, grad_one], 1)
    head_pack = lax.all_gather(head_pack, BOTH, axis=0)
    grad_stream = norm_back(grad_cls, final[0], unit_three, scale_three)
    grad_branch = grad_stream.astype(BF16)
    grad_hidden = gelu_back(hidden, down_w.back(grad_branch)).astype(BF16)
    grad_normed = up_w.back(grad_hidden)
    grad_middle = grad_stream + norm_back(grad_normed, norms[2], unit_two, scale_two)
    grad_mixed = grad_middle.astype(BF16)
    grad_att = out_w.back(grad_mixed).astype(BF16)
    body_pack = jnp.concatenate(
        [attended, normed_two, act, grad_mixed, grad_hidden, grad_branch, grad_att], 1
    )
    body_pack = lax.all_gather(body_pack, BOTH, axis=0)
    mixed_pack = lax.all_gather(mixed, BOTH, axis=0)

    pieces = trunk_backward(pixels, wide, qkv_w, grad_att, grad_middle, trunk_kept)
    partial = jnp.concatenate(
        pieces[:5]
        + (
            jnp.sum(grad_normed * unit_two, 0, keepdims=True),
            jnp.sum(grad_normed, 0, keepdims=True),
            jnp.zeros((FINAL_ROW - PD - NTOK - 4, D), F32),
            jnp.sum(grad_cls * unit_three, 0, keepdims=True),
            jnp.sum(grad_cls, 0, keepdims=True),
        )
        + pieces[5:],
        0,
    )
    depth = round_up(-(-partial.shape[0] // half), 8)
    partial = jnp.pad(partial, ((0, half * depth - partial.shape[0]), (0, 0)))
    partial = lax.all_to_all(
        partial.astype(BF16).reshape(half, depth, D), BOTH, 0, 0, axis_index_groups=halves
    )
    partial = jnp.sum(partial.astype(F32), 0)
    summed = lax.all_gather(partial, BOTH, axis=0)[:half].reshape(-1, D)

    head_rows = head_pack[:half].reshape(half * views, -1)
    body_rows = body_pack[:half].reshape(half * views, -1)
    mixed_rows = mixed_pack[:half].reshape(half * views, HEADS, D)
    rows_all = jnp.concatenate(
        [body_rows[:, : 2 * D + F], head_rows[:, : D + 2 * H]], 1
    ).astype(F32)
    rows_all = jnp.pad(rows_all.T, ((0, CHUNK), (0, 0)))
    cols_all = jnp.concatenate(
        [body_rows[:, 2 * D + F : 4 * D + 2 * F], head_rows[:, D + 2 * H :]], 1
    )
    spans = [
        None,
        None,
        (0, 0),
        (D, D),
        (2 * D, D + F),
        None,
        (2 * D + F, 2 * D + F + B + H),
        (3 * D + F, 2 * D + F + B),
        (3 * D + F + H, 2 * D + F),
    ]
    qkv_row = jnp.asarray(
        [
            max([0] + [p[1] // 8 * 8 for p in shard_parts(d * plan.size, (d + 1) * plan.size, PIECES) if p[0] == 1])
            for d in range(count)
        ],
        jnp.int32,
    )[device]
    qkv_rows = round_up(min(D, -(-plan.size // (3 * D)) + 9), CHUNK)
    base = FINAL_ROW
    sum_query, reach = summed[base + 2], summed[base + 3 : base + 3 + HEADS]

    def slab(values):
        return lax.dynamic_slice_in_dim(
            jnp.pad(values, ((0, 0),) * (values.ndim - 1) + ((0, qkv_rows),)),
            qkv_row,
            qkv_rows,
            values.ndim - 1,
        )

    class_normed, query = trunk_kept[5].astype(F32), trunk_kept[6].astype(F32)
    qkv_q = slab(class_normed).T * sum_query[None]
    qkv_k = lax.dot_general(
        slab(reach), jnp.where(head_mask(), query, 0.0), (((0,), (0,)), ((), ())), precision=PRECISE
    )
    grad_att_rows = body_rows[:, 4 * D + 2 * F :].reshape(-1, HEADS, HDIM)
    qkv_v = jnp.einsum(
        "vhd,vhc->dhc", slab(mixed_rows), grad_att_rows, preferred_element_type=F32
    ).reshape(qkv_rows, D)
    qkv_grad = jnp.concatenate([qkv_q, qkv_k, qkv_v], 1)
    wide_grad = jnp.pad(summed[: base + 2], ((0, 8 * CHUNK), (0, 0)))
    flat_lines = pl.pallas_call(
        functools.partial(grad_kernel, plan, spans),
        out_shape=jax.ShapeDtypeStruct((plan.lines, LANES), F32),
        in_specs=[pl.BlockSpec(memory_space=pltpu.SMEM)]
        + [pl.BlockSpec(memory_space=pltpu.VMEM)] * 4,
        out_specs=pl.BlockSpec(memory_space=pltpu.VMEM),
        scratch_shapes=[pltpu.VMEM((plan.grad_scratch, LANES), F32)],
        compiler_params=pltpu.CompilerParams(vmem_limit_bytes=48 * 1024 * 1024),
    )(jnp.asarray(plan.grad_table)[device], rows_all, cols_all, wide_grad, qkv_grad)
    grad_flat = flat_lines.reshape(-1)[: plan.size]

    squares = jnp.sum(grad_flat * grad_flat) + jnp.sum(grad_protos * grad_protos)
    squares = lax.all_to_all(
        jnp.broadcast_to(squares.reshape(1, 1, 1), (count, 1, LANES)), BOTH, 0, 0
    )
    grad_norm = jnp.sqrt(jnp.sum(squares[:, 0, 0]))
    factor = jnp.minimum(1.0, CLIP_NORM / (grad_norm + 1e-06))
    new_params, new_first, new_second = adam_update(
        params, grad_flat * factor, first_moment, second_moment, LEARNING_RATE
    )
    new_protos, new_proto_first, new_proto_second = adam_update(
        protos, grad_protos * factor, proto_first, proto_second, PROTO_RATE
    )
    new_teacher = TEACHER_MOMENTUM * teacher + (1.0 - TEACHER_MOMENTUM) * new_params
    new_teacher_protos = TEACHER_MOMENTUM * teacher_protos + (1.0 - TEACHER_MOMENTUM) * new_protos
    return (
        new_params,
        new_first,
        new_second,
        new_teacher,
        new_protos,
        new_proto_first,
        new_proto_second,
        new_teacher_protos,
        new_center,
        loss_value,
        grad_norm,
    )


def solution(mesh):
    placed = (
        P(BOTH),
        P(BOTH),
        P(BOTH),
        P(BOTH),
        P("rep", "grp"),
        P("rep", "grp"),
        P("rep", "grp"),
        P("rep", "grp"),
        P("grp"),
        P(BOTH, None, None),
        P(BOTH),
    )
    plan = Plan(math.prod(mesh.shape.values()))
    return jax.shard_map(
        functools.partial(per_device, plan),
        mesh=mesh,
        in_specs=placed,
        out_specs=placed[:9] + (P(), P()),
        check_vma=False,
    )
```

```python
import functools

import jax
import jax.numpy as jnp
import numpy as np
from jax import lax
from jax.experimental import pallas as pl
from jax.experimental.pallas import tpu as pltpu
from jax.sharding import PartitionSpec as P

D = 768
HEADS = 12
HDIM = 64
F = 3072
PD = 768
NTOK = 197
H = 2048
B = 256
STEP = 10
NPATCH = NTOK - 1

PRECISE = lax.Precision.HIGHEST
STUDENT_TEMP = 0.1
TEACHER_TEMP = 0.04
CENTER_MOMENTUM = 0.9
TEACHER_MOMENTUM = 0.8
CLIP_NORM = 0.05
LEARNING_RATE = 0.03
PROTO_RATE = 0.6
BETA_FIRST = 0.9
BETA_SECOND = 0.999
ADAM_EPSILON = 1e-08
WEIGHT_DECAY = 0.04
BOTH = ("rep", "grp")
LANES = 128
F32 = jnp.float32
BF16 = jnp.bfloat16

SEGMENTS = []
_offset = 0
for _rows, _cols in ((PD + NTOK + 4, D), (D, 3 * D), (D, D), (D, F), (F + 2, D), (D + H, H), (H, B)):
    SEGMENTS.append((_offset, _rows, _cols))
    _offset += _rows * _cols
PFLAT = _offset
WIDTHS = sorted({cols // LANES for _, _, cols in SEGMENTS})

PIECES = []
_offset = 0
for _rows, _cols in (
    (PD + NTOK + 4, D),
    (D, 3 * D),
    (D, D),
    (D, F),
    (F, D),
    (2, D),
    (D, H),
    (H, H),
    (H, B),
):
    PIECES.append((_offset, _rows, _cols))
    _offset += _rows * _cols
FRONT = 24
GRAD_FRONT = 8 * FRONT
CHUNK = 64


def round_up(value, step):
    return -(-value // step) * step


def shard_parts(start, stop, table):
    parts = []
    line0 = start // LANES
    for index, (offset, rows, cols) in enumerate(table):
        low, high = max(start, offset), min(stop, offset + rows * cols)
        if low >= high:
            continue
        row0 = (low - offset) // cols
        row1 = -(-(high - offset) // cols)
        parts.append((index, row0, row1 - row0, (offset + row0 * cols) // LANES - line0))
    return parts


FINAL_ROW = round_up(PD + NTOK + 4, 8)


class Plan:
    def __init__(self, reps, groups):
        count = reps * groups
        self.count, self.groups = count, groups
        self.size = PFLAT // count
        self.lines = round_up(-(-self.size // LANES) + 1, CHUNK)
        self.scratch = FRONT + self.lines + 8 * max(WIDTHS) + 16
        table = []
        self.blocks = [[] for _ in SEGMENTS]
        longest = 0
        for device in range(count):
            start = device * self.size
            entry = [start % LANES]
            target = 0
            parts = shard_parts(start, start + self.size, SEGMENTS)
            for index, row0, rows, line in parts:
                width = SEGMENTS[index][2] // LANES
                tiles = round_up(rows, 8) // 8
                self.blocks[index].append((device, target, row0, tiles * 8))
                entry += [WIDTHS.index(width), FRONT + line, tiles, target]
                target += tiles * 8 * width
            longest = max(longest, target)
            entry += [-1, 0, 0, 0] * (2 - len(parts))
            table.append(entry)
        self.buffer = round_up(longest, 16)
        self.lay_table = np.array(table, np.int32)
        self.grad_table = self.tabulate(lambda index: index > 1)
        self.late_table = self.tabulate(lambda index: index < 2)
        edge = SEGMENTS[0][1] * SEGMENTS[0][2]
        self.odd_owner = any(
            device * self.size < edge and self.place(device)[1] for device in range(count)
        )
        self.grad_scratch = GRAD_FRONT + self.lines + CHUNK * max(WIDTHS) + 16


    def place(self, device):
        rep, grp = divmod(device, self.groups)
        return rep // 2 * self.groups + grp, rep % 2

    def tabulate(self, chosen):
        table = []
        for device in range(self.count):
            start = device * self.size
            entry = []
            for index, row0, rows, line in shard_parts(start, start + self.size, PIECES):
                if not chosen(index):
                    continue
                skew = row0 % 8
                line -= skew * (PIECES[index][2] // LANES)
                entry += [index, GRAD_FRONT + line, -(-(rows + skew) // CHUNK), row0 - skew]
            table.append(entry)
        most = max(len(entry) for entry in table) // 4
        for device, entry in enumerate(table):
            entry += [-1, 0, 0, 0] * (most - len(entry) // 4)
            entry.insert(0, device * self.size % LANES)
        return np.array(table, np.int32)


def lay_kernel(plan, tab_ref, x_ref, out_ref, line_ref):
    shift = tab_ref[0]
    lane = lax.broadcasted_iota(jnp.int32, (CHUNK + 8, LANES), 1)
    line_ref[pl.ds(0, FRONT), :] = jnp.zeros((FRONT, LANES), F32)
    tail = plan.scratch - FRONT - plan.lines
    line_ref[pl.ds(FRONT + plan.lines, tail), :] = jnp.zeros((tail, LANES), F32)

    def align(step, carry):
        base = pl.multiple_of(step * CHUNK, 8)
        here = pltpu.roll(x_ref[pl.ds(base, CHUNK + 8), :], shift, 1)
        above = pltpu.roll(here, 1, 0)
        both = jnp.where(lane >= shift, here, above)
        line_ref[pl.ds(pl.multiple_of(FRONT + base, 8), CHUNK), :] = both[8:]
        return carry

    lax.fori_loop(0, plan.lines // CHUNK, align, 0)
    for part in range(2):
        kind, base, tiles, target = (tab_ref[1 + 4 * part + i] for i in range(4))
        for index, width in enumerate(WIDTHS):

            @pl.when(kind == index)
            def _():
                def move(tile, carry):
                    row = base + tile * (8 * width)
                    goal = target + tile * (8 * width)
                    for pair in range(0, width, 2):
                        two = jnp.concatenate(
                            [
                                line_ref[pl.ds(row + pair, 8, stride=width), :],
                                line_ref[pl.ds(row + pair + 1, 8, stride=width), :],
                            ],
                            0,
                        )
                        out_ref[pl.ds(pl.multiple_of(goal + 8 * pair, 16), 16), :] = two.astype(BF16)
                    return carry

                lax.fori_loop(0, tiles, move, 0)


def lay_out(plan, table, flat):
    padded = jnp.pad(flat, (8 * LANES, plan.lines * LANES - plan.size))
    lines = padded.reshape(8 + plan.lines, LANES)
    return pl.pallas_call(
        functools.partial(lay_kernel, plan),
        out_shape=jax.ShapeDtypeStruct((plan.buffer, LANES), BF16),
        in_specs=[
            pl.BlockSpec(memory_space=pltpu.SMEM),
            pl.BlockSpec(memory_space=pltpu.VMEM),
        ],
        out_specs=pl.BlockSpec(memory_space=pltpu.VMEM),
        scratch_shapes=[pltpu.VMEM((plan.scratch, LANES), F32)],
        compiler_params=pltpu.CompilerParams(vmem_limit_bytes=24 * 1024 * 1024),
    )(table, lines)


def blocks_of(plan, index, first, count):
    return [
        (device, target, row0 - first, rows)
        for device, target, row0, rows in plan.blocks[index]
        if row0 < first + count and row0 + rows > first
    ]


MATRICES = (
    (0, 0, PD + NTOK + 4),
    (1, 0, D),
    (2, 0, D),
    (3, 0, D),
    (4, 0, F),
    (4, F, 2),
    (5, 0, D),
    (5, D, H),
    (6, 0, H),
)


class Rows:
    def __init__(self, plan, gathered, which):
        index, first, self.count = MATRICES[which]
        width = SEGMENTS[index][2] // LANES
        blocks = blocks_of(plan, index, first, self.count)
        self.blocks = [block[2:] for block in blocks]
        pieces = [
            gathered[plan.place(device)][target : target + rows * width]
            for device, target, _, rows in blocks
        ]
        tiles = jnp.concatenate(pieces, 0).reshape(-1, width, 8, LANES)
        self.matrix = tiles.transpose(0, 2, 1, 3).reshape(-1, width * LANES)

    def spread(self, values):
        before = max(0, -min(row0 for row0, _ in self.blocks))
        after = max(0, max(row0 + rows for row0, rows in self.blocks) - self.count)
        padded = jnp.pad(values, ((0, 0), (before, after)))
        return jnp.concatenate(
            [padded[:, before + row0 : before + row0 + rows] for row0, rows in self.blocks], 1
        )

    def times(self, values):
        return product(self.spread(values), self.matrix)

    def back(self, values):
        wide = product_t(values, self.matrix)
        total, place = 0.0, 0
        for row0, rows in self.blocks:
            low, high = max(0, row0), min(self.count, row0 + rows)
            piece = wide[:, place + low - row0 : place + high - row0]
            total = total + jnp.pad(piece, ((0, 0), (low, self.count - high)))
            place += rows
        return total

    def folded(self):
        total, place = 0.0, 0
        for row0, rows in self.blocks:
            low, high = max(0, row0), min(self.count, row0 + rows)
            piece = self.matrix[place + low - row0 : place + high - row0]
            total = total + jnp.pad(piece, ((low, self.count - high), (0, 0)))
            place += rows
        return total


def product(left, right):
    return jnp.dot(left, right, preferred_element_type=F32)


def product_t(left, right):
    return lax.dot_general(
        left, right, (((left.ndim - 1,), (1,)), ((), ())), preferred_element_type=F32
    )


def activate(values):
    return jax.nn.gelu(values, approximate=False)


def gelu_back(values, grad):
    return jax.vjp(activate, values)[1](grad)[0]


def normalised(values):
    centred = values - jnp.mean(values, -1, keepdims=True)
    scale = lax.rsqrt(jnp.mean(centred * centred, -1, keepdims=True) + 1e-06)
    return centred * scale, scale


def norm_back(grad, gain, unit, scale):
    inner = grad * gain
    return scale * (
        inner
        - jnp.mean(inner, -1, keepdims=True)
        - unit * jnp.mean(inner * unit, -1, keepdims=True)
    )


def head_mask():
    return jnp.arange(HEADS)[:, None] == jnp.arange(D)[None, :] // HDIM


def trunk_forward(patches, wide, qkv_w):
    views = patches.shape[0]
    position = wide[PD : PD + NTOK].astype(F32)
    norms = wide[PD + NTOK :].astype(F32)
    embedded = product(patches, wide[:PD])
    unit, scale = normalised(embedded + position[1:])
    normed = (unit * norms[0] + norms[1]).astype(BF16)
    class_unit, class_scale = normalised(position[:1])
    class_normed = (class_unit * norms[0] + norms[1]).astype(BF16)
    query = product(class_normed, qkv_w[:, :D]).astype(BF16)
    by_head = jnp.where(head_mask(), query, 0).astype(BF16)
    looked = product_t(by_head, qkv_w[:, D : 2 * D]).astype(BF16)
    temper = HDIM ** (-0.5)
    scores = jnp.einsum("hd,vkd->vhk", looked, normed, preferred_element_type=F32) * temper
    class_score = product_t(looked, class_normed)[None] * temper
    top = jnp.maximum(jnp.max(scores, -1, keepdims=True), class_score)
    total = jnp.sum(jnp.exp(scores - top), -1, keepdims=True) + jnp.exp(class_score - top)
    row_top = top + jnp.log(total)
    probs = jnp.exp(scores - row_top)
    class_probs = jnp.exp(class_score - row_top)
    mixed = jnp.einsum("vhk,vkd->vhd", probs.astype(BF16), normed, preferred_element_type=F32)
    mixed = mixed + class_probs.astype(BF16).astype(F32) * class_normed.astype(F32)
    mixed = mixed.astype(BF16)
    valued = product(mixed.reshape(-1, D), qkv_w[:, 2 * D :]).reshape(views, HEADS, D)
    attended = jnp.sum(jnp.where(head_mask(), valued, 0.0), 1).astype(BF16)
    kept = (unit, scale, normed, class_unit, class_scale, class_normed, query, looked)
    return position[0], attended, mixed, kept + (probs, class_probs)


def trunk_backward(patches, wide, qkv_w, grad_att, grad_class, kept):
    unit, scale, normed, class_unit, class_scale, class_normed, query, looked = kept[:8]
    probs, class_probs = kept[8:]
    views = patches.shape[0]
    norms = wide[PD + NTOK :].astype(F32)
    temper = HDIM ** (-0.5)
    spread = jnp.where(head_mask(), grad_att[:, None], 0).astype(BF16).reshape(-1, D)
    back = product_t(spread, qkv_w[:, 2 * D :]).astype(BF16).reshape(views, HEADS, D)
    grad_probs = jnp.einsum("vhd,vkd->vhk", back, normed, preferred_element_type=F32)
    class_grad = jnp.sum(
        back.astype(F32) * class_normed.astype(F32), -1, keepdims=True
    )
    delta = jnp.sum(probs * grad_probs, -1, keepdims=True) + class_probs * class_grad
    grad_scores = (probs * (grad_probs - delta)).astype(BF16)
    class_scores = (class_probs * (class_grad - delta)).astype(BF16)
    reach = jnp.einsum("vhk,vkd->vhd", grad_scores, normed, preferred_element_type=F32)
    reach = (reach + class_scores.astype(F32) * class_normed.astype(F32)) * temper
    keyed = product(reach.astype(BF16).reshape(-1, D), qkv_w[:, D : 2 * D])
    keyed = keyed.reshape(views, HEADS, D)
    grad_query = jnp.sum(jnp.where(head_mask(), keyed, 0.0), 1).astype(BF16)
    left = jnp.concatenate([grad_scores, probs.astype(BF16)], 1)
    right = jnp.concatenate(
        [jnp.broadcast_to((looked.astype(F32) * temper).astype(BF16), back.shape), back], 1
    )
    grad_normed = jnp.einsum("vhk,vhd->vkd", left, right, preferred_element_type=F32)
    class_left = jnp.concatenate([class_scores, class_probs.astype(BF16)], 1).astype(F32)
    class_row = jnp.sum(class_left * right.astype(F32), 1) + product_t(grad_query, qkv_w[:, :D])
    gain = jnp.sum(grad_normed * unit, (0, 1)) + jnp.sum(class_row * class_unit, 0)
    offset = jnp.sum(grad_normed, (0, 1)) + jnp.sum(class_row, 0)
    grad_stream = norm_back(grad_normed, norms[0], unit, scale)
    class_stream = norm_back(class_row, norms[0], class_unit, class_scale) + grad_class
    grad_patch = lax.dot_general(
        patches.reshape(-1, PD),
        grad_stream.astype(BF16).reshape(-1, D),
        (((0,), (0,)), ((), ())),
        preferred_element_type=F32,
    )
    return (
        grad_patch,
        jnp.sum(class_stream, 0, keepdims=True),
        jnp.sum(grad_stream, 0),
        gain[None],
        offset[None],
        jnp.sum(grad_query.astype(F32), 0, keepdims=True),
        jnp.sum(reach, 0),
    )


def grad_kernel(plan, most, spans, tab_ref, *refs):
    refs, out_ref, line_ref = refs[:-2], refs[-2], refs[-1]
    line_ref[...] = jnp.zeros(line_ref.shape, F32)
    for part in range(most):
        kind, base, chunks, row0 = (tab_ref[1 + 4 * part + i] for i in range(4))
        for index, span in spans.items():
            cols = PIECES[index][2]
            width = cols // LANES

            @pl.when(kind == index)
            def _():
                def move(step, carry, span=span, cols=cols, width=width):
                    row = pl.multiple_of(row0 + step * CHUNK, 8)
                    goal = base + step * (CHUNK * width)
                    if len(span) == 2:
                        first = step * CHUNK if span[1] else row
                        block = refs[span[0]][pl.ds(pl.multiple_of(first, 8), CHUNK), :]
                    else:
                        first, column = span[1:3]
                        first = pl.multiple_of(first + row, 8)
                        left = refs[0][pl.ds(first, CHUNK), :].astype(BF16)
                        block = product(left, refs[1][:, column : column + cols])
                    for tile in range(width):
                        line_ref[pl.ds(goal + tile, CHUNK, stride=width), :] = block[
                            :, tile * LANES : (tile + 1) * LANES
                        ]
                    return carry

                lax.fori_loop(0, chunks, move, 0)

    shift = tab_ref[0]
    turn = lax.rem(LANES - shift, LANES)
    lane = lax.broadcasted_iota(jnp.int32, (CHUNK + 8, LANES), 1)

    def align(step, carry):
        start = pl.multiple_of(step * CHUNK, 8)
        here = pltpu.roll(line_ref[pl.ds(pl.multiple_of(GRAD_FRONT + start, 8), CHUNK + 8), :], turn, 1)
        below = pltpu.roll(here, CHUNK + 7, 0)
        both = jnp.where(lane < LANES - shift, here, below)
        out_ref[pl.ds(start, CHUNK), :] = both[:CHUNK]
        return carry

    lax.fori_loop(0, plan.lines // CHUNK, align, 0)


def flat_gradient(plan, table, spans, refs, device):
    return pl.pallas_call(
        functools.partial(grad_kernel, plan, table.shape[1] // 4, spans),
        out_shape=jax.ShapeDtypeStruct((plan.lines, LANES), F32),
        in_specs=[pl.BlockSpec(memory_space=pltpu.SMEM)]
        + [pl.BlockSpec(memory_space=pltpu.VMEM)] * len(refs),
        out_specs=pl.BlockSpec(memory_space=pltpu.VMEM),
        scratch_shapes=[pltpu.VMEM((plan.grad_scratch, LANES), F32)],
        compiler_params=pltpu.CompilerParams(vmem_limit_bytes=48 * 1024 * 1024),
    )(jnp.asarray(table)[device], *refs).reshape(-1)[: plan.size]


def adam_update(weight, grad, first, second, rate):
    first = BETA_FIRST * first + (1.0 - BETA_FIRST) * grad
    second = BETA_SECOND * second + (1.0 - BETA_SECOND) * grad * grad
    stepped = (
        first
        / (1.0 - BETA_FIRST**STEP)
        / (jnp.sqrt(second / (1.0 - BETA_SECOND**STEP)) + ADAM_EPSILON)
    )
    return (weight - rate * (stepped + WEIGHT_DECAY * weight), first, second)


def per_device(
    plan,
    params,
    first_moment,
    second_moment,
    teacher,
    protos,
    proto_first,
    proto_second,
    teacher_protos,
    center,
    patches,
    partner,
):
    reps, groups = lax.axis_size("rep"), lax.axis_size("grp")
    count, half = reps * groups, reps * groups // 2
    rep, grp = lax.axis_index("rep"), lax.axis_index("grp")
    device = rep * groups + grp
    low = rep % 2 == 0
    place = rep // 2 * groups + grp
    halves = [
        [r * groups + g for r in range(parity, reps, 2) for g in range(groups)] for parity in (0, 1)
    ]
    swap = [(r, r ^ 1) for r in range(reps)]
    own_views = patches.shape[0]
    views = 2 * own_views

    def trade(values):
        return lax.ppermute(values, "rep", swap)

    def trade_low(values):
        return jnp.where(low, values, trade(values))

    def in_order(values):
        other = trade(values)
        return jnp.where(low, values, other), jnp.where(low, other, values)

    table = jnp.asarray(plan.lay_table)[device]
    kept = lay_out(plan, table, jnp.where(low, params, teacher))
    given = trade(lay_out(plan, table, jnp.where(low, teacher, params)))
    patches, partner, given = lax.optimization_barrier((patches, partner, given))
    shards = jnp.stack([jnp.where(low, kept, given), jnp.where(low, given, kept)])
    gathered = lax.all_gather(shards, BOTH, axis=0, axis_index_groups=halves)
    pixels = jnp.concatenate(in_order(patches), 0)
    places = in_order(partner.astype(F32))
    tables = jnp.stack([protos, teacher_protos]).astype(BF16)
    tables, gathered = lax.optimization_barrier((tables, gathered))
    tables = lax.all_gather(tables, "rep", axis=1, tiled=True).astype(F32)

    def columns_of(values):
        scale = lax.rsqrt(jnp.sum(values * values, 0, keepdims=True) + 1e-06)
        return (values * scale).astype(BF16), scale

    columns, column_scale = columns_of(tables[0])
    teacher_columns = columns_of(tables[1])[0]

    wide = Rows(plan, gathered, 0).folded()
    qkv_w = Rows(plan, gathered, 1).folded()
    out_w, up_w, down_w = (Rows(plan, gathered, which) for which in (2, 3, 4))
    final = Rows(plan, gathered, 5).folded().astype(F32)
    head_one, head_two, head_three = (Rows(plan, gathered, which) for which in (6, 7, 8))
    norms = wide[PD + NTOK :].astype(F32)

    class_row, attended, mixed, trunk_kept = trunk_forward(pixels, wide, qkv_w)
    middle = class_row + out_w.times(attended)
    unit_two, scale_two = normalised(middle)
    normed_two = (unit_two * norms[2] + norms[3]).astype(BF16)
    hidden = up_w.times(normed_two)
    act = activate(hidden).astype(BF16)
    stream = middle + down_w.times(act)
    unit_three, scale_three = normalised(stream)
    cls = (unit_three * final[0] + final[1]).astype(BF16)
    pre_one = head_one.times(cls)
    first = activate(pre_one).astype(BF16)
    pre_two = head_two.times(first)
    second = activate(pre_two).astype(BF16)
    bottle = head_three.times(second)
    bottle_scale = lax.rsqrt(jnp.sum(bottle * bottle, -1, keepdims=True) + 1e-06)
    rows = (bottle * bottle_scale).astype(BF16)

    def gather_rows(values):
        values = trade_low(values)
        return lax.all_gather(values, BOTH, axis=0, axis_index_groups=halves).reshape(
            half * views, -1
        )

    ahead = [attended, normed_two, act, cls, first, second, mixed.reshape(views, -1)]
    ahead = gather_rows(jnp.concatenate(ahead, 1))

    here = jnp.arange(views)
    source = jnp.concatenate([places[0], places[1] + own_views]).astype(jnp.int32)
    source = jnp.where(low, here, source)
    rows = product((source[:, None] == here[None, :]).astype(BF16), rows).astype(BF16)
    all_rows = lax.all_to_all(
        jnp.broadcast_to(rows[None], (count, views, B)), BOTH, 0, 0
    )
    all_rows = all_rows.reshape(reps // 2, 2, groups * views, B)
    student_rows = all_rows[:, 0].reshape(-1, B)
    teacher_rows = all_rows[:, 1].reshape(-1, B)

    teacher_logits = product(teacher_rows, teacher_columns)
    new_center = CENTER_MOMENTUM * center + (1.0 - CENTER_MOMENTUM) * jnp.mean(teacher_logits, 0)
    exp_teacher = jnp.exp((teacher_logits - center) / TEACHER_TEMP)
    scaled = product(student_rows, columns) / STUDENT_TEMP
    exp_student = jnp.exp(scaled)
    sums = jnp.stack(
        [jnp.sum(exp_student, 1), jnp.sum(exp_teacher, 1), jnp.sum(exp_teacher * scaled, 1)]
    )
    band = groups * views
    start = rep // 2 * band
    pulls = jnp.concatenate(
        [
            lax.dynamic_slice_in_dim(exp_student, start, band, 0),
            lax.dynamic_slice_in_dim(exp_teacher, start, band, 0),
        ],
        0,
    )
    pulls = lax.dot_general(
        pulls, columns.astype(F32), (((1,), (1,)), ((), ())), precision=PRECISE
    ).reshape(2, groups, views * B)
    note = jnp.concatenate(
        [
            pulls.transpose(1, 0, 2).reshape(groups, -1),
            jnp.broadcast_to(sums.reshape(1, -1), (groups, sums.size)),
        ],
        1,
    ).reshape(groups, -1, LANES)
    note = jnp.sum(lax.all_to_all(note, "grp", 0, 0), 0).reshape(-1)
    pulls = note[: 2 * views * B].reshape(2, views, B)
    sum_student, sum_teacher, crossed = note[2 * views * B :].reshape(3, -1)
    loss_value = jnp.sum(jnp.log(sum_student) - crossed / sum_teacher)
    own = place * views
    own_student = lax.dynamic_slice_in_dim(sum_student, own, views)[:, None]
    own_teacher = lax.dynamic_slice_in_dim(sum_teacher, own, views)[:, None]
    grad_rows = (pulls[0] / own_student - pulls[1] / own_teacher) / STUDENT_TEMP
    grad_rows = jnp.where(low, grad_rows, 0.0).astype(BF16).astype(F32)

    grad_logits = (
        exp_student / sum_student[:, None] - exp_teacher / sum_teacher[:, None]
    ) / STUDENT_TEMP
    grad_columns = lax.dot_general(
        student_rows.astype(F32), grad_logits, (((0,), (0,)), ((), ())), precision=PRECISE
    )
    inner = jnp.sum(grad_columns * tables[0], 0, keepdims=True)
    depth = protos.shape[0]
    grad_protos = (
        lax.dynamic_slice_in_dim(grad_columns, rep * depth, depth, 0) * column_scale
        - protos.astype(BF16).astype(F32) * column_scale**3 * inner
    )

    grad_bottle = (
        grad_rows * bottle_scale
        - bottle * bottle_scale**3 * jnp.sum(grad_rows * bottle, -1, keepdims=True)
    ).astype(BF16)
    grad_two = gelu_back(pre_two, head_three.back(grad_bottle)).astype(BF16)
    grad_one = gelu_back(pre_one, head_two.back(grad_two)).astype(BF16)
    grad_cls = head_one.back(grad_one)
    grad_stream = norm_back(grad_cls, final[0], unit_three, scale_three)
    grad_branch = grad_stream.astype(BF16)
    grad_hidden = gelu_back(hidden, down_w.back(grad_branch)).astype(BF16)
    grad_normed = up_w.back(grad_hidden)
    grad_middle = grad_stream + norm_back(grad_normed, norms[2], unit_two, scale_two)
    grad_mixed = grad_middle.astype(BF16)
    grad_att = out_w.back(grad_mixed).astype(BF16)
    behind = [grad_mixed, grad_hidden, grad_branch, grad_bottle, grad_two, grad_one, grad_att]
    behind += [(grad_cls * unit_three).astype(BF16), grad_cls.astype(BF16)]
    cols_all = gather_rows(jnp.concatenate(behind, 1))

    pieces = trunk_backward(pixels, wide, qkv_w, grad_att, grad_middle, trunk_kept)
    partial = jnp.concatenate(
        pieces[:5]
        + (
            jnp.sum(grad_normed * unit_two, 0, keepdims=True),
            jnp.sum(grad_normed, 0, keepdims=True),
        ),
        0,
    )
    base = PD + NTOK + 4
    depth = -(-base // half)
    partial = jnp.pad(partial, ((0, half * depth - base), (0, 0))).reshape(half, depth, D)
    shared = jnp.concatenate(pieces[5:], 0)
    slots = round_up(depth + shared.shape[0], 8)
    partial = jnp.concatenate(
        [
            partial,
            jnp.broadcast_to(shared[None], (half,) + shared.shape),
            jnp.zeros((half, slots - depth - shared.shape[0], D), F32),
        ],
        1,
    ).astype(BF16)
    partial = lax.all_to_all(partial, BOTH, 0, 0, axis_index_groups=halves)
    partial = jnp.sum(partial.astype(F32), 0)
    shared = partial[depth : depth + shared.shape[0]]
    shared = jnp.where(low, shared, trade(shared))
    partial = partial[:depth]
    slots = round_up(depth, 8)
    summed = jnp.pad(partial, ((0, slots - depth), (0, 0))).astype(BF16)
    summed = lax.all_to_all(
        jnp.broadcast_to(summed[None], (half, slots, D)), BOTH, 0, 0, axis_index_groups=halves
    )
    summed = summed[:, :depth].reshape(-1, D)[:base]
    if plan.odd_owner:
        summed = trade_low(summed)
    summed = summed.astype(F32)

    split = 3 * D + F + 2 * H
    rows_all = jnp.pad(ahead[:, :split].astype(F32).T, ((0, CHUNK), (0, 0)))
    mixed_rows = ahead[:, split:].reshape(half * views, HEADS, D)
    ends = jnp.sum(cols_all[:, -2 * D :].astype(F32), 0).reshape(2, D)
    ends = jnp.pad(ends, ((0, CHUNK - 2), (0, 0)))
    spans = {
        2: (0, 0, 0),
        3: (0, D, D),
        4: (0, 2 * D, D + F),
        5: (2, False),
        6: (0, 2 * D + F, 2 * D + F + B + H),
        7: (0, 3 * D + F, 2 * D + F + B),
        8: (0, 3 * D + F + H, 2 * D + F),
    }
    early = flat_gradient(plan, plan.grad_table, spans, (rows_all, cols_all, ends), device)
    values_att = cols_all[:, 2 * D + F + B + 2 * H : 3 * D + F + B + 2 * H]
    values_att = values_att.reshape(-1, HEADS, HDIM)
    qkv_v = jnp.einsum(
        "vhd,vhc->dhc", mixed_rows, values_att, preferred_element_type=F32
    ).reshape(D, D)

    class_normed, query = (trade_low(trunk_kept[which].astype(F32)) for which in (5, 6))
    by_head = jnp.where(head_mask(), query, 0.0)
    sum_query, reach = shared[0], shared[1:]
    outer = jnp.sum(class_normed * class_normed) * jnp.sum(sum_query * sum_query) + jnp.sum(
        jnp.sum(reach * reach, 1) * jnp.sum(by_head * by_head, 1)
    )
    squares = jnp.sum(partial * partial) + (jnp.sum(qkv_v * qkv_v) + outer) / half
    squares = jnp.where(low, squares, 0.0)
    squares = squares + jnp.sum(early * early) + jnp.sum(grad_protos * grad_protos)
    squares = lax.all_to_all(
        jnp.broadcast_to(squares.reshape(1, 1, 1), (count, 1, LANES)), BOTH, 0, 0
    )
    grad_norm = jnp.sqrt(jnp.sum(squares[:, 0, 0]))
    factor = jnp.minimum(1.0, CLIP_NORM / (grad_norm + 1e-06))

    qkv_grad = jnp.concatenate(
        [
            class_normed.T * sum_query[None],
            lax.dot_general(reach, by_head, (((0,), (0,)), ((), ())), precision=PRECISE),
            qkv_v,
        ],
        1,
    )
    qkv_grad = jnp.pad(qkv_grad, ((0, CHUNK), (0, 0)))
    wide_grad = jnp.pad(summed, ((0, CHUNK), (0, 0)))
    late = flat_gradient(
        plan, plan.late_table, {0: (0, False), 1: (1, False)}, (wide_grad, qkv_grad), device
    )
    grad_flat = early + late
    new_params, new_first, new_second = adam_update(
        params, grad_flat * factor, first_moment, second_moment, LEARNING_RATE
    )
    new_protos, new_proto_first, new_proto_second = adam_update(
        protos, grad_protos * factor, proto_first, proto_second, PROTO_RATE
    )
    new_teacher = TEACHER_MOMENTUM * teacher + (1.0 - TEACHER_MOMENTUM) * new_params
    new_teacher_protos = TEACHER_MOMENTUM * teacher_protos + (1.0 - TEACHER_MOMENTUM) * new_protos
    return (
        new_params,
        new_first,
        new_second,
        new_teacher,
        new_protos,
        new_proto_first,
        new_proto_second,
        new_teacher_protos,
        new_center,
        loss_value,
        grad_norm,
    )


def solution(mesh):
    placed = (
        P(BOTH),
        P(BOTH),
        P(BOTH),
        P(BOTH),
        P("rep", "grp"),
        P("rep", "grp"),
        P("rep", "grp"),
        P("rep", "grp"),
        P("grp"),
        P(BOTH, None, None),
        P(BOTH),
    )
    plan = Plan(mesh.shape["rep"], mesh.shape["grp"])
    return jax.shard_map(
        functools.partial(per_device, plan),
        mesh=mesh,
        in_specs=placed,
        out_specs=placed[:9] + (P(), P()),
        check_vma=False,
    )
```

```python
import functools

import jax
import jax.numpy as jnp
import numpy as np
from jax import lax
from jax.experimental import pallas as pl
from jax.experimental.pallas import tpu as pltpu
from jax.sharding import PartitionSpec as P

D = 768
HEADS = 12
HDIM = 64
F = 3072
PD = 768
NTOK = 197
H = 2048
B = 256
STEP = 10
NPATCH = NTOK - 1

PRECISE = lax.Precision.HIGHEST
STUDENT_TEMP = 0.1
TEACHER_TEMP = 0.04
CENTER_MOMENTUM = 0.9
TEACHER_MOMENTUM = 0.8
CLIP_NORM = 0.05
LEARNING_RATE = 0.03
PROTO_RATE = 0.6
BETA_FIRST = 0.9
BETA_SECOND = 0.999
ADAM_EPSILON = 1e-08
WEIGHT_DECAY = 0.04
BOTH = ("rep", "grp")
LANES = 128
F32 = jnp.float32
BF16 = jnp.bfloat16

SEGMENTS = []
_offset = 0
for _rows, _cols in ((PD + NTOK + 4, D), (D, 3 * D), (D, D), (D, F), (F + 2, D), (D + H, H), (H, B)):
    SEGMENTS.append((_offset, _rows, _cols))
    _offset += _rows * _cols
PFLAT = _offset
WIDTHS = sorted({cols // LANES for _, _, cols in SEGMENTS})

PIECES = []
_offset = 0
for _rows, _cols in (
    (PD + NTOK + 4, D),
    (D, 3 * D),
    (D, D),
    (D, F),
    (F, D),
    (2, D),
    (D, H),
    (H, H),
    (H, B),
):
    PIECES.append((_offset, _rows, _cols))
    _offset += _rows * _cols
FRONT = 192
CHUNK = 64
TILE = 16
TOKENS = 208
HEADROWS = 16
VMEM_LIMIT = 60 * 1024 * 1024


def round_up(value, step):
    return -(-value // step) * step


def shard_parts(start, stop, table):
    parts = []
    line0 = start // LANES
    for index, (offset, rows, cols) in enumerate(table):
        low, high = max(start, offset), min(stop, offset + rows * cols)
        if low >= high:
            continue
        row0 = (low - offset) // cols
        row1 = -(-(high - offset) // cols)
        parts.append((index, row0, row1 - row0, (offset + row0 * cols) // LANES - line0))
    return parts


FINAL_ROW = round_up(PD + NTOK + 4, 8)


class Plan:
    def __init__(self, reps, groups):
        count = reps * groups
        self.count, self.groups = count, groups
        self.size = PFLAT // count
        self.lines = round_up(-(-self.size // LANES) + 1, CHUNK)
        self.scratch = FRONT + self.lines + 8 * max(WIDTHS) + 16
        table = []
        self.blocks = [[] for _ in SEGMENTS]
        longest = 0
        for device in range(count):
            start = device * self.size
            entry = [start % LANES]
            target = 0
            for index, row0, rows, line in shard_parts(start, start + self.size, SEGMENTS):
                width = SEGMENTS[index][2] // LANES
                skew = row0 % 8
                tiles = -(-(rows + skew) // 8)
                self.blocks[index].append((device, target // TILE, row0 // 8, tiles))
                entry += [
                    WIDTHS.index(width),
                    FRONT + line - skew * width,
                    tiles // 2,
                    tiles % 2,
                    target // TILE,
                ]
                target += tiles * 8 * width
            longest = max(longest, target)
            entry += [-1, 0, 0, 0, 0] * (2 - len(entry) // 5)
            table.append(entry)
        self.buffer = round_up(longest, 16)
        self.lay_table = np.array(table, np.int32)
        self.grad_table = self.tabulate(lambda index: index > 1)
        self.late_table = self.tabulate(lambda index: index < 2)
        edge = SEGMENTS[0][1] * SEGMENTS[0][2]
        self.odd_owner = any(
            device * self.size < edge and self.place(device)[1] for device in range(count)
        )
        self.grad_scratch = FRONT + self.lines + CHUNK * max(WIDTHS) + 16


    def largest(self):
        longest = max(8 * block[3] for blocks in self.blocks for block in blocks)
        return max(len(blocks) for blocks in self.blocks), round_up(longest, LANES) + 2 * LANES

    def place(self, device):
        rep, grp = divmod(device, self.groups)
        return rep // 2 * self.groups + grp, rep % 2

    def tabulate(self, chosen):
        table = []
        for device in range(self.count):
            start = device * self.size
            entry = []
            for index, row0, rows, line in shard_parts(start, start + self.size, PIECES):
                if not chosen(index):
                    continue
                skew = row0 % 8
                line -= skew * (PIECES[index][2] // LANES)
                entry += [index, FRONT + line, -(-(rows + skew) // CHUNK), row0 - skew]
            table.append(entry)
        most = max(len(entry) for entry in table) // 4
        for device, entry in enumerate(table):
            entry += [-1, 0, 0, 0] * (most - len(entry) // 4)
            entry.insert(0, device * self.size % LANES)
        return np.array(table, np.int32)


def lay_kernel(plan, tab_ref, x_ref, out_ref, line_ref):
    shift = tab_ref[0]
    lane = lax.broadcasted_iota(jnp.int32, (CHUNK + 8, LANES), 1)
    line_ref[pl.ds(0, FRONT), :] = jnp.zeros((FRONT, LANES), F32)
    tail = plan.scratch - FRONT - plan.lines
    line_ref[pl.ds(FRONT + plan.lines, tail), :] = jnp.zeros((tail, LANES), F32)

    def align(step, carry):
        base = pl.multiple_of(step * CHUNK, 8)
        here = pltpu.roll(x_ref[pl.ds(base, CHUNK + 8), :], shift, 1)
        above = pltpu.roll(here, 1, 0)
        both = jnp.where(lane >= shift, here, above)
        line_ref[pl.ds(pl.multiple_of(FRONT + base, 8), CHUNK), :] = both[8:]
        return carry

    lax.fori_loop(0, plan.lines // CHUNK, align, 0)
    for part in range(2):
        kind, base, pairs, odd, target = (tab_ref[1 + 5 * part + i] for i in range(5))
        for index, width in enumerate(WIDTHS):

            @pl.when(kind == index)
            def _(width=width):
                def move(step, carry):
                    row = base + step * (TILE * width)
                    goal = (target + step * width) * TILE
                    for tile in range(width):
                        both = line_ref[pl.ds(row + tile, TILE, stride=width), :]
                        place = pl.multiple_of(goal + TILE * tile, TILE)
                        out_ref[pl.ds(place, TILE), :] = both.astype(BF16)
                    return carry

                def last(step, carry):
                    row = base + pairs * (TILE * width)
                    goal = (target + pairs * width) * TILE
                    for tile in range(0, width, 2):
                        both = [
                            line_ref[pl.ds(row + tile + side, 8, stride=width), :]
                            for side in range(2)
                        ]
                        place = pl.multiple_of(goal + 8 * tile, TILE)
                        out_ref[pl.ds(place, TILE), :] = jnp.concatenate(both, 0).astype(BF16)
                    return carry

                lax.fori_loop(0, pairs, move, 0)
                lax.fori_loop(0, odd, last, 0)


def lay_out(plan, table, flat):
    padded = jnp.pad(flat, (8 * LANES, plan.lines * LANES - plan.size))
    lines = padded.reshape(8 + plan.lines, LANES)
    return pl.pallas_call(
        functools.partial(lay_kernel, plan),
        out_shape=jax.ShapeDtypeStruct((plan.buffer, LANES), BF16),
        in_specs=[
            pl.BlockSpec(memory_space=pltpu.SMEM),
            pl.BlockSpec(memory_space=pltpu.VMEM),
        ],
        out_specs=pl.BlockSpec(memory_space=pltpu.VMEM),
        scratch_shapes=[pltpu.VMEM((plan.scratch, LANES), F32)],
        compiler_params=pltpu.CompilerParams(vmem_limit_bytes=24 * 1024 * 1024),
    )(table, lines)


class Shards:
    def __init__(self, plan, gathered_ref, ref, sems, order):
        self.plan, self.ref, self.sems, self.waited = plan, ref, sems, set()
        self.copies = {}
        for device in order:
            place, side = plan.place(device)
            copy = pltpu.make_async_copy(
                gathered_ref.at[place, side], ref.at[device], sems.at[device]
            )
            copy.start()
            self.copies[device] = copy

    def wait(self, device):
        if device in self.copies:
            self.copies.pop(device).wait()

    def finish(self):
        for device in list(self.copies):
            self.wait(device)

    def blocks(self, index, first, count):
        found = [
            block
            for block in self.plan.blocks[index]
            if 8 * block[2] < first + count and 8 * (block[2] + block[3]) > first
        ]
        for block in found:
            self.wait(block[0])
        return found

    def eight(self, index, tile, pair, side):
        width = SEGMENTS[index][2] // LANES
        total = None
        for device, target, tile0, tiles in self.plan.blocks[index]:
            own = tile - tile0
            if not 0 <= own < tiles:
                continue
            if own < tiles // 2 * 2:
                both = self.ref[device, target + own // 2 * width + 2 * pair + side]
                half = own % 2
            else:
                both = self.ref[device, target + tiles // 2 * width + pair]
                half = side
            piece = both.astype(F32)[8 * half : 8 * half + 8]
            total = piece if total is None else total + piece
        return total

    def assemble(self, index, out_ref):
        width = SEGMENTS[index][2] // LANES
        rows = out_ref.shape[0]
        self.blocks(index, 0, rows)

        def column(pair, carry):
            for side in range(2):
                lanes = pl.ds(pl.multiple_of(pair * 2 * LANES + side * LANES, LANES), LANES)
                for group in range(rows // TILE):
                    both = [
                        self.eight(index, 2 * group + half, pair, side) for half in range(2)
                    ]
                    out_ref[TILE * group : TILE * (group + 1), lanes] = jnp.concatenate(
                        both, 0
                    ).astype(BF16)
            return carry

        lax.fori_loop(0, width // 2, column, 0)

    def columns(self, index, block, pair):
        width = SEGMENTS[index][2] // LANES
        device, target, _, tiles = block
        sides = []
        for side in range(2):
            pieces = [
                self.ref[device, target + step * width + 2 * pair + side]
                for step in range(tiles // 2)
            ]
            if tiles % 2:
                both = self.ref[device, target + tiles // 2 * width + pair].astype(F32)
                pieces.append(both[8 * side : 8 * side + 8].astype(BF16))
            sides.append(jnp.concatenate(pieces, 0))
        return jnp.concatenate(sides, 1)

    def times(self, index, first, values, left_ref, out_ref):
        views, count = values.shape
        blocks = self.blocks(index, first, count)
        top = max([first + count] + [8 * (tile0 + tiles) for _, _, tile0, tiles in blocks])
        top = round_up(top, LANES) + LANES
        parts = [values, jnp.zeros((views, top - first - count), F32)]
        if first:
            parts.insert(0, jnp.zeros((views, first), F32))
        wide = jnp.concatenate(parts, 1)
        for number, (_, _, tile0, tiles) in enumerate(blocks):
            start = 8 * tile0 // LANES * LANES
            turn = 8 * tile0 - start
            piece = wide[:, start : start + round_up(turn + 8 * tiles, LANES)]
            if turn:
                piece = pltpu.roll(piece, piece.shape[1] - turn, 1)
            left_ref[number, :, : 8 * tiles] = piece[:, : 8 * tiles]

        def column(pair, carry):
            total = jnp.zeros((views, 2 * LANES), F32)
            for number, block in enumerate(blocks):
                left = left_ref[number, :, : 8 * block[3]].astype(BF16)
                total += product(left, self.columns(index, block, pair))
            out_ref[:, pl.ds(pl.multiple_of(pair * 2 * LANES, LANES), 2 * LANES)] = total
            return carry

        lax.fori_loop(0, SEGMENTS[index][2] // LANES // 2, column, 0)


    def back(self, index, first, count, values, grad_ref, left_ref, wide_ref):
        views, cols = values.shape
        grad_ref[:, :cols] = values
        blocks = self.blocks(index, first, count)
        top = max([first + count] + [8 * (tile0 + tiles) for _, _, tile0, tiles in blocks])
        wide_ref[:, : round_up(top, LANES) + LANES] = jnp.zeros(
            (views, round_up(top, LANES) + LANES), F32
        )
        for block in blocks:
            _, _, tile0, tiles = block

            def column(pair, total, block=block):
                lanes = pl.ds(pl.multiple_of(pair * 2 * LANES, LANES), 2 * LANES)
                left = grad_ref[:, lanes].astype(BF16)
                return total + product_t(left, self.columns(index, block, pair))

            total = lax.fori_loop(
                0, cols // LANES // 2, column, jnp.zeros((views, 8 * tiles), F32)
            )
            start = 8 * tile0 // LANES * LANES
            turn = 8 * tile0 - start
            size = round_up(turn + 8 * tiles, LANES)
            left_ref[0, :, :size] = jnp.zeros((views, size), F32)
            left_ref[0, :, : 8 * tiles] = total
            piece = left_ref[0, :, :size]
            if turn:
                piece = pltpu.roll(piece, turn, 1)
            wide_ref[:, start : start + size] += piece
        return wide_ref[:, first : first + count]


def product(left, right):
    return jnp.dot(left, right, preferred_element_type=F32)


def product_t(left, right):
    return lax.dot_general(
        left, right, (((left.ndim - 1,), (1,)), ((), ())), preferred_element_type=F32
    )


def normal_share(values):
    return 0.5 + 0.5 * lax.erf(values * 2**-0.5)


def activate(values):
    return values * normal_share(values)


def gelu_back(values, grad):
    density = jnp.exp(-0.5 * values * values) * (2 * np.pi) ** -0.5
    return grad * (normal_share(values) + values * density)


def normalised(values):
    centred = values - jnp.mean(values, -1, keepdims=True)
    scale = lax.rsqrt(jnp.mean(centred * centred, -1, keepdims=True) + 1e-06)
    return centred * scale, scale


def norm_back(grad, gain, unit, scale):
    inner = grad * gain
    return scale * (
        inner
        - jnp.mean(inner, -1, keepdims=True)
        - unit * jnp.mean(inner * unit, -1, keepdims=True)
    )


def head_mask():
    shape = (HEADROWS, D)
    return lax.broadcasted_iota(jnp.int32, shape, 0) == (
        lax.broadcasted_iota(jnp.int32, shape, 1) // HDIM
    )


def token_norms(unit, norms, class_normed):
    token = lax.broadcasted_iota(jnp.int32, (TOKENS, D), 0)
    normed = unit * norms[0:1] + norms[1:2]
    return jnp.where(
        token < NPATCH, normed, jnp.where(token == NPATCH, class_normed, 0.0)
    ).astype(BF16)


def forward_kernel(
    plan,
    gathered_ref,
    pixels_ref,
    unit_ref,
    scale_ref,
    probs_ref,
    mixed_ref,
    looked_ref,
    class_ref,
    qkv_ref,
    pack_ref,
    hidden_ref,
    one_ref,
    two_ref,
    bottle_ref,
    middle_ref,
    rows_ref,
    shards_ref,
    wide_ref,
    place_ref,
    left_ref,
    sums_ref,
    sems,
):
    shards = Shards(plan, gathered_ref, shards_ref, sems, range(plan.count))
    views = pixels_ref.shape[0]
    temper = HDIM ** (-0.5)
    shards.assemble(0, wide_ref)
    position = wide_ref[PD : PD + TOKENS].astype(F32)
    place_ref[...] = pltpu.roll(position, TOKENS - 1, 0)
    class_place = position[0:1]
    norms = position[NTOK : NTOK + 4]
    class_unit, class_scale = normalised(class_place)
    class_normed = (class_unit * norms[0:1] + norms[1:2]).astype(BF16).astype(F32)
    shards.assemble(1, qkv_ref)
    mask = head_mask()
    query = jnp.broadcast_to(class_normed, (HEADROWS, D)).astype(BF16)
    query = product(query, qkv_ref[:, :D]).astype(BF16).astype(F32)
    by_head = jnp.where(mask, query, 0.0).astype(BF16)
    looked = product_t(by_head, qkv_ref[:, D : 2 * D]).astype(BF16)
    looked_ref[...] = looked

    def view(v, carry):
        embedded = product(pixels_ref[v], wide_ref[:PD]) + place_ref[...]
        unit, scale = normalised(embedded)
        unit_ref[v] = unit
        scale_ref[v] = jnp.broadcast_to(scale, (TOKENS, LANES))
        normed = token_norms(unit, norms, class_normed)
        scores = product_t(looked, normed) * temper
        token = lax.broadcasted_iota(jnp.int32, scores.shape, 1)
        scores = jnp.where(token < NTOK, scores, -1e30)
        top = jnp.max(scores, -1, keepdims=True)
        top = top + jnp.log(jnp.sum(jnp.exp(scores - top), -1, keepdims=True))
        head = lax.broadcasted_iota(jnp.int32, scores.shape, 0)
        probs = jnp.where(head < HEADS, jnp.exp(scores - top), 0.0)
        probs_ref[v] = probs
        mixed_ref[v] = product(probs.astype(BF16), normed).astype(BF16)
        return carry

    lax.fori_loop(0, views, view, 0)
    mixed = mixed_ref[...].reshape(views * HEADROWS, D)
    valued = product(mixed, qkv_ref[:, 2 * D :]).reshape(views, HEADROWS, D)
    attended = jnp.sum(jnp.where(mask[None], valued, 0.0), 1).astype(BF16)
    pack_ref[:, :D] = attended
    shards.times(2, 0, attended.astype(F32), left_ref, sums_ref)
    middle = class_place + sums_ref[...]
    unit, scale = normalised(middle)
    middle_ref[0], middle_ref[1] = unit, jnp.broadcast_to(scale, (views, D))
    normed = (unit * norms[2:3] + norms[3:4]).astype(BF16)
    pack_ref[:, D : 2 * D] = normed
    shards.times(3, 0, normed.astype(F32), left_ref, hidden_ref)
    act = activate(hidden_ref[...]).astype(BF16)
    pack_ref[:, 2 * D : 2 * D + F] = act
    shards.times(4, 0, act.astype(F32), left_ref, sums_ref)
    unit, scale = normalised(middle + sums_ref[...])
    middle_ref[2], middle_ref[3] = unit, jnp.broadcast_to(scale, (views, D))
    final = jnp.concatenate(
        [shards.eight(4, F // 8, tile // 2, tile % 2) for tile in range(D // LANES)], 1
    )
    cls = (unit * final[0:1] + final[1:2]).astype(BF16)
    place = 2 * D + F
    pack_ref[:, place : place + D] = cls
    shards.times(5, 0, cls.astype(F32), left_ref, one_ref)
    first = activate(one_ref[...]).astype(BF16)
    pack_ref[:, place + D : place + D + H] = first
    shards.times(5, D, first.astype(F32), left_ref, two_ref)
    second = activate(two_ref[...]).astype(BF16)
    pack_ref[:, place + D + H :] = second
    shards.times(6, 0, second.astype(F32), left_ref, bottle_ref)
    bottle = bottle_ref[...]
    scale = lax.rsqrt(jnp.sum(bottle * bottle, -1, keepdims=True) + 1e-06)
    rows_ref[...] = (bottle * scale).astype(BF16)
    class_ref[...] = jnp.concatenate(
        [
            class_unit,
            class_normed,
            query[0:1],
            jnp.broadcast_to(class_scale, (1, D)),
            norms,
            final,
        ],
        0,
    )
    shards.finish()


def forward(plan, gathered, pixels):
    views = pixels.shape[0]
    shapes = [
        ((views, TOKENS, D), F32),
        ((views, TOKENS, LANES), F32),
        ((views, HEADROWS, TOKENS), F32),
        ((views, HEADROWS, D), BF16),
        ((HEADROWS, D), BF16),
        ((16, D), F32),
        ((D, 3 * D), BF16),
        ((views, 3 * D + F + 2 * H), BF16),
        ((views, F), F32),
        ((views, H), F32),
        ((views, H), F32),
        ((views, B), F32),
        ((4, views, D), F32),
        ((views, B), BF16),
    ]
    most, longest = plan.largest()
    return pl.pallas_call(
        functools.partial(forward_kernel, plan),
        out_shape=[jax.ShapeDtypeStruct(shape, dtype) for shape, dtype in shapes],
        in_specs=[
            pl.BlockSpec(memory_space=pl.ANY),
            pl.BlockSpec(memory_space=pltpu.VMEM),
        ],
        out_specs=[pl.BlockSpec(memory_space=pltpu.VMEM)] * len(shapes),
        scratch_shapes=[
            pltpu.VMEM((plan.count, plan.buffer // TILE, TILE, LANES), BF16),
            pltpu.VMEM((round_up(PD + NTOK + 4, TILE), D), BF16),
            pltpu.VMEM((TOKENS, D), F32),
            pltpu.VMEM((most, views, longest), F32),
            pltpu.VMEM((views, D), F32),
            pltpu.SemaphoreType.DMA((plan.count,)),
        ],
        compiler_params=pltpu.CompilerParams(vmem_limit_bytes=VMEM_LIMIT),
        cost_estimate=pl.CostEstimate(
            flops=60 * 10**9, bytes_accessed=40 * 10**6, transcendentals=10**5
        ),
    )(gathered, pixels)


def backward_kernel(
    plan,
    gathered_ref,
    grad_ref,
    unit_ref,
    scale_ref,
    probs_ref,
    looked_ref,
    class_ref,
    qkv_ref,
    hidden_ref,
    one_ref,
    two_ref,
    bottle_ref,
    middle_ref,
    pack_ref,
    token_ref,
    place_ref,
    extra_ref,
    reach_ref,
    shards_ref,
    left_ref,
    values_ref,
    wide_ref,
    back_ref,
    mixed_ref,
    rows_ref,
    sems,
):
    shards = Shards(plan, gathered_ref, shards_ref, sems, reversed(range(plan.count)))
    views = grad_ref.shape[0]
    temper = HDIM ** (-0.5)
    work = (values_ref, left_ref, wide_ref)
    mask = head_mask()
    norms, final = class_ref[4:8], class_ref[8:10]
    class_unit, class_normed, class_scale = (class_ref[row : row + 1] for row in (0, 1, 3))

    grad_rows, bottle = grad_ref[...], bottle_ref[...]
    scale = lax.rsqrt(jnp.sum(bottle * bottle, -1, keepdims=True) + 1e-06)
    grad_bottle = (
        grad_rows * scale - bottle * scale**3 * jnp.sum(grad_rows * bottle, -1, keepdims=True)
    ).astype(BF16)
    place = 2 * D + F
    pack_ref[:, place : place + B] = grad_bottle
    grad_two = shards.back(6, 0, H, grad_bottle.astype(F32), *work)
    grad_two = gelu_back(two_ref[...], grad_two).astype(BF16)
    pack_ref[:, place + B : place + B + H] = grad_two
    grad_one = shards.back(5, D, H, grad_two.astype(F32), *work)
    grad_one = gelu_back(one_ref[...], grad_one).astype(BF16)
    pack_ref[:, place + B + H : place + B + 2 * H] = grad_one
    grad_cls = shards.back(5, 0, D, grad_one.astype(F32), *work)
    unit, scale = middle_ref[2], middle_ref[3]
    pack_ref[:, place + B + 2 * H + D : place + B + 2 * H + 2 * D] = (grad_cls * unit).astype(BF16)
    pack_ref[:, place + B + 2 * H + 2 * D :] = grad_cls.astype(BF16)
    grad_stream = norm_back(grad_cls, final[0:1], unit, scale)
    grad_branch = grad_stream.astype(BF16)
    pack_ref[:, D + F : 2 * D + F] = grad_branch
    grad_hidden = shards.back(4, 0, F, grad_branch.astype(F32), *work)
    grad_hidden = gelu_back(hidden_ref[...], grad_hidden).astype(BF16)
    pack_ref[:, D : D + F] = grad_hidden
    grad_normed = shards.back(3, 0, D, grad_hidden.astype(F32), *work)
    unit, scale = middle_ref[0], middle_ref[1]
    gain_two = jnp.sum(grad_normed * unit, 0, keepdims=True)
    shift_two = jnp.sum(grad_normed, 0, keepdims=True)
    grad_middle = grad_stream + norm_back(grad_normed, norms[2:3], unit, scale)
    grad_mixed = grad_middle.astype(BF16)
    pack_ref[:, :D] = grad_mixed
    grad_att = shards.back(2, 0, D, grad_mixed.astype(F32), *work).astype(BF16)
    pack_ref[:, place + B + 2 * H : place + B + 2 * H + D] = grad_att
    shards.finish()

    spread = jnp.where(mask[None], grad_att.astype(F32)[:, None, :], 0.0).astype(BF16)
    back = product_t(spread.reshape(views * HEADROWS, D), qkv_ref[:, 2 * D :])
    back_ref[...] = back.astype(BF16).reshape(views, HEADROWS, D)
    looked = (looked_ref[...].astype(F32) * temper).astype(BF16)
    place_ref[...] = jnp.zeros((TOKENS, D), F32)
    reach_ref[...] = jnp.zeros((HEADROWS, D), F32)
    rows_ref[...] = jnp.zeros(rows_ref.shape, F32)

    def view(v, carry):
        unit = unit_ref[v]
        scale = scale_ref[v][:, :1]
        normed = token_norms(unit, norms, class_normed)
        back = back_ref[v]
        probs = probs_ref[v]
        grad_probs = product_t(back, normed)
        delta = jnp.sum(probs * grad_probs, -1, keepdims=True)
        grad_scores = (probs * (grad_probs - delta)).astype(BF16)
        reach = product(grad_scores, normed) * temper
        mixed_ref[v] = reach.astype(BF16)
        reach_ref[...] += reach
        left = jnp.concatenate([grad_scores.astype(F32), probs.astype(BF16).astype(F32)], 0)
        right = jnp.concatenate([looked, back], 0)
        grad = product(left.T.astype(BF16), right)
        row = lax.broadcasted_iota(jnp.int32, (8, D), 0)
        rows_ref[0] += jnp.where(row == v, grad[NPATCH : NPATCH + 1], 0.0)
        token = lax.broadcasted_iota(jnp.int32, (TOKENS, D), 0)
        grad = jnp.where(token < NPATCH, grad, 0.0)
        rows_ref[1, 0:1] += jnp.sum(grad * unit, 0, keepdims=True)
        rows_ref[2, 0:1] += jnp.sum(grad, 0, keepdims=True)
        stream = norm_back(grad, norms[0:1], unit, scale)
        place_ref[...] += stream
        token_ref[v] = stream.astype(BF16)
        return carry

    lax.fori_loop(0, views, view, 0)
    keyed = product(mixed_ref[...].reshape(views * HEADROWS, D), qkv_ref[:, D : 2 * D])
    keyed = jnp.where(mask[None], keyed.reshape(views, HEADROWS, D), 0.0)
    grad_query = jnp.sum(keyed, 1).astype(BF16)
    class_row = rows_ref[0][:views] + product_t(grad_query, qkv_ref[:, :D])
    class_stream = norm_back(class_row, norms[0:1], class_unit, class_scale) + grad_middle
    extra_ref[...] = jnp.concatenate(
        [
            jnp.sum(class_stream, 0, keepdims=True),
            rows_ref[1, 0:1] + jnp.sum(class_row * class_unit, 0, keepdims=True),
            rows_ref[2, 0:1] + jnp.sum(class_row, 0, keepdims=True),
            gain_two,
            shift_two,
            jnp.sum(grad_query.astype(F32), 0, keepdims=True),
            jnp.zeros((2, D), F32),
        ],
        0,
    )


def backward(plan, gathered, grad_rows, kept):
    views = grad_rows.shape[0]
    shapes = [
        ((views, 5 * D + F + B + 2 * H), BF16),
        ((views, TOKENS, D), BF16),
        ((TOKENS, D), F32),
        ((8, D), F32),
        ((HEADROWS, D), F32),
    ]
    most, longest = plan.largest()
    return pl.pallas_call(
        functools.partial(backward_kernel, plan),
        out_shape=[jax.ShapeDtypeStruct(shape, dtype) for shape, dtype in shapes],
        in_specs=[pl.BlockSpec(memory_space=pl.ANY)]
        + [pl.BlockSpec(memory_space=pltpu.VMEM)] * (1 + len(kept)),
        out_specs=[pl.BlockSpec(memory_space=pltpu.VMEM)] * len(shapes),
        scratch_shapes=[
            pltpu.VMEM((plan.count, plan.buffer // TILE, TILE, LANES), BF16),
            pltpu.VMEM((1, views, longest), F32),
            pltpu.VMEM((views, F), F32),
            pltpu.VMEM((views, F + 2 * LANES), F32),
            pltpu.VMEM((views, HEADROWS, D), BF16),
            pltpu.VMEM((views, HEADROWS, D), BF16),
            pltpu.VMEM((3, 8, D), F32),
            pltpu.SemaphoreType.DMA((plan.count,)),
        ],
        compiler_params=pltpu.CompilerParams(vmem_limit_bytes=VMEM_LIMIT),
        cost_estimate=pl.CostEstimate(
            flops=60 * 10**9, bytes_accessed=40 * 10**6, transcendentals=10**5
        ),
    )(gathered, grad_rows, *kept)


def grad_kernel(plan, most, spans, tab_ref, *refs):
    refs, out_ref, line_ref = refs[:-2], refs[-2], refs[-1]
    line_ref[...] = jnp.zeros(line_ref.shape, F32)
    for part in range(most):
        kind, base, chunks, row0 = (tab_ref[1 + 4 * part + i] for i in range(4))
        for index, span in spans.items():
            cols = PIECES[index][2]
            width = cols // LANES

            @pl.when(kind == index)
            def _():
                def move(step, carry, span=span, cols=cols, width=width):
                    row = pl.multiple_of(row0 + step * CHUNK, 8)
                    goal = base + step * (CHUNK * width)
                    if len(span) == 2:
                        first = step * CHUNK if span[1] else row
                        block = refs[span[0]][pl.ds(pl.multiple_of(first, 8), CHUNK), :]
                    else:
                        first, column = span[1:3]
                        first = pl.multiple_of(first + row, 8)
                        left = refs[0][pl.ds(first, CHUNK), :].astype(BF16)
                        block = product(left, refs[1][:, column : column + cols])
                    for tile in range(width):
                        line_ref[pl.ds(goal + tile, CHUNK, stride=width), :] = block[
                            :, tile * LANES : (tile + 1) * LANES
                        ]
                    return carry

                lax.fori_loop(0, chunks, move, 0)

    shift = tab_ref[0]
    turn = lax.rem(LANES - shift, LANES)
    lane = lax.broadcasted_iota(jnp.int32, (CHUNK + 8, LANES), 1)

    def align(step, carry):
        start = pl.multiple_of(step * CHUNK, 8)
        here = pltpu.roll(line_ref[pl.ds(pl.multiple_of(FRONT + start, 8), CHUNK + 8), :], turn, 1)
        below = pltpu.roll(here, CHUNK + 7, 0)
        both = jnp.where(lane < LANES - shift, here, below)
        out_ref[pl.ds(start, CHUNK), :] = both[:CHUNK]
        return carry

    lax.fori_loop(0, plan.lines // CHUNK, align, 0)


def flat_gradient(plan, table, spans, refs, device):
    return pl.pallas_call(
        functools.partial(grad_kernel, plan, table.shape[1] // 4, spans),
        out_shape=jax.ShapeDtypeStruct((plan.lines, LANES), F32),
        in_specs=[pl.BlockSpec(memory_space=pltpu.SMEM)]
        + [pl.BlockSpec(memory_space=pltpu.VMEM)] * len(refs),
        out_specs=pl.BlockSpec(memory_space=pltpu.VMEM),
        scratch_shapes=[pltpu.VMEM((plan.grad_scratch, LANES), F32)],
        compiler_params=pltpu.CompilerParams(vmem_limit_bytes=48 * 1024 * 1024),
    )(jnp.asarray(table)[device], *refs).reshape(-1)[: plan.size]


def adam_update(weight, grad, first, second, rate):
    first = BETA_FIRST * first + (1.0 - BETA_FIRST) * grad
    second = BETA_SECOND * second + (1.0 - BETA_SECOND) * grad * grad
    stepped = (
        first
        / (1.0 - BETA_FIRST**STEP)
        / (jnp.sqrt(second / (1.0 - BETA_SECOND**STEP)) + ADAM_EPSILON)
    )
    return (weight - rate * (stepped + WEIGHT_DECAY * weight), first, second)


def per_device(
    plan,
    params,
    first_moment,
    second_moment,
    teacher,
    protos,
    proto_first,
    proto_second,
    teacher_protos,
    center,
    patches,
    partner,
):
    reps, groups = lax.axis_size("rep"), lax.axis_size("grp")
    count, half = reps * groups, reps * groups // 2
    rep, grp = lax.axis_index("rep"), lax.axis_index("grp")
    device = rep * groups + grp
    low = rep % 2 == 0
    place = rep // 2 * groups + grp
    halves = [
        [r * groups + g for r in range(parity, reps, 2) for g in range(groups)] for parity in (0, 1)
    ]
    swap = [(r, r ^ 1) for r in range(reps)]
    own_views = patches.shape[0]
    views = 2 * own_views

    def trade(values):
        return lax.ppermute(values, "rep", swap)

    def trade_low(values):
        return jnp.where(low, values, trade(values))

    def in_order(values):
        other = trade(values)
        return jnp.where(low, values, other), jnp.where(low, other, values)

    table = jnp.asarray(plan.lay_table)[device]
    kept = lay_out(plan, table, jnp.where(low, params, teacher))
    given = trade(lay_out(plan, table, jnp.where(low, teacher, params)))
    patches, partner, given = lax.optimization_barrier((patches, partner, given))
    shards = jnp.stack([jnp.where(low, kept, given), jnp.where(low, given, kept)])
    gathered = lax.all_gather(shards, BOTH, axis=0, axis_index_groups=halves)
    gathered = gathered.reshape(half, 2, -1, TILE, LANES)
    pixels = jnp.concatenate(in_order(patches), 0)
    pixels = jnp.pad(pixels, ((0, 0), (0, TOKENS - NPATCH), (0, 0)))
    places = in_order(partner.astype(F32))
    tables = jnp.stack([protos, teacher_protos]).astype(BF16)
    tables, gathered = lax.optimization_barrier((tables, gathered))
    tables = lax.all_gather(tables, "rep", axis=1, tiled=True).astype(F32)

    def columns_of(values):
        scale = lax.rsqrt(jnp.sum(values * values, 0, keepdims=True) + 1e-06)
        return (values * scale).astype(BF16), scale

    columns, column_scale = columns_of(tables[0])
    teacher_columns = columns_of(tables[1])[0]

    kept = forward(plan, gathered, pixels)
    unit, scale, probs, mixed, looked, classes, qkv_w, ahead = kept[:8]
    rows = kept[-1]

    def gather_rows(values):
        values = trade_low(values)
        return lax.all_gather(values, BOTH, axis=0, axis_index_groups=halves).reshape(
            half * views, -1
        )

    ahead = gather_rows(
        jnp.concatenate([ahead, mixed[:, :HEADS].reshape(views, -1)], 1)
    )

    here = jnp.arange(views)
    source = jnp.concatenate([places[0], places[1] + own_views]).astype(jnp.int32)
    source = jnp.where(low, here, source)
    rows = product((source[:, None] == here[None, :]).astype(BF16), rows).astype(BF16)
    all_rows = lax.all_to_all(
        jnp.broadcast_to(rows[None], (count, views, B)), BOTH, 0, 0
    )
    all_rows = all_rows.reshape(reps // 2, 2, groups * views, B)
    student_rows = all_rows[:, 0].reshape(-1, B)
    teacher_rows = all_rows[:, 1].reshape(-1, B)

    teacher_logits = product(teacher_rows, teacher_columns)
    new_center = CENTER_MOMENTUM * center + (1.0 - CENTER_MOMENTUM) * jnp.mean(teacher_logits, 0)
    exp_teacher = jnp.exp((teacher_logits - center) / TEACHER_TEMP)
    scaled = product(student_rows, columns) / STUDENT_TEMP
    exp_student = jnp.exp(scaled)
    sums = jnp.stack(
        [jnp.sum(exp_student, 1), jnp.sum(exp_teacher, 1), jnp.sum(exp_teacher * scaled, 1)]
    )
    band = groups * views
    start = rep // 2 * band
    pulls = jnp.concatenate(
        [
            lax.dynamic_slice_in_dim(exp_student, start, band, 0),
            lax.dynamic_slice_in_dim(exp_teacher, start, band, 0),
        ],
        0,
    )
    pulls = lax.dot_general(
        pulls, columns.astype(F32), (((1,), (1,)), ((), ())), precision=PRECISE
    ).reshape(2, groups, views * B)
    note = jnp.concatenate(
        [
            pulls.transpose(1, 0, 2).reshape(groups, -1),
            jnp.broadcast_to(sums.reshape(1, -1), (groups, sums.size)),
        ],
        1,
    ).reshape(groups, -1, LANES)
    note = jnp.sum(lax.all_to_all(note, "grp", 0, 0), 0).reshape(-1)
    pulls = note[: 2 * views * B].reshape(2, views, B)
    sum_student, sum_teacher, crossed = note[2 * views * B :].reshape(3, -1)
    loss_value = jnp.sum(jnp.log(sum_student) - crossed / sum_teacher)
    own = place * views
    own_student = lax.dynamic_slice_in_dim(sum_student, own, views)[:, None]
    own_teacher = lax.dynamic_slice_in_dim(sum_teacher, own, views)[:, None]
    grad_rows = (pulls[0] / own_student - pulls[1] / own_teacher) / STUDENT_TEMP
    grad_rows = jnp.where(low, grad_rows, 0.0).astype(BF16).astype(F32)

    grad_logits = (
        exp_student / sum_student[:, None] - exp_teacher / sum_teacher[:, None]
    ) / STUDENT_TEMP
    grad_columns = lax.dot_general(
        student_rows.astype(F32), grad_logits, (((0,), (0,)), ((), ())), precision=PRECISE
    )
    inner = jnp.sum(grad_columns * tables[0], 0, keepdims=True)
    depth = protos.shape[0]
    grad_protos = (
        lax.dynamic_slice_in_dim(grad_columns, rep * depth, depth, 0) * column_scale
        - protos.astype(BF16).astype(F32) * column_scale**3 * inner
    )

    saved = (unit, scale, probs, looked, classes, qkv_w) + tuple(kept[8:13])
    behind, tokens, grad_place, extra, reach = backward(plan, gathered, grad_rows, saved)
    cols_all = gather_rows(behind)
    grad_patch = lax.dot_general(
        pixels.reshape(-1, PD),
        tokens.reshape(-1, D),
        (((0,), (0,)), ((), ())),
        preferred_element_type=F32,
    )
    partial = jnp.concatenate([grad_patch, extra[:1], grad_place[:NPATCH], extra[1:5]], 0)
    shared = jnp.concatenate([extra[5:6], reach[:HEADS]], 0)
    base = PD + NTOK + 4
    depth = -(-base // half)
    partial = jnp.pad(partial, ((0, half * depth - base), (0, 0))).reshape(half, depth, D)
    slots = round_up(depth + shared.shape[0], 8)
    partial = jnp.concatenate(
        [
            partial,
            jnp.broadcast_to(shared[None], (half,) + shared.shape),
            jnp.zeros((half, slots - depth - shared.shape[0], D), F32),
        ],
        1,
    ).astype(BF16)
    partial = lax.all_to_all(partial, BOTH, 0, 0, axis_index_groups=halves)
    partial = jnp.sum(partial.astype(F32), 0)
    shared = partial[depth : depth + shared.shape[0]]
    shared = jnp.where(low, shared, trade(shared))
    partial = partial[:depth]
    slots = round_up(depth, 8)
    summed = jnp.pad(partial, ((0, slots - depth), (0, 0))).astype(BF16)
    summed = lax.all_to_all(
        jnp.broadcast_to(summed[None], (half, slots, D)), BOTH, 0, 0, axis_index_groups=halves
    )
    summed = summed[:, :depth].reshape(-1, D)[:base]
    if plan.odd_owner:
        summed = trade_low(summed)
    summed = summed.astype(F32)

    split = 3 * D + F + 2 * H
    rows_all = jnp.pad(ahead[:, :split].astype(F32).T, ((0, CHUNK), (0, 0)))
    mixed_rows = ahead[:, split:].reshape(half * views, HEADS, D)
    ends = jnp.sum(cols_all[:, -2 * D :].astype(F32), 0).reshape(2, D)
    ends = jnp.pad(ends, ((0, CHUNK - 2), (0, 0)))
    spans = {
        2: (0, 0, 0),
        3: (0, D, D),
        4: (0, 2 * D, D + F),
        5: (2, False),
        6: (0, 2 * D + F, 2 * D + F + B + H),
        7: (0, 3 * D + F, 2 * D + F + B),
        8: (0, 3 * D + F + H, 2 * D + F),
    }
    early = flat_gradient(plan, plan.grad_table, spans, (rows_all, cols_all, ends), device)
    values_att = cols_all[:, 2 * D + F + B + 2 * H : 3 * D + F + B + 2 * H]
    values_att = values_att.reshape(-1, HEADS, HDIM)
    qkv_v = jnp.einsum(
        "vhd,vhc->dhc", mixed_rows, values_att, preferred_element_type=F32
    ).reshape(D, D)

    classes = trade_low(classes)
    class_normed, query = classes[1:2], classes[2:3]
    by_head = jnp.where(head_mask()[:HEADS], query, 0.0)
    sum_query, reach = shared[0], shared[1:]
    outer = jnp.sum(class_normed * class_normed) * jnp.sum(sum_query * sum_query) + jnp.sum(
        jnp.sum(reach * reach, 1) * jnp.sum(by_head * by_head, 1)
    )
    squares = jnp.sum(partial * partial) + (jnp.sum(qkv_v * qkv_v) + outer) / half
    squares = jnp.where(low, squares, 0.0)
    squares = squares + jnp.sum(early * early) + jnp.sum(grad_protos * grad_protos)
    squares = lax.all_to_all(
        jnp.broadcast_to(squares.reshape(1, 1, 1), (count, 1, LANES)), BOTH, 0, 0
    )
    grad_norm = jnp.sqrt(jnp.sum(squares[:, 0, 0]))
    factor = jnp.minimum(1.0, CLIP_NORM / (grad_norm + 1e-06))

    qkv_grad = jnp.concatenate(
        [
            class_normed.T * sum_query[None],
            lax.dot_general(reach, by_head, (((0,), (0,)), ((), ())), precision=PRECISE),
            qkv_v,
        ],
        1,
    )
    qkv_grad = jnp.pad(qkv_grad, ((0, CHUNK), (0, 0)))
    wide_grad = jnp.pad(summed, ((0, CHUNK), (0, 0)))
    late = flat_gradient(
        plan, plan.late_table, {0: (0, False), 1: (1, False)}, (wide_grad, qkv_grad), device
    )
    grad_flat = early + late
    new_params, new_first, new_second = adam_update(
        params, grad_flat * factor, first_moment, second_moment, LEARNING_RATE
    )
    new_protos, new_proto_first, new_proto_second = adam_update(
        protos, grad_protos * factor, proto_first, proto_second, PROTO_RATE
    )
    new_teacher = TEACHER_MOMENTUM * teacher + (1.0 - TEACHER_MOMENTUM) * new_params
    new_teacher_protos = TEACHER_MOMENTUM * teacher_protos + (1.0 - TEACHER_MOMENTUM) * new_protos
    return (
        new_params,
        new_first,
        new_second,
        new_teacher,
        new_protos,
        new_proto_first,
        new_proto_second,
        new_teacher_protos,
        new_center,
        loss_value,
        grad_norm,
    )


def solution(mesh):
    placed = (
        P(BOTH),
        P(BOTH),
        P(BOTH),
        P(BOTH),
        P("rep", "grp"),
        P("rep", "grp"),
        P("rep", "grp"),
        P("rep", "grp"),
        P("grp"),
        P(BOTH, None, None),
        P(BOTH),
    )
    plan = Plan(mesh.shape["rep"], mesh.shape["grp"])
    return jax.shard_map(
        functools.partial(per_device, plan),
        mesh=mesh,
        in_specs=placed,
        out_specs=placed[:9] + (P(), P()),
        check_vma=False,
    )
```

```python
import functools

import jax
import jax.numpy as jnp
import numpy as np
from jax import lax
from jax.experimental import pallas as pl
from jax.experimental.pallas import tpu as pltpu
from jax.sharding import PartitionSpec as P

D = 768
HEADS = 12
HDIM = 64
F = 3072
PD = 768
NTOK = 197
H = 2048
B = 256
STEP = 10
NPATCH = NTOK - 1

PRECISE = lax.Precision.HIGHEST
STUDENT_TEMP = 0.1
TEACHER_TEMP = 0.04
CENTER_MOMENTUM = 0.9
TEACHER_MOMENTUM = 0.8
CLIP_NORM = 0.05
LEARNING_RATE = 0.03
PROTO_RATE = 0.6
BETA_FIRST = 0.9
BETA_SECOND = 0.999
ADAM_EPSILON = 1e-08
WEIGHT_DECAY = 0.04
BOTH = ("rep", "grp")
LANES = 128
F32 = jnp.float32
BF16 = jnp.bfloat16

SEGMENTS = []
_offset = 0
for _rows, _cols in ((PD + NTOK + 4, D), (D, 3 * D), (D, D), (D, F), (F + 2, D), (D + H, H), (H, B)):
    SEGMENTS.append((_offset, _rows, _cols))
    _offset += _rows * _cols
PFLAT = _offset
WIDTHS = sorted({cols // LANES for _, _, cols in SEGMENTS})

PIECES = []
_offset = 0
for _rows, _cols in (
    (PD + NTOK + 4, D),
    (D, 3 * D),
    (D, D),
    (D, F),
    (F, D),
    (2, D),
    (D, H),
    (H, H),
    (H, B),
):
    PIECES.append((_offset, _rows, _cols))
    _offset += _rows * _cols
FRONT = 192
CHUNK = 128
SET = 288
SHARED = 32
STEPS = 64
AHEAD = 3 * D + F + 2 * H
BEHIND = 5 * D + F + B + 2 * H
TILE = 16
TOKENS = 208
HEADROWS = 16
VMEM_LIMIT = 60 * 1024 * 1024


def round_up(value, step):
    return -(-value // step) * step


def shard_parts(start, stop, table):
    parts = []
    line0 = start // LANES
    for index, (offset, rows, cols) in enumerate(table):
        low, high = max(start, offset), min(stop, offset + rows * cols)
        if low >= high:
            continue
        row0 = (low - offset) // cols
        row1 = -(-(high - offset) // cols)
        parts.append((index, row0, row1 - row0, (offset + row0 * cols) // LANES - line0))
    return parts


FINAL_ROW = round_up(PD + NTOK + 4, 8)


class Plan:
    def __init__(self, reps, groups):
        count = reps * groups
        self.count, self.groups = count, groups
        self.size = PFLAT // count
        self.lines = round_up(-(-self.size // LANES) + 1, STEPS)
        self.scratch = FRONT + self.lines + 8 * max(WIDTHS) + 16
        table = []
        self.blocks = [[] for _ in SEGMENTS]
        longest = 0
        for device in range(count):
            start = device * self.size
            entry = [start % LANES]
            target = 0
            for index, row0, rows, line in shard_parts(start, start + self.size, SEGMENTS):
                width = SEGMENTS[index][2] // LANES
                skew = row0 % 8
                tiles = -(-(rows + skew) // 8)
                self.blocks[index].append((device, target // TILE, row0 // 8, tiles))
                entry += [
                    WIDTHS.index(width),
                    FRONT + line - skew * width,
                    tiles // 2,
                    tiles % 2,
                    target // TILE,
                ]
                target += tiles * 8 * width
            longest = max(longest, target)
            entry += [-1, 0, 0, 0, 0] * (2 - len(entry) // 5)
            table.append(entry)
        self.buffer = round_up(longest, 16)
        self.lay_table = np.array(table, np.int32)
        edge = SEGMENTS[0][1] * SEGMENTS[0][2]
        owners = [device for device in range(count) if device * self.size < edge]
        self.odd_owner = any(self.place(device)[1] for device in owners)
        self.all_sets = len(owners) > 2
        self.grad_table = self.tabulate(lambda index: index)
        self.late_table = self.tabulate(lambda index: index < 2, self.wide_row)
        self.grad_scratch = FRONT + self.lines + CHUNK * max(WIDTHS) + 16


    def largest(self):
        longest = max(8 * block[3] for blocks in self.blocks for block in blocks)
        return max(len(blocks) for blocks in self.blocks), round_up(longest, LANES) + 2 * LANES

    def place(self, device):
        rep, grp = divmod(device, self.groups)
        return rep // 2 * self.groups + grp, rep % 2

    def tabulate(self, chosen, rows_of=lambda device, index, row0: row0):
        table = []
        for device in range(self.count):
            start = device * self.size
            entry = []
            for index, row0, rows, line in shard_parts(start, start + self.size, PIECES):
                if not chosen(index):
                    continue
                skew = row0 % 8
                line -= skew * (PIECES[index][2] // LANES)
                chunks = -(-(rows + skew) // CHUNK)
                entry += [index, FRONT + line, chunks, rows_of(device, index, row0 - skew)]
            table.append(entry)
        most = max(len(entry) for entry in table) // 4
        for device, entry in enumerate(table):
            entry += [-1, 0, 0, 0] * (most - len(entry) // 4)
            entry.insert(0, device * self.size % LANES)
        return np.array(table, np.int32)

    def wide_row(self, device, index, row0):
        if index:
            return row0
        late = row0 >= 2 * SET - 8
        if not self.all_sets:
            if late != device % 2:
                raise ValueError("owner")
            return row0 - (2 * SET - 8) * late
        return row0 + 8 * late


def lay_kernel(plan, tab_ref, x_ref, out_ref, line_ref):
    shift = tab_ref[0]
    lane = lax.broadcasted_iota(jnp.int32, (STEPS + 8, LANES), 1)
    line_ref[pl.ds(0, FRONT), :] = jnp.zeros((FRONT, LANES), F32)
    tail = plan.scratch - FRONT - plan.lines
    line_ref[pl.ds(FRONT + plan.lines, tail), :] = jnp.zeros((tail, LANES), F32)

    def align(step, carry):
        base = pl.multiple_of(step * STEPS, 8)
        here = pltpu.roll(x_ref[pl.ds(base, STEPS + 8), :], shift, 1)
        above = pltpu.roll(here, 1, 0)
        both = jnp.where(lane >= shift, here, above)
        line_ref[pl.ds(pl.multiple_of(FRONT + base, 8), STEPS), :] = both[8:]
        return carry

    lax.fori_loop(0, plan.lines // STEPS, align, 0)
    for part in range(2):
        kind, base, pairs, odd, target = (tab_ref[1 + 5 * part + i] for i in range(5))
        for index, width in enumerate(WIDTHS):

            @pl.when(kind == index)
            def _(width=width):
                def move(step, carry):
                    row = base + step * (TILE * width)
                    goal = (target + step * width) * TILE
                    for tile in range(width):
                        both = line_ref[pl.ds(row + tile, TILE, stride=width), :]
                        place = pl.multiple_of(goal + TILE * tile, TILE)
                        out_ref[pl.ds(place, TILE), :] = both.astype(BF16)
                    return carry

                def last(step, carry):
                    row = base + pairs * (TILE * width)
                    goal = (target + pairs * width) * TILE
                    for tile in range(0, width, 2):
                        both = [
                            line_ref[pl.ds(row + tile + side, 8, stride=width), :]
                            for side in range(2)
                        ]
                        place = pl.multiple_of(goal + 8 * tile, TILE)
                        out_ref[pl.ds(place, TILE), :] = jnp.concatenate(both, 0).astype(BF16)
                    return carry

                lax.fori_loop(0, pairs, move, 0)
                lax.fori_loop(0, odd, last, 0)


def lay_out(plan, table, flat):
    padded = jnp.pad(flat, (8 * LANES, plan.lines * LANES - plan.size))
    lines = padded.reshape(8 + plan.lines, LANES)
    return pl.pallas_call(
        functools.partial(lay_kernel, plan),
        out_shape=jax.ShapeDtypeStruct((plan.buffer, LANES), BF16),
        in_specs=[
            pl.BlockSpec(memory_space=pltpu.SMEM),
            pl.BlockSpec(memory_space=pltpu.VMEM),
        ],
        out_specs=pl.BlockSpec(memory_space=pltpu.VMEM),
        scratch_shapes=[pltpu.VMEM((plan.scratch, LANES), F32)],
        compiler_params=pltpu.CompilerParams(vmem_limit_bytes=24 * 1024 * 1024),
    )(table, lines)


class Shards:
    def __init__(self, plan, gathered_ref, ref, sems, order):
        self.plan, self.ref, self.sems, self.waited = plan, ref, sems, set()
        self.copies = {}
        for device in order:
            place, side = plan.place(device)
            copy = pltpu.make_async_copy(
                gathered_ref.at[place, side], ref.at[device], sems.at[device]
            )
            copy.start()
            self.copies[device] = copy

    def wait(self, device):
        if device in self.copies:
            self.copies.pop(device).wait()

    def finish(self):
        for device in list(self.copies):
            self.wait(device)

    def blocks(self, index, first, count):
        found = [
            block
            for block in self.plan.blocks[index]
            if 8 * block[2] < first + count and 8 * (block[2] + block[3]) > first
        ]
        for block in found:
            self.wait(block[0])
        return found

    def eight(self, index, tile, pair, side):
        width = SEGMENTS[index][2] // LANES
        total = None
        for device, target, tile0, tiles in self.plan.blocks[index]:
            own = tile - tile0
            if not 0 <= own < tiles:
                continue
            if own < tiles // 2 * 2:
                both = self.ref[device, target + own // 2 * width + 2 * pair + side]
                half = own % 2
            else:
                both = self.ref[device, target + tiles // 2 * width + pair]
                half = side
            piece = both.astype(F32)[8 * half : 8 * half + 8]
            total = piece if total is None else total + piece
        return total

    def assemble(self, index, out_ref):
        width = SEGMENTS[index][2] // LANES
        rows = out_ref.shape[0]
        self.blocks(index, 0, rows)

        def column(pair, carry):
            for side in range(2):
                lanes = pl.ds(pl.multiple_of(pair * 2 * LANES + side * LANES, LANES), LANES)
                for group in range(rows // TILE):
                    both = [
                        self.eight(index, 2 * group + half, pair, side) for half in range(2)
                    ]
                    out_ref[TILE * group : TILE * (group + 1), lanes] = jnp.concatenate(
                        both, 0
                    ).astype(BF16)
            return carry

        lax.fori_loop(0, width // 2, column, 0)

    def columns(self, index, block, pair):
        width = SEGMENTS[index][2] // LANES
        device, target, _, tiles = block
        sides = []
        for side in range(2):
            pieces = [
                self.ref[device, target + step * width + 2 * pair + side]
                for step in range(tiles // 2)
            ]
            if tiles % 2:
                both = self.ref[device, target + tiles // 2 * width + pair].astype(F32)
                pieces.append(both[8 * side : 8 * side + 8].astype(BF16))
            sides.append(jnp.concatenate(pieces, 0))
        return jnp.concatenate(sides, 1)

    def times(self, index, first, values, left_ref, out_ref):
        views, count = values.shape
        blocks = self.blocks(index, first, count)
        top = max([first + count] + [8 * (tile0 + tiles) for _, _, tile0, tiles in blocks])
        top = round_up(top, LANES) + LANES
        parts = [values, jnp.zeros((views, top - first - count), F32)]
        if first:
            parts.insert(0, jnp.zeros((views, first), F32))
        wide = jnp.concatenate(parts, 1)
        for number, (_, _, tile0, tiles) in enumerate(blocks):
            start = 8 * tile0 // LANES * LANES
            turn = 8 * tile0 - start
            piece = wide[:, start : start + round_up(turn + 8 * tiles, LANES)]
            if turn:
                piece = pltpu.roll(piece, piece.shape[1] - turn, 1)
            left_ref[number, :, : 8 * tiles] = piece[:, : 8 * tiles]

        def column(pair, carry):
            total = jnp.zeros((views, 2 * LANES), F32)
            for number, block in enumerate(blocks):
                left = left_ref[number, :, : 8 * block[3]].astype(BF16)
                total += product(left, self.columns(index, block, pair))
            out_ref[:, pl.ds(pl.multiple_of(pair * 2 * LANES, LANES), 2 * LANES)] = total
            return carry

        lax.fori_loop(0, SEGMENTS[index][2] // LANES // 2, column, 0)


    def back(self, index, first, count, values, grad_ref, left_ref, wide_ref):
        views, cols = values.shape
        grad_ref[:, :cols] = values
        blocks = self.blocks(index, first, count)
        top = max([first + count] + [8 * (tile0 + tiles) for _, _, tile0, tiles in blocks])
        wide_ref[:, : round_up(top, LANES) + LANES] = jnp.zeros(
            (views, round_up(top, LANES) + LANES), F32
        )
        for number, (_, _, _, tiles) in enumerate(blocks):
            size = round_up(8 * tiles, LANES) + LANES
            left_ref[number, :, :size] = jnp.zeros((views, size), F32)

        def column(pair, carry):
            lanes = pl.ds(pl.multiple_of(pair * 2 * LANES, LANES), 2 * LANES)
            left = grad_ref[:, lanes].astype(BF16)
            for number, block in enumerate(blocks):
                size = 8 * block[3]
                left_ref[number, :, :size] += product_t(left, self.columns(index, block, pair))
            return carry

        lax.fori_loop(0, cols // LANES // 2, column, 0)
        for number, (_, _, tile0, tiles) in enumerate(blocks):
            start = 8 * tile0 // LANES * LANES
            turn = 8 * tile0 - start
            size = round_up(turn + 8 * tiles, LANES)
            piece = left_ref[number, :, :size]
            if turn:
                piece = pltpu.roll(piece, turn, 1)
            wide_ref[:, start : start + size] += piece
        return wide_ref[:, first : first + count]


def product(left, right):
    return jnp.dot(left, right, preferred_element_type=F32)


def product_t(left, right):
    return lax.dot_general(
        left, right, (((left.ndim - 1,), (1,)), ((), ())), preferred_element_type=F32
    )


def normal_share(values):
    return 0.5 + 0.5 * lax.erf(values * 2**-0.5)


def activate(values):
    return values * normal_share(values)


def gelu_back(values, grad):
    density = jnp.exp(-0.5 * values * values) * (2 * np.pi) ** -0.5
    return grad * (normal_share(values) + values * density)


def normalised(values):
    centred = values - jnp.mean(values, -1, keepdims=True)
    scale = lax.rsqrt(jnp.mean(centred * centred, -1, keepdims=True) + 1e-06)
    return centred * scale, scale


def norm_back(grad, gain, unit, scale):
    inner = grad * gain
    return scale * (
        inner
        - jnp.mean(inner, -1, keepdims=True)
        - unit * jnp.mean(inner * unit, -1, keepdims=True)
    )


def head_mask():
    shape = (HEADROWS, D)
    return lax.broadcasted_iota(jnp.int32, shape, 0) == (
        lax.broadcasted_iota(jnp.int32, shape, 1) // HDIM
    )


def token_norms(unit, norms, class_normed):
    token = lax.broadcasted_iota(jnp.int32, (TOKENS, D), 0)
    normed = unit * norms[0:1] + norms[1:2]
    return jnp.where(
        token < NPATCH, normed, jnp.where(token == NPATCH, class_normed, 0.0)
    ).astype(BF16)


def forward_kernel(
    plan,
    gathered_ref,
    pixels_ref,
    unit_ref,
    scale_ref,
    probs_ref,
    mixed_ref,
    looked_ref,
    class_ref,
    qkv_ref,
    pack_ref,
    hidden_ref,
    one_ref,
    two_ref,
    bottle_ref,
    middle_ref,
    rows_ref,
    shards_ref,
    wide_ref,
    place_ref,
    left_ref,
    sums_ref,
    sems,
):
    shards = Shards(plan, gathered_ref, shards_ref, sems, range(plan.count))
    views = pixels_ref.shape[0]
    temper = HDIM ** (-0.5)
    shards.assemble(0, wide_ref)
    position = wide_ref[PD : PD + TOKENS].astype(F32)
    place_ref[...] = pltpu.roll(position, TOKENS - 1, 0)
    class_place = position[0:1]
    norms = position[NTOK : NTOK + 4]
    class_unit, class_scale = normalised(class_place)
    class_normed = (class_unit * norms[0:1] + norms[1:2]).astype(BF16).astype(F32)
    shards.assemble(1, qkv_ref)
    mask = head_mask()
    query = jnp.broadcast_to(class_normed, (HEADROWS, D)).astype(BF16)
    query = product(query, qkv_ref[:, :D]).astype(BF16).astype(F32)
    by_head = jnp.where(mask, query, 0.0).astype(BF16)
    looked = product_t(by_head, qkv_ref[:, D : 2 * D]).astype(BF16)
    looked_ref[...] = looked

    def view(v, carry):
        embedded = product(pixels_ref[v], wide_ref[:PD]) + place_ref[...]
        unit, scale = normalised(embedded)
        unit_ref[v] = unit
        scale_ref[v] = jnp.broadcast_to(scale, (TOKENS, LANES))
        normed = token_norms(unit, norms, class_normed)
        scores = product_t(looked, normed) * temper
        token = lax.broadcasted_iota(jnp.int32, scores.shape, 1)
        scores = jnp.where(token < NTOK, scores, -1e30)
        top = jnp.max(scores, -1, keepdims=True)
        top = top + jnp.log(jnp.sum(jnp.exp(scores - top), -1, keepdims=True))
        head = lax.broadcasted_iota(jnp.int32, scores.shape, 0)
        probs = jnp.where(head < HEADS, jnp.exp(scores - top), 0.0)
        probs_ref[v] = probs
        mixed_ref[v] = product(probs.astype(BF16), normed).astype(BF16)
        return carry

    lax.fori_loop(0, views, view, 0)
    mixed = mixed_ref[...].reshape(views * HEADROWS, D)
    valued = product(mixed, qkv_ref[:, 2 * D :]).reshape(views, HEADROWS, D)
    attended = jnp.sum(jnp.where(mask[None], valued, 0.0), 1).astype(BF16)
    pack_ref[:, :D] = attended
    shards.times(2, 0, attended.astype(F32), left_ref, sums_ref)
    middle = class_place + sums_ref[...]
    unit, scale = normalised(middle)
    middle_ref[0], middle_ref[1] = unit, jnp.broadcast_to(scale, (views, D))
    normed = (unit * norms[2:3] + norms[3:4]).astype(BF16)
    pack_ref[:, D : 2 * D] = normed
    shards.times(3, 0, normed.astype(F32), left_ref, hidden_ref)
    act = activate(hidden_ref[...]).astype(BF16)
    pack_ref[:, 2 * D : 2 * D + F] = act
    shards.times(4, 0, act.astype(F32), left_ref, sums_ref)
    unit, scale = normalised(middle + sums_ref[...])
    middle_ref[2], middle_ref[3] = unit, jnp.broadcast_to(scale, (views, D))
    final = jnp.concatenate(
        [shards.eight(4, F // 8, tile // 2, tile % 2) for tile in range(D // LANES)], 1
    )
    cls = (unit * final[0:1] + final[1:2]).astype(BF16)
    place = 2 * D + F
    pack_ref[:, place : place + D] = cls
    shards.times(5, 0, cls.astype(F32), left_ref, one_ref)
    first = activate(one_ref[...]).astype(BF16)
    pack_ref[:, place + D : place + D + H] = first
    shards.times(5, D, first.astype(F32), left_ref, two_ref)
    second = activate(two_ref[...]).astype(BF16)
    pack_ref[:, place + D + H :] = second
    shards.times(6, 0, second.astype(F32), left_ref, bottle_ref)
    bottle = bottle_ref[...]
    scale = lax.rsqrt(jnp.sum(bottle * bottle, -1, keepdims=True) + 1e-06)
    rows_ref[...] = (bottle * scale).astype(BF16)
    class_ref[...] = jnp.concatenate(
        [
            class_unit,
            class_normed,
            query[0:1],
            jnp.broadcast_to(class_scale, (1, D)),
            norms,
            final,
        ],
        0,
    )
    shards.finish()


def forward(plan, gathered, pixels):
    views = pixels.shape[0]
    shapes = [
        ((views, TOKENS, D), F32),
        ((views, TOKENS, LANES), F32),
        ((views, HEADROWS, TOKENS), F32),
        ((views, HEADROWS, D), BF16),
        ((HEADROWS, D), BF16),
        ((16, D), F32),
        ((D, 3 * D), BF16),
        ((views, 3 * D + F + 2 * H), BF16),
        ((views, F), F32),
        ((views, H), F32),
        ((views, H), F32),
        ((views, B), F32),
        ((4, views, D), F32),
        ((views, B), BF16),
    ]
    most, longest = plan.largest()
    return pl.pallas_call(
        functools.partial(forward_kernel, plan),
        out_shape=[jax.ShapeDtypeStruct(shape, dtype) for shape, dtype in shapes],
        in_specs=[
            pl.BlockSpec(memory_space=pl.ANY),
            pl.BlockSpec(memory_space=pltpu.VMEM),
        ],
        out_specs=[pl.BlockSpec(memory_space=pltpu.VMEM)] * len(shapes),
        scratch_shapes=[
            pltpu.VMEM((plan.count, plan.buffer // TILE, TILE, LANES), BF16),
            pltpu.VMEM((round_up(PD + NTOK + 4, TILE), D), BF16),
            pltpu.VMEM((TOKENS, D), F32),
            pltpu.VMEM((most, views, longest), F32),
            pltpu.VMEM((views, D), F32),
            pltpu.SemaphoreType.DMA((plan.count,)),
        ],
        compiler_params=pltpu.CompilerParams(vmem_limit_bytes=VMEM_LIMIT),
        cost_estimate=pl.CostEstimate(
            flops=60 * 10**9, bytes_accessed=40 * 10**6, transcendentals=10**5
        ),
    )(gathered, pixels)


def rows_back_kernel(
    plan,
    gathered_ref,
    grad_ref,
    class_ref,
    hidden_ref,
    one_ref,
    two_ref,
    bottle_ref,
    middle_ref,
    pack_ref,
    stream_ref,
    extra_ref,
    shards_ref,
    left_ref,
    values_ref,
    wide_ref,
    sems,
):
    shards = Shards(plan, gathered_ref, shards_ref, sems, reversed(range(plan.count)))
    work = (values_ref, left_ref, wide_ref)
    norms, final = class_ref[4:8], class_ref[8:10]

    grad_rows, bottle = grad_ref[...], bottle_ref[...]
    scale = lax.rsqrt(jnp.sum(bottle * bottle, -1, keepdims=True) + 1e-06)
    grad_bottle = (
        grad_rows * scale - bottle * scale**3 * jnp.sum(grad_rows * bottle, -1, keepdims=True)
    ).astype(BF16)
    place = 2 * D + F
    pack_ref[:, place : place + B] = grad_bottle
    grad_two = shards.back(6, 0, H, grad_bottle.astype(F32), *work)
    grad_two = gelu_back(two_ref[...], grad_two).astype(BF16)
    pack_ref[:, place + B : place + B + H] = grad_two
    grad_one = shards.back(5, D, H, grad_two.astype(F32), *work)
    grad_one = gelu_back(one_ref[...], grad_one).astype(BF16)
    pack_ref[:, place + B + H : place + B + 2 * H] = grad_one
    grad_cls = shards.back(5, 0, D, grad_one.astype(F32), *work)
    unit, scale = middle_ref[2], middle_ref[3]
    pack_ref[:, place + B + 2 * H + D : place + B + 2 * H + 2 * D] = (grad_cls * unit).astype(BF16)
    pack_ref[:, place + B + 2 * H + 2 * D :] = grad_cls.astype(BF16)
    grad_stream = norm_back(grad_cls, final[0:1], unit, scale)
    grad_branch = grad_stream.astype(BF16)
    pack_ref[:, D + F : 2 * D + F] = grad_branch
    grad_hidden = shards.back(4, 0, F, grad_branch.astype(F32), *work)
    grad_hidden = gelu_back(hidden_ref[...], grad_hidden).astype(BF16)
    pack_ref[:, D : D + F] = grad_hidden
    grad_normed = shards.back(3, 0, D, grad_hidden.astype(F32), *work)
    unit, scale = middle_ref[0], middle_ref[1]
    extra_ref[...] = jnp.concatenate(
        [
            jnp.sum(grad_normed * unit, 0, keepdims=True),
            jnp.sum(grad_normed, 0, keepdims=True),
            jnp.zeros((6, D), F32),
        ],
        0,
    )
    grad_middle = grad_stream + norm_back(grad_normed, norms[2:3], unit, scale)
    stream_ref[...] = grad_middle
    grad_mixed = grad_middle.astype(BF16)
    pack_ref[:, :D] = grad_mixed
    grad_att = shards.back(2, 0, D, grad_mixed.astype(F32), *work).astype(BF16)
    pack_ref[:, place + B + 2 * H : place + B + 2 * H + D] = grad_att
    shards.finish()


def rows_back(plan, gathered, grad_rows, kept):
    views = grad_rows.shape[0]
    shapes = [((views, 5 * D + F + B + 2 * H), BF16), ((views, D), F32), ((8, D), F32)]
    most, longest = plan.largest()
    return pl.pallas_call(
        functools.partial(rows_back_kernel, plan),
        out_shape=[jax.ShapeDtypeStruct(shape, dtype) for shape, dtype in shapes],
        in_specs=[pl.BlockSpec(memory_space=pl.ANY)]
        + [pl.BlockSpec(memory_space=pltpu.VMEM)] * (1 + len(kept)),
        out_specs=[pl.BlockSpec(memory_space=pltpu.VMEM)] * len(shapes),
        scratch_shapes=[
            pltpu.VMEM((plan.count, plan.buffer // TILE, TILE, LANES), BF16),
            pltpu.VMEM((most, views, longest), F32),
            pltpu.VMEM((views, F), F32),
            pltpu.VMEM((views, F + 2 * LANES), F32),
            pltpu.SemaphoreType.DMA((plan.count,)),
        ],
        compiler_params=pltpu.CompilerParams(vmem_limit_bytes=VMEM_LIMIT),
        cost_estimate=pl.CostEstimate(
            flops=30 * 10**9, bytes_accessed=30 * 10**6, transcendentals=10**5
        ),
    )(gathered, grad_rows, *kept)


def tokens_back_kernel(
    odd_ref,
    behind_ref,
    stream_ref,
    ends_ref,
    unit_ref,
    scale_ref,
    probs_ref,
    looked_ref,
    class_ref,
    qkv_ref,
    pixels_ref,
    kept_ref,
    sent_ref,
    patch_ref,
    place_ref,
    reach_ref,
    back_ref,
    mixed_ref,
    rows_ref,
):
    v = pl.program_id(0)
    views = stream_ref.shape[0]
    temper = HDIM ** (-0.5)
    norms = class_ref[4:8]
    class_unit, class_normed, class_scale = (class_ref[row : row + 1] for row in (0, 1, 3))

    @pl.when(v == 0)
    def _():
        place = 2 * D + F + B + 2 * H
        grad_att = behind_ref[:, place : place + D].astype(F32)
        spread = jnp.where(head_mask()[None], grad_att[:, None, :], 0.0).astype(BF16)
        back = product_t(spread.reshape(views * HEADROWS, D), qkv_ref[:, 2 * D :])
        back_ref[...] = back.astype(BF16).reshape(views, HEADROWS, D)
        patch_ref[...] = jnp.zeros(patch_ref.shape, F32)
        place_ref[...] = jnp.zeros(place_ref.shape, F32)
        reach_ref[...] = jnp.zeros(reach_ref.shape, F32)
        rows_ref[...] = jnp.zeros(rows_ref.shape, F32)

    unit = unit_ref[0]
    scale = scale_ref[0][:, :1]
    normed = token_norms(unit, norms, class_normed)
    back = back_ref[v]
    probs = probs_ref[0]
    grad_probs = product_t(back, normed)
    delta = jnp.sum(probs * grad_probs, -1, keepdims=True)
    grad_scores = (probs * (grad_probs - delta)).astype(BF16)
    reach = product(grad_scores, normed) * temper
    mixed_ref[v] = reach.astype(BF16)
    reach_ref[...] += reach
    left = jnp.concatenate([grad_scores.astype(F32), probs.astype(BF16).astype(F32)], 0)
    looked = (looked_ref[...].astype(F32) * temper).astype(BF16)
    grad = product(left.T.astype(BF16), jnp.concatenate([looked, back], 0))
    row = lax.broadcasted_iota(jnp.int32, (8, D), 0)
    rows_ref[0] += jnp.where(row == v, grad[NPATCH : NPATCH + 1], 0.0)
    token = lax.broadcasted_iota(jnp.int32, (TOKENS, D), 0)
    grad = jnp.where(token < NPATCH, grad, 0.0)
    rows_ref[1, 0:1] += jnp.sum(grad * unit, 0, keepdims=True)
    rows_ref[2, 0:1] += jnp.sum(grad, 0, keepdims=True)
    stream = norm_back(grad, norms[0:1], unit, scale)
    place_ref[...] += stream
    patch_ref[...] += product(pixels_ref[0], stream.astype(BF16))

    @pl.when(v == views - 1)
    def _():
        keyed = product(mixed_ref[...].reshape(views * HEADROWS, D), qkv_ref[:, D : 2 * D])
        keyed = jnp.where(head_mask()[None], keyed.reshape(views, HEADROWS, D), 0.0)
        grad_query = jnp.sum(keyed, 1).astype(BF16)
        class_row = rows_ref[0][:views] + product_t(grad_query, qkv_ref[:, :D])
        class_stream = norm_back(class_row, norms[0:1], class_unit, class_scale)
        class_stream = class_stream + stream_ref[...]
        ends = [
            (0, jnp.sum(class_stream, 0, keepdims=True)),
            (NTOK, rows_ref[1, 0:1] + jnp.sum(class_row * class_unit, 0, keepdims=True)),
            (NTOK + 1, rows_ref[2, 0:1] + jnp.sum(class_row, 0, keepdims=True)),
            (NTOK + 2, ends_ref[0:1]),
            (NTOK + 3, ends_ref[1:2]),
        ]
        tail = pltpu.roll(place_ref[...], 1, 0)
        for row, value in ends:
            tail = jnp.where(token == row, value, tail)
        upper = 2 * SET - 8
        rest = jnp.zeros((2 * SET - (PD - upper) - TOKENS, D), F32)
        query_row = lax.broadcasted_iota(jnp.int32, (SHARED - HEADROWS, D), 0) == 0
        total = jnp.sum(grad_query.astype(F32), 0, keepdims=True)
        shared = jnp.concatenate([reach_ref[...], jnp.where(query_row, total, 0.0)], 0)
        kept_ref[2 * SET :] = shared
        sent_ref[2 * SET :] = shared.astype(BF16)
        last = jnp.concatenate([patch_ref[upper:], tail, rest], 0)

        @pl.when(odd_ref[0] == 0)
        def _():
            kept_ref[: 2 * SET] = patch_ref[: 2 * SET]
            sent_ref[: 2 * SET] = last.astype(BF16)

        @pl.when(odd_ref[0] != 0)
        def _():
            kept_ref[: 2 * SET] = last
            sent_ref[: 2 * SET] = patch_ref[: 2 * SET].astype(BF16)


def tokens_back(odd, behind, grad_middle, ends, kept, pixels):
    views = grad_middle.shape[0]

    def whole(values):
        return pl.BlockSpec(values.shape, lambda v: (0,) * values.ndim)

    def by_view(values):
        return pl.BlockSpec((1,) + values.shape[1:], lambda v: (v,) + (0,) * (values.ndim - 1))

    unit, scale, probs, looked, classes, qkv_w = kept
    shape = (2 * SET + SHARED, D)
    return pl.pallas_call(
        tokens_back_kernel,
        grid=(views,),
        out_shape=[jax.ShapeDtypeStruct(shape, F32), jax.ShapeDtypeStruct(shape, BF16)],
        in_specs=[
            pl.BlockSpec(memory_space=pltpu.SMEM),
            whole(behind),
            whole(grad_middle),
            whole(ends),
            by_view(unit),
            by_view(scale),
            by_view(probs),
            whole(looked),
            whole(classes),
            whole(qkv_w),
            by_view(pixels),
        ],
        out_specs=[pl.BlockSpec(shape, lambda v: (0, 0))] * 2,
        scratch_shapes=[
            pltpu.VMEM((PD, D), F32),
            pltpu.VMEM((TOKENS, D), F32),
            pltpu.VMEM((HEADROWS, D), F32),
            pltpu.VMEM((views, HEADROWS, D), BF16),
            pltpu.VMEM((views, HEADROWS, D), BF16),
            pltpu.VMEM((3, 8, D), F32),
        ],
        compiler_params=pltpu.CompilerParams(vmem_limit_bytes=40 * 1024 * 1024),
        cost_estimate=pl.CostEstimate(
            flops=15 * 10**9, bytes_accessed=15 * 10**6, transcendentals=10**5
        ),
    )(odd, behind, grad_middle, ends, unit, scale, probs, looked, classes, qkv_w, pixels)


SPANS = {
    2: (0, 0),
    3: (D, D),
    4: (2 * D, D + F),
    6: (2 * D + F, 2 * D + F + B + H),
    7: (3 * D + F, 2 * D + F + B),
    8: (3 * D + F + H, 2 * D + F),
}
ATT_COLUMN = 2 * D + F + B + 2 * H


def early_kernel(plan, most, tab_ref, ahead_ref, behind_ref, line_ref, square_ref):
    line_ref[...] = jnp.zeros(line_ref.shape, F32)

    def turned(lane):
        start = pl.multiple_of(lane // LANES * LANES, LANES)
        both = ahead_ref[:, pl.ds(start, 2 * LANES)].astype(F32)
        both = pltpu.roll(both, lax.rem(2 * LANES - (lane - start), 2 * LANES), 1)
        return both[:, :LANES].T.astype(BF16)

    def store(goal, width, tile, block):
        line_ref[pl.ds(goal + tile, block.shape[0], stride=width), :] = block

    for part in range(most):
        kind, base, chunks, row0 = (tab_ref[1 + 4 * part + i] for i in range(4))
        for index, (lane, column) in SPANS.items():
            cols = PIECES[index][2]
            width = cols // LANES

            @pl.when(kind == index)
            def _(lane=lane, column=column, cols=cols, width=width):
                def move(step, carry):
                    goal = base + step * (CHUNK * width)
                    left = turned(lane + row0 + step * CHUNK)
                    block = product(left, behind_ref[:, column : column + cols])
                    for tile in range(width):
                        store(goal, width, tile, block[:, tile * LANES : (tile + 1) * LANES])
                    return carry

                lax.fori_loop(0, chunks, move, 0)

        @pl.when(kind == 1)
        def _():
            def move(step, carry):
                width = 3 * D // LANES
                goal = base + step * (CHUNK * width)
                side = lax.broadcasted_iota(jnp.int32, (CHUNK, LANES), 1)
                for pair in range(HEADS // 2):
                    column = ATT_COLUMN + pair * LANES
                    right = behind_ref[:, column : column + LANES]
                    lane = AHEAD + 2 * pair * D + row0 + step * CHUNK
                    first, second = (product(turned(lane + D * head), right) for head in range(2))
                    block = jnp.where(side < HDIM, first, second)
                    store(goal, width, 2 * D // LANES + pair, block)
                return carry

            lax.fori_loop(0, chunks, move, 0)

        @pl.when(kind == 5)
        def _():
            ends = jnp.sum(behind_ref[:, BEHIND - 2 * D :].astype(F32), 0, keepdims=True)
            for tile in range(D // LANES):
                rows = [
                    ends[:, place + tile * LANES : place + (tile + 1) * LANES] for place in (0, D)
                ]
                rows.append(jnp.zeros((6, LANES), F32))
                store(base, D // LANES, tile, jnp.concatenate(rows, 0))

    shift = tab_ref[0]
    shape = (STEPS, LANES)
    place = lax.broadcasted_iota(jnp.int32, shape, 0) * LANES
    place = place + lax.broadcasted_iota(jnp.int32, shape, 1) - shift

    def clear(step, total):
        start = pl.multiple_of(step * STEPS, 8)
        entry = place + start * LANES
        lines = pl.ds(pl.multiple_of(FRONT + start, 8), STEPS)
        kept = jnp.where((entry >= 0) & (entry < plan.size), line_ref[lines, :], 0.0)
        line_ref[lines, :] = kept
        return total + kept * kept

    total = lax.fori_loop(0, plan.lines // STEPS, clear, jnp.zeros(shape, F32))
    square_ref[...] = jnp.sum(total.reshape(STEPS // 8, 8, LANES), 0)


def early_gradient(plan, table, ahead, behind):
    return pl.pallas_call(
        functools.partial(early_kernel, plan, table.shape[0] // 4),
        out_shape=[
            jax.ShapeDtypeStruct((plan.grad_scratch, LANES), F32),
            jax.ShapeDtypeStruct((8, LANES), F32),
        ],
        in_specs=[pl.BlockSpec(memory_space=pltpu.SMEM)]
        + [pl.BlockSpec(memory_space=pltpu.VMEM)] * 2,
        out_specs=[pl.BlockSpec(memory_space=pltpu.VMEM)] * 2,
        compiler_params=pltpu.CompilerParams(vmem_limit_bytes=48 * 1024 * 1024),
        cost_estimate=pl.CostEstimate(
            flops=10 * 10**9, bytes_accessed=10 * 10**6, transcendentals=0
        ),
    )(table, ahead, behind)


def late_kernel(plan, most, tab_ref, lines_ref, wide_ref, left_ref, right_ref, out_ref, line_ref):
    line_ref[...] = lines_ref[...]

    def add(goal, width, tile, block):
        lines = pl.ds(goal + tile, CHUNK, stride=width)
        line_ref[lines, :] = line_ref[lines, :] + block

    for part in range(most):
        kind, base, chunks, row0 = (tab_ref[1 + 4 * part + i] for i in range(4))

        @pl.when(kind == 0)
        def _():
            def move(step, carry):
                width = D // LANES
                rows = pl.ds(pl.multiple_of(row0 + step * CHUNK, 8), CHUNK)
                for tile in range(width):
                    block = wide_ref[rows, tile * LANES : (tile + 1) * LANES]
                    add(base + step * (CHUNK * width), width, tile, block)
                return carry

            lax.fori_loop(0, chunks, move, 0)

        @pl.when(kind == 1)
        def _():
            def move(step, carry):
                width = 3 * D // LANES
                rows = pl.ds(pl.multiple_of(row0 + step * CHUNK, 8), CHUNK)
                block = jnp.dot(
                    left_ref[rows, :],
                    right_ref[...],
                    precision=PRECISE,
                    preferred_element_type=F32,
                )
                for tile in range(2 * D // LANES):
                    piece = block[:, tile * LANES : (tile + 1) * LANES]
                    add(base + step * (CHUNK * width), width, tile, piece)
                return carry

            lax.fori_loop(0, chunks, move, 0)

    shift = tab_ref[0]
    turn = lax.rem(LANES - shift, LANES)
    lane = lax.broadcasted_iota(jnp.int32, (STEPS + 8, LANES), 1)

    def align(step, carry):
        start = pl.multiple_of(step * STEPS, 8)
        lines = pl.ds(pl.multiple_of(FRONT + start, 8), STEPS + 8)
        here = pltpu.roll(line_ref[lines, :], turn, 1)
        below = pltpu.roll(here, STEPS + 7, 0)
        both = jnp.where(lane < LANES - shift, here, below)
        out_ref[pl.ds(start, STEPS), :] = both[:STEPS]
        return carry

    lax.fori_loop(0, plan.lines // STEPS, align, 0)


def late_gradient(plan, table, lines, wide, left, right):
    return pl.pallas_call(
        functools.partial(late_kernel, plan, table.shape[0] // 4),
        out_shape=jax.ShapeDtypeStruct((plan.lines, LANES), F32),
        in_specs=[pl.BlockSpec(memory_space=pltpu.SMEM)]
        + [pl.BlockSpec(memory_space=pltpu.VMEM)] * 4,
        out_specs=pl.BlockSpec(memory_space=pltpu.VMEM),
        scratch_shapes=[pltpu.VMEM((plan.grad_scratch, LANES), F32)],
        compiler_params=pltpu.CompilerParams(vmem_limit_bytes=32 * 1024 * 1024),
    )(table, lines, wide, left, right).reshape(-1)[: plan.size]


def adam_update(weight, grad, first, second, rate):
    first = BETA_FIRST * first + (1.0 - BETA_FIRST) * grad
    second = BETA_SECOND * second + (1.0 - BETA_SECOND) * grad * grad
    stepped = (
        first
        / (1.0 - BETA_FIRST**STEP)
        / (jnp.sqrt(second / (1.0 - BETA_SECOND**STEP)) + ADAM_EPSILON)
    )
    return (weight - rate * (stepped + WEIGHT_DECAY * weight), first, second)


def per_device(
    plan,
    params,
    first_moment,
    second_moment,
    teacher,
    protos,
    proto_first,
    proto_second,
    teacher_protos,
    center,
    patches,
    partner,
):
    reps, groups = lax.axis_size("rep"), lax.axis_size("grp")
    count, half = reps * groups, reps * groups // 2
    rep, grp = lax.axis_index("rep"), lax.axis_index("grp")
    device = rep * groups + grp
    low = rep % 2 == 0
    place = rep // 2 * groups + grp
    halves = [
        [r * groups + g for r in range(parity, reps, 2) for g in range(groups)] for parity in (0, 1)
    ]
    swap = [(r, r ^ 1) for r in range(reps)]
    own_views = patches.shape[0]
    views = 2 * own_views

    def trade(values):
        return lax.ppermute(values, "rep", swap)

    def trade_low(values):
        return jnp.where(low, values, trade(values))

    def in_order(values):
        other = trade(values)
        return jnp.where(low, values, other), jnp.where(low, other, values)

    pairs = [list(range(parity, reps, 2)) for parity in (0, 1)]
    tables = jnp.stack([protos, teacher_protos]).astype(BF16)
    tables = lax.all_to_all(
        jnp.broadcast_to(tables[None], (reps // 2,) + tables.shape),
        "rep",
        0,
        0,
        axis_index_groups=pairs,
    )

    table = jnp.asarray(plan.lay_table)[device]
    kept = lay_out(plan, table, jnp.where(low, params, teacher))
    given = trade(lay_out(plan, table, jnp.where(low, teacher, params)))
    patches, partner, tables, given = lax.optimization_barrier((patches, partner, tables, given))
    shards = jnp.stack([jnp.where(low, kept, given), jnp.where(low, given, kept)])
    gathered = lax.all_gather(shards, BOTH, axis=0, axis_index_groups=halves)
    gathered = gathered.reshape(half, 2, -1, TILE, LANES)
    pixels = jnp.concatenate(in_order(patches), 0)
    pixels = jnp.pad(pixels, ((0, 0), (0, TOKENS - NPATCH), (0, 0)))
    tables = jnp.stack(in_order(tables))
    tables = tables.transpose(2, 1, 0, 3, 4).reshape(2, B, -1).astype(F32)
    places = in_order(partner.astype(F32))
    def columns_of(values):
        scale = lax.rsqrt(jnp.sum(values * values, 0, keepdims=True) + 1e-06)
        return (values * scale).astype(BF16), scale

    columns, column_scale = columns_of(tables[0])
    teacher_columns = columns_of(tables[1])[0]

    kept = forward(plan, gathered, pixels)
    unit, scale, probs, mixed, looked, classes, qkv_w, ahead = kept[:8]
    rows = kept[-1]

    def gather_rows(values):
        return lax.all_gather(values, BOTH, axis=0, axis_index_groups=halves).reshape(
            half * views, -1
        )

    ahead = [ahead, mixed[:, :HEADS].reshape(views, -1)]
    ahead.append(jnp.pad(classes[1:3], ((0, views - 2), (0, 0))).astype(BF16))
    ahead = trade_low(jnp.concatenate(ahead, 1))

    here = jnp.arange(views)
    source = jnp.concatenate([places[0], places[1] + own_views]).astype(jnp.int32)
    source = jnp.where(low, here, source)
    rows = product((source[:, None] == here[None, :]).astype(BF16), rows).astype(BF16)
    all_rows = lax.all_to_all(
        jnp.broadcast_to(rows[None], (count, views, B)), BOTH, 0, 0
    )
    all_rows, ahead = lax.optimization_barrier((all_rows, ahead))
    ahead = gather_rows(ahead)
    all_rows = all_rows.reshape(reps // 2, 2, groups * views, B)
    student_rows = all_rows[:, 0].reshape(-1, B)
    teacher_rows = all_rows[:, 1].reshape(-1, B)

    teacher_logits = product(teacher_rows, teacher_columns)
    new_center = CENTER_MOMENTUM * center + (1.0 - CENTER_MOMENTUM) * jnp.mean(teacher_logits, 0)
    exp_teacher = jnp.exp((teacher_logits - center) / TEACHER_TEMP)
    scaled = product(student_rows, columns) / STUDENT_TEMP
    exp_student = jnp.exp(scaled)
    sums = jnp.stack(
        [jnp.sum(exp_student, 1), jnp.sum(exp_teacher, 1), jnp.sum(exp_teacher * scaled, 1)]
    )
    band = groups * views
    start = rep // 2 * band
    pulls = jnp.concatenate(
        [
            lax.dynamic_slice_in_dim(exp_student, start, band, 0),
            lax.dynamic_slice_in_dim(exp_teacher, start, band, 0),
        ],
        0,
    )
    pulls = lax.dot_general(
        pulls, columns.astype(F32), (((1,), (1,)), ((), ())), precision=PRECISE
    ).reshape(2, groups, views * B)
    note = jnp.concatenate(
        [
            pulls.transpose(1, 0, 2).reshape(groups, -1),
            jnp.broadcast_to(sums.reshape(1, -1), (groups, sums.size)),
        ],
        1,
    ).reshape(groups, -1, LANES)
    note = jnp.sum(lax.all_to_all(note, "grp", 0, 0), 0).reshape(-1)
    pulls = note[: 2 * views * B].reshape(2, views, B)
    sum_student, sum_teacher, crossed = note[2 * views * B :].reshape(3, -1)
    loss_value = jnp.sum(jnp.log(sum_student) - crossed / sum_teacher)
    own = place * views
    own_student = lax.dynamic_slice_in_dim(sum_student, own, views)[:, None]
    own_teacher = lax.dynamic_slice_in_dim(sum_teacher, own, views)[:, None]
    grad_rows = (pulls[0] / own_student - pulls[1] / own_teacher) / STUDENT_TEMP
    grad_rows = jnp.where(low, grad_rows, 0.0).astype(BF16).astype(F32)

    grad_logits = (
        exp_student / sum_student[:, None] - exp_teacher / sum_teacher[:, None]
    ) / STUDENT_TEMP
    grad_columns = lax.dot_general(
        student_rows.astype(F32), grad_logits, (((0,), (0,)), ((), ())), precision=PRECISE
    )
    inner = jnp.sum(grad_columns * tables[0], 0, keepdims=True)
    depth = protos.shape[0]
    grad_protos = (
        lax.dynamic_slice_in_dim(grad_columns, rep * depth, depth, 0) * column_scale
        - protos.astype(BF16).astype(F32) * column_scale**3 * inner
    )

    behind, grad_middle, ends = rows_back(
        plan, gathered, grad_rows, (classes,) + tuple(kept[8:13])
    )
    odd, far = grp % 2 == 1, grp // 2 % 2 == 1
    behind_rows = trade_low(behind)
    kept_rows, sent_rows = tokens_back(
        odd.astype(jnp.int32)[None],
        behind,
        grad_middle,
        ends,
        (unit, scale, probs, looked, classes, qkv_w),
        pixels.transpose(0, 2, 1),
    )
    behind_rows, sent_rows = lax.optimization_barrier((behind_rows, sent_rows))
    behind_rows = gather_rows(behind_rows)

    def across(bit, values):
        return lax.ppermute(values, "grp", [(g, g ^ bit) for g in range(groups)])

    partial = kept_rows + across(1, sent_rows).astype(F32)
    first, second = partial[:SET], partial[SET : 2 * SET]
    shared = partial[2 * SET :]
    other = jnp.concatenate([jnp.where(far, first, second), shared], 0).astype(BF16)
    partial = jnp.concatenate([jnp.where(far, second, first), shared], 0)
    partial = partial + across(2, other).astype(F32)
    lines = reps // 2
    depth = partial.shape[0] // lines
    partial = lax.all_to_all(
        partial.astype(BF16).reshape(lines, depth, D), "rep", 0, 0, axis_index_groups=pairs
    )
    partial = jnp.sum(partial.astype(F32), 0)
    summed = lax.all_to_all(
        jnp.broadcast_to(partial.astype(BF16)[None], (lines, depth, D)),
        "rep",
        0,
        0,
        axis_index_groups=pairs,
    ).reshape(-1, D)
    shared, summed = trade_low(summed[SET:]).astype(F32), summed[:SET]
    other = across(2, summed)
    summed = jnp.concatenate([jnp.where(far, other, summed), jnp.where(far, summed, other)], 0)
    if plan.all_sets:
        other = across(1, summed)
        summed = jnp.concatenate([jnp.where(odd, other, summed), jnp.where(odd, summed, other)], 0)
    if plan.odd_owner:
        summed = trade_low(summed)
    wide_grad = jnp.pad(summed.astype(F32), ((0, CHUNK), (0, 0)))

    early, squares = early_gradient(
        plan, jnp.asarray(plan.grad_table)[device], ahead, behind_rows
    )
    class_rows = ahead[:2, AHEAD + HEADS * D :].astype(F32)
    class_normed, query = class_rows[0:1], class_rows[1:2]
    by_head = jnp.where(head_mask()[:HEADS], query, 0.0)
    twice = odd & ~far & (jnp.arange(SET) < 8)
    weights = jnp.concatenate(
        [
            jnp.where(twice, 0.0, 1.0),
            jnp.sum(by_head * by_head, 1) / groups,
            jnp.zeros((HEADROWS - HEADS,), F32),
            jnp.sum(class_normed * class_normed)[None] / groups,
            jnp.zeros((SHARED - HEADROWS - 1,), F32),
        ]
    )
    weights = lax.dynamic_slice_in_dim(weights, rep // 2 * depth, depth)
    pieces = jnp.sum(weights * jnp.sum(partial * partial, 1))
    squares = jnp.sum(squares) + jnp.where(low, pieces, 0.0)
    squares = squares + jnp.sum(grad_protos * grad_protos)
    squares = lax.all_to_all(
        jnp.broadcast_to(squares.reshape(1, 1, 1), (count, 1, LANES)), BOTH, 0, 0
    )
    grad_norm = jnp.sqrt(jnp.sum(squares[:, 0, 0]))
    factor = jnp.minimum(1.0, CLIP_NORM / (grad_norm + 1e-06))

    sum_query, reach = shared[HEADROWS : HEADROWS + 1], shared[:HEADS]
    left = jnp.concatenate([class_normed, reach, jnp.zeros((LANES - 1 - HEADS, D), F32)], 0)
    left = jnp.pad(left.T, ((0, CHUNK), (0, 0)))
    right = jnp.concatenate(
        [
            jnp.pad(sum_query, ((0, 0), (0, D))),
            jnp.pad(by_head, ((0, 0), (D, 0))),
            jnp.zeros((LANES - 1 - HEADS, 2 * D), F32),
        ],
        0,
    )
    grad_flat = late_gradient(
        plan, jnp.asarray(plan.late_table)[device], early, wide_grad, left, right
    )
    new_params, new_first, new_second = adam_update(
        params, grad_flat * factor, first_moment, second_moment, LEARNING_RATE
    )
    new_protos, new_proto_first, new_proto_second = adam_update(
        protos, grad_protos * factor, proto_first, proto_second, PROTO_RATE
    )
    new_teacher = TEACHER_MOMENTUM * teacher + (1.0 - TEACHER_MOMENTUM) * new_params
    new_teacher_protos = TEACHER_MOMENTUM * teacher_protos + (1.0 - TEACHER_MOMENTUM) * new_protos
    return (
        new_params,
        new_first,
        new_second,
        new_teacher,
        new_protos,
        new_proto_first,
        new_proto_second,
        new_teacher_protos,
        new_center,
        loss_value,
        grad_norm,
    )


def solution(mesh):
    placed = (
        P(BOTH),
        P(BOTH),
        P(BOTH),
        P(BOTH),
        P("rep", "grp"),
        P("rep", "grp"),
        P("rep", "grp"),
        P("rep", "grp"),
        P("grp"),
        P(BOTH, None, None),
        P(BOTH),
    )
    plan = Plan(mesh.shape["rep"], mesh.shape["grp"])
    return jax.shard_map(
        functools.partial(per_device, plan),
        mesh=mesh,
        in_specs=placed,
        out_specs=placed[:9] + (P(), P()),
        check_vma=False,
    )
```

```python
import functools

import jax
import jax.numpy as jnp
import numpy as np
from jax import lax
from jax.experimental import pallas as pl
from jax.experimental.pallas import tpu as pltpu
from jax.sharding import PartitionSpec as P

D = 768
HEADS = 12
HDIM = 64
F = 3072
PD = 768
NTOK = 197
H = 2048
B = 256
STEP = 10
NPATCH = NTOK - 1

PRECISE = lax.Precision.HIGHEST
STUDENT_TEMP = 0.1
TEACHER_TEMP = 0.04
CENTER_MOMENTUM = 0.9
TEACHER_MOMENTUM = 0.8
CLIP_NORM = 0.05
LEARNING_RATE = 0.03
PROTO_RATE = 0.6
BETA_FIRST = 0.9
BETA_SECOND = 0.999
ADAM_EPSILON = 1e-08
WEIGHT_DECAY = 0.04
BOTH = ("rep", "grp")
LANES = 128
F32 = jnp.float32
BF16 = jnp.bfloat16

SEGMENTS = []
_offset = 0
for _rows, _cols in ((PD + NTOK + 4, D), (D, 3 * D), (D, D), (D, F), (F + 2, D), (D + H, H), (H, B)):
    SEGMENTS.append((_offset, _rows, _cols))
    _offset += _rows * _cols
PFLAT = _offset
WIDTHS = sorted({cols // LANES for _, _, cols in SEGMENTS})

PIECES = []
_offset = 0
for _rows, _cols in (
    (PD + NTOK + 4, D),
    (D, 3 * D),
    (D, D),
    (D, F),
    (F, D),
    (2, D),
    (D, H),
    (H, H),
    (H, B),
):
    PIECES.append((_offset, _rows, _cols))
    _offset += _rows * _cols
FRONT = 192
CHUNK = 128
SET = 288
SHARED = 32
STEPS = 64
AHEAD = 3 * D + F + H
TILE = 16
TOKENS = 208
HEADROWS = 16
VMEM_LIMIT = 62 * 1024 * 1024


SPANS = {
    2: (0, 0),
    3: (D, D),
    4: (2 * D, D + F),
    6: (2 * D + F, 2 * D + F + B + H),
    7: (3 * D + F, 2 * D + F + B),
}
ATT_COLUMN = 2 * D + F + B + 2 * H
SECOND = HEADS * D
CLASS = SECOND + H


def round_up(value, step):
    return -(-value // step) * step


def shard_parts(start, stop, table):
    parts = []
    line0 = start // LANES
    for index, (offset, rows, cols) in enumerate(table):
        low, high = max(start, offset), min(stop, offset + rows * cols)
        if low >= high:
            continue
        row0 = (low - offset) // cols
        row1 = -(-(high - offset) // cols)
        parts.append((index, row0, row1 - row0, (offset + row0 * cols) // LANES - line0))
    return parts


FINAL_ROW = round_up(PD + NTOK + 4, 8)


class Plan:
    def __init__(self, reps, groups):
        count = reps * groups
        self.count, self.groups = count, groups
        self.size = PFLAT // count
        self.lines = round_up(-(-self.size // LANES) + 1, STEPS)
        self.scratch = FRONT + self.lines + 8 * max(WIDTHS) + 16
        table = []
        self.blocks = [[] for _ in SEGMENTS]
        longest = 0
        for device in range(count):
            start = device * self.size
            entry = [start % LANES]
            target = 0
            for index, row0, rows, line in shard_parts(start, start + self.size, SEGMENTS):
                width = SEGMENTS[index][2] // LANES
                skew = row0 % 8
                tiles = -(-(rows + skew) // 8)
                self.blocks[index].append((device, target // TILE, row0 // 8, tiles))
                entry += [
                    WIDTHS.index(width),
                    FRONT + line - skew * width,
                    tiles // 2,
                    tiles % 2,
                    target // TILE,
                ]
                target += tiles * 8 * width
            longest = max(longest, target)
            entry += [-1, 0, 0, 0, 0] * (2 - len(entry) // 5)
            table.append(entry)
        self.buffer = round_up(longest, 16)
        self.lay_table = np.array(table, np.int32)
        edge = SEGMENTS[0][1] * SEGMENTS[0][2]
        owners = [device for device in range(count) if device * self.size < edge]
        self.odd_owner = any(self.place(device)[1] for device in owners)
        self.all_sets = len(owners) > 2
        self.sent = [[] for _ in range(count)]
        self.grad_table = self.tabulate(lambda index: index, self.sent_row)
        self.late_table = self.tabulate(lambda index: index in (0, 1, 5), self.wide_row)
        self.reach = max(place + size for sent in self.sent for _, size, place in sent)
        self.grad_scratch = FRONT + self.lines + CHUNK * max(WIDTHS) + 16


    def largest(self):
        longest = max(8 * block[3] for blocks in self.blocks for block in blocks)
        return max(len(blocks) for blocks in self.blocks), round_up(longest, LANES) + 2 * LANES

    def place(self, device):
        rep, grp = divmod(device, self.groups)
        return rep // 2 * self.groups + grp, rep % 2

    def tabulate(self, chosen, rows_of):
        table = []
        for device in range(self.count):
            start = device * self.size
            entry = []
            for index, row0, rows, line in shard_parts(start, start + self.size, PIECES):
                if not chosen(index):
                    continue
                skew = row0 % 8
                line -= skew * (PIECES[index][2] // LANES)
                chunks = -(-(rows + skew) // CHUNK)
                entry += [index, FRONT + line, chunks, rows_of(device, index, row0 - skew, chunks)]
            table.append(entry)
        most = max(len(entry) for entry in table) // 4
        for device, entry in enumerate(table):
            entry += [-1, 0, 0, 0] * (most - len(entry) // 4)
            entry.insert(0, device * self.size % LANES)
        return np.array(table, np.int32)

    def sent_row(self, device, index, row0, chunks):
        if index not in SPANS:
            return row0
        sent, size = self.sent[device], chunks * CHUNK
        place = sum(before for _, before, _ in sent)
        sent.append((SPANS[index][0] + row0, size, place))
        return place

    def wide_row(self, device, index, row0, chunks):
        if index:
            return row0
        late = row0 >= 2 * SET - 8
        if not self.all_sets:
            if late != device % 2:
                raise ValueError("owner")
            return row0 - (2 * SET - 8) * late
        return row0 + 8 * late


def lay_kernel(plan, tab_ref, x_ref, out_ref, line_ref):
    shift = tab_ref[0]
    lane = lax.broadcasted_iota(jnp.int32, (STEPS + 8, LANES), 1)
    line_ref[pl.ds(0, FRONT), :] = jnp.zeros((FRONT, LANES), F32)
    tail = plan.scratch - FRONT - plan.lines
    line_ref[pl.ds(FRONT + plan.lines, tail), :] = jnp.zeros((tail, LANES), F32)

    def align(step, carry):
        base = pl.multiple_of(step * STEPS, 8)
        here = pltpu.roll(x_ref[pl.ds(base, STEPS + 8), :], shift, 1)
        above = pltpu.roll(here, 1, 0)
        both = jnp.where(lane >= shift, here, above)
        line_ref[pl.ds(pl.multiple_of(FRONT + base, 8), STEPS), :] = both[8:]
        return carry

    lax.fori_loop(0, plan.lines // STEPS, align, 0)
    for part in range(2):
        kind, base, pairs, odd, target = (tab_ref[1 + 5 * part + i] for i in range(5))
        for index, width in enumerate(WIDTHS):

            @pl.when(kind == index)
            def _(width=width):
                def move(step, carry):
                    row = base + step * (TILE * width)
                    goal = (target + step * width) * TILE
                    for tile in range(width):
                        both = line_ref[pl.ds(row + tile, TILE, stride=width), :]
                        place = pl.multiple_of(goal + TILE * tile, TILE)
                        out_ref[pl.ds(place, TILE), :] = both.astype(BF16)
                    return carry

                def last(step, carry):
                    row = base + pairs * (TILE * width)
                    goal = (target + pairs * width) * TILE
                    for tile in range(0, width, 2):
                        both = [
                            line_ref[pl.ds(row + tile + side, 8, stride=width), :]
                            for side in range(2)
                        ]
                        place = pl.multiple_of(goal + 8 * tile, TILE)
                        out_ref[pl.ds(place, TILE), :] = jnp.concatenate(both, 0).astype(BF16)
                    return carry

                lax.fori_loop(0, pairs, move, 0)
                lax.fori_loop(0, odd, last, 0)


def lay_out(plan, table, flat):
    padded = jnp.pad(flat, (8 * LANES, plan.lines * LANES - plan.size))
    lines = padded.reshape(8 + plan.lines, LANES)
    return pl.pallas_call(
        functools.partial(lay_kernel, plan),
        out_shape=jax.ShapeDtypeStruct((plan.buffer, LANES), BF16),
        in_specs=[
            pl.BlockSpec(memory_space=pltpu.SMEM),
            pl.BlockSpec(memory_space=pltpu.VMEM),
        ],
        out_specs=pl.BlockSpec(memory_space=pltpu.VMEM),
        scratch_shapes=[pltpu.VMEM((plan.scratch, LANES), F32)],
        compiler_params=pltpu.CompilerParams(vmem_limit_bytes=24 * 1024 * 1024),
    )(table, lines)


class Shards:
    def __init__(self, plan, gathered_ref, ref, sems, order):
        self.plan, self.ref, self.sems, self.waited = plan, ref, sems, set()
        self.copies = {}
        for device in order:
            place, side = plan.place(device)
            copy = pltpu.make_async_copy(
                gathered_ref.at[place, side], ref.at[device], sems.at[device]
            )
            copy.start()
            self.copies[device] = copy

    def wait(self, device):
        if device in self.copies:
            self.copies.pop(device).wait()

    def finish(self):
        for device in list(self.copies):
            self.wait(device)

    def blocks(self, index, first, count):
        found = [
            block
            for block in self.plan.blocks[index]
            if 8 * block[2] < first + count and 8 * (block[2] + block[3]) > first
        ]
        for block in found:
            self.wait(block[0])
        return found

    def eight(self, index, tile, pair, side):
        width = SEGMENTS[index][2] // LANES
        total = None
        for device, target, tile0, tiles in self.plan.blocks[index]:
            own = tile - tile0
            if not 0 <= own < tiles:
                continue
            if own < tiles // 2 * 2:
                both = self.ref[device, target + own // 2 * width + 2 * pair + side]
                half = own % 2
            else:
                both = self.ref[device, target + tiles // 2 * width + pair]
                half = side
            piece = both.astype(F32)[8 * half : 8 * half + 8]
            total = piece if total is None else total + piece
        return total

    def assemble(self, index, out_ref):
        width = SEGMENTS[index][2] // LANES
        rows = out_ref.shape[0]
        self.blocks(index, 0, rows)

        def column(pair, carry):
            for side in range(2):
                lanes = pl.ds(pl.multiple_of(pair * 2 * LANES + side * LANES, LANES), LANES)
                for group in range(rows // TILE):
                    both = [
                        self.eight(index, 2 * group + half, pair, side) for half in range(2)
                    ]
                    out_ref[TILE * group : TILE * (group + 1), lanes] = jnp.concatenate(
                        both, 0
                    ).astype(BF16)
            return carry

        lax.fori_loop(0, width // 2, column, 0)

    def columns(self, index, block, pair):
        width = SEGMENTS[index][2] // LANES
        device, target, _, tiles = block
        sides = []
        for side in range(2):
            pieces = [
                self.ref[device, target + step * width + 2 * pair + side]
                for step in range(tiles // 2)
            ]
            if tiles % 2:
                both = self.ref[device, target + tiles // 2 * width + pair].astype(F32)
                pieces.append(both[8 * side : 8 * side + 8].astype(BF16))
            sides.append(jnp.concatenate(pieces, 0))
        return jnp.concatenate(sides, 1)

    def times(self, index, first, values, left_ref, out_ref):
        views, count = values.shape
        blocks = self.blocks(index, first, count)
        top = max([first + count] + [8 * (tile0 + tiles) for _, _, tile0, tiles in blocks])
        top = round_up(top, LANES) + LANES
        parts = [values, jnp.zeros((views, top - first - count), F32)]
        if first:
            parts.insert(0, jnp.zeros((views, first), F32))
        wide = jnp.concatenate(parts, 1)
        for number, (_, _, tile0, tiles) in enumerate(blocks):
            start = 8 * tile0 // LANES * LANES
            turn = 8 * tile0 - start
            piece = wide[:, start : start + round_up(turn + 8 * tiles, LANES)]
            if turn:
                piece = pltpu.roll(piece, piece.shape[1] - turn, 1)
            left_ref[number, :, : 8 * tiles] = piece[:, : 8 * tiles]

        def column(pair, carry):
            total = jnp.zeros((views, 2 * LANES), F32)
            for number, block in enumerate(blocks):
                left = left_ref[number, :, : 8 * block[3]].astype(BF16)
                total += product(left, self.columns(index, block, pair))
            out_ref[:, pl.ds(pl.multiple_of(pair * 2 * LANES, LANES), 2 * LANES)] = total
            return carry

        lax.fori_loop(0, SEGMENTS[index][2] // LANES // 2, column, 0)


    def back(self, index, first, count, values, grad_ref, left_ref, wide_ref):
        views, cols = values.shape
        grad_ref[:, :cols] = values
        blocks = self.blocks(index, first, count)
        top = max([first + count] + [8 * (tile0 + tiles) for _, _, tile0, tiles in blocks])
        wide_ref[:, : round_up(top, LANES) + LANES] = jnp.zeros(
            (views, round_up(top, LANES) + LANES), F32
        )
        for number, (_, _, _, tiles) in enumerate(blocks):
            size = round_up(8 * tiles, LANES) + LANES
            left_ref[number, :, :size] = jnp.zeros((views, size), F32)

        def column(pair, carry):
            lanes = pl.ds(pl.multiple_of(pair * 2 * LANES, LANES), 2 * LANES)
            left = grad_ref[:, lanes].astype(BF16)
            for number, block in enumerate(blocks):
                size = 8 * block[3]
                left_ref[number, :, :size] += product_t(left, self.columns(index, block, pair))
            return carry

        lax.fori_loop(0, cols // LANES // 2, column, 0)
        for number, (_, _, tile0, tiles) in enumerate(blocks):
            start = 8 * tile0 // LANES * LANES
            turn = 8 * tile0 - start
            size = round_up(turn + 8 * tiles, LANES)
            piece = left_ref[number, :, :size]
            if turn:
                piece = pltpu.roll(piece, turn, 1)
            wide_ref[:, start : start + size] += piece
        return wide_ref[:, first : first + count]


def product(left, right):
    return jnp.dot(left, right, preferred_element_type=F32)


def product_t(left, right):
    return lax.dot_general(
        left, right, (((left.ndim - 1,), (1,)), ((), ())), preferred_element_type=F32
    )


def normal_share(values):
    return 0.5 + 0.5 * lax.erf(values * 2**-0.5)


def activate(values):
    return values * normal_share(values)


def gelu_back(values, grad):
    density = jnp.exp(-0.5 * values * values) * (2 * np.pi) ** -0.5
    return grad * (normal_share(values) + values * density)


def normalised(values):
    centred = values - jnp.mean(values, -1, keepdims=True)
    scale = lax.rsqrt(jnp.mean(centred * centred, -1, keepdims=True) + 1e-06)
    return centred * scale, scale


def norm_back(grad, gain, unit, scale):
    inner = grad * gain
    return scale * (
        inner
        - jnp.mean(inner, -1, keepdims=True)
        - unit * jnp.mean(inner * unit, -1, keepdims=True)
    )


def head_mask():
    shape = (HEADROWS, D)
    return lax.broadcasted_iota(jnp.int32, shape, 0) == (
        lax.broadcasted_iota(jnp.int32, shape, 1) // HDIM
    )


def token_norms(unit, norms, class_normed):
    token = lax.broadcasted_iota(jnp.int32, (TOKENS, D), 0)
    normed = unit * norms[0:1] + norms[1:2]
    return jnp.where(
        token < NPATCH, normed, jnp.where(token == NPATCH, class_normed, 0.0)
    ).astype(BF16)


def forward_kernel(
    plan,
    gathered_ref,
    pixels_ref,
    turn_ref,
    unit_out,
    scale_out,
    probs_ref,
    mixed_ref,
    looked_ref,
    class_ref,
    qkv_out,
    second_ref,
    hidden_ref,
    one_ref,
    two_ref,
    bottle_ref,
    middle_ref,
    send_ref,
    shards_ref,
    wide_ref,
    place_ref,
    left_ref,
    sums_ref,
    pack_ref,
    unit_ref,
    scale_ref,
    qkv_ref,
    out_sems,
    sems,
):
    shards = Shards(plan, gathered_ref, shards_ref, sems, range(plan.count))
    views = pixels_ref.shape[0]
    temper = HDIM ** (-0.5)
    shards.assemble(0, wide_ref)
    position = wide_ref[PD : PD + TOKENS].astype(F32)
    place_ref[...] = pltpu.roll(position, TOKENS - 1, 0)
    class_place = position[0:1]
    norms = position[NTOK : NTOK + 4]
    class_unit, class_scale = normalised(class_place)
    class_normed = (class_unit * norms[0:1] + norms[1:2]).astype(BF16).astype(F32)
    shards.assemble(1, qkv_ref)
    qkv_copy = pltpu.make_async_copy(qkv_ref, qkv_out, out_sems.at[4])
    qkv_copy.start()
    mask = head_mask()
    query = jnp.broadcast_to(class_normed, (HEADROWS, D)).astype(BF16)
    query = product(query, qkv_ref[:, :D]).astype(BF16).astype(F32)
    by_head = jnp.where(mask, query, 0.0).astype(BF16)
    looked = product_t(by_head, qkv_ref[:, D : 2 * D]).astype(BF16)
    looked_ref[...] = looked

    def copies(v):
        slot = lax.rem(v, 2)
        return (
            pltpu.make_async_copy(unit_ref.at[slot], unit_out.at[v], out_sems.at[slot]),
            pltpu.make_async_copy(scale_ref.at[slot], scale_out.at[v], out_sems.at[2 + slot]),
        )

    def view(v, carry):
        embedded = product(pixels_ref[v], wide_ref[:PD]) + place_ref[...]
        unit, scale = normalised(embedded)

        @pl.when(v >= 2)
        def _():
            for copy in copies(v - 2):
                copy.wait()

        unit_ref[lax.rem(v, 2)] = unit
        scale_ref[lax.rem(v, 2)] = jnp.broadcast_to(scale, (TOKENS, LANES))
        for copy in copies(v):
            copy.start()
        normed = token_norms(unit, norms, class_normed)
        scores = product_t(looked, normed) * temper
        token = lax.broadcasted_iota(jnp.int32, scores.shape, 1)
        scores = jnp.where(token < NTOK, scores, -1e30)
        top = jnp.max(scores, -1, keepdims=True)
        top = top + jnp.log(jnp.sum(jnp.exp(scores - top), -1, keepdims=True))
        head = lax.broadcasted_iota(jnp.int32, scores.shape, 0)
        probs = jnp.where(head < HEADS, jnp.exp(scores - top), 0.0)
        probs_ref[v] = probs
        mixed_ref[v] = product(probs.astype(BF16), normed).astype(BF16)
        return carry

    lax.fori_loop(0, views, view, 0)
    mixed = mixed_ref[...].reshape(views * HEADROWS, D)
    valued = product(mixed, qkv_ref[:, 2 * D :]).reshape(views, HEADROWS, D)
    attended = jnp.sum(jnp.where(mask[None], valued, 0.0), 1).astype(BF16)
    pack_ref[:, :D] = attended.astype(F32)
    shards.times(2, 0, pack_ref[:, :D], left_ref, sums_ref)
    middle = class_place + sums_ref[...]
    unit, scale = normalised(middle)
    middle_ref[0], middle_ref[1] = unit, jnp.broadcast_to(scale, (views, D))
    normed = (unit * norms[2:3] + norms[3:4]).astype(BF16)
    pack_ref[:, D : 2 * D] = normed.astype(F32)
    shards.times(3, 0, pack_ref[:, D : 2 * D], left_ref, hidden_ref)
    act = activate(hidden_ref[...]).astype(BF16)
    pack_ref[:, 2 * D : 2 * D + F] = act.astype(F32)
    shards.times(4, 0, act.astype(F32), left_ref, sums_ref)
    unit, scale = normalised(middle + sums_ref[...])
    middle_ref[2], middle_ref[3] = unit, jnp.broadcast_to(scale, (views, D))
    final = jnp.concatenate(
        [shards.eight(4, F // 8, tile // 2, tile % 2) for tile in range(D // LANES)], 1
    )
    cls = (unit * final[0:1] + final[1:2]).astype(BF16)
    place = 2 * D + F
    pack_ref[:, place : place + D] = cls.astype(F32)
    shards.times(5, 0, cls.astype(F32), left_ref, one_ref)
    first = activate(one_ref[...]).astype(BF16)
    pack_ref[:, place + D : AHEAD] = first.astype(F32)
    pack_ref[:, AHEAD:] = jnp.zeros((views, pack_ref.shape[1] - AHEAD), F32)
    shards.times(5, D, first.astype(F32), left_ref, two_ref)
    second = activate(two_ref[...]).astype(BF16)
    second_ref[...] = second
    shards.times(6, 0, second.astype(F32), left_ref, bottle_ref)
    bottle = bottle_ref[...]
    scale = lax.rsqrt(jnp.sum(bottle * bottle, -1, keepdims=True) + 1e-06)
    rows = product(turn_ref[...], (bottle * scale).astype(BF16)).astype(BF16)
    for device, sent in enumerate(plan.sent):
        send_ref[device, :, :B] = rows
        for lane, size, place in sent:
            start = lane // LANES * LANES
            piece = pack_ref[:, start : start + size + (LANES if lane > start else 0)]
            if lane > start:
                piece = pltpu.roll(piece, piece.shape[1] - (lane - start), 1)
            send_ref[device, :, B + place : B + place + size] = piece[:, :size].astype(BF16)
    class_ref[...] = jnp.concatenate(
        [
            class_unit,
            class_normed,
            query[0:1],
            jnp.broadcast_to(class_scale, (1, D)),
            norms,
            final,
        ],
        0,
    )
    for v in range(max(0, views - 2), views):
        for copy in copies(v):
            copy.wait()
    qkv_copy.wait()
    shards.finish()


def forward(plan, gathered, pixels, turn):
    views = pixels.shape[0]
    shapes = [
        ((views, TOKENS, D), F32),
        ((views, TOKENS, LANES), F32),
        ((views, HEADROWS, TOKENS), F32),
        ((views, HEADROWS, D), BF16),
        ((HEADROWS, D), BF16),
        ((16, D), F32),
        ((D, 3 * D), BF16),
        ((views, H), BF16),
        ((views, F), F32),
        ((views, H), F32),
        ((views, H), F32),
        ((views, B), F32),
        ((4, views, D), F32),
        ((plan.count, views, B + plan.reach), BF16),
    ]
    most, longest = plan.largest()
    return pl.pallas_call(
        functools.partial(forward_kernel, plan),
        out_shape=[jax.ShapeDtypeStruct(shape, dtype) for shape, dtype in shapes],
        in_specs=[pl.BlockSpec(memory_space=pl.ANY)]
        + [pl.BlockSpec(memory_space=pltpu.VMEM)] * 2,
        out_specs=[
            pl.BlockSpec(memory_space=pl.ANY if index in (0, 1, 6) else pltpu.VMEM)
            for index in range(len(shapes))
        ],
        scratch_shapes=[
            pltpu.VMEM((plan.count, plan.buffer // TILE, TILE, LANES), BF16),
            pltpu.VMEM((round_up(PD + NTOK + 4, TILE), D), BF16),
            pltpu.VMEM((TOKENS, D), F32),
            pltpu.VMEM((most, views, longest), F32),
            pltpu.VMEM((views, D), F32),
            pltpu.VMEM((views, round_up(AHEAD + CHUNK, LANES) + LANES), F32),
            pltpu.VMEM((2, TOKENS, D), F32),
            pltpu.VMEM((2, TOKENS, LANES), F32),
            pltpu.VMEM((D, 3 * D), BF16),
            pltpu.SemaphoreType.DMA((5,)),
            pltpu.SemaphoreType.DMA((plan.count,)),
        ],
        compiler_params=pltpu.CompilerParams(vmem_limit_bytes=VMEM_LIMIT),
        cost_estimate=pl.CostEstimate(
            flops=60 * 10**9, bytes_accessed=40 * 10**6, transcendentals=10**5
        ),
    )(gathered, pixels, turn)


def proto_kernel(
    start_ref,
    rows_ref,
    columns_ref,
    others_ref,
    center_ref,
    note_ref,
    center_out_ref,
    student_ref,
    teacher_ref,
    sums_ref,
):
    count, groups = rows_ref.shape[1], note_ref.shape[0]
    views = (note_ref.shape[1] - 8 * -(-count // B)) // 3
    logits = product(rows_ref[1], others_ref[...])
    center = center_ref[...]
    center_out_ref[...] = CENTER_MOMENTUM * center + (1.0 - CENTER_MOMENTUM) * jnp.mean(
        logits, 0, keepdims=True
    )
    exp_teacher = jnp.exp((logits - center) / TEACHER_TEMP)
    teacher_ref[...] = exp_teacher
    scaled = product(rows_ref[0], columns_ref[...]) / STUDENT_TEMP
    exp_student = jnp.exp(scaled)
    student_ref[...] = exp_student
    turned = []
    for which, values in enumerate((exp_student, exp_teacher, exp_teacher * scaled)):
        total = jnp.broadcast_to(jnp.sum(values, 1, keepdims=True), (count, LANES))
        turned.append(total.T[0:1])
        if which < 2:
            sums_ref[:, which * LANES : (which + 1) * LANES] = total
    turned = jnp.concatenate(turned + [jnp.zeros((5, count), F32)], 0)
    for step in range(-(-count // B)):
        part = turned[:, step * B : (step + 1) * B]
        lines = slice(3 * views + 8 * step, 3 * views + 8 * (step + 1))
        note_ref[:, lines, : part.shape[1]] = jnp.broadcast_to(part[None], (groups,) + part.shape)
        if part.shape[1] < B:
            note_ref[:, lines, part.shape[1] :] = jnp.zeros((groups, 8, B - part.shape[1]), F32)
    start = pl.multiple_of(start_ref[0], 8)
    columns = columns_ref[...].astype(F32)
    for which, source in enumerate((student_ref, teacher_ref)):
        pulls = lax.dot_general(
            source[pl.ds(start, groups * views), :],
            columns,
            (((1,), (1,)), ((), ())),
            precision=PRECISE,
            preferred_element_type=F32,
        )
        note_ref[:, which * views : (which + 1) * views, :] = pulls.reshape(groups, views, B)
    own = sums_ref[pl.ds(start, groups * views), :]
    note_ref[:, 2 * views : 3 * views, :] = own.reshape(groups, views, B)


def prototypes(start, rows, columns, others, center, groups, views):
    count, width = rows.shape[1], columns.shape[1]
    shapes = [(groups, 3 * views + 8 * -(-count // B), B), (1, width)]
    return pl.pallas_call(
        proto_kernel,
        out_shape=[jax.ShapeDtypeStruct(shape, F32) for shape in shapes],
        in_specs=[pl.BlockSpec(memory_space=pltpu.SMEM)]
        + [pl.BlockSpec(memory_space=pltpu.VMEM)] * 4,
        out_specs=[pl.BlockSpec(memory_space=pltpu.VMEM)] * len(shapes),
        scratch_shapes=[pltpu.VMEM((count, width), F32)] * 2
        + [pltpu.VMEM((count, 2 * LANES), F32)],
        compiler_params=pltpu.CompilerParams(vmem_limit_bytes=32 * 1024 * 1024),
        cost_estimate=pl.CostEstimate(
            flops=3 * 10**9, bytes_accessed=6 * 10**6, transcendentals=10**6
        ),
    )(start, rows, columns, others, center)


def proto_back_kernel(
    start_ref,
    rows_ref,
    columns_ref,
    others_ref,
    center_ref,
    totals_ref,
    table_ref,
    scale_ref,
    grad_ref,
    square_ref,
    work_ref,
):
    count = rows_ref.shape[1]
    totals = jnp.broadcast_to(totals_ref[0:2][:, None, :], (2, 8, count))
    student, teacher = (totals[which].T[:, :1] for which in range(2))
    logits = product(rows_ref[1], others_ref[...])
    targets = jnp.exp((logits - center_ref[...]) / TEACHER_TEMP) / teacher
    scaled = product(rows_ref[0], columns_ref[...]) / STUDENT_TEMP
    grad = (jnp.exp(scaled) / student - targets) / STUDENT_TEMP
    work_ref[...] = jnp.dot(
        rows_ref[0].astype(F32).T, grad, precision=PRECISE, preferred_element_type=F32
    )
    scale = scale_ref[...]
    inner = jnp.sum(work_ref[...] * table_ref[...], 0, keepdims=True)
    start = pl.multiple_of(start_ref[0], 8)
    lines = pl.ds(start, grad_ref.shape[0])
    grad = work_ref[lines, :] * scale - table_ref[lines, :] * (scale * scale * scale * inner)
    grad_ref[...] = grad
    square = jnp.sum(grad * grad, 0, keepdims=True)
    square_ref[...] = jnp.broadcast_to(square, square_ref.shape)


def prototypes_back(start, depth, *values):
    count, width = values[0].shape[1], values[1].shape[1]
    shapes = [(depth, width), (8, width)]
    return pl.pallas_call(
        proto_back_kernel,
        out_shape=[jax.ShapeDtypeStruct(shape, F32) for shape in shapes],
        in_specs=[pl.BlockSpec(memory_space=pltpu.SMEM)]
        + [pl.BlockSpec(memory_space=pltpu.VMEM)] * len(values),
        out_specs=[pl.BlockSpec(memory_space=pltpu.VMEM)] * len(shapes),
        scratch_shapes=[pltpu.VMEM((B, width), F32)],
        compiler_params=pltpu.CompilerParams(vmem_limit_bytes=32 * 1024 * 1024),
        cost_estimate=pl.CostEstimate(
            flops=3 * 10**9, bytes_accessed=6 * 10**6, transcendentals=10**6
        ),
    )(start, *values)


def rows_back_kernel(
    plan,
    low_ref,
    gathered_ref,
    note_ref,
    class_ref,
    hidden_ref,
    one_ref,
    two_ref,
    bottle_ref,
    middle_ref,
    pack_ref,
    stream_ref,
    extra_ref,
    shards_ref,
    left_ref,
    values_ref,
    wide_ref,
    sems,
):
    shards = Shards(plan, gathered_ref, shards_ref, sems, reversed(range(plan.count)))
    work = (values_ref, left_ref, wide_ref)
    norms, final = class_ref[4:8], class_ref[8:10]

    views = bottle_ref.shape[0]
    note = jnp.sum(note_ref[...], 0)
    sums = note[2 * views : 3 * views]
    student, teacher = sums[:, :1], sums[:, LANES : LANES + 1]
    grad_rows = (note[:views] / student - note[views : 2 * views] / teacher) / STUDENT_TEMP
    grad_rows = jnp.where(low_ref[0] == 0, 0.0, grad_rows).astype(BF16).astype(F32)
    bottle = bottle_ref[...]
    scale = lax.rsqrt(jnp.sum(bottle * bottle, -1, keepdims=True) + 1e-06)
    grad_bottle = (
        grad_rows * scale - bottle * scale**3 * jnp.sum(grad_rows * bottle, -1, keepdims=True)
    ).astype(BF16)
    place = 2 * D + F
    pack_ref[:, place : place + B] = grad_bottle
    grad_two = shards.back(6, 0, H, grad_bottle.astype(F32), *work)
    grad_two = gelu_back(two_ref[...], grad_two).astype(BF16)
    pack_ref[:, place + B : place + B + H] = grad_two
    grad_one = shards.back(5, D, H, grad_two.astype(F32), *work)
    grad_one = gelu_back(one_ref[...], grad_one).astype(BF16)
    pack_ref[:, place + B + H : place + B + 2 * H] = grad_one
    grad_cls = shards.back(5, 0, D, grad_one.astype(F32), *work)
    unit, scale = middle_ref[2], middle_ref[3]
    gain_last = jnp.sum(grad_cls * unit, 0, keepdims=True)
    shift_last = jnp.sum(grad_cls, 0, keepdims=True)
    grad_stream = norm_back(grad_cls, final[0:1], unit, scale)
    grad_branch = grad_stream.astype(BF16)
    pack_ref[:, D + F : 2 * D + F] = grad_branch
    grad_hidden = shards.back(4, 0, F, grad_branch.astype(F32), *work)
    grad_hidden = gelu_back(hidden_ref[...], grad_hidden).astype(BF16)
    pack_ref[:, D : D + F] = grad_hidden
    grad_normed = shards.back(3, 0, D, grad_hidden.astype(F32), *work)
    unit, scale = middle_ref[0], middle_ref[1]
    extra_ref[...] = jnp.concatenate(
        [
            jnp.sum(grad_normed * unit, 0, keepdims=True),
            jnp.sum(grad_normed, 0, keepdims=True),
            gain_last,
            shift_last,
            jnp.zeros((4, D), F32),
        ],
        0,
    )
    grad_middle = grad_stream + norm_back(grad_normed, norms[2:3], unit, scale)
    stream_ref[...] = grad_middle
    grad_mixed = grad_middle.astype(BF16)
    pack_ref[:, :D] = grad_mixed
    grad_att = shards.back(2, 0, D, grad_mixed.astype(F32), *work).astype(BF16)
    pack_ref[:, place + B + 2 * H : place + B + 2 * H + D] = grad_att
    shards.finish()


def rows_back(plan, low, gathered, note, kept):
    views = kept[-1].shape[1]
    shapes = [((views, 3 * D + F + B + 2 * H), BF16), ((views, D), F32), ((8, D), F32)]
    most, longest = plan.largest()
    return pl.pallas_call(
        functools.partial(rows_back_kernel, plan),
        out_shape=[jax.ShapeDtypeStruct(shape, dtype) for shape, dtype in shapes],
        in_specs=[pl.BlockSpec(memory_space=pltpu.SMEM), pl.BlockSpec(memory_space=pl.ANY)]
        + [pl.BlockSpec(memory_space=pltpu.VMEM)] * (1 + len(kept)),
        out_specs=[pl.BlockSpec(memory_space=pltpu.VMEM)] * len(shapes),
        scratch_shapes=[
            pltpu.VMEM((plan.count, plan.buffer // TILE, TILE, LANES), BF16),
            pltpu.VMEM((most, views, longest), F32),
            pltpu.VMEM((views, F), F32),
            pltpu.VMEM((views, F + 2 * LANES), F32),
            pltpu.SemaphoreType.DMA((plan.count,)),
        ],
        compiler_params=pltpu.CompilerParams(vmem_limit_bytes=40 * 1024 * 1024),
        cost_estimate=pl.CostEstimate(
            flops=30 * 10**9, bytes_accessed=30 * 10**6, transcendentals=10**5
        ),
    )(low, gathered, note, *kept)


def tokens_back_kernel(
    odd_ref,
    behind_ref,
    stream_ref,
    ends_ref,
    unit_ref,
    scale_ref,
    probs_ref,
    looked_ref,
    class_ref,
    qkv_ref,
    pixels_ref,
    first_ref,
    second_ref,
    kept_ref,
    sent_ref,
    patch_ref,
    place_ref,
    reach_ref,
    back_ref,
    mixed_ref,
    rows_ref,
):
    v = pl.program_id(0)
    views = stream_ref.shape[0]
    temper = HDIM ** (-0.5)
    norms = class_ref[4:8]
    class_unit, class_normed, class_scale = (class_ref[row : row + 1] for row in (0, 1, 3))

    @pl.when(v == 0)
    def _():
        place = 2 * D + F + B + 2 * H
        grad_att = behind_ref[:, place : place + D].astype(F32)
        spread = jnp.where(head_mask()[None], grad_att[:, None, :], 0.0).astype(BF16)
        back = product_t(spread.reshape(views * HEADROWS, D), qkv_ref[:, 2 * D :])
        back_ref[...] = back.astype(BF16).reshape(views, HEADROWS, D)
        patch_ref[...] = jnp.zeros(patch_ref.shape, F32)
        place_ref[...] = jnp.zeros(place_ref.shape, F32)
        reach_ref[...] = jnp.zeros(reach_ref.shape, F32)
        rows_ref[...] = jnp.zeros(rows_ref.shape, F32)

    unit = unit_ref[0]
    scale = scale_ref[0][:, :1]
    normed = token_norms(unit, norms, class_normed)
    back = back_ref[v]
    probs = probs_ref[0]
    grad_probs = product_t(back, normed)
    delta = jnp.sum(probs * grad_probs, -1, keepdims=True)
    grad_scores = (probs * (grad_probs - delta)).astype(BF16)
    reach = product(grad_scores, normed) * temper
    mixed_ref[v] = reach.astype(BF16)
    reach_ref[...] += reach
    left = jnp.concatenate([grad_scores.astype(F32), probs.astype(BF16).astype(F32)], 0)
    looked = (looked_ref[...].astype(F32) * temper).astype(BF16)
    grad = product(left.T.astype(BF16), jnp.concatenate([looked, back], 0))
    row = lax.broadcasted_iota(jnp.int32, (8, D), 0)
    rows_ref[0] += jnp.where(row == v, grad[NPATCH : NPATCH + 1], 0.0)
    token = lax.broadcasted_iota(jnp.int32, (TOKENS, D), 0)
    grad = jnp.where(token < NPATCH, grad, 0.0)
    rows_ref[1, 0:1] += jnp.sum(grad * unit, 0, keepdims=True)
    rows_ref[2, 0:1] += jnp.sum(grad, 0, keepdims=True)
    stream = norm_back(grad, norms[0:1], unit, scale)
    place_ref[...] += stream
    patch_ref[...] += product(pixels_ref[0], stream.astype(BF16))

    @pl.when(v == views - 1)
    def _():
        keyed = product(mixed_ref[...].reshape(views * HEADROWS, D), qkv_ref[:, D : 2 * D])
        keyed = jnp.where(head_mask()[None], keyed.reshape(views, HEADROWS, D), 0.0)
        grad_query = jnp.sum(keyed, 1).astype(BF16)
        class_row = rows_ref[0][:views] + product_t(grad_query, qkv_ref[:, :D])
        class_stream = norm_back(class_row, norms[0:1], class_unit, class_scale)
        class_stream = class_stream + stream_ref[...]
        ends = [
            (0, jnp.sum(class_stream, 0, keepdims=True)),
            (NTOK, rows_ref[1, 0:1] + jnp.sum(class_row * class_unit, 0, keepdims=True)),
            (NTOK + 1, rows_ref[2, 0:1] + jnp.sum(class_row, 0, keepdims=True)),
            (NTOK + 2, ends_ref[0:1]),
            (NTOK + 3, ends_ref[1:2]),
        ]
        tail = pltpu.roll(place_ref[...], 1, 0)
        for row, value in ends:
            tail = jnp.where(token == row, value, tail)
        upper = 2 * SET - 8
        rest = jnp.zeros((2 * SET - (PD - upper) - TOKENS, D), F32)
        query_row = lax.broadcasted_iota(jnp.int32, (8, D), 0) == 0
        total = jnp.sum(grad_query.astype(F32), 0, keepdims=True)
        shared = [reach_ref[...], jnp.where(query_row, total, pltpu.roll(ends_ref[...], 7, 0))]
        shared = jnp.concatenate(shared + [jnp.zeros((SHARED - HEADROWS - 8, D), F32)], 0)
        kept_ref[2 * SET :] = shared
        sent_ref[2 * SET :] = shared.astype(BF16)
        last = jnp.concatenate([patch_ref[upper:], tail, rest], 0)

        @pl.when(odd_ref[0] == 0)
        def _():
            kept_ref[: 2 * SET] = patch_ref[: 2 * SET]
            sent_ref[: 2 * SET] = last.astype(BF16)

        @pl.when(odd_ref[0] != 0)
        def _():
            kept_ref[: 2 * SET] = last
            sent_ref[: 2 * SET] = patch_ref[: 2 * SET].astype(BF16)


def tokens_back(odd, behind, grad_middle, ends, kept, pixels, *before):
    views = grad_middle.shape[0]

    def whole(values):
        return pl.BlockSpec(values.shape, lambda v: (0,) * values.ndim)

    def by_view(values):
        return pl.BlockSpec((1,) + values.shape[1:], lambda v: (v,) + (0,) * (values.ndim - 1))

    unit, scale, probs, looked, classes, qkv_w = kept
    shape = (2 * SET + SHARED, D)
    return pl.pallas_call(
        tokens_back_kernel,
        grid=(views,),
        out_shape=[jax.ShapeDtypeStruct(shape, F32), jax.ShapeDtypeStruct(shape, BF16)],
        in_specs=[
            pl.BlockSpec(memory_space=pltpu.SMEM),
            whole(behind),
            whole(grad_middle),
            whole(ends),
            by_view(unit),
            by_view(scale),
            by_view(probs),
            whole(looked),
            whole(classes),
            whole(qkv_w),
            by_view(pixels),
        ]
        + [pl.BlockSpec(memory_space=pl.ANY)] * len(before),
        out_specs=[pl.BlockSpec(shape, lambda v: (0, 0))] * 2,
        scratch_shapes=[
            pltpu.VMEM((PD, D), F32),
            pltpu.VMEM((TOKENS, D), F32),
            pltpu.VMEM((HEADROWS, D), F32),
            pltpu.VMEM((views, HEADROWS, D), BF16),
            pltpu.VMEM((views, HEADROWS, D), BF16),
            pltpu.VMEM((3, 8, D), F32),
        ],
        compiler_params=pltpu.CompilerParams(vmem_limit_bytes=60 * 1024 * 1024),
        cost_estimate=pl.CostEstimate(
            flops=15 * 10**9, bytes_accessed=15 * 10**6, transcendentals=10**5
        ),
    )(odd, behind, grad_middle, ends, unit, scale, probs, looked, classes, qkv_w, pixels, *before)


def early_kernel(
    plan,
    most,
    tab_ref,
    ahead_ref,
    common_hbm,
    behind_hbm,
    line_ref,
    square_ref,
    common_ref,
    behind_ref,
    sem,
):
    line_ref[...] = jnp.zeros(line_ref.shape, F32)

    def fetch(source, target, column, size):
        copy = pltpu.make_async_copy(
            source.at[:, pl.ds(column, size)], target.at[:, pl.ds(0, size)], sem
        )
        copy.start()
        copy.wait()

    def turned(lane):
        start = pl.multiple_of(lane // LANES * LANES, LANES)
        both = common_ref[:, pl.ds(start, 2 * LANES)].astype(F32)
        both = pltpu.roll(both, lax.rem(2 * LANES - (lane - start), 2 * LANES), 1)
        return both[:, :LANES].T.astype(BF16)

    def store(goal, width, tile, block):
        line_ref[pl.ds(goal + tile, block.shape[0], stride=width), :] = block

    for part in range(most):
        kind, base, chunks, row0 = (tab_ref[1 + 4 * part + i] for i in range(4))
        for index, (_, column) in SPANS.items():
            cols = PIECES[index][2]
            width = cols // LANES

            @pl.when(kind == index)
            def _(column=column, cols=cols, width=width):
                fetch(behind_hbm, behind_ref, column, cols)

                def move(step, carry):
                    goal = base + step * (CHUNK * width)
                    lanes = pl.ds(pl.multiple_of(row0 + step * CHUNK, LANES), CHUNK)
                    left = ahead_ref[:, lanes].astype(F32).T.astype(BF16)
                    block = product(left, behind_ref[:, :cols])
                    for tile in range(width):
                        store(goal, width, tile, block[:, tile * LANES : (tile + 1) * LANES])
                    return carry

                lax.fori_loop(0, chunks, move, 0)

        @pl.when(kind == 8)
        def _():
            fetch(behind_hbm, behind_ref, 2 * D + F, B)
            fetch(common_hbm, common_ref, SECOND, H + D)

            def move(step, carry):
                left = turned(row0 + step * CHUNK)
                block = product(left, behind_ref[:, :B])
                for tile in range(B // LANES):
                    piece = block[:, tile * LANES : (tile + 1) * LANES]
                    store(base + step * (CHUNK * B // LANES), B // LANES, tile, piece)
                return carry

            lax.fori_loop(0, chunks, move, 0)

        @pl.when(kind == 5)
        def _():
            for tile in range(D // LANES):
                store(base, D // LANES, tile, jnp.zeros((8, LANES), F32))

        @pl.when(kind == 1)
        def _():
            fetch(behind_hbm, behind_ref, ATT_COLUMN, D)
            fetch(common_hbm, common_ref, 0, common_ref.shape[1])

            def move(step, carry):
                width = 3 * D // LANES
                goal = base + step * (CHUNK * width)
                side = lax.broadcasted_iota(jnp.int32, (CHUNK, LANES), 1)
                for pair in range(HEADS // 2):
                    right = behind_ref[:, pair * LANES : (pair + 1) * LANES]
                    lane = 2 * pair * D + row0 + step * CHUNK
                    first, second = (product(turned(lane + D * head), right) for head in range(2))
                    block = jnp.where(side < HDIM, first, second)
                    store(goal, width, 2 * D // LANES + pair, block)
                return carry

            lax.fori_loop(0, chunks, move, 0)

    shift = tab_ref[0]
    shape = (STEPS, LANES)
    place = lax.broadcasted_iota(jnp.int32, shape, 0) * LANES
    place = place + lax.broadcasted_iota(jnp.int32, shape, 1) - shift

    def clear(step, total):
        start = pl.multiple_of(step * STEPS, 8)
        entry = place + start * LANES
        lines = pl.ds(pl.multiple_of(FRONT + start, 8), STEPS)
        kept = jnp.where((entry >= 0) & (entry < plan.size), line_ref[lines, :], 0.0)
        line_ref[lines, :] = kept
        return total + kept * kept

    total = lax.fori_loop(0, plan.lines // STEPS, clear, jnp.zeros(shape, F32))
    square_ref[...] = jnp.sum(total.reshape(STEPS // 8, 8, LANES), 0)


def early_gradient(plan, table, ahead, common, behind):
    return pl.pallas_call(
        functools.partial(early_kernel, plan, table.shape[0] // 4),
        out_shape=[
            jax.ShapeDtypeStruct((plan.grad_scratch, LANES), F32),
            jax.ShapeDtypeStruct((8, LANES), F32),
        ],
        in_specs=[
            pl.BlockSpec(memory_space=pltpu.SMEM),
            pl.BlockSpec(memory_space=pltpu.VMEM),
            pl.BlockSpec(memory_space=pl.ANY),
            pl.BlockSpec(memory_space=pl.ANY),
        ],
        out_specs=[pl.BlockSpec(memory_space=pltpu.VMEM)] * 2,
        scratch_shapes=[
            pltpu.VMEM(common.shape, BF16),
            pltpu.VMEM((behind.shape[0], F), BF16),
            pltpu.SemaphoreType.DMA,
        ],
        compiler_params=pltpu.CompilerParams(vmem_limit_bytes=60 * 1024 * 1024),
        cost_estimate=pl.CostEstimate(
            flops=10 * 10**9, bytes_accessed=10 * 10**6, transcendentals=0
        ),
    )(table, ahead, common, behind)


def late_kernel(
    plan,
    most,
    tab_ref,
    lines_ref,
    wide_ref,
    left_ref,
    right_ref,
    ends_ref,
    out_ref,
    line_ref,
    sem,
):
    used = FRONT + plan.lines + 8
    copy = pltpu.make_async_copy(lines_ref.at[pl.ds(0, used)], line_ref.at[pl.ds(0, used)], sem)
    copy.start()
    copy.wait()

    def add(goal, width, tile, block):
        lines = pl.ds(goal + tile, CHUNK, stride=width)
        line_ref[lines, :] = line_ref[lines, :] + block

    for part in range(most):
        kind, base, chunks, row0 = (tab_ref[1 + 4 * part + i] for i in range(4))

        @pl.when(kind == 0)
        def _():
            def move(step, carry):
                width = D // LANES
                rows = pl.ds(pl.multiple_of(row0 + step * CHUNK, 8), CHUNK)
                for tile in range(width):
                    block = wide_ref[rows, tile * LANES : (tile + 1) * LANES]
                    add(base + step * (CHUNK * width), width, tile, block)
                return carry

            lax.fori_loop(0, chunks, move, 0)

        @pl.when(kind == 1)
        def _():
            def move(step, carry):
                width = 3 * D // LANES
                rows = pl.ds(pl.multiple_of(row0 + step * CHUNK, 8), CHUNK)
                block = jnp.dot(
                    left_ref[rows, :],
                    right_ref[...],
                    precision=PRECISE,
                    preferred_element_type=F32,
                )
                for tile in range(2 * D // LANES):
                    piece = block[:, tile * LANES : (tile + 1) * LANES]
                    add(base + step * (CHUNK * width), width, tile, piece)
                return carry

            lax.fori_loop(0, chunks, move, 0)

        @pl.when(kind == 5)
        def _():
            width = D // LANES
            for tile in range(width):
                lines = pl.ds(base + tile, 8, stride=width)
                block = ends_ref[:, tile * LANES : (tile + 1) * LANES]
                line_ref[lines, :] = line_ref[lines, :] + block

    shift = tab_ref[0]
    turn = lax.rem(LANES - shift, LANES)
    lane = lax.broadcasted_iota(jnp.int32, (STEPS + 8, LANES), 1)

    def align(step, carry):
        start = pl.multiple_of(step * STEPS, 8)
        lines = pl.ds(pl.multiple_of(FRONT + start, 8), STEPS + 8)
        here = pltpu.roll(line_ref[lines, :], turn, 1)
        below = pltpu.roll(here, STEPS + 7, 0)
        both = jnp.where(lane < LANES - shift, here, below)
        out_ref[pl.ds(start, STEPS), :] = both[:STEPS]
        return carry

    lax.fori_loop(0, plan.lines // STEPS, align, 0)


def late_gradient(plan, table, lines, *values):
    return pl.pallas_call(
        functools.partial(late_kernel, plan, table.shape[0] // 4),
        out_shape=jax.ShapeDtypeStruct((plan.lines, LANES), F32),
        in_specs=[pl.BlockSpec(memory_space=pltpu.SMEM), pl.BlockSpec(memory_space=pl.ANY)]
        + [pl.BlockSpec(memory_space=pltpu.VMEM)] * len(values),
        out_specs=pl.BlockSpec(memory_space=pltpu.VMEM),
        scratch_shapes=[
            pltpu.VMEM((plan.grad_scratch, LANES), F32),
            pltpu.SemaphoreType.DMA,
        ],
        compiler_params=pltpu.CompilerParams(vmem_limit_bytes=24 * 1024 * 1024),
    )(table, lines, *values).reshape(-1)[: plan.size]


def adam_update(weight, grad, first, second, rate):
    first = BETA_FIRST * first + (1.0 - BETA_FIRST) * grad
    second = BETA_SECOND * second + (1.0 - BETA_SECOND) * grad * grad
    stepped = (
        first
        / (1.0 - BETA_FIRST**STEP)
        / (jnp.sqrt(second / (1.0 - BETA_SECOND**STEP)) + ADAM_EPSILON)
    )
    return (weight - rate * (stepped + WEIGHT_DECAY * weight), first, second)


def per_device(
    plan,
    params,
    first_moment,
    second_moment,
    teacher,
    protos,
    proto_first,
    proto_second,
    teacher_protos,
    center,
    patches,
    partner,
):
    reps, groups = lax.axis_size("rep"), lax.axis_size("grp")
    count, half = reps * groups, reps * groups // 2
    rep, grp = lax.axis_index("rep"), lax.axis_index("grp")
    device = rep * groups + grp
    low = rep % 2 == 0
    place = rep // 2 * groups + grp
    halves = [
        [r * groups + g for r in range(parity, reps, 2) for g in range(groups)] for parity in (0, 1)
    ]
    swap = [(r, r ^ 1) for r in range(reps)]
    own_views = patches.shape[0]
    views = 2 * own_views

    def trade(values):
        return lax.ppermute(values, "rep", swap)

    def trade_low(values):
        return jnp.where(low, values, trade(values))

    def in_order(values):
        other = trade(values)
        return jnp.where(low, values, other), jnp.where(low, other, values)

    pairs = [list(range(parity, reps, 2)) for parity in (0, 1)]
    lines = reps // 2
    tables = jnp.stack([protos, teacher_protos]).astype(BF16)
    around = [tables]
    for step in range(2, reps, 2):
        around.append(lax.ppermute(tables, "rep", [(r, (r + step) % reps) for r in range(reps)]))

    table = jnp.asarray(plan.lay_table)[device]
    given = trade(lay_out(plan, table, jnp.where(low, teacher, params)))
    kept = lay_out(plan, table, jnp.where(low, params, teacher))
    given, around = lax.optimization_barrier((given, around))
    shards = jnp.stack([jnp.where(low, kept, given), jnp.where(low, given, kept)])
    gathered = lax.all_gather(shards, BOTH, axis=0, axis_index_groups=halves)
    gathered = gathered.reshape(half, 2, -1, TILE, LANES)
    patches, partner, given = lax.optimization_barrier((patches, partner, given))
    pixels = jnp.concatenate(in_order(patches), 0)
    pixels = jnp.pad(pixels, ((0, 0), (0, TOKENS - NPATCH), (0, 0)))
    around = jnp.concatenate([jnp.stack(around[::-1])] * 2)
    around = lax.dynamic_slice_in_dim(around, lines - 1 - rep // 2, lines, 0)
    tables = jnp.stack(in_order(around))
    tables = tables.transpose(2, 1, 0, 3, 4).reshape(2, B, -1).astype(F32)
    places = in_order(partner.astype(F32))

    def columns_of(values):
        scale = lax.rsqrt(jnp.sum(values * values, 0, keepdims=True) + 1e-06)
        return (values * scale).astype(BF16), scale

    columns, column_scale = columns_of(tables[0])
    teacher_columns = columns_of(tables[1])[0]

    here = jnp.arange(views)
    source = jnp.concatenate([places[0], places[1] + own_views]).astype(jnp.int32)
    source = jnp.where(low, here, source)
    turn = (source[:, None] == here[None, :]).astype(BF16)

    turn, columns, teacher_columns = lax.optimization_barrier((turn, columns, teacher_columns))
    kept = forward(plan, gathered, pixels, turn)
    unit, scale, probs, mixed, looked, classes, qkv_w, second = kept[:8]
    received = lax.all_to_all(kept[-1], BOTH, 0, 0)
    received = received.reshape(reps // 2, 2, groups * views, -1)
    all_rows = received[..., :B]
    ahead = received[:, 0, :, B:].reshape(half * views, -1)

    def gather_rows(values):
        return lax.all_gather(values, BOTH, axis=0, axis_index_groups=halves).reshape(
            half * views, -1
        )

    common = [mixed[:, :HEADS].reshape(views, -1), second]
    common.append(jnp.pad(classes[1:3], ((0, views - 2), (0, 0))).astype(BF16))
    common = jnp.concatenate(common, 1)
    other = trade(common)
    all_rows, ahead, other = lax.optimization_barrier((all_rows, ahead, other))
    common = jnp.where(low, common, other)

    all_rows = all_rows.transpose(1, 0, 2, 3).reshape(2, -1, B)
    start = (rep // 2 * groups * views).astype(jnp.int32)[None]
    note, new_center = prototypes(
        start, all_rows, columns, teacher_columns, center[None], groups, views
    )
    common = gather_rows(common)
    new_center = new_center[0]
    note = lax.all_to_all(note, "grp", 0, 0)
    totals = jnp.sum(note[:, 3 * views :], 0)
    totals = totals.reshape(-1, 8, B).transpose(1, 0, 2).reshape(8, -1)[:, : half * views]
    loss_value = jnp.sum(jnp.log(totals[0]) - totals[2] / totals[1])
    depth = protos.shape[0]
    grad_protos, proto_squares = prototypes_back(
        (rep * depth).astype(jnp.int32)[None],
        depth,
        all_rows,
        columns,
        teacher_columns,
        center[None],
        totals,
        tables[0],
        column_scale,
    )
    behind, grad_middle, ends = rows_back(
        plan, low.astype(jnp.int32)[None], gathered, note, (classes,) + tuple(kept[8:13])
    )
    odd, far = grp % 2 == 1, grp // 2 % 2 == 1
    behind_rows = trade_low(behind)
    kept_rows, sent_rows = tokens_back(
        odd.astype(jnp.int32)[None],
        behind,
        grad_middle,
        ends,
        (unit, scale, probs, looked, classes, qkv_w),
        pixels.transpose(0, 2, 1),
        behind_rows,
        grad_protos,
    )

    def across(bit, values):
        return lax.ppermute(values, "grp", [(g, g ^ bit) for g in range(groups)])

    partial = kept_rows + across(1, sent_rows).astype(F32)
    first, second = partial[:SET], partial[SET : 2 * SET]
    shared = partial[2 * SET :]
    other = jnp.concatenate([jnp.where(far, first, second), shared], 0).astype(BF16)
    partial = jnp.concatenate([jnp.where(far, second, first), shared], 0)
    partial = partial + across(2, other).astype(F32)
    behind_rows, partial = lax.optimization_barrier((behind_rows, partial))
    behind_rows = gather_rows(behind_rows)
    depth = partial.shape[0] // lines
    partial = lax.all_to_all(
        partial.astype(BF16).reshape(lines, depth, D), "rep", 0, 0, axis_index_groups=pairs
    )
    partial = jnp.sum(partial.astype(F32), 0)
    early, squares = early_gradient(
        plan, jnp.asarray(plan.grad_table)[device], ahead, common, behind_rows
    )
    class_rows = common[:2, CLASS:].astype(F32)
    class_normed, query = class_rows[0:1], class_rows[1:2]
    by_head = jnp.where(head_mask()[:HEADS], query, 0.0)
    twice = odd & ~far & (jnp.arange(SET) < 8)
    weights = jnp.concatenate(
        [
            jnp.where(twice, 0.0, 1.0),
            jnp.sum(by_head * by_head, 1) / groups,
            jnp.zeros((HEADROWS - HEADS,), F32),
            jnp.sum(class_normed * class_normed)[None] / groups,
            jnp.full((2,), 1.0 / groups, F32),
            jnp.zeros((SHARED - HEADROWS - 3,), F32),
        ]
    )
    weights = lax.dynamic_slice_in_dim(weights, rep // 2 * depth, depth)
    pieces = jnp.sum(weights * jnp.sum(partial * partial, 1))
    squares = jnp.sum(squares) + jnp.where(low, pieces, 0.0)
    squares = squares + jnp.sum(proto_squares[0])
    summed = lax.all_to_all(
        jnp.broadcast_to(partial.astype(BF16)[None], (lines, depth, D)),
        "rep",
        0,
        0,
        axis_index_groups=pairs,
    ).reshape(-1, D)
    shared, summed = trade_low(summed[SET:]).astype(F32), summed[:SET]
    other, squares = lax.optimization_barrier((across(2, summed), squares))
    squares = lax.all_to_all(
        jnp.broadcast_to(squares.reshape(1, 1, 1), (count, 1, LANES)), BOTH, 0, 0
    )
    grad_norm = jnp.sqrt(jnp.sum(squares[:, 0, 0]))
    factor = jnp.minimum(1.0, CLIP_NORM / (grad_norm + 1e-06))
    summed = jnp.concatenate([jnp.where(far, other, summed), jnp.where(far, summed, other)], 0)
    if plan.all_sets:
        other = across(1, summed)
        summed = jnp.concatenate([jnp.where(odd, other, summed), jnp.where(odd, summed, other)], 0)
    if plan.odd_owner:
        summed = trade_low(summed)
    wide_grad = jnp.pad(summed.astype(F32), ((0, CHUNK), (0, 0)))

    sum_query, reach = shared[HEADROWS : HEADROWS + 1], shared[:HEADS]
    ends = jnp.pad(shared[HEADROWS + 1 : HEADROWS + 3], ((0, 6), (0, 0)))
    left = jnp.concatenate([class_normed, reach, jnp.zeros((LANES - 1 - HEADS, D), F32)], 0)
    left = jnp.pad(left.T, ((0, CHUNK), (0, 0)))
    right = jnp.concatenate(
        [
            jnp.pad(sum_query, ((0, 0), (0, D))),
            jnp.pad(by_head, ((0, 0), (D, 0))),
            jnp.zeros((LANES - 1 - HEADS, 2 * D), F32),
        ],
        0,
    )
    grad_flat = late_gradient(
        plan, jnp.asarray(plan.late_table)[device], early, wide_grad, left, right, ends
    )
    new_params, new_first, new_second = adam_update(
        params, grad_flat * factor, first_moment, second_moment, LEARNING_RATE
    )
    new_protos, new_proto_first, new_proto_second = adam_update(
        protos, grad_protos * factor, proto_first, proto_second, PROTO_RATE
    )
    new_teacher = TEACHER_MOMENTUM * teacher + (1.0 - TEACHER_MOMENTUM) * new_params
    new_teacher_protos = TEACHER_MOMENTUM * teacher_protos + (1.0 - TEACHER_MOMENTUM) * new_protos
    return (
        new_params,
        new_first,
        new_second,
        new_teacher,
        new_protos,
        new_proto_first,
        new_proto_second,
        new_teacher_protos,
        new_center,
        loss_value,
        grad_norm,
    )


def solution(mesh):
    placed = (
        P(BOTH),
        P(BOTH),
        P(BOTH),
        P(BOTH),
        P("rep", "grp"),
        P("rep", "grp"),
        P("rep", "grp"),
        P("rep", "grp"),
        P("grp"),
        P(BOTH, None, None),
        P(BOTH),
    )
    plan = Plan(mesh.shape["rep"], mesh.shape["grp"])
    return jax.shard_map(
        functools.partial(per_device, plan),
        mesh=mesh,
        in_specs=placed,
        out_specs=placed[:9] + (P(), P()),
        check_vma=False,
    )
```

```python
import functools

import jax
import jax.numpy as jnp
import numpy as np
from jax import lax
from jax.experimental import pallas as pl
from jax.experimental.pallas import tpu as pltpu
from jax.sharding import PartitionSpec as P

D = 768
HEADS = 12
HDIM = 64
F = 3072
PD = 768
NTOK = 197
H = 2048
B = 256
STEP = 10
NPATCH = NTOK - 1

PRECISE = lax.Precision.HIGHEST
STUDENT_TEMP = 0.1
TEACHER_TEMP = 0.04
CENTER_MOMENTUM = 0.9
TEACHER_MOMENTUM = 0.8
CLIP_NORM = 0.05
LEARNING_RATE = 0.03
PROTO_RATE = 0.6
BETA_FIRST = 0.9
BETA_SECOND = 0.999
ADAM_EPSILON = 1e-08
WEIGHT_DECAY = 0.04
BOTH = ("rep", "grp")
LANES = 128
F32 = jnp.float32
BF16 = jnp.bfloat16

SEGMENTS = []
_offset = 0
for _rows, _cols in ((PD + NTOK + 4, D), (D, 3 * D), (D, D), (D, F), (F + 2, D), (D + H, H), (H, B)):
    SEGMENTS.append((_offset, _rows, _cols))
    _offset += _rows * _cols
PFLAT = _offset
WIDTHS = sorted({cols // LANES for _, _, cols in SEGMENTS})

PIECES = []
_offset = 0
for _rows, _cols in (
    (PD + NTOK + 4, D),
    (D, 3 * D),
    (D, D),
    (D, F),
    (F, D),
    (2, D),
    (D, H),
    (H, H),
    (H, B),
):
    PIECES.append((_offset, _rows, _cols))
    _offset += _rows * _cols
FRONT = 192
CHUNK = 128
SET = 288
SHARED = 32
STEPS = 64
AHEAD = 3 * D + F + H
TILE = 16
TOKENS = 208
HEADROWS = 16
VMEM_LIMIT = 62 * 1024 * 1024


SPANS = {
    2: (0, 0),
    3: (D, D),
    4: (2 * D, D + F),
    6: (2 * D + F, 2 * D + F + B + H),
    7: (3 * D + F, 2 * D + F + B),
}
ATT_COLUMN = 2 * D + F + B + 2 * H
SECOND = HEADS * D
CLASS = SECOND + H


def round_up(value, step):
    return -(-value // step) * step


def shard_parts(start, stop, table):
    parts = []
    line0 = start // LANES
    for index, (offset, rows, cols) in enumerate(table):
        low, high = max(start, offset), min(stop, offset + rows * cols)
        if low >= high:
            continue
        row0 = (low - offset) // cols
        row1 = -(-(high - offset) // cols)
        parts.append((index, row0, row1 - row0, (offset + row0 * cols) // LANES - line0))
    return parts


FINAL_ROW = round_up(PD + NTOK + 4, 8)


class Plan:
    def __init__(self, reps, groups):
        count = reps * groups
        self.count, self.groups = count, groups
        self.size = PFLAT // count
        self.lines = round_up(-(-self.size // LANES) + 1, STEPS)
        self.scratch = FRONT + self.lines + 8 * max(WIDTHS) + 16
        table = []
        self.blocks = [[] for _ in SEGMENTS]
        longest = 0
        for device in range(count):
            start = device * self.size
            entry = [start % LANES]
            target = 0
            for index, row0, rows, line in shard_parts(start, start + self.size, SEGMENTS):
                width = SEGMENTS[index][2] // LANES
                skew = row0 % 8
                tiles = -(-(rows + skew) // 8)
                self.blocks[index].append((device, target // TILE, row0 // 8, tiles))
                entry += [
                    WIDTHS.index(width),
                    FRONT + line - skew * width,
                    tiles // 2,
                    tiles % 2,
                    target // TILE,
                ]
                target += tiles * 8 * width
            longest = max(longest, target)
            entry += [-1, 0, 0, 0, 0] * (2 - len(entry) // 5)
            table.append(entry)
        self.buffer = round_up(longest, 16)
        self.lay_table = np.array(table, np.int32)
        edge = SEGMENTS[0][1] * SEGMENTS[0][2]
        owners = [device for device in range(count) if device * self.size < edge]
        self.odd_owner = any(self.place(device)[1] for device in owners)
        self.all_sets = len(owners) > 2
        edge = sum(rows * cols for _, rows, cols in SEGMENTS[:2])
        self.near = all(
            device < 2 * groups for device in range(count) if device * self.size < edge
        )
        offset, rows, cols = PIECES[5]
        self.final_reps = sorted(
            {
                device // groups
                for device in range(count)
                if device * self.size < offset + rows * cols and (device + 1) * self.size > offset
            }
        )
        self.sent = [[] for _ in range(count)]
        self.grad_table = self.tabulate(lambda index: index, self.sent_row)
        self.late_table = self.tabulate(lambda index: index in (0, 1, 5), self.wide_row)
        self.reach = max(place + size for sent in self.sent for _, size, place in sent)
        self.grad_scratch = FRONT + self.lines + CHUNK * max(WIDTHS) + 16


    def largest(self):
        longest = max(8 * block[3] for blocks in self.blocks for block in blocks)
        return max(len(blocks) for blocks in self.blocks), round_up(longest, LANES) + 2 * LANES

    def place(self, device):
        rep, grp = divmod(device, self.groups)
        return rep // 2 * self.groups + grp, rep % 2

    def tabulate(self, chosen, rows_of):
        table = []
        for device in range(self.count):
            start = device * self.size
            entry = []
            for index, row0, rows, line in shard_parts(start, start + self.size, PIECES):
                if not chosen(index):
                    continue
                skew = row0 % 8
                line -= skew * (PIECES[index][2] // LANES)
                chunks = -(-(rows + skew) // CHUNK)
                entry += [index, FRONT + line, chunks, rows_of(device, index, row0 - skew, chunks)]
            table.append(entry)
        most = max(len(entry) for entry in table) // 4
        for device, entry in enumerate(table):
            entry += [-1, 0, 0, 0] * (most - len(entry) // 4)
            entry.insert(0, device * self.size % LANES)
        return np.array(table, np.int32)

    def sent_row(self, device, index, row0, chunks):
        if index not in SPANS:
            return row0
        sent, size = self.sent[device], chunks * CHUNK
        place = sum(before for _, before, _ in sent)
        sent.append((SPANS[index][0] + row0, size, place))
        return place

    def wide_row(self, device, index, row0, chunks):
        if index:
            return row0
        late = row0 >= 2 * SET - 8
        if not self.all_sets:
            if late != device % 2:
                raise ValueError("owner")
            return row0 - (2 * SET - 8) * late
        return row0 + 8 * late


def lay_kernel(plan, tab_ref, x_ref, out_ref, line_ref):
    shift = tab_ref[0]
    lane = lax.broadcasted_iota(jnp.int32, (STEPS + 8, LANES), 1)
    line_ref[pl.ds(0, FRONT), :] = jnp.zeros((FRONT, LANES), F32)
    tail = plan.scratch - FRONT - plan.lines
    line_ref[pl.ds(FRONT + plan.lines, tail), :] = jnp.zeros((tail, LANES), F32)

    def align(step, carry):
        base = pl.multiple_of(step * STEPS, 8)
        here = pltpu.roll(x_ref[pl.ds(base, STEPS + 8), :], shift, 1)
        above = pltpu.roll(here, 1, 0)
        both = jnp.where(lane >= shift, here, above)
        line_ref[pl.ds(pl.multiple_of(FRONT + base, 8), STEPS), :] = both[8:]
        return carry

    lax.fori_loop(0, plan.lines // STEPS, align, 0)
    for part in range(2):
        kind, base, pairs, odd, target = (tab_ref[1 + 5 * part + i] for i in range(5))
        for index, width in enumerate(WIDTHS):

            @pl.when(kind == index)
            def _(width=width):
                def move(step, carry):
                    row = base + step * (TILE * width)
                    goal = (target + step * width) * TILE
                    for tile in range(width):
                        both = line_ref[pl.ds(row + tile, TILE, stride=width), :]
                        place = pl.multiple_of(goal + TILE * tile, TILE)
                        out_ref[pl.ds(place, TILE), :] = both.astype(BF16)
                    return carry

                def last(step, carry):
                    row = base + pairs * (TILE * width)
                    goal = (target + pairs * width) * TILE
                    for tile in range(0, width, 2):
                        both = [
                            line_ref[pl.ds(row + tile + side, 8, stride=width), :]
                            for side in range(2)
                        ]
                        place = pl.multiple_of(goal + 8 * tile, TILE)
                        out_ref[pl.ds(place, TILE), :] = jnp.concatenate(both, 0).astype(BF16)
                    return carry

                lax.fori_loop(0, pairs, move, 0)
                lax.fori_loop(0, odd, last, 0)


def lay_out(plan, table, flat):
    padded = jnp.pad(flat, (8 * LANES, plan.lines * LANES - plan.size))
    lines = padded.reshape(8 + plan.lines, LANES)
    return pl.pallas_call(
        functools.partial(lay_kernel, plan),
        out_shape=jax.ShapeDtypeStruct((plan.buffer, LANES), BF16),
        in_specs=[
            pl.BlockSpec(memory_space=pltpu.SMEM),
            pl.BlockSpec(memory_space=pltpu.VMEM),
        ],
        out_specs=pl.BlockSpec(memory_space=pltpu.VMEM),
        scratch_shapes=[pltpu.VMEM((plan.scratch, LANES), F32)],
        compiler_params=pltpu.CompilerParams(vmem_limit_bytes=24 * 1024 * 1024),
    )(table, lines)


class Shards:
    def __init__(self, plan, gathered_ref, ref, sems, order):
        self.plan, self.ref, self.sems, self.waited = plan, ref, sems, set()
        self.copies = {}
        for device in order:
            place, side = plan.place(device)
            copy = pltpu.make_async_copy(
                gathered_ref.at[place, side], ref.at[device], sems.at[device]
            )
            copy.start()
            self.copies[device] = copy

    def wait(self, device):
        if device in self.copies:
            self.copies.pop(device).wait()

    def finish(self):
        for device in list(self.copies):
            self.wait(device)

    def blocks(self, index, first, count):
        found = [
            block
            for block in self.plan.blocks[index]
            if 8 * block[2] < first + count and 8 * (block[2] + block[3]) > first
        ]
        for block in found:
            self.wait(block[0])
        return found

    def eight(self, index, tile, pair, side):
        width = SEGMENTS[index][2] // LANES
        total = None
        for device, target, tile0, tiles in self.plan.blocks[index]:
            own = tile - tile0
            if not 0 <= own < tiles:
                continue
            if own < tiles // 2 * 2:
                both = self.ref[device, target + own // 2 * width + 2 * pair + side]
                half = own % 2
            else:
                both = self.ref[device, target + tiles // 2 * width + pair]
                half = side
            piece = both.astype(F32)[8 * half : 8 * half + 8]
            total = piece if total is None else total + piece
        return total

    def assemble(self, index, out_ref):
        width = SEGMENTS[index][2] // LANES
        rows = out_ref.shape[0]
        self.blocks(index, 0, rows)

        def column(pair, carry):
            for side in range(2):
                lanes = pl.ds(pl.multiple_of(pair * 2 * LANES + side * LANES, LANES), LANES)
                for group in range(rows // TILE):
                    both = [
                        self.eight(index, 2 * group + half, pair, side) for half in range(2)
                    ]
                    out_ref[TILE * group : TILE * (group + 1), lanes] = jnp.concatenate(
                        both, 0
                    ).astype(BF16)
            return carry

        lax.fori_loop(0, width // 2, column, 0)

    def columns(self, index, block, pair):
        width = SEGMENTS[index][2] // LANES
        device, target, _, tiles = block
        sides = []
        for side in range(2):
            pieces = [
                self.ref[device, target + step * width + 2 * pair + side]
                for step in range(tiles // 2)
            ]
            if tiles % 2:
                both = self.ref[device, target + tiles // 2 * width + pair].astype(F32)
                pieces.append(both[8 * side : 8 * side + 8].astype(BF16))
            sides.append(jnp.concatenate(pieces, 0))
        return jnp.concatenate(sides, 1)

    def times(self, index, first, values, left_ref, out_ref):
        views, count = values.shape
        blocks = self.blocks(index, first, count)
        top = max([first + count] + [8 * (tile0 + tiles) for _, _, tile0, tiles in blocks])
        top = round_up(top, LANES) + LANES
        parts = [values, jnp.zeros((views, top - first - count), F32)]
        if first:
            parts.insert(0, jnp.zeros((views, first), F32))
        wide = jnp.concatenate(parts, 1)
        for number, (_, _, tile0, tiles) in enumerate(blocks):
            start = 8 * tile0 // LANES * LANES
            turn = 8 * tile0 - start
            piece = wide[:, start : start + round_up(turn + 8 * tiles, LANES)]
            if turn:
                piece = pltpu.roll(piece, piece.shape[1] - turn, 1)
            left_ref[number, :, : 8 * tiles] = piece[:, : 8 * tiles]

        def column(pair, carry):
            total = jnp.zeros((views, 2 * LANES), F32)
            for number, block in enumerate(blocks):
                left = left_ref[number, :, : 8 * block[3]].astype(BF16)
                total += product(left, self.columns(index, block, pair))
            out_ref[:, pl.ds(pl.multiple_of(pair * 2 * LANES, LANES), 2 * LANES)] = total
            return carry

        lax.fori_loop(0, SEGMENTS[index][2] // LANES // 2, column, 0, unroll=2)


    def back(self, index, first, count, values, grad_ref, left_ref, wide_ref):
        views, cols = values.shape
        grad_ref[:, :cols] = values
        blocks = self.blocks(index, first, count)
        top = max([first + count] + [8 * (tile0 + tiles) for _, _, tile0, tiles in blocks])
        wide_ref[:, : round_up(top, LANES) + LANES] = jnp.zeros(
            (views, round_up(top, LANES) + LANES), F32
        )
        for number, (_, _, _, tiles) in enumerate(blocks):
            size = round_up(8 * tiles, LANES) + LANES
            left_ref[number, :, :size] = jnp.zeros((views, size), F32)

        def column(pair, carry):
            lanes = pl.ds(pl.multiple_of(pair * 2 * LANES, LANES), 2 * LANES)
            left = grad_ref[:, lanes].astype(BF16)
            for number, block in enumerate(blocks):
                size = 8 * block[3]
                left_ref[number, :, :size] += product_t(left, self.columns(index, block, pair))
            return carry

        lax.fori_loop(0, cols // LANES // 2, column, 0, unroll=2)
        for number, (_, _, tile0, tiles) in enumerate(blocks):
            start = 8 * tile0 // LANES * LANES
            turn = 8 * tile0 - start
            size = round_up(turn + 8 * tiles, LANES)
            piece = left_ref[number, :, :size]
            if turn:
                piece = pltpu.roll(piece, turn, 1)
            wide_ref[:, start : start + size] += piece
        return wide_ref[:, first : first + count]


def product(left, right):
    return jnp.dot(left, right, preferred_element_type=F32)


def product_t(left, right):
    return lax.dot_general(
        left, right, (((left.ndim - 1,), (1,)), ((), ())), preferred_element_type=F32
    )


def normal_share(values):
    return 0.5 + 0.5 * lax.erf(values * 2**-0.5)


def activate(values):
    return values * normal_share(values)


def gelu_back(values, grad):
    density = jnp.exp(-0.5 * values * values) * (2 * np.pi) ** -0.5
    return grad * (normal_share(values) + values * density)


def normalised(values):
    centred = values - jnp.mean(values, -1, keepdims=True)
    scale = lax.rsqrt(jnp.mean(centred * centred, -1, keepdims=True) + 1e-06)
    return centred * scale, scale


def norm_back(grad, gain, unit, scale):
    inner = grad * gain
    return scale * (
        inner
        - jnp.mean(inner, -1, keepdims=True)
        - unit * jnp.mean(inner * unit, -1, keepdims=True)
    )


def head_mask():
    shape = (HEADROWS, D)
    return lax.broadcasted_iota(jnp.int32, shape, 0) == (
        lax.broadcasted_iota(jnp.int32, shape, 1) // HDIM
    )


def token_norms(unit, norms, class_normed):
    token = lax.broadcasted_iota(jnp.int32, (TOKENS, D), 0)
    normed = unit * norms[0:1] + norms[1:2]
    return jnp.where(
        token < NPATCH, normed, jnp.where(token == NPATCH, class_normed, 0.0)
    ).astype(BF16)


def forward_kernel(
    plan,
    gathered_ref,
    pixels_ref,
    turn_ref,
    unit_out,
    scale_out,
    probs_ref,
    mixed_ref,
    looked_ref,
    class_ref,
    qkv_out,
    second_ref,
    hidden_ref,
    one_ref,
    two_ref,
    bottle_ref,
    middle_ref,
    send_ref,
    shards_ref,
    wide_ref,
    place_ref,
    left_ref,
    sums_ref,
    pack_ref,
    unit_ref,
    scale_ref,
    qkv_ref,
    out_sems,
    sems,
):
    shards = Shards(plan, gathered_ref, shards_ref, sems, range(plan.count))
    views = pixels_ref.shape[0]
    temper = HDIM ** (-0.5)
    shards.assemble(0, wide_ref)
    position = wide_ref[PD : PD + TOKENS].astype(F32)
    place_ref[...] = pltpu.roll(position, TOKENS - 1, 0)
    class_place = position[0:1]
    norms = position[NTOK : NTOK + 4]
    class_unit, class_scale = normalised(class_place)
    class_normed = (class_unit * norms[0:1] + norms[1:2]).astype(BF16).astype(F32)
    shards.assemble(1, qkv_ref)
    qkv_copy = pltpu.make_async_copy(qkv_ref, qkv_out, out_sems.at[4])
    qkv_copy.start()
    mask = head_mask()
    query = jnp.broadcast_to(class_normed, (HEADROWS, D)).astype(BF16)
    query = product(query, qkv_ref[:, :D]).astype(BF16).astype(F32)
    by_head = jnp.where(mask, query, 0.0).astype(BF16)
    looked = product_t(by_head, qkv_ref[:, D : 2 * D]).astype(BF16)
    looked_ref[...] = looked

    def copies(v):
        slot = lax.rem(v, 2)
        return (
            pltpu.make_async_copy(unit_ref.at[slot], unit_out.at[v], out_sems.at[slot]),
            pltpu.make_async_copy(scale_ref.at[slot], scale_out.at[v], out_sems.at[2 + slot]),
        )

    def view(v, carry):
        embedded = product(pixels_ref[v], wide_ref[:PD]) + place_ref[...]
        unit, scale = normalised(embedded)

        @pl.when(v >= 2)
        def _():
            for copy in copies(v - 2):
                copy.wait()

        unit_ref[lax.rem(v, 2)] = unit
        scale_ref[lax.rem(v, 2)] = jnp.broadcast_to(scale, (TOKENS, LANES))
        for copy in copies(v):
            copy.start()
        normed = token_norms(unit, norms, class_normed)
        scores = product_t(looked, normed) * temper
        token = lax.broadcasted_iota(jnp.int32, scores.shape, 1)
        scores = jnp.where(token < NTOK, scores, -1e30)
        top = jnp.max(scores, -1, keepdims=True)
        top = top + jnp.log(jnp.sum(jnp.exp(scores - top), -1, keepdims=True))
        head = lax.broadcasted_iota(jnp.int32, scores.shape, 0)
        probs = jnp.where(head < HEADS, jnp.exp(scores - top), 0.0)
        probs_ref[v] = probs
        mixed_ref[v] = product(probs.astype(BF16), normed).astype(BF16)
        return carry

    lax.fori_loop(0, views, view, 0, unroll=2)
    mixed = mixed_ref[...].reshape(views * HEADROWS, D)
    valued = product(mixed, qkv_ref[:, 2 * D :]).reshape(views, HEADROWS, D)
    attended = jnp.sum(jnp.where(mask[None], valued, 0.0), 1).astype(BF16)
    pack_ref[:, :D] = attended.astype(F32)
    shards.times(2, 0, pack_ref[:, :D], left_ref, sums_ref)
    middle = class_place + sums_ref[...]
    unit, scale = normalised(middle)
    middle_ref[0], middle_ref[1] = unit, jnp.broadcast_to(scale, (views, D))
    normed = (unit * norms[2:3] + norms[3:4]).astype(BF16)
    pack_ref[:, D : 2 * D] = normed.astype(F32)
    shards.times(3, 0, pack_ref[:, D : 2 * D], left_ref, hidden_ref)
    act = activate(hidden_ref[...]).astype(BF16)
    pack_ref[:, 2 * D : 2 * D + F] = act.astype(F32)
    shards.times(4, 0, act.astype(F32), left_ref, sums_ref)
    unit, scale = normalised(middle + sums_ref[...])
    middle_ref[2], middle_ref[3] = unit, jnp.broadcast_to(scale, (views, D))
    final = jnp.concatenate(
        [shards.eight(4, F // 8, tile // 2, tile % 2) for tile in range(D // LANES)], 1
    )
    cls = (unit * final[0:1] + final[1:2]).astype(BF16)
    place = 2 * D + F
    pack_ref[:, place : place + D] = cls.astype(F32)
    shards.times(5, 0, cls.astype(F32), left_ref, one_ref)
    first = activate(one_ref[...]).astype(BF16)
    pack_ref[:, place + D : AHEAD] = first.astype(F32)
    pack_ref[:, AHEAD:] = jnp.zeros((views, pack_ref.shape[1] - AHEAD), F32)
    shards.times(5, D, first.astype(F32), left_ref, two_ref)
    second = activate(two_ref[...]).astype(BF16)
    second_ref[...] = second
    shards.times(6, 0, second.astype(F32), left_ref, bottle_ref)
    bottle = bottle_ref[...]
    scale = lax.rsqrt(jnp.sum(bottle * bottle, -1, keepdims=True) + 1e-06)
    rows = product(turn_ref[...], (bottle * scale).astype(BF16)).astype(BF16)
    for device, sent in enumerate(plan.sent):
        send_ref[device, :, :B] = rows
        for lane, size, place in sent:
            start = lane // LANES * LANES
            piece = pack_ref[:, start : start + size + (LANES if lane > start else 0)]
            if lane > start:
                piece = pltpu.roll(piece, piece.shape[1] - (lane - start), 1)
            send_ref[device, :, B + place : B + place + size] = piece[:, :size].astype(BF16)
    class_ref[...] = jnp.concatenate(
        [
            class_unit,
            class_normed,
            query[0:1],
            jnp.broadcast_to(class_scale, (1, D)),
            norms,
            final,
        ],
        0,
    )
    for v in range(max(0, views - 2), views):
        for copy in copies(v):
            copy.wait()
    qkv_copy.wait()
    shards.finish()


def forward(plan, gathered, pixels, turn):
    views = pixels.shape[0]
    shapes = [
        ((views, TOKENS, D), F32),
        ((views, TOKENS, LANES), F32),
        ((views, HEADROWS, TOKENS), F32),
        ((views, HEADROWS, D), BF16),
        ((HEADROWS, D), BF16),
        ((16, D), F32),
        ((D, 3 * D), BF16),
        ((views, H), BF16),
        ((views, F), F32),
        ((views, H), F32),
        ((views, H), F32),
        ((views, B), F32),
        ((4, views, D), F32),
        ((plan.count, views, B + plan.reach), BF16),
    ]
    most, longest = plan.largest()
    return pl.pallas_call(
        functools.partial(forward_kernel, plan),
        out_shape=[jax.ShapeDtypeStruct(shape, dtype) for shape, dtype in shapes],
        in_specs=[pl.BlockSpec(memory_space=pl.ANY)]
        + [pl.BlockSpec(memory_space=pltpu.VMEM)] * 2,
        out_specs=[
            pl.BlockSpec(memory_space=pl.ANY if index in (0, 1, 6) else pltpu.VMEM)
            for index in range(len(shapes))
        ],
        scratch_shapes=[
            pltpu.VMEM((plan.count, plan.buffer // TILE, TILE, LANES), BF16),
            pltpu.VMEM((round_up(PD + NTOK + 4, TILE), D), BF16),
            pltpu.VMEM((TOKENS, D), F32),
            pltpu.VMEM((most, views, longest), F32),
            pltpu.VMEM((views, D), F32),
            pltpu.VMEM((views, round_up(AHEAD + CHUNK, LANES) + LANES), F32),
            pltpu.VMEM((2, TOKENS, D), F32),
            pltpu.VMEM((2, TOKENS, LANES), F32),
            pltpu.VMEM((D, 3 * D), BF16),
            pltpu.SemaphoreType.DMA((5,)),
            pltpu.SemaphoreType.DMA((plan.count,)),
        ],
        compiler_params=pltpu.CompilerParams(vmem_limit_bytes=VMEM_LIMIT),
        cost_estimate=pl.CostEstimate(
            flops=60 * 10**9, bytes_accessed=40 * 10**6, transcendentals=10**5
        ),
    )(gathered, pixels, turn)


def proto_kernel(
    start_ref,
    rows_ref,
    columns_ref,
    others_ref,
    center_ref,
    note_ref,
    center_out_ref,
    student_ref,
    teacher_ref,
    sums_ref,
):
    count, groups = rows_ref.shape[1], note_ref.shape[0]
    views = (note_ref.shape[1] - 8 * -(-count // B)) // 3
    logits = product(rows_ref[1], others_ref[...])
    center = center_ref[...]
    center_out_ref[...] = CENTER_MOMENTUM * center + (1.0 - CENTER_MOMENTUM) * jnp.mean(
        logits, 0, keepdims=True
    )
    exp_teacher = jnp.exp((logits - center) / TEACHER_TEMP)
    teacher_ref[...] = exp_teacher
    scaled = product(rows_ref[0], columns_ref[...]) / STUDENT_TEMP
    exp_student = jnp.exp(scaled)
    student_ref[...] = exp_student
    turned = []
    for which, values in enumerate((exp_student, exp_teacher, exp_teacher * scaled)):
        total = jnp.broadcast_to(jnp.sum(values, 1, keepdims=True), (count, LANES))
        turned.append(total.T[0:1])
        if which < 2:
            sums_ref[:, which * LANES : (which + 1) * LANES] = total
    turned = jnp.concatenate(turned + [jnp.zeros((5, count), F32)], 0)
    for step in range(-(-count // B)):
        part = turned[:, step * B : (step + 1) * B]
        lines = slice(3 * views + 8 * step, 3 * views + 8 * (step + 1))
        note_ref[:, lines, : part.shape[1]] = jnp.broadcast_to(part[None], (groups,) + part.shape)
        if part.shape[1] < B:
            note_ref[:, lines, part.shape[1] :] = jnp.zeros((groups, 8, B - part.shape[1]), F32)
    start = pl.multiple_of(start_ref[0], 8)
    columns = columns_ref[...].astype(F32)
    for which, source in enumerate((student_ref, teacher_ref)):
        pulls = lax.dot_general(
            source[pl.ds(start, groups * views), :],
            columns,
            (((1,), (1,)), ((), ())),
            precision=PRECISE,
            preferred_element_type=F32,
        )
        note_ref[:, which * views : (which + 1) * views, :] = pulls.reshape(groups, views, B)
    own = sums_ref[pl.ds(start, groups * views), :]
    note_ref[:, 2 * views : 3 * views, :] = own.reshape(groups, views, B)


def prototypes(start, rows, columns, others, center, groups, views):
    count, width = rows.shape[1], columns.shape[1]
    shapes = [(groups, 3 * views + 8 * -(-count // B), B), (1, width)]
    return pl.pallas_call(
        proto_kernel,
        out_shape=[jax.ShapeDtypeStruct(shape, F32) for shape in shapes],
        in_specs=[pl.BlockSpec(memory_space=pltpu.SMEM)]
        + [pl.BlockSpec(memory_space=pltpu.VMEM)] * 4,
        out_specs=[pl.BlockSpec(memory_space=pltpu.VMEM)] * len(shapes),
        scratch_shapes=[pltpu.VMEM((count, width), F32)] * 2
        + [pltpu.VMEM((count, 2 * LANES), F32)],
        compiler_params=pltpu.CompilerParams(vmem_limit_bytes=32 * 1024 * 1024),
        cost_estimate=pl.CostEstimate(
            flops=3 * 10**9, bytes_accessed=6 * 10**6, transcendentals=10**6
        ),
    )(start, rows, columns, others, center)


def proto_back_kernel(
    start_ref,
    rows_ref,
    columns_ref,
    others_ref,
    center_ref,
    totals_ref,
    table_ref,
    scale_ref,
    grad_ref,
    square_ref,
    work_ref,
):
    count = rows_ref.shape[1]
    totals = jnp.broadcast_to(totals_ref[0:2][:, None, :], (2, 8, count))
    student, teacher = (totals[which].T[:, :1] for which in range(2))
    logits = product(rows_ref[1], others_ref[...])
    targets = jnp.exp((logits - center_ref[...]) / TEACHER_TEMP) / teacher
    scaled = product(rows_ref[0], columns_ref[...]) / STUDENT_TEMP
    grad = (jnp.exp(scaled) / student - targets) / STUDENT_TEMP
    work_ref[...] = jnp.dot(
        rows_ref[0].astype(F32).T, grad, precision=PRECISE, preferred_element_type=F32
    )
    scale = scale_ref[...]
    inner = jnp.sum(work_ref[...] * table_ref[...], 0, keepdims=True)
    start = pl.multiple_of(start_ref[0], 8)
    lines = pl.ds(start, grad_ref.shape[0])
    grad = work_ref[lines, :] * scale - table_ref[lines, :] * (scale * scale * scale * inner)
    grad_ref[...] = grad
    square = jnp.sum(grad * grad, 0, keepdims=True)
    square_ref[...] = jnp.broadcast_to(square, square_ref.shape)


def prototypes_back(start, depth, *values):
    count, width = values[0].shape[1], values[1].shape[1]
    shapes = [(depth, width), (8, width)]
    return pl.pallas_call(
        proto_back_kernel,
        out_shape=[jax.ShapeDtypeStruct(shape, F32) for shape in shapes],
        in_specs=[pl.BlockSpec(memory_space=pltpu.SMEM)]
        + [pl.BlockSpec(memory_space=pltpu.VMEM)] * len(values),
        out_specs=[pl.BlockSpec(memory_space=pltpu.VMEM)] * len(shapes),
        scratch_shapes=[pltpu.VMEM((B, width), F32)],
        compiler_params=pltpu.CompilerParams(vmem_limit_bytes=32 * 1024 * 1024),
        cost_estimate=pl.CostEstimate(
            flops=3 * 10**9, bytes_accessed=6 * 10**6, transcendentals=10**6
        ),
    )(start, *values)


def rows_back_kernel(
    plan,
    low_ref,
    gathered_ref,
    note_ref,
    class_ref,
    hidden_ref,
    one_ref,
    two_ref,
    bottle_ref,
    middle_ref,
    pack_ref,
    stream_ref,
    extra_ref,
    shards_ref,
    left_ref,
    values_ref,
    wide_ref,
    sems,
):
    used = {block[0] for blocks in plan.blocks[2:] for block in blocks}
    shards = Shards(plan, gathered_ref, shards_ref, sems, sorted(used, reverse=True))
    work = (values_ref, left_ref, wide_ref)
    norms, final = class_ref[4:8], class_ref[8:10]

    views = bottle_ref.shape[0]
    note = jnp.sum(note_ref[...], 0)
    sums = note[2 * views : 3 * views]
    student, teacher = sums[:, :1], sums[:, LANES : LANES + 1]
    grad_rows = (note[:views] / student - note[views : 2 * views] / teacher) / STUDENT_TEMP
    grad_rows = jnp.where(low_ref[0] == 0, 0.0, grad_rows).astype(BF16).astype(F32)
    bottle = bottle_ref[...]
    scale = lax.rsqrt(jnp.sum(bottle * bottle, -1, keepdims=True) + 1e-06)
    grad_bottle = (
        grad_rows * scale - bottle * scale**3 * jnp.sum(grad_rows * bottle, -1, keepdims=True)
    ).astype(BF16)
    place = 2 * D + F
    pack_ref[:, place : place + B] = grad_bottle
    grad_two = shards.back(6, 0, H, grad_bottle.astype(F32), *work)
    grad_two = gelu_back(two_ref[...], grad_two).astype(BF16)
    pack_ref[:, place + B : place + B + H] = grad_two
    grad_one = shards.back(5, D, H, grad_two.astype(F32), *work)
    grad_one = gelu_back(one_ref[...], grad_one).astype(BF16)
    pack_ref[:, place + B + H : place + B + 2 * H] = grad_one
    grad_cls = shards.back(5, 0, D, grad_one.astype(F32), *work)
    unit, scale = middle_ref[2], middle_ref[3]
    gain_last = jnp.sum(grad_cls * unit, 0, keepdims=True)
    shift_last = jnp.sum(grad_cls, 0, keepdims=True)
    grad_stream = norm_back(grad_cls, final[0:1], unit, scale)
    grad_branch = grad_stream.astype(BF16)
    pack_ref[:, D + F : 2 * D + F] = grad_branch
    grad_hidden = shards.back(4, 0, F, grad_branch.astype(F32), *work)
    grad_hidden = gelu_back(hidden_ref[...], grad_hidden).astype(BF16)
    pack_ref[:, D : D + F] = grad_hidden
    grad_normed = shards.back(3, 0, D, grad_hidden.astype(F32), *work)
    unit, scale = middle_ref[0], middle_ref[1]
    extra_ref[...] = jnp.concatenate(
        [
            jnp.sum(grad_normed * unit, 0, keepdims=True),
            jnp.sum(grad_normed, 0, keepdims=True),
            gain_last,
            shift_last,
            jnp.zeros((4, D), F32),
        ],
        0,
    )
    grad_middle = grad_stream + norm_back(grad_normed, norms[2:3], unit, scale)
    stream_ref[...] = grad_middle
    grad_mixed = grad_middle.astype(BF16)
    pack_ref[:, :D] = grad_mixed
    grad_att = shards.back(2, 0, D, grad_mixed.astype(F32), *work).astype(BF16)
    pack_ref[:, place + B + 2 * H : place + B + 2 * H + D] = grad_att
    shards.finish()


def rows_back(plan, low, gathered, note, kept):
    views = kept[-1].shape[1]
    shapes = [((views, 3 * D + F + B + 2 * H), BF16), ((views, D), F32), ((8, D), F32)]
    most, longest = plan.largest()
    return pl.pallas_call(
        functools.partial(rows_back_kernel, plan),
        out_shape=[jax.ShapeDtypeStruct(shape, dtype) for shape, dtype in shapes],
        in_specs=[pl.BlockSpec(memory_space=pltpu.SMEM), pl.BlockSpec(memory_space=pl.ANY)]
        + [pl.BlockSpec(memory_space=pltpu.VMEM)] * (1 + len(kept)),
        out_specs=[pl.BlockSpec(memory_space=pltpu.VMEM)] * len(shapes),
        scratch_shapes=[
            pltpu.VMEM((plan.count, plan.buffer // TILE, TILE, LANES), BF16),
            pltpu.VMEM((most, views, longest), F32),
            pltpu.VMEM((views, F), F32),
            pltpu.VMEM((views, F + 2 * LANES), F32),
            pltpu.SemaphoreType.DMA((plan.count,)),
        ],
        compiler_params=pltpu.CompilerParams(vmem_limit_bytes=40 * 1024 * 1024),
        cost_estimate=pl.CostEstimate(
            flops=30 * 10**9, bytes_accessed=30 * 10**6, transcendentals=10**5
        ),
    )(low, gathered, note, *kept)


def tokens_back_kernel(
    odd_ref,
    behind_ref,
    stream_ref,
    ends_ref,
    unit_ref,
    scale_ref,
    probs_ref,
    looked_ref,
    class_ref,
    qkv_ref,
    pixels_ref,
    first_ref,
    second_ref,
    kept_ref,
    sent_ref,
    patch_ref,
    place_ref,
    reach_ref,
    back_ref,
    mixed_ref,
    rows_ref,
):
    v = pl.program_id(0)
    views = stream_ref.shape[0]
    temper = HDIM ** (-0.5)
    norms = class_ref[4:8]
    class_unit, class_normed, class_scale = (class_ref[row : row + 1] for row in (0, 1, 3))

    @pl.when(v == 0)
    def _():
        place = 2 * D + F + B + 2 * H
        grad_att = behind_ref[:, place : place + D].astype(F32)
        spread = jnp.where(head_mask()[None], grad_att[:, None, :], 0.0).astype(BF16)
        back = product_t(spread.reshape(views * HEADROWS, D), qkv_ref[:, 2 * D :])
        back_ref[...] = back.astype(BF16).reshape(views, HEADROWS, D)
        patch_ref[...] = jnp.zeros(patch_ref.shape, F32)
        place_ref[...] = jnp.zeros(place_ref.shape, F32)
        reach_ref[...] = jnp.zeros(reach_ref.shape, F32)
        rows_ref[...] = jnp.zeros(rows_ref.shape, F32)

    unit = unit_ref[0]
    scale = scale_ref[0][:, :1]
    normed = token_norms(unit, norms, class_normed)
    back = back_ref[v]
    probs = probs_ref[0]
    grad_probs = product_t(back, normed)
    delta = jnp.sum(probs * grad_probs, -1, keepdims=True)
    grad_scores = (probs * (grad_probs - delta)).astype(BF16)
    reach = product(grad_scores, normed) * temper
    mixed_ref[v] = reach.astype(BF16)
    reach_ref[...] += reach
    left = jnp.concatenate([grad_scores.astype(F32), probs.astype(BF16).astype(F32)], 0)
    looked = (looked_ref[...].astype(F32) * temper).astype(BF16)
    grad = product(left.T.astype(BF16), jnp.concatenate([looked, back], 0))
    row = lax.broadcasted_iota(jnp.int32, (8, D), 0)
    rows_ref[0] += jnp.where(row == v, grad[NPATCH : NPATCH + 1], 0.0)
    token = lax.broadcasted_iota(jnp.int32, (TOKENS, D), 0)
    grad = jnp.where(token < NPATCH, grad, 0.0)
    rows_ref[1, 0:1] += jnp.sum(grad * unit, 0, keepdims=True)
    rows_ref[2, 0:1] += jnp.sum(grad, 0, keepdims=True)
    stream = norm_back(grad, norms[0:1], unit, scale)
    place_ref[...] += stream
    patch_ref[...] += product(pixels_ref[0], stream.astype(BF16))

    @pl.when(v == views - 1)
    def _():
        keyed = product(mixed_ref[...].reshape(views * HEADROWS, D), qkv_ref[:, D : 2 * D])
        keyed = jnp.where(head_mask()[None], keyed.reshape(views, HEADROWS, D), 0.0)
        grad_query = jnp.sum(keyed, 1).astype(BF16)
        class_row = rows_ref[0][:views] + product_t(grad_query, qkv_ref[:, :D])
        class_stream = norm_back(class_row, norms[0:1], class_unit, class_scale)
        class_stream = class_stream + stream_ref[...]
        ends = [
            (0, jnp.sum(class_stream, 0, keepdims=True)),
            (NTOK, rows_ref[1, 0:1] + jnp.sum(class_row * class_unit, 0, keepdims=True)),
            (NTOK + 1, rows_ref[2, 0:1] + jnp.sum(class_row, 0, keepdims=True)),
            (NTOK + 2, ends_ref[0:1]),
            (NTOK + 3, ends_ref[1:2]),
        ]
        tail = pltpu.roll(place_ref[...], 1, 0)
        for row, value in ends:
            tail = jnp.where(token == row, value, tail)
        upper = 2 * SET - 8
        rest = jnp.zeros((2 * SET - (PD - upper) - TOKENS, D), F32)
        query_row = lax.broadcasted_iota(jnp.int32, (8, D), 0) == 0
        total = jnp.sum(grad_query.astype(F32), 0, keepdims=True)
        shared = [reach_ref[...], jnp.where(query_row, total, pltpu.roll(ends_ref[...], 7, 0))]
        shared = jnp.concatenate(shared + [jnp.zeros((SHARED - HEADROWS - 8, D), F32)], 0)
        kept_ref[2 * SET :] = shared
        sent_ref[2 * SET :] = shared.astype(BF16)
        last = jnp.concatenate([patch_ref[upper:], tail, rest], 0)

        @pl.when(odd_ref[0] == 0)
        def _():
            kept_ref[: 2 * SET] = patch_ref[: 2 * SET]
            sent_ref[: 2 * SET] = last.astype(BF16)

        @pl.when(odd_ref[0] != 0)
        def _():
            kept_ref[: 2 * SET] = last
            sent_ref[: 2 * SET] = patch_ref[: 2 * SET].astype(BF16)


def tokens_back(odd, behind, grad_middle, ends, kept, pixels, *before):
    views = grad_middle.shape[0]

    def whole(values):
        return pl.BlockSpec(values.shape, lambda v: (0,) * values.ndim)

    def by_view(values):
        return pl.BlockSpec((1,) + values.shape[1:], lambda v: (v,) + (0,) * (values.ndim - 1))

    unit, scale, probs, looked, classes, qkv_w = kept
    shape = (2 * SET + SHARED, D)
    return pl.pallas_call(
        tokens_back_kernel,
        grid=(views,),
        out_shape=[jax.ShapeDtypeStruct(shape, F32), jax.ShapeDtypeStruct(shape, BF16)],
        in_specs=[
            pl.BlockSpec(memory_space=pltpu.SMEM),
            whole(behind),
            whole(grad_middle),
            whole(ends),
            by_view(unit),
            by_view(scale),
            by_view(probs),
            whole(looked),
            whole(classes),
            whole(qkv_w),
            by_view(pixels),
        ]
        + [pl.BlockSpec(memory_space=pl.ANY)] * len(before),
        out_specs=[pl.BlockSpec(shape, lambda v: (0, 0))] * 2,
        scratch_shapes=[
            pltpu.VMEM((PD, D), F32),
            pltpu.VMEM((TOKENS, D), F32),
            pltpu.VMEM((HEADROWS, D), F32),
            pltpu.VMEM((views, HEADROWS, D), BF16),
            pltpu.VMEM((views, HEADROWS, D), BF16),
            pltpu.VMEM((3, 8, D), F32),
        ],
        compiler_params=pltpu.CompilerParams(vmem_limit_bytes=60 * 1024 * 1024),
        cost_estimate=pl.CostEstimate(
            flops=15 * 10**9, bytes_accessed=15 * 10**6, transcendentals=10**5
        ),
    )(odd, behind, grad_middle, ends, unit, scale, probs, looked, classes, qkv_w, pixels, *before)


def early_kernel(
    plan,
    most,
    tab_ref,
    ahead_ref,
    common_hbm,
    behind_hbm,
    rest_ref,
    line_ref,
    square_ref,
    common_ref,
    behind_ref,
    sem,
):
    line_ref[...] = jnp.zeros(line_ref.shape, F32)

    def fetch(source, target, column, size):
        copy = pltpu.make_async_copy(
            source.at[:, pl.ds(column, size)], target.at[:, pl.ds(0, size)], sem
        )
        copy.start()
        copy.wait()

    def turned(lane):
        start = pl.multiple_of(lane // LANES * LANES, LANES)
        both = common_ref[:, pl.ds(start, 2 * LANES)].astype(F32)
        both = pltpu.roll(both, lax.rem(2 * LANES - (lane - start), 2 * LANES), 1)
        return both[:, :LANES].T.astype(BF16)

    def store(goal, width, tile, block):
        line_ref[pl.ds(goal + tile, block.shape[0], stride=width), :] = block

    for part in range(most):
        kind, base, chunks, row0 = (tab_ref[1 + 4 * part + i] for i in range(4))
        for index, (_, column) in SPANS.items():
            cols = PIECES[index][2]
            width = cols // LANES

            @pl.when(kind == index)
            def _(column=column, cols=cols, width=width):
                fetch(behind_hbm, behind_ref, column, cols)

                def move(step, carry):
                    goal = base + step * (CHUNK * width)
                    lanes = pl.ds(pl.multiple_of(row0 + step * CHUNK, LANES), CHUNK)
                    left = ahead_ref[:, lanes].astype(F32).T.astype(BF16)
                    block = product(left, behind_ref[:, :cols])
                    for tile in range(width):
                        store(goal, width, tile, block[:, tile * LANES : (tile + 1) * LANES])
                    return carry

                lax.fori_loop(0, chunks, move, 0)

        @pl.when(kind == 8)
        def _():
            fetch(behind_hbm, behind_ref, 2 * D + F, B)
            fetch(common_hbm, common_ref, SECOND, H + D)

            def move(step, carry):
                left = turned(row0 + step * CHUNK)
                block = product(left, behind_ref[:, :B])
                for tile in range(B // LANES):
                    piece = block[:, tile * LANES : (tile + 1) * LANES]
                    store(base + step * (CHUNK * B // LANES), B // LANES, tile, piece)
                return carry

            lax.fori_loop(0, chunks, move, 0)

        @pl.when(kind == 5)
        def _():
            for tile in range(D // LANES):
                store(base, D // LANES, tile, jnp.zeros((8, LANES), F32))

        @pl.when(kind == 1)
        def _():
            fetch(behind_hbm, behind_ref, ATT_COLUMN, D)
            fetch(common_hbm, common_ref, 0, common_ref.shape[1])

            def move(step, carry):
                width = 3 * D // LANES
                goal = base + step * (CHUNK * width)
                side = lax.broadcasted_iota(jnp.int32, (CHUNK, LANES), 1)
                for pair in range(HEADS // 2):
                    right = behind_ref[:, pair * LANES : (pair + 1) * LANES]
                    lane = 2 * pair * D + row0 + step * CHUNK
                    first, second = (product(turned(lane + D * head), right) for head in range(2))
                    block = jnp.where(side < HDIM, first, second)
                    store(goal, width, 2 * D // LANES + pair, block)
                return carry

            lax.fori_loop(0, chunks, move, 0)

    shift = tab_ref[0]
    shape = (STEPS, LANES)
    place = lax.broadcasted_iota(jnp.int32, shape, 0) * LANES
    place = place + lax.broadcasted_iota(jnp.int32, shape, 1) - shift

    def clear(step, total):
        start = pl.multiple_of(step * STEPS, 8)
        entry = place + start * LANES
        lines = pl.ds(pl.multiple_of(FRONT + start, 8), STEPS)
        kept = jnp.where((entry >= 0) & (entry < plan.size), line_ref[lines, :], 0.0)
        line_ref[lines, :] = kept
        return total + kept * kept

    total = lax.fori_loop(0, plan.lines // STEPS, clear, jnp.zeros(shape, F32))
    total = jnp.sum(total, keepdims=True) + rest_ref[...]
    square_ref[...] = jnp.broadcast_to(total[None], square_ref.shape)


def early_gradient(plan, table, ahead, common, behind, rest):
    return pl.pallas_call(
        functools.partial(early_kernel, plan, table.shape[0] // 4),
        out_shape=[
            jax.ShapeDtypeStruct((plan.grad_scratch, LANES), F32),
            jax.ShapeDtypeStruct((plan.count, 1, LANES), F32),
        ],
        in_specs=[
            pl.BlockSpec(memory_space=pltpu.SMEM),
            pl.BlockSpec(memory_space=pltpu.VMEM),
            pl.BlockSpec(memory_space=pl.ANY),
            pl.BlockSpec(memory_space=pl.ANY),
            pl.BlockSpec(memory_space=pltpu.VMEM),
        ],
        out_specs=[pl.BlockSpec(memory_space=pltpu.VMEM)] * 2,
        scratch_shapes=[
            pltpu.VMEM(common.shape, BF16),
            pltpu.VMEM((behind.shape[0], F), BF16),
            pltpu.SemaphoreType.DMA,
        ],
        compiler_params=pltpu.CompilerParams(vmem_limit_bytes=60 * 1024 * 1024),
        cost_estimate=pl.CostEstimate(
            flops=10 * 10**9, bytes_accessed=10 * 10**6, transcendentals=0
        ),
    )(table, ahead, common, behind, rest)


def late_kernel(
    plan,
    most,
    tab_ref,
    lines_ref,
    wide_ref,
    left_ref,
    right_ref,
    ends_ref,
    out_ref,
    line_ref,
    sem,
):
    used = FRONT + plan.lines + 8
    copy = pltpu.make_async_copy(lines_ref.at[pl.ds(0, used)], line_ref.at[pl.ds(0, used)], sem)
    copy.start()
    copy.wait()

    def add(goal, width, tile, block):
        lines = pl.ds(goal + tile, CHUNK, stride=width)
        line_ref[lines, :] = line_ref[lines, :] + block

    for part in range(most):
        kind, base, chunks, row0 = (tab_ref[1 + 4 * part + i] for i in range(4))

        @pl.when(kind == 0)
        def _():
            def move(step, carry):
                width = D // LANES
                rows = pl.ds(pl.multiple_of(row0 + step * CHUNK, 8), CHUNK)
                for tile in range(width):
                    block = wide_ref[rows, tile * LANES : (tile + 1) * LANES]
                    add(base + step * (CHUNK * width), width, tile, block)
                return carry

            lax.fori_loop(0, chunks, move, 0)

        @pl.when(kind == 1)
        def _():
            def move(step, carry):
                width = 3 * D // LANES
                rows = pl.ds(pl.multiple_of(row0 + step * CHUNK, 8), CHUNK)
                block = jnp.dot(
                    left_ref[rows, :],
                    right_ref[...],
                    precision=PRECISE,
                    preferred_element_type=F32,
                )
                for tile in range(2 * D // LANES):
                    piece = block[:, tile * LANES : (tile + 1) * LANES]
                    add(base + step * (CHUNK * width), width, tile, piece)
                return carry

            lax.fori_loop(0, chunks, move, 0)

        @pl.when(kind == 5)
        def _():
            width = D // LANES
            for tile in range(width):
                lines = pl.ds(base + tile, 8, stride=width)
                block = ends_ref[:, tile * LANES : (tile + 1) * LANES]
                line_ref[lines, :] = line_ref[lines, :] + block

    shift = tab_ref[0]
    turn = lax.rem(LANES - shift, LANES)
    lane = lax.broadcasted_iota(jnp.int32, (STEPS + 8, LANES), 1)

    def align(step, carry):
        start = pl.multiple_of(step * STEPS, 8)
        lines = pl.ds(pl.multiple_of(FRONT + start, 8), STEPS + 8)
        here = pltpu.roll(line_ref[lines, :], turn, 1)
        below = pltpu.roll(here, STEPS + 7, 0)
        both = jnp.where(lane < LANES - shift, here, below)
        out_ref[pl.ds(start, STEPS), :] = both[:STEPS]
        return carry

    lax.fori_loop(0, plan.lines // STEPS, align, 0)


def late_gradient(plan, table, lines, *values):
    return pl.pallas_call(
        functools.partial(late_kernel, plan, table.shape[0] // 4),
        out_shape=jax.ShapeDtypeStruct((plan.lines, LANES), F32),
        in_specs=[pl.BlockSpec(memory_space=pltpu.SMEM), pl.BlockSpec(memory_space=pl.ANY)]
        + [pl.BlockSpec(memory_space=pltpu.VMEM)] * len(values),
        out_specs=pl.BlockSpec(memory_space=pltpu.VMEM),
        scratch_shapes=[
            pltpu.VMEM((plan.grad_scratch, LANES), F32),
            pltpu.SemaphoreType.DMA,
        ],
        compiler_params=pltpu.CompilerParams(vmem_limit_bytes=24 * 1024 * 1024),
    )(table, lines, *values).reshape(-1)[: plan.size]


def adam_update(weight, grad, first, second, rate):
    first = BETA_FIRST * first + (1.0 - BETA_FIRST) * grad
    second = BETA_SECOND * second + (1.0 - BETA_SECOND) * grad * grad
    stepped = (
        first
        / (1.0 - BETA_FIRST**STEP)
        / (jnp.sqrt(second / (1.0 - BETA_SECOND**STEP)) + ADAM_EPSILON)
    )
    return (weight - rate * (stepped + WEIGHT_DECAY * weight), first, second)


def per_device(
    plan,
    params,
    first_moment,
    second_moment,
    teacher,
    protos,
    proto_first,
    proto_second,
    teacher_protos,
    center,
    patches,
    partner,
):
    reps, groups = lax.axis_size("rep"), lax.axis_size("grp")
    count, half = reps * groups, reps * groups // 2
    rep, grp = lax.axis_index("rep"), lax.axis_index("grp")
    device = rep * groups + grp
    low = rep % 2 == 0
    place = rep // 2 * groups + grp
    halves = [
        [r * groups + g for r in range(parity, reps, 2) for g in range(groups)] for parity in (0, 1)
    ]
    swap = [(r, r ^ 1) for r in range(reps)]
    own_views = patches.shape[0]
    views = 2 * own_views

    def trade(values):
        return lax.ppermute(values, "rep", swap)

    def trade_low(values):
        return jnp.where(low, values, trade(values))

    def in_order(values):
        other = trade(values)
        return jnp.where(low, values, other), jnp.where(low, other, values)

    pairs = [list(range(parity, reps, 2)) for parity in (0, 1)]
    lines = reps // 2
    tables = jnp.stack([protos, teacher_protos]).astype(BF16)
    around = [tables]
    for step in range(2, reps, 2):
        around.append(lax.ppermute(tables, "rep", [(r, (r + step) % reps) for r in range(reps)]))

    table = jnp.asarray(plan.lay_table)[device]
    given = trade(lay_out(plan, table, jnp.where(low, teacher, params)))
    kept = lay_out(plan, table, jnp.where(low, params, teacher))
    given, around = lax.optimization_barrier((given, around))
    shards = jnp.stack([jnp.where(low, kept, given), jnp.where(low, given, kept)])
    gathered = lax.all_gather(shards, BOTH, axis=0, axis_index_groups=halves)
    gathered = gathered.reshape(half, 2, -1, TILE, LANES)
    patches, partner, given = lax.optimization_barrier((patches, partner, given))
    pixels = jnp.concatenate(in_order(patches), 0)
    pixels = jnp.pad(pixels, ((0, 0), (0, TOKENS - NPATCH), (0, 0)))
    around = jnp.concatenate([jnp.stack(around[::-1])] * 2)
    around = lax.dynamic_slice_in_dim(around, lines - 1 - rep // 2, lines, 0)
    tables = jnp.stack(in_order(around))
    tables = tables.transpose(2, 1, 0, 3, 4).reshape(2, B, -1).astype(F32)
    places = in_order(partner.astype(F32))

    def columns_of(values):
        scale = lax.rsqrt(jnp.sum(values * values, 0, keepdims=True) + 1e-06)
        return (values * scale).astype(BF16), scale

    columns, column_scale = columns_of(tables[0])
    teacher_columns = columns_of(tables[1])[0]

    here = jnp.arange(views)
    source = jnp.concatenate([places[0], places[1] + own_views]).astype(jnp.int32)
    source = jnp.where(low, here, source)
    turn = (source[:, None] == here[None, :]).astype(BF16)

    turn, columns, teacher_columns = lax.optimization_barrier((turn, columns, teacher_columns))
    kept = forward(plan, gathered, pixels, turn)
    unit, scale, probs, mixed, looked, classes, qkv_w, second = kept[:8]
    received = lax.all_to_all(kept[-1], BOTH, 0, 0)
    received = received.reshape(reps // 2, 2, groups * views, -1)
    all_rows = received[..., :B]
    ahead = received[:, 0, :, B:].reshape(half * views, -1)

    def gather_rows(values):
        return lax.all_gather(values, BOTH, axis=0, axis_index_groups=halves).reshape(
            half * views, -1
        )

    common = [mixed[:, :HEADS].reshape(views, -1), second]
    common.append(jnp.pad(classes[1:3], ((0, views - 2), (0, 0))).astype(BF16))
    common = jnp.concatenate(common, 1)
    other = trade(common)
    all_rows, ahead, other = lax.optimization_barrier((all_rows, ahead, other))
    common = jnp.where(low, common, other)

    all_rows = all_rows.transpose(1, 0, 2, 3).reshape(2, -1, B)
    start = (rep // 2 * groups * views).astype(jnp.int32)[None]
    note, new_center = prototypes(
        start, all_rows, columns, teacher_columns, center[None], groups, views
    )
    common = gather_rows(common)
    new_center = new_center[0]
    note = lax.all_to_all(note, "grp", 0, 0)
    totals = jnp.sum(note[:, 3 * views :], 0)
    totals = totals.reshape(-1, 8, B).transpose(1, 0, 2).reshape(8, -1)[:, : half * views]
    loss_value = jnp.sum(jnp.log(totals[0]) - totals[2] / totals[1])
    depth = protos.shape[0]
    grad_protos, proto_squares = prototypes_back(
        (rep * depth).astype(jnp.int32)[None],
        depth,
        all_rows,
        columns,
        teacher_columns,
        center[None],
        totals,
        tables[0],
        column_scale,
    )
    behind, grad_middle, ends = rows_back(
        plan, low.astype(jnp.int32)[None], gathered, note, (classes,) + tuple(kept[8:13])
    )
    odd, far = grp % 2 == 1, grp // 2 % 2 == 1
    behind_rows = trade_low(behind)
    kept_rows, sent_rows = tokens_back(
        odd.astype(jnp.int32)[None],
        behind,
        grad_middle,
        ends,
        (unit, scale, probs, looked, classes, qkv_w),
        pixels.transpose(0, 2, 1),
        behind_rows,
        grad_protos,
    )

    def across(bit, values):
        return lax.ppermute(values, "grp", [(g, g ^ bit) for g in range(groups)])

    partial = kept_rows + across(1, sent_rows).astype(F32)
    first, second = partial[:SET], partial[SET : 2 * SET]
    shared = partial[2 * SET :]
    other = jnp.concatenate([jnp.where(far, first, second), shared], 0).astype(BF16)
    partial = jnp.concatenate([jnp.where(far, second, first), shared], 0)
    partial = partial + across(2, other).astype(F32)
    behind_rows, partial = lax.optimization_barrier((behind_rows, partial))
    behind_rows = gather_rows(behind_rows)
    if plan.near:
        step = 1
        while step < lines:
            hops = [(r, r - 2 * step) for r in range(reps) if r // 2 % (2 * step) == step]
            partial = partial + lax.ppermute(partial.astype(BF16), "rep", hops).astype(F32)
            step *= 2
        depth, first_rows, holds = partial.shape[0], 0, rep == 0
    else:
        depth = partial.shape[0] // lines
        partial = lax.all_to_all(
            partial.astype(BF16).reshape(lines, depth, D), "rep", 0, 0, axis_index_groups=pairs
        )
        partial = jnp.sum(partial.astype(F32), 0)
        first_rows, holds = rep // 2 * depth, low
    class_rows = common[:2, CLASS:].astype(F32)
    class_normed, query = class_rows[0:1], class_rows[1:2]
    by_head = jnp.where(head_mask()[:HEADS], query, 0.0)
    twice = odd & ~far & (jnp.arange(SET) < 8)
    weights = jnp.concatenate(
        [
            jnp.where(twice, 0.0, 1.0),
            jnp.sum(by_head * by_head, 1) / groups,
            jnp.zeros((HEADROWS - HEADS,), F32),
            jnp.sum(class_normed * class_normed)[None] / groups,
            jnp.full((2,), 1.0 / groups, F32),
            jnp.zeros((SHARED - HEADROWS - 3,), F32),
        ]
    )
    weights = lax.dynamic_slice_in_dim(weights, first_rows, depth)
    pieces = jnp.sum(weights * jnp.sum(partial * partial, 1))
    rest = jnp.where(holds, pieces, 0.0) + jnp.sum(proto_squares[0])
    early, squares = early_gradient(
        plan, jnp.asarray(plan.grad_table)[device], ahead, common, behind_rows, rest.reshape(1, 1)
    )
    summed = partial.astype(BF16)
    if not plan.near:
        summed = lax.all_to_all(
            jnp.broadcast_to(summed[None], (lines, depth, D)), "rep", 0, 0, axis_index_groups=pairs
        ).reshape(-1, D)
    shared, summed = summed[SET:], summed[:SET]
    other, squares = lax.optimization_barrier((across(2, summed), squares))
    squares = lax.all_to_all(squares, BOTH, 0, 0)
    grad_norm = jnp.sqrt(jnp.sum(squares[:, 0, 0]))
    factor = jnp.minimum(1.0, CLIP_NORM / (grad_norm + 1e-06))
    summed = jnp.concatenate([jnp.where(far, other, summed), jnp.where(far, summed, other)], 0)
    if plan.all_sets:
        other = across(1, summed)
        summed = jnp.concatenate([jnp.where(odd, other, summed), jnp.where(odd, summed, other)], 0)
    if plan.odd_owner:
        summed = trade_low(summed)
    wide_grad = jnp.pad(summed.astype(F32), ((0, CHUNK), (0, 0)))

    ends = shared[HEADROWS + 1 : HEADROWS + 3]
    shared = trade_low(shared).astype(F32)
    if plan.near:
        for owner in plan.final_reps:
            moved = lax.ppermute(ends, "rep", [(0, owner)]) if owner else ends
            ends = jnp.where(rep == owner, moved, ends)
        ends = ends.astype(F32)
    else:
        ends = shared[HEADROWS + 1 : HEADROWS + 3]
    ends = jnp.pad(ends, ((0, 6), (0, 0)))
    sum_query, reach = shared[HEADROWS : HEADROWS + 1], shared[:HEADS]
    left = jnp.concatenate([class_normed, reach, jnp.zeros((LANES - 1 - HEADS, D), F32)], 0)
    left = jnp.pad(left.T, ((0, CHUNK), (0, 0)))
    right = jnp.concatenate(
        [
            jnp.pad(sum_query, ((0, 0), (0, D))),
            jnp.pad(by_head, ((0, 0), (D, 0))),
            jnp.zeros((LANES - 1 - HEADS, 2 * D), F32),
        ],
        0,
    )
    grad_flat = late_gradient(
        plan, jnp.asarray(plan.late_table)[device], early, wide_grad, left, right, ends
    )
    new_params, new_first, new_second = adam_update(
        params, grad_flat * factor, first_moment, second_moment, LEARNING_RATE
    )
    new_protos, new_proto_first, new_proto_second = adam_update(
        protos, grad_protos * factor, proto_first, proto_second, PROTO_RATE
    )
    new_teacher = TEACHER_MOMENTUM * teacher + (1.0 - TEACHER_MOMENTUM) * new_params
    new_teacher_protos = TEACHER_MOMENTUM * teacher_protos + (1.0 - TEACHER_MOMENTUM) * new_protos
    return (
        new_params,
        new_first,
        new_second,
        new_teacher,
        new_protos,
        new_proto_first,
        new_proto_second,
        new_teacher_protos,
        new_center,
        loss_value,
        grad_norm,
    )


def solution(mesh):
    placed = (
        P(BOTH),
        P(BOTH),
        P(BOTH),
        P(BOTH),
        P("rep", "grp"),
        P("rep", "grp"),
        P("rep", "grp"),
        P("rep", "grp"),
        P("grp"),
        P(BOTH, None, None),
        P(BOTH),
    )
    plan = Plan(mesh.shape["rep"], mesh.shape["grp"])
    return jax.shard_map(
        functools.partial(per_device, plan),
        mesh=mesh,
        in_specs=placed,
        out_specs=placed[:9] + (P(), P()),
        check_vma=False,
    )
```

```python
import functools

import jax
import jax.numpy as jnp
import numpy as np
from jax import lax
from jax.experimental import pallas as pl
from jax.experimental.pallas import tpu as pltpu
from jax.sharding import PartitionSpec as P

D = 768
HEADS = 12
HDIM = 64
F = 3072
PD = 768
NTOK = 197
H = 2048
B = 256
STEP = 10
NPATCH = NTOK - 1

PRECISE = lax.Precision.HIGHEST
STUDENT_TEMP = 0.1
TEACHER_TEMP = 0.04
CENTER_MOMENTUM = 0.9
TEACHER_MOMENTUM = 0.8
CLIP_NORM = 0.05
LEARNING_RATE = 0.03
PROTO_RATE = 0.6
BETA_FIRST = 0.9
BETA_SECOND = 0.999
ADAM_EPSILON = 1e-08
WEIGHT_DECAY = 0.04
BOTH = ("rep", "grp")
LANES = 128
F32 = jnp.float32
BF16 = jnp.bfloat16

SEGMENTS = []
_offset = 0
for _rows, _cols in ((PD + NTOK + 4, D), (D, 3 * D), (D, D), (D, F), (F + 2, D), (D + H, H), (H, B)):
    SEGMENTS.append((_offset, _rows, _cols))
    _offset += _rows * _cols
PFLAT = _offset
WIDTHS = sorted({cols // LANES for _, _, cols in SEGMENTS})

PIECES = []
_offset = 0
for _rows, _cols in (
    (PD + NTOK + 4, D),
    (D, 3 * D),
    (D, D),
    (D, F),
    (F, D),
    (2, D),
    (D, H),
    (H, H),
    (H, B),
):
    PIECES.append((_offset, _rows, _cols))
    _offset += _rows * _cols
FRONT = 192
CHUNK = 128
SET = 288
SHARED = 32
STEPS = 64
AHEAD = 3 * D + F + H
TILE = 16
TOKENS = 208
HEADROWS = 16
VMEM_LIMIT = 62 * 1024 * 1024


SPANS = {
    2: (0, 0),
    3: (D, D),
    4: (2 * D, D + F),
    6: (2 * D + F, 2 * D + F + B + H),
    7: (3 * D + F, 2 * D + F + B),
}
ATT_COLUMN = 2 * D + F + B + 2 * H
SECOND = HEADS * D
CLASS = SECOND + H


def round_up(value, step):
    return -(-value // step) * step


def steps_at_once(count):
    return max(size for size in range(1, 8) if count % size == 0)


def shard_parts(start, stop, table):
    parts = []
    line0 = start // LANES
    for index, (offset, rows, cols) in enumerate(table):
        low, high = max(start, offset), min(stop, offset + rows * cols)
        if low >= high:
            continue
        row0 = (low - offset) // cols
        row1 = -(-(high - offset) // cols)
        parts.append((index, row0, row1 - row0, (offset + row0 * cols) // LANES - line0))
    return parts


FINAL_ROW = round_up(PD + NTOK + 4, 8)


class Plan:
    def __init__(self, reps, groups):
        count = reps * groups
        self.count, self.groups = count, groups
        self.size = PFLAT // count
        self.lines = round_up(-(-self.size // LANES) + 1, STEPS)
        self.steps = self.lines // STEPS
        self.scratch = FRONT + self.lines + 8 * max(WIDTHS) + 16
        table = []
        self.blocks = [[] for _ in SEGMENTS]
        longest = 0
        for device in range(count):
            start = device * self.size
            entry = [start % LANES]
            target = 0
            for index, row0, rows, line in shard_parts(start, start + self.size, SEGMENTS):
                width = SEGMENTS[index][2] // LANES
                skew = row0 % 8
                tiles = -(-(rows + skew) // 8)
                self.blocks[index].append((device, target // TILE, row0 // 8, tiles))
                entry += [
                    WIDTHS.index(width),
                    FRONT + line - skew * width,
                    tiles // 2,
                    tiles % 2,
                    target // TILE,
                ]
                target += tiles * 8 * width
            longest = max(longest, target)
            entry += [-1, 0, 0, 0, 0] * (2 - len(entry) // 5)
            table.append(entry)
        self.buffer = round_up(longest, 16)
        self.lay_table = np.array(table, np.int32)
        edge = SEGMENTS[0][1] * SEGMENTS[0][2]
        owners = [device for device in range(count) if device * self.size < edge]
        self.odd_owner = any(self.place(device)[1] for device in owners)
        self.all_sets = len(owners) > 2
        edge = sum(rows * cols for _, rows, cols in SEGMENTS[:2])
        self.near = all(
            device < 2 * groups for device in range(count) if device * self.size < edge
        )
        offset, rows, cols = PIECES[5]
        self.final_reps = sorted(
            {
                device // groups
                for device in range(count)
                if device * self.size < offset + rows * cols and (device + 1) * self.size > offset
            }
        )
        self.sent = [[] for _ in range(count)]
        self.grad_table = self.tabulate(lambda index: index, self.sent_row)
        self.late_table = self.tabulate(lambda index: index in (0, 1, 5), self.wide_row)
        self.reach = max(place + size for sent in self.sent for _, size, place in sent)
        self.grad_scratch = FRONT + self.lines + CHUNK * max(WIDTHS) + 16


    def largest(self):
        longest = max(8 * block[3] for blocks in self.blocks for block in blocks)
        return max(len(blocks) for blocks in self.blocks), round_up(longest, LANES) + 2 * LANES

    def place(self, device):
        rep, grp = divmod(device, self.groups)
        return rep // 2 * self.groups + grp, rep % 2

    def tabulate(self, chosen, rows_of):
        table = []
        for device in range(self.count):
            start = device * self.size
            entry = []
            for index, row0, rows, line in shard_parts(start, start + self.size, PIECES):
                if not chosen(index):
                    continue
                skew = row0 % 8
                line -= skew * (PIECES[index][2] // LANES)
                chunks = -(-(rows + skew) // CHUNK)
                entry += [index, FRONT + line, chunks, rows_of(device, index, row0 - skew, chunks)]
            table.append(entry)
        most = max(len(entry) for entry in table) // 4
        for device, entry in enumerate(table):
            entry += [-1, 0, 0, 0] * (most - len(entry) // 4)
            entry.insert(0, device * self.size % LANES)
            entry += [device < self.groups, device % 4 == 1]
        return np.array(table, np.int32)

    def sent_row(self, device, index, row0, chunks):
        if index not in SPANS:
            return row0
        sent, size = self.sent[device], chunks * CHUNK
        place = sum(before for _, before, _ in sent)
        sent.append((SPANS[index][0] + row0, size, place))
        return place

    def wide_row(self, device, index, row0, chunks):
        if index:
            return row0
        late = row0 >= 2 * SET - 8
        if not self.all_sets:
            if late != device % 2:
                raise ValueError("owner")
            return row0 - (2 * SET - 8) * late
        return row0 + 8 * late


def lay_kernel(plan, tab_ref, x_ref, out_ref, line_ref):
    shift = tab_ref[0]
    lane = lax.broadcasted_iota(jnp.int32, (STEPS + 8, LANES), 1)
    line_ref[pl.ds(0, FRONT), :] = jnp.zeros((FRONT, LANES), F32)
    tail = plan.scratch - FRONT - plan.lines
    line_ref[pl.ds(FRONT + plan.lines, tail), :] = jnp.zeros((tail, LANES), F32)

    def align(step, carry):
        base = pl.multiple_of(step * STEPS, 8)
        here = pltpu.roll(x_ref[pl.ds(base, STEPS + 8), :], shift, 1)
        above = pltpu.roll(here, 1, 0)
        both = jnp.where(lane >= shift, here, above)
        line_ref[pl.ds(pl.multiple_of(FRONT + base, 8), STEPS), :] = both[8:]
        return carry

    lax.fori_loop(0, plan.steps, align, 0, unroll=steps_at_once(plan.steps))
    for part in range(2):
        kind, base, pairs, odd, target = (tab_ref[1 + 5 * part + i] for i in range(5))
        for index, width in enumerate(WIDTHS):

            @pl.when(kind == index)
            def _(width=width):
                def move(step, carry):
                    row = base + step * (TILE * width)
                    goal = (target + step * width) * TILE
                    for tile in range(width):
                        both = line_ref[pl.ds(row + tile, TILE, stride=width), :]
                        place = pl.multiple_of(goal + TILE * tile, TILE)
                        out_ref[pl.ds(place, TILE), :] = both.astype(BF16)
                    return carry

                def last(step, carry):
                    row = base + pairs * (TILE * width)
                    goal = (target + pairs * width) * TILE
                    for tile in range(0, width, 2):
                        both = [
                            line_ref[pl.ds(row + tile + side, 8, stride=width), :]
                            for side in range(2)
                        ]
                        place = pl.multiple_of(goal + 8 * tile, TILE)
                        out_ref[pl.ds(place, TILE), :] = jnp.concatenate(both, 0).astype(BF16)
                    return carry

                lax.fori_loop(0, pairs, move, 0)
                lax.fori_loop(0, odd, last, 0)


def lay_out(plan, table, flat):
    padded = jnp.pad(flat, (8 * LANES, plan.lines * LANES - plan.size))
    lines = padded.reshape(8 + plan.lines, LANES)
    return pl.pallas_call(
        functools.partial(lay_kernel, plan),
        out_shape=jax.ShapeDtypeStruct((plan.buffer, LANES), BF16),
        in_specs=[
            pl.BlockSpec(memory_space=pltpu.SMEM),
            pl.BlockSpec(memory_space=pltpu.VMEM),
        ],
        out_specs=pl.BlockSpec(memory_space=pltpu.VMEM),
        scratch_shapes=[pltpu.VMEM((plan.scratch, LANES), F32)],
        compiler_params=pltpu.CompilerParams(vmem_limit_bytes=24 * 1024 * 1024),
    )(table, lines)


class Shards:
    def __init__(self, plan, gathered_ref, ref, sems, order):
        self.plan, self.ref, self.sems, self.waited = plan, ref, sems, set()
        self.copies = {}
        for device in order:
            place, side = plan.place(device)
            copy = pltpu.make_async_copy(
                gathered_ref.at[place, side], ref.at[device], sems.at[device]
            )
            copy.start()
            self.copies[device] = copy

    def wait(self, device):
        if device in self.copies:
            self.copies.pop(device).wait()

    def finish(self):
        for device in list(self.copies):
            self.wait(device)

    def blocks(self, index, first, count):
        found = [
            block
            for block in self.plan.blocks[index]
            if 8 * block[2] < first + count and 8 * (block[2] + block[3]) > first
        ]
        for block in found:
            self.wait(block[0])
        return found

    def eight(self, index, tile, pair, side):
        width = SEGMENTS[index][2] // LANES
        total = None
        for device, target, tile0, tiles in self.plan.blocks[index]:
            own = tile - tile0
            if not 0 <= own < tiles:
                continue
            if own < tiles // 2 * 2:
                both = self.ref[device, target + own // 2 * width + 2 * pair + side]
                half = own % 2
            else:
                both = self.ref[device, target + tiles // 2 * width + pair]
                half = side
            piece = both.astype(F32)[8 * half : 8 * half + 8]
            total = piece if total is None else total + piece
        return total

    def assemble(self, index, out_ref):
        width = SEGMENTS[index][2] // LANES
        rows = out_ref.shape[0]
        self.blocks(index, 0, rows)

        def column(pair, carry):
            for side in range(2):
                lanes = pl.ds(pl.multiple_of(pair * 2 * LANES + side * LANES, LANES), LANES)
                for group in range(rows // TILE):
                    both = [
                        self.eight(index, 2 * group + half, pair, side) for half in range(2)
                    ]
                    out_ref[TILE * group : TILE * (group + 1), lanes] = jnp.concatenate(
                        both, 0
                    ).astype(BF16)
            return carry

        lax.fori_loop(0, width // 2, column, 0)

    def columns(self, index, block, pair):
        width = SEGMENTS[index][2] // LANES
        device, target, _, tiles = block
        sides = []
        for side in range(2):
            pieces = [
                self.ref[device, target + step * width + 2 * pair + side]
                for step in range(tiles // 2)
            ]
            if tiles % 2:
                both = self.ref[device, target + tiles // 2 * width + pair].astype(F32)
                pieces.append(both[8 * side : 8 * side + 8].astype(BF16))
            sides.append(jnp.concatenate(pieces, 0))
        return jnp.concatenate(sides, 1)

    def times(self, index, first, values, left_ref, out_ref):
        views, count = values.shape
        blocks = self.blocks(index, first, count)
        top = max([first + count] + [8 * (tile0 + tiles) for _, _, tile0, tiles in blocks])
        top = round_up(top, LANES) + LANES
        parts = [values, jnp.zeros((views, top - first - count), F32)]
        if first:
            parts.insert(0, jnp.zeros((views, first), F32))
        wide = jnp.concatenate(parts, 1)
        for number, (_, _, tile0, tiles) in enumerate(blocks):
            start = 8 * tile0 // LANES * LANES
            turn = 8 * tile0 - start
            piece = wide[:, start : start + round_up(turn + 8 * tiles, LANES)]
            if turn:
                piece = pltpu.roll(piece, piece.shape[1] - turn, 1)
            left_ref[number, :, : 8 * tiles] = piece[:, : 8 * tiles]

        def column(pair, carry):
            total = jnp.zeros((views, 2 * LANES), F32)
            for number, block in enumerate(blocks):
                left = left_ref[number, :, : 8 * block[3]].astype(BF16)
                total += product(left, self.columns(index, block, pair))
            out_ref[:, pl.ds(pl.multiple_of(pair * 2 * LANES, LANES), 2 * LANES)] = total
            return carry

        lax.fori_loop(0, SEGMENTS[index][2] // LANES // 2, column, 0, unroll=2)


    def back(self, index, first, count, values, grad_ref, left_ref, wide_ref):
        views, cols = values.shape
        grad_ref[:, :cols] = values
        blocks = self.blocks(index, first, count)
        top = max([first + count] + [8 * (tile0 + tiles) for _, _, tile0, tiles in blocks])
        wide_ref[:, : round_up(top, LANES) + LANES] = jnp.zeros(
            (views, round_up(top, LANES) + LANES), F32
        )
        for number, (_, _, _, tiles) in enumerate(blocks):
            size = round_up(8 * tiles, LANES) + LANES
            left_ref[number, :, :size] = jnp.zeros((views, size), F32)

        def column(pair, carry):
            lanes = pl.ds(pl.multiple_of(pair * 2 * LANES, LANES), 2 * LANES)
            left = grad_ref[:, lanes].astype(BF16)
            for number, block in enumerate(blocks):
                size = 8 * block[3]
                left_ref[number, :, :size] += product_t(left, self.columns(index, block, pair))
            return carry

        lax.fori_loop(0, cols // LANES // 2, column, 0, unroll=2)
        for number, (_, _, tile0, tiles) in enumerate(blocks):
            start = 8 * tile0 // LANES * LANES
            turn = 8 * tile0 - start
            size = round_up(turn + 8 * tiles, LANES)
            piece = left_ref[number, :, :size]
            if turn:
                piece = pltpu.roll(piece, turn, 1)
            wide_ref[:, start : start + size] += piece
        return wide_ref[:, first : first + count]


def product(left, right):
    return jnp.dot(left, right, preferred_element_type=F32)


def product_t(left, right):
    return lax.dot_general(
        left, right, (((left.ndim - 1,), (1,)), ((), ())), preferred_element_type=F32
    )


def normal_share(values):
    return 0.5 + 0.5 * lax.erf(values * 2**-0.5)


def activate(values):
    return values * normal_share(values)


def gelu_back(values, grad):
    density = jnp.exp(-0.5 * values * values) * (2 * np.pi) ** -0.5
    return grad * (normal_share(values) + values * density)


def normalised(values):
    centred = values - jnp.mean(values, -1, keepdims=True)
    scale = lax.rsqrt(jnp.mean(centred * centred, -1, keepdims=True) + 1e-06)
    return centred * scale, scale


def norm_back(grad, gain, unit, scale):
    inner = grad * gain
    return scale * (
        inner
        - jnp.mean(inner, -1, keepdims=True)
        - unit * jnp.mean(inner * unit, -1, keepdims=True)
    )


def head_mask():
    shape = (HEADROWS, D)
    return lax.broadcasted_iota(jnp.int32, shape, 0) == (
        lax.broadcasted_iota(jnp.int32, shape, 1) // HDIM
    )


def token_norms(unit, norms, class_normed):
    token = lax.broadcasted_iota(jnp.int32, (TOKENS, D), 0)
    normed = unit * norms[0:1] + norms[1:2]
    return jnp.where(
        token < NPATCH, normed, jnp.where(token == NPATCH, class_normed, 0.0)
    ).astype(BF16)


def forward_kernel(
    plan,
    gathered_ref,
    pixels_ref,
    turn_ref,
    unit_out,
    scale_out,
    probs_ref,
    mixed_ref,
    looked_ref,
    class_ref,
    qkv_out,
    second_ref,
    hidden_ref,
    one_ref,
    two_ref,
    bottle_ref,
    middle_ref,
    send_ref,
    shards_ref,
    wide_ref,
    place_ref,
    left_ref,
    sums_ref,
    pack_ref,
    unit_ref,
    scale_ref,
    qkv_ref,
    out_sems,
    sems,
):
    shards = Shards(plan, gathered_ref, shards_ref, sems, range(plan.count))
    views = pixels_ref.shape[0]
    temper = HDIM ** (-0.5)
    shards.assemble(0, wide_ref)
    position = wide_ref[PD : PD + TOKENS].astype(F32)
    place_ref[...] = pltpu.roll(position, TOKENS - 1, 0)
    class_place = position[0:1]
    norms = position[NTOK : NTOK + 4]
    class_unit, class_scale = normalised(class_place)
    class_normed = (class_unit * norms[0:1] + norms[1:2]).astype(BF16).astype(F32)
    shards.assemble(1, qkv_ref)
    qkv_copy = pltpu.make_async_copy(qkv_ref, qkv_out, out_sems.at[4])
    qkv_copy.start()
    mask = head_mask()
    query = jnp.broadcast_to(class_normed, (HEADROWS, D)).astype(BF16)
    query = product(query, qkv_ref[:, :D]).astype(BF16).astype(F32)
    by_head = jnp.where(mask, query, 0.0).astype(BF16)
    looked = product_t(by_head, qkv_ref[:, D : 2 * D]).astype(BF16)
    looked_ref[...] = looked

    def copies(v):
        slot = lax.rem(v, 2)
        return (
            pltpu.make_async_copy(unit_ref.at[slot], unit_out.at[v], out_sems.at[slot]),
            pltpu.make_async_copy(scale_ref.at[slot], scale_out.at[v], out_sems.at[2 + slot]),
        )

    def view(v, carry):
        embedded = product(pixels_ref[v], wide_ref[:PD]) + place_ref[...]
        unit, scale = normalised(embedded)

        @pl.when(v >= 2)
        def _():
            for copy in copies(v - 2):
                copy.wait()

        unit_ref[lax.rem(v, 2)] = unit
        scale_ref[lax.rem(v, 2)] = jnp.broadcast_to(scale, (TOKENS, LANES))
        for copy in copies(v):
            copy.start()
        normed = token_norms(unit, norms, class_normed)
        scores = product_t(looked, normed) * temper
        token = lax.broadcasted_iota(jnp.int32, scores.shape, 1)
        scores = jnp.where(token < NTOK, scores, -1e30)
        top = jnp.max(scores, -1, keepdims=True)
        top = top + jnp.log(jnp.sum(jnp.exp(scores - top), -1, keepdims=True))
        head = lax.broadcasted_iota(jnp.int32, scores.shape, 0)
        probs = jnp.where(head < HEADS, jnp.exp(scores - top), 0.0)
        probs_ref[v] = probs
        mixed_ref[v] = product(probs.astype(BF16), normed).astype(BF16)
        return carry

    lax.fori_loop(0, views, view, 0, unroll=2)
    mixed = mixed_ref[...].reshape(views * HEADROWS, D)
    valued = product(mixed, qkv_ref[:, 2 * D :]).reshape(views, HEADROWS, D)
    attended = jnp.sum(jnp.where(mask[None], valued, 0.0), 1).astype(BF16)
    pack_ref[:, :D] = attended.astype(F32)
    shards.times(2, 0, pack_ref[:, :D], left_ref, sums_ref)
    middle = class_place + sums_ref[...]
    unit, scale = normalised(middle)
    middle_ref[0], middle_ref[1] = unit, jnp.broadcast_to(scale, (views, D))
    normed = (unit * norms[2:3] + norms[3:4]).astype(BF16)
    pack_ref[:, D : 2 * D] = normed.astype(F32)
    shards.times(3, 0, pack_ref[:, D : 2 * D], left_ref, hidden_ref)
    act = activate(hidden_ref[...]).astype(BF16)
    pack_ref[:, 2 * D : 2 * D + F] = act.astype(F32)
    shards.times(4, 0, act.astype(F32), left_ref, sums_ref)
    unit, scale = normalised(middle + sums_ref[...])
    middle_ref[2], middle_ref[3] = unit, jnp.broadcast_to(scale, (views, D))
    final = jnp.concatenate(
        [shards.eight(4, F // 8, tile // 2, tile % 2) for tile in range(D // LANES)], 1
    )
    cls = (unit * final[0:1] + final[1:2]).astype(BF16)
    place = 2 * D + F
    pack_ref[:, place : place + D] = cls.astype(F32)
    shards.times(5, 0, cls.astype(F32), left_ref, one_ref)
    first = activate(one_ref[...]).astype(BF16)
    pack_ref[:, place + D : AHEAD] = first.astype(F32)
    pack_ref[:, AHEAD:] = jnp.zeros((views, pack_ref.shape[1] - AHEAD), F32)
    shards.times(5, D, first.astype(F32), left_ref, two_ref)
    second = activate(two_ref[...]).astype(BF16)
    second_ref[...] = second
    shards.times(6, 0, second.astype(F32), left_ref, bottle_ref)
    bottle = bottle_ref[...]
    scale = lax.rsqrt(jnp.sum(bottle * bottle, -1, keepdims=True) + 1e-06)
    rows = product(turn_ref[...], (bottle * scale).astype(BF16)).astype(BF16)
    for device, sent in enumerate(plan.sent):
        send_ref[device, :, :B] = rows
        for lane, size, place in sent:
            start = lane // LANES * LANES
            piece = pack_ref[:, start : start + size + (LANES if lane > start else 0)]
            if lane > start:
                piece = pltpu.roll(piece, piece.shape[1] - (lane - start), 1)
            send_ref[device, :, B + place : B + place + size] = piece[:, :size].astype(BF16)
    class_ref[...] = jnp.concatenate(
        [
            class_unit,
            class_normed,
            query[0:1],
            jnp.broadcast_to(class_scale, (1, D)),
            norms,
            final,
        ],
        0,
    )
    for v in range(max(0, views - 2), views):
        for copy in copies(v):
            copy.wait()
    qkv_copy.wait()
    shards.finish()


def forward(plan, gathered, pixels, turn):
    views = pixels.shape[0]
    shapes = [
        ((views, TOKENS, D), F32),
        ((views, TOKENS, LANES), F32),
        ((views, HEADROWS, TOKENS), F32),
        ((views, HEADROWS, D), BF16),
        ((HEADROWS, D), BF16),
        ((16, D), F32),
        ((D, 3 * D), BF16),
        ((views, H), BF16),
        ((views, F), F32),
        ((views, H), F32),
        ((views, H), F32),
        ((views, B), F32),
        ((4, views, D), F32),
        ((plan.count, views, B + plan.reach), BF16),
    ]
    most, longest = plan.largest()
    return pl.pallas_call(
        functools.partial(forward_kernel, plan),
        out_shape=[jax.ShapeDtypeStruct(shape, dtype) for shape, dtype in shapes],
        in_specs=[pl.BlockSpec(memory_space=pl.ANY)]
        + [pl.BlockSpec(memory_space=pltpu.VMEM)] * 2,
        out_specs=[
            pl.BlockSpec(memory_space=pl.ANY if index in (0, 1, 6) else pltpu.VMEM)
            for index in range(len(shapes))
        ],
        scratch_shapes=[
            pltpu.VMEM((plan.count, plan.buffer // TILE, TILE, LANES), BF16),
            pltpu.VMEM((round_up(PD + NTOK + 4, TILE), D), BF16),
            pltpu.VMEM((TOKENS, D), F32),
            pltpu.VMEM((most, views, longest), F32),
            pltpu.VMEM((views, D), F32),
            pltpu.VMEM((views, round_up(AHEAD + CHUNK, LANES) + LANES), F32),
            pltpu.VMEM((2, TOKENS, D), F32),
            pltpu.VMEM((2, TOKENS, LANES), F32),
            pltpu.VMEM((D, 3 * D), BF16),
            pltpu.SemaphoreType.DMA((5,)),
            pltpu.SemaphoreType.DMA((plan.count,)),
        ],
        compiler_params=pltpu.CompilerParams(vmem_limit_bytes=VMEM_LIMIT),
        cost_estimate=pl.CostEstimate(
            flops=60 * 10**9, bytes_accessed=40 * 10**6, transcendentals=10**5
        ),
    )(gathered, pixels, turn)


def proto_kernel(
    start_ref,
    rows_ref,
    columns_ref,
    others_ref,
    center_ref,
    note_ref,
    center_out_ref,
    student_ref,
    teacher_ref,
    sums_ref,
):
    count, groups = rows_ref.shape[1], note_ref.shape[0]
    views = (note_ref.shape[1] - 8 * -(-count // B)) // 3
    logits = product(rows_ref[1], others_ref[...])
    center = center_ref[...]
    center_out_ref[...] = CENTER_MOMENTUM * center + (1.0 - CENTER_MOMENTUM) * jnp.mean(
        logits, 0, keepdims=True
    )
    exp_teacher = jnp.exp((logits - center) / TEACHER_TEMP)
    teacher_ref[...] = exp_teacher
    scaled = product(rows_ref[0], columns_ref[...]) / STUDENT_TEMP
    exp_student = jnp.exp(scaled)
    student_ref[...] = exp_student
    turned = []
    for which, values in enumerate((exp_student, exp_teacher, exp_teacher * scaled)):
        total = jnp.broadcast_to(jnp.sum(values, 1, keepdims=True), (count, LANES))
        turned.append(total.T[0:1])
        if which < 2:
            sums_ref[:, which * LANES : (which + 1) * LANES] = total
    turned = jnp.concatenate(turned + [jnp.zeros((5, count), F32)], 0)
    for step in range(-(-count // B)):
        part = turned[:, step * B : (step + 1) * B]
        lines = slice(3 * views + 8 * step, 3 * views + 8 * (step + 1))
        note_ref[:, lines, : part.shape[1]] = jnp.broadcast_to(part[None], (groups,) + part.shape)
        if part.shape[1] < B:
            note_ref[:, lines, part.shape[1] :] = jnp.zeros((groups, 8, B - part.shape[1]), F32)
    start = pl.multiple_of(start_ref[0], 8)
    columns = columns_ref[...].astype(F32)
    for which, source in enumerate((student_ref, teacher_ref)):
        pulls = lax.dot_general(
            source[pl.ds(start, groups * views), :],
            columns,
            (((1,), (1,)), ((), ())),
            precision=PRECISE,
            preferred_element_type=F32,
        )
        note_ref[:, which * views : (which + 1) * views, :] = pulls.reshape(groups, views, B)
    own = sums_ref[pl.ds(start, groups * views), :]
    note_ref[:, 2 * views : 3 * views, :] = own.reshape(groups, views, B)


def prototypes(start, rows, columns, others, center, groups, views):
    count, width = rows.shape[1], columns.shape[1]
    shapes = [(groups, 3 * views + 8 * -(-count // B), B), (1, width)]
    return pl.pallas_call(
        proto_kernel,
        out_shape=[jax.ShapeDtypeStruct(shape, F32) for shape in shapes],
        in_specs=[pl.BlockSpec(memory_space=pltpu.SMEM)]
        + [pl.BlockSpec(memory_space=pltpu.VMEM)] * 4,
        out_specs=[pl.BlockSpec(memory_space=pltpu.VMEM)] * len(shapes),
        scratch_shapes=[pltpu.VMEM((count, width), F32)] * 2
        + [pltpu.VMEM((count, 2 * LANES), F32)],
        compiler_params=pltpu.CompilerParams(vmem_limit_bytes=32 * 1024 * 1024),
        cost_estimate=pl.CostEstimate(
            flops=3 * 10**9, bytes_accessed=6 * 10**6, transcendentals=10**6
        ),
    )(start, rows, columns, others, center)


def proto_back_kernel(
    start_ref,
    rows_ref,
    columns_ref,
    others_ref,
    center_ref,
    totals_ref,
    table_ref,
    scale_ref,
    grad_ref,
    square_ref,
    work_ref,
):
    count = rows_ref.shape[1]
    totals = jnp.broadcast_to(totals_ref[0:2][:, None, :], (2, 8, count))
    student, teacher = (totals[which].T[:, :1] for which in range(2))
    logits = product(rows_ref[1], others_ref[...])
    targets = jnp.exp((logits - center_ref[...]) / TEACHER_TEMP) / teacher
    scaled = product(rows_ref[0], columns_ref[...]) / STUDENT_TEMP
    grad = (jnp.exp(scaled) / student - targets) / STUDENT_TEMP
    work_ref[...] = jnp.dot(
        rows_ref[0].astype(F32).T, grad, precision=PRECISE, preferred_element_type=F32
    )
    scale = scale_ref[...]
    inner = jnp.sum(work_ref[...] * table_ref[...], 0, keepdims=True)
    start = pl.multiple_of(start_ref[0], 8)
    lines = pl.ds(start, grad_ref.shape[0])
    grad = work_ref[lines, :] * scale - table_ref[lines, :] * (scale * scale * scale * inner)
    grad_ref[...] = grad
    square_ref[...] = jnp.broadcast_to(jnp.sum(grad * grad, keepdims=True), square_ref.shape)


def prototypes_back(start, depth, *values):
    count, width = values[0].shape[1], values[1].shape[1]
    shapes = [(depth, width), (8, LANES)]
    return pl.pallas_call(
        proto_back_kernel,
        out_shape=[jax.ShapeDtypeStruct(shape, F32) for shape in shapes],
        in_specs=[pl.BlockSpec(memory_space=pltpu.SMEM)]
        + [pl.BlockSpec(memory_space=pltpu.VMEM)] * len(values),
        out_specs=[pl.BlockSpec(memory_space=pltpu.VMEM)] * len(shapes),
        scratch_shapes=[pltpu.VMEM((B, width), F32)],
        compiler_params=pltpu.CompilerParams(vmem_limit_bytes=32 * 1024 * 1024),
        cost_estimate=pl.CostEstimate(
            flops=3 * 10**9, bytes_accessed=6 * 10**6, transcendentals=10**6
        ),
    )(start, *values)


def rows_back_kernel(
    plan,
    low_ref,
    gathered_ref,
    note_ref,
    class_ref,
    hidden_ref,
    one_ref,
    two_ref,
    bottle_ref,
    middle_ref,
    pack_ref,
    stream_ref,
    extra_ref,
    shards_ref,
    left_ref,
    values_ref,
    wide_ref,
    sems,
):
    used = {block[0] for blocks in plan.blocks[2:] for block in blocks}
    shards = Shards(plan, gathered_ref, shards_ref, sems, sorted(used, reverse=True))
    work = (values_ref, left_ref, wide_ref)
    norms, final = class_ref[4:8], class_ref[8:10]

    views = bottle_ref.shape[0]
    note = jnp.sum(note_ref[...], 0)
    sums = note[2 * views : 3 * views]
    student, teacher = sums[:, :1], sums[:, LANES : LANES + 1]
    grad_rows = (note[:views] / student - note[views : 2 * views] / teacher) / STUDENT_TEMP
    grad_rows = jnp.where(low_ref[0] == 0, 0.0, grad_rows).astype(BF16).astype(F32)
    bottle = bottle_ref[...]
    scale = lax.rsqrt(jnp.sum(bottle * bottle, -1, keepdims=True) + 1e-06)
    grad_bottle = (
        grad_rows * scale - bottle * scale**3 * jnp.sum(grad_rows * bottle, -1, keepdims=True)
    ).astype(BF16)
    place = 2 * D + F
    pack_ref[:, place : place + B] = grad_bottle
    grad_two = shards.back(6, 0, H, grad_bottle.astype(F32), *work)
    grad_two = gelu_back(two_ref[...], grad_two).astype(BF16)
    pack_ref[:, place + B : place + B + H] = grad_two
    grad_one = shards.back(5, D, H, grad_two.astype(F32), *work)
    grad_one = gelu_back(one_ref[...], grad_one).astype(BF16)
    pack_ref[:, place + B + H : place + B + 2 * H] = grad_one
    grad_cls = shards.back(5, 0, D, grad_one.astype(F32), *work)
    unit, scale = middle_ref[2], middle_ref[3]
    gain_last = jnp.sum(grad_cls * unit, 0, keepdims=True)
    shift_last = jnp.sum(grad_cls, 0, keepdims=True)
    grad_stream = norm_back(grad_cls, final[0:1], unit, scale)
    grad_branch = grad_stream.astype(BF16)
    pack_ref[:, D + F : 2 * D + F] = grad_branch
    grad_hidden = shards.back(4, 0, F, grad_branch.astype(F32), *work)
    grad_hidden = gelu_back(hidden_ref[...], grad_hidden).astype(BF16)
    pack_ref[:, D : D + F] = grad_hidden
    grad_normed = shards.back(3, 0, D, grad_hidden.astype(F32), *work)
    unit, scale = middle_ref[0], middle_ref[1]
    extra_ref[...] = jnp.concatenate(
        [
            jnp.sum(grad_normed * unit, 0, keepdims=True),
            jnp.sum(grad_normed, 0, keepdims=True),
            gain_last,
            shift_last,
            jnp.zeros((4, D), F32),
        ],
        0,
    )
    grad_middle = grad_stream + norm_back(grad_normed, norms[2:3], unit, scale)
    stream_ref[...] = grad_middle
    grad_mixed = grad_middle.astype(BF16)
    pack_ref[:, :D] = grad_mixed
    grad_att = shards.back(2, 0, D, grad_mixed.astype(F32), *work).astype(BF16)
    pack_ref[:, place + B + 2 * H : place + B + 2 * H + D] = grad_att
    shards.finish()


def rows_back(plan, low, gathered, note, kept):
    views = kept[-1].shape[1]
    shapes = [((views, 3 * D + F + B + 2 * H), BF16), ((views, D), F32), ((8, D), F32)]
    most, longest = plan.largest()
    return pl.pallas_call(
        functools.partial(rows_back_kernel, plan),
        out_shape=[jax.ShapeDtypeStruct(shape, dtype) for shape, dtype in shapes],
        in_specs=[pl.BlockSpec(memory_space=pltpu.SMEM), pl.BlockSpec(memory_space=pl.ANY)]
        + [pl.BlockSpec(memory_space=pltpu.VMEM)] * (1 + len(kept)),
        out_specs=[pl.BlockSpec(memory_space=pltpu.VMEM)] * len(shapes),
        scratch_shapes=[
            pltpu.VMEM((plan.count, plan.buffer // TILE, TILE, LANES), BF16),
            pltpu.VMEM((most, views, longest), F32),
            pltpu.VMEM((views, F), F32),
            pltpu.VMEM((views, F + 2 * LANES), F32),
            pltpu.SemaphoreType.DMA((plan.count,)),
        ],
        compiler_params=pltpu.CompilerParams(vmem_limit_bytes=40 * 1024 * 1024),
        cost_estimate=pl.CostEstimate(
            flops=30 * 10**9, bytes_accessed=30 * 10**6, transcendentals=10**5
        ),
    )(low, gathered, note, *kept)


def tokens_back_kernel(
    odd_ref,
    behind_ref,
    stream_ref,
    ends_ref,
    unit_ref,
    scale_ref,
    probs_ref,
    looked_ref,
    class_ref,
    qkv_ref,
    pixels_ref,
    first_ref,
    second_ref,
    kept_ref,
    sent_ref,
    patch_ref,
    place_ref,
    reach_ref,
    back_ref,
    mixed_ref,
    rows_ref,
):
    v = pl.program_id(0)
    views = stream_ref.shape[0]
    temper = HDIM ** (-0.5)
    norms = class_ref[4:8]
    class_unit, class_normed, class_scale = (class_ref[row : row + 1] for row in (0, 1, 3))

    @pl.when(v == 0)
    def _():
        place = 2 * D + F + B + 2 * H
        grad_att = behind_ref[:, place : place + D].astype(F32)
        spread = jnp.where(head_mask()[None], grad_att[:, None, :], 0.0).astype(BF16)
        back = product_t(spread.reshape(views * HEADROWS, D), qkv_ref[:, 2 * D :])
        back_ref[...] = back.astype(BF16).reshape(views, HEADROWS, D)
        patch_ref[...] = jnp.zeros(patch_ref.shape, F32)
        place_ref[...] = jnp.zeros(place_ref.shape, F32)
        reach_ref[...] = jnp.zeros(reach_ref.shape, F32)
        rows_ref[...] = jnp.zeros(rows_ref.shape, F32)

    unit = unit_ref[0]
    scale = scale_ref[0][:, :1]
    normed = token_norms(unit, norms, class_normed)
    back = back_ref[v]
    probs = probs_ref[0]
    grad_probs = product_t(back, normed)
    delta = jnp.sum(probs * grad_probs, -1, keepdims=True)
    grad_scores = (probs * (grad_probs - delta)).astype(BF16)
    reach = product(grad_scores, normed) * temper
    mixed_ref[v] = reach.astype(BF16)
    reach_ref[...] += reach
    left = jnp.concatenate([grad_scores.astype(F32), probs.astype(BF16).astype(F32)], 0)
    looked = (looked_ref[...].astype(F32) * temper).astype(BF16)
    grad = product(left.T.astype(BF16), jnp.concatenate([looked, back], 0))
    row = lax.broadcasted_iota(jnp.int32, (8, D), 0)
    rows_ref[0] += jnp.where(row == v, grad[NPATCH : NPATCH + 1], 0.0)
    token = lax.broadcasted_iota(jnp.int32, (TOKENS, D), 0)
    grad = jnp.where(token < NPATCH, grad, 0.0)
    rows_ref[1, 0:1] += jnp.sum(grad * unit, 0, keepdims=True)
    rows_ref[2, 0:1] += jnp.sum(grad, 0, keepdims=True)
    stream = norm_back(grad, norms[0:1], unit, scale)
    place_ref[...] += stream
    patch_ref[...] += product(pixels_ref[0], stream.astype(BF16))

    @pl.when(v == views - 1)
    def _():
        keyed = product(mixed_ref[...].reshape(views * HEADROWS, D), qkv_ref[:, D : 2 * D])
        keyed = jnp.where(head_mask()[None], keyed.reshape(views, HEADROWS, D), 0.0)
        grad_query = jnp.sum(keyed, 1).astype(BF16)
        class_row = rows_ref[0][:views] + product_t(grad_query, qkv_ref[:, :D])
        class_stream = norm_back(class_row, norms[0:1], class_unit, class_scale)
        class_stream = class_stream + stream_ref[...]
        ends = [
            (0, jnp.sum(class_stream, 0, keepdims=True)),
            (NTOK, rows_ref[1, 0:1] + jnp.sum(class_row * class_unit, 0, keepdims=True)),
            (NTOK + 1, rows_ref[2, 0:1] + jnp.sum(class_row, 0, keepdims=True)),
            (NTOK + 2, ends_ref[0:1]),
            (NTOK + 3, ends_ref[1:2]),
        ]
        tail = pltpu.roll(place_ref[...], 1, 0)
        for row, value in ends:
            tail = jnp.where(token == row, value, tail)
        upper = 2 * SET - 8
        rest = jnp.zeros((2 * SET - (PD - upper) - TOKENS, D), F32)
        query_row = lax.broadcasted_iota(jnp.int32, (8, D), 0) == 0
        total = jnp.sum(grad_query.astype(F32), 0, keepdims=True)
        shared = [reach_ref[...], jnp.where(query_row, total, pltpu.roll(ends_ref[...], 7, 0))]
        shared = jnp.concatenate(shared + [jnp.zeros((SHARED - HEADROWS - 8, D), F32)], 0)
        kept_ref[2 * SET :] = shared
        sent_ref[2 * SET :] = shared.astype(BF16)
        last = jnp.concatenate([patch_ref[upper:], tail, rest], 0)

        @pl.when(odd_ref[0] == 0)
        def _():
            kept_ref[: 2 * SET] = patch_ref[: 2 * SET]
            sent_ref[: 2 * SET] = last.astype(BF16)

        @pl.when(odd_ref[0] != 0)
        def _():
            kept_ref[: 2 * SET] = last
            sent_ref[: 2 * SET] = patch_ref[: 2 * SET].astype(BF16)


def tokens_back(odd, behind, grad_middle, ends, kept, pixels, *before):
    views = grad_middle.shape[0]

    def whole(values):
        return pl.BlockSpec(values.shape, lambda v: (0,) * values.ndim)

    def by_view(values):
        return pl.BlockSpec((1,) + values.shape[1:], lambda v: (v,) + (0,) * (values.ndim - 1))

    unit, scale, probs, looked, classes, qkv_w = kept
    shape = (2 * SET + SHARED, D)
    return pl.pallas_call(
        tokens_back_kernel,
        grid=(views,),
        out_shape=[jax.ShapeDtypeStruct(shape, F32), jax.ShapeDtypeStruct(shape, BF16)],
        in_specs=[
            pl.BlockSpec(memory_space=pltpu.SMEM),
            whole(behind),
            whole(grad_middle),
            whole(ends),
            by_view(unit),
            by_view(scale),
            by_view(probs),
            whole(looked),
            whole(classes),
            whole(qkv_w),
            by_view(pixels),
        ]
        + [pl.BlockSpec(memory_space=pl.ANY)] * len(before),
        out_specs=[pl.BlockSpec(shape, lambda v: (0, 0))] * 2,
        scratch_shapes=[
            pltpu.VMEM((PD, D), F32),
            pltpu.VMEM((TOKENS, D), F32),
            pltpu.VMEM((HEADROWS, D), F32),
            pltpu.VMEM((views, HEADROWS, D), BF16),
            pltpu.VMEM((views, HEADROWS, D), BF16),
            pltpu.VMEM((3, 8, D), F32),
        ],
        compiler_params=pltpu.CompilerParams(vmem_limit_bytes=60 * 1024 * 1024),
        cost_estimate=pl.CostEstimate(
            flops=15 * 10**9, bytes_accessed=15 * 10**6, transcendentals=10**5
        ),
    )(odd, behind, grad_middle, ends, unit, scale, probs, looked, classes, qkv_w, pixels, *before)


def early_kernel(
    plan,
    most,
    tab_ref,
    ahead_ref,
    common_hbm,
    behind_hbm,
    rest_ref,
    *refs,
):
    line_ref, square_ref, common_ref, behind_ref, class_ref, sem, class_sem = refs[-7:]
    class_copy = pltpu.make_async_copy(
        common_hbm.at[pl.ds(0, TILE), pl.ds(CLASS, D)], class_ref, class_sem
    )
    class_copy.start()
    line_ref[...] = jnp.zeros(line_ref.shape, F32)

    def fetch(source, target, column, size):
        copy = pltpu.make_async_copy(
            source.at[:, pl.ds(column, size)], target.at[:, pl.ds(0, size)], sem
        )
        copy.start()
        copy.wait()

    def turned(lane):
        start = pl.multiple_of(lane // LANES * LANES, LANES)
        both = common_ref[:, pl.ds(start, 2 * LANES)].astype(F32)
        both = pltpu.roll(both, lax.rem(2 * LANES - (lane - start), 2 * LANES), 1)
        return both[:, :LANES].T.astype(BF16)

    def store(goal, width, tile, block):
        line_ref[pl.ds(goal + tile, block.shape[0], stride=width), :] = block

    for part in range(most):
        kind, base, chunks, row0 = (tab_ref[1 + 4 * part + i] for i in range(4))
        for index, (_, column) in SPANS.items():
            cols = PIECES[index][2]
            width = cols // LANES

            @pl.when(kind == index)
            def _(column=column, cols=cols, width=width):
                fetch(behind_hbm, behind_ref, column, cols)

                def move(step, carry):
                    goal = base + step * (CHUNK * width)
                    lanes = pl.ds(pl.multiple_of(row0 + step * CHUNK, LANES), CHUNK)
                    left = ahead_ref[:, lanes].astype(F32).T.astype(BF16)
                    block = product(left, behind_ref[:, :cols])
                    for tile in range(width):
                        store(goal, width, tile, block[:, tile * LANES : (tile + 1) * LANES])
                    return carry

                lax.fori_loop(0, chunks, move, 0)

        @pl.when(kind == 8)
        def _():
            fetch(behind_hbm, behind_ref, 2 * D + F, B)
            fetch(common_hbm, common_ref, SECOND, H + D)

            def move(step, carry):
                left = turned(row0 + step * CHUNK)
                block = product(left, behind_ref[:, :B])
                for tile in range(B // LANES):
                    piece = block[:, tile * LANES : (tile + 1) * LANES]
                    store(base + step * (CHUNK * B // LANES), B // LANES, tile, piece)
                return carry

            lax.fori_loop(0, chunks, move, 0)

        @pl.when(kind == 5)
        def _():
            for tile in range(D // LANES):
                store(base, D // LANES, tile, jnp.zeros((8, LANES), F32))

        @pl.when(kind == 1)
        def _():
            fetch(behind_hbm, behind_ref, ATT_COLUMN, D)
            fetch(common_hbm, common_ref, 0, common_ref.shape[1])

            def move(step, carry):
                width = 3 * D // LANES
                goal = base + step * (CHUNK * width)
                side = lax.broadcasted_iota(jnp.int32, (CHUNK, LANES), 1)
                for pair in range(HEADS // 2):
                    right = behind_ref[:, pair * LANES : (pair + 1) * LANES]
                    lane = 2 * pair * D + row0 + step * CHUNK
                    first, second = (product(turned(lane + D * head), right) for head in range(2))
                    block = jnp.where(side < HDIM, first, second)
                    store(goal, width, 2 * D // LANES + pair, block)
                return carry

            lax.fori_loop(0, chunks, move, 0)

    shift = tab_ref[0]
    shape = (STEPS, LANES)
    place = lax.broadcasted_iota(jnp.int32, shape, 0) * LANES
    place = place + lax.broadcasted_iota(jnp.int32, shape, 1) - shift

    def clear(step, total):
        start = pl.multiple_of(step * STEPS, 8)
        entry = place + start * LANES
        lines = pl.ds(pl.multiple_of(FRONT + start, 8), STEPS)
        kept = jnp.where((entry >= 0) & (entry < plan.size), line_ref[lines, :], 0.0)
        line_ref[lines, :] = kept
        return total + kept * kept

    total = lax.fori_loop(
        0, plan.steps, clear, jnp.zeros(shape, F32), unroll=steps_at_once(plan.steps)
    )
    total = jnp.sum(total, keepdims=True) + rest_ref[0:1, 0:1]
    class_copy.wait()
    if len(refs) > 7:
        holds, twice = (tab_ref[1 + 4 * most + which] for which in range(2))
        rows = jnp.sum(refs[0][...] * refs[0][...], 1, keepdims=True)
        place = lax.broadcasted_iota(jnp.int32, (SET, 1), 0)
        pieces = jnp.sum(jnp.where((place < 8) & (twice != 0), 0.0, rows[:SET]), keepdims=True)
        classes = class_ref[...].astype(F32)
        by_head = jnp.where(head_mask(), classes[1:2], 0.0)
        by_head = jnp.sum(by_head * by_head, 1, keepdims=True)
        normed = jnp.sum(classes[0:1] * classes[0:1], 1, keepdims=True)
        outer = jnp.sum(rows[SET : SET + HEADROWS] * by_head, keepdims=True)
        outer = outer + rows[SET + HEADROWS : SET + HEADROWS + 1] * normed
        outer = outer + rows[SET + HEADROWS + 1 : SET + HEADROWS + 2]
        outer = outer + rows[SET + HEADROWS + 2 : SET + HEADROWS + 3]
        total = total + jnp.where(holds != 0, pieces + outer / plan.groups, 0.0)
    square_ref[...] = jnp.broadcast_to(total[None], square_ref.shape)


def early_gradient(plan, table, ahead, common, behind, *values):
    return pl.pallas_call(
        functools.partial(early_kernel, plan, (table.shape[0] - 3) // 4),
        out_shape=[
            jax.ShapeDtypeStruct((plan.grad_scratch, LANES), F32),
            jax.ShapeDtypeStruct((plan.count, 1, LANES), F32),
        ],
        in_specs=[
            pl.BlockSpec(memory_space=pltpu.SMEM),
            pl.BlockSpec(memory_space=pltpu.VMEM),
            pl.BlockSpec(memory_space=pl.ANY),
            pl.BlockSpec(memory_space=pl.ANY),
        ]
        + [pl.BlockSpec(memory_space=pltpu.VMEM)] * len(values),
        out_specs=[pl.BlockSpec(memory_space=pltpu.VMEM)] * 2,
        scratch_shapes=[
            pltpu.VMEM(common.shape, BF16),
            pltpu.VMEM((behind.shape[0], F), BF16),
            pltpu.VMEM((TILE, D), BF16),
            pltpu.SemaphoreType.DMA,
            pltpu.SemaphoreType.DMA,
        ],
        compiler_params=pltpu.CompilerParams(vmem_limit_bytes=60 * 1024 * 1024),
        cost_estimate=pl.CostEstimate(
            flops=10 * 10**9, bytes_accessed=10 * 10**6, transcendentals=0
        ),
    )(table, ahead, common, behind, *values)


def late_kernel(
    plan,
    most,
    tab_ref,
    lines_ref,
    wide_ref,
    left_ref,
    right_ref,
    ends_ref,
    out_ref,
    line_ref,
    sem,
):
    used = FRONT + plan.lines + 8
    copy = pltpu.make_async_copy(lines_ref.at[pl.ds(0, used)], line_ref.at[pl.ds(0, used)], sem)
    copy.start()
    copy.wait()

    def add(goal, width, tile, block):
        lines = pl.ds(goal + tile, CHUNK, stride=width)
        line_ref[lines, :] = line_ref[lines, :] + block

    for part in range(most):
        kind, base, chunks, row0 = (tab_ref[1 + 4 * part + i] for i in range(4))

        @pl.when(kind == 0)
        def _():
            def move(step, carry):
                width = D // LANES
                rows = pl.ds(pl.multiple_of(row0 + step * CHUNK, 8), CHUNK)
                for tile in range(width):
                    block = wide_ref[rows, tile * LANES : (tile + 1) * LANES]
                    add(base + step * (CHUNK * width), width, tile, block)
                return carry

            lax.fori_loop(0, chunks, move, 0)

        @pl.when(kind == 1)
        def _():
            def move(step, carry):
                width = 3 * D // LANES
                rows = pl.ds(pl.multiple_of(row0 + step * CHUNK, 8), CHUNK)
                block = jnp.dot(
                    left_ref[rows, :],
                    right_ref[...],
                    precision=PRECISE,
                    preferred_element_type=F32,
                )
                for tile in range(2 * D // LANES):
                    piece = block[:, tile * LANES : (tile + 1) * LANES]
                    add(base + step * (CHUNK * width), width, tile, piece)
                return carry

            lax.fori_loop(0, chunks, move, 0)

        @pl.when(kind == 5)
        def _():
            width = D // LANES
            for tile in range(width):
                lines = pl.ds(base + tile, 8, stride=width)
                block = ends_ref[:, tile * LANES : (tile + 1) * LANES]
                line_ref[lines, :] = line_ref[lines, :] + block

    shift = tab_ref[0]
    turn = lax.rem(LANES - shift, LANES)
    lane = lax.broadcasted_iota(jnp.int32, (STEPS + 8, LANES), 1)

    def align(step, carry):
        start = pl.multiple_of(step * STEPS, 8)
        lines = pl.ds(pl.multiple_of(FRONT + start, 8), STEPS + 8)
        here = pltpu.roll(line_ref[lines, :], turn, 1)
        below = pltpu.roll(here, STEPS + 7, 0)
        both = jnp.where(lane < LANES - shift, here, below)
        out_ref[pl.ds(start, STEPS), :] = both[:STEPS]
        return carry

    lax.fori_loop(0, plan.steps, align, 0, unroll=steps_at_once(plan.steps))


def late_gradient(plan, table, lines, *values):
    return pl.pallas_call(
        functools.partial(late_kernel, plan, (table.shape[0] - 3) // 4),
        out_shape=jax.ShapeDtypeStruct((plan.lines, LANES), F32),
        in_specs=[pl.BlockSpec(memory_space=pltpu.SMEM), pl.BlockSpec(memory_space=pl.ANY)]
        + [pl.BlockSpec(memory_space=pltpu.VMEM)] * len(values),
        out_specs=pl.BlockSpec(memory_space=pltpu.VMEM),
        scratch_shapes=[
            pltpu.VMEM((plan.grad_scratch, LANES), F32),
            pltpu.SemaphoreType.DMA,
        ],
        compiler_params=pltpu.CompilerParams(vmem_limit_bytes=24 * 1024 * 1024),
    )(table, lines, *values).reshape(-1)[: plan.size]


def adam_update(weight, grad, first, second, rate):
    first = BETA_FIRST * first + (1.0 - BETA_FIRST) * grad
    second = BETA_SECOND * second + (1.0 - BETA_SECOND) * grad * grad
    stepped = (
        first
        / (1.0 - BETA_FIRST**STEP)
        / (jnp.sqrt(second / (1.0 - BETA_SECOND**STEP)) + ADAM_EPSILON)
    )
    return (weight - rate * (stepped + WEIGHT_DECAY * weight), first, second)


def per_device(
    plan,
    params,
    first_moment,
    second_moment,
    teacher,
    protos,
    proto_first,
    proto_second,
    teacher_protos,
    center,
    patches,
    partner,
):
    reps, groups = lax.axis_size("rep"), lax.axis_size("grp")
    count, half = reps * groups, reps * groups // 2
    rep, grp = lax.axis_index("rep"), lax.axis_index("grp")
    device = rep * groups + grp
    low = rep % 2 == 0
    place = rep // 2 * groups + grp
    halves = [
        [r * groups + g for r in range(parity, reps, 2) for g in range(groups)] for parity in (0, 1)
    ]
    swap = [(r, r ^ 1) for r in range(reps)]
    own_views = patches.shape[0]
    views = 2 * own_views

    def trade(values):
        return lax.ppermute(values, "rep", swap)

    def trade_low(values):
        return jnp.where(low, values, trade(values))

    def in_order(values):
        other = trade(values)
        return jnp.where(low, values, other), jnp.where(low, other, values)

    pairs = [list(range(parity, reps, 2)) for parity in (0, 1)]
    lines = reps // 2
    tables = jnp.stack([protos, teacher_protos]).astype(BF16)
    around = [tables]
    for step in range(2, reps, 2):
        around.append(lax.ppermute(tables, "rep", [(r, (r + step) % reps) for r in range(reps)]))

    table = jnp.asarray(plan.lay_table)[device]
    given = trade(lay_out(plan, table, jnp.where(low, teacher, params)))
    kept = lay_out(plan, table, jnp.where(low, params, teacher))
    given, around = lax.optimization_barrier((given, around))
    shards = jnp.stack([jnp.where(low, kept, given), jnp.where(low, given, kept)])
    gathered = lax.all_gather(shards, BOTH, axis=0, axis_index_groups=halves)
    gathered = gathered.reshape(half, 2, -1, TILE, LANES)
    patches, partner, given = lax.optimization_barrier((patches, partner, given))
    pixels = jnp.concatenate(in_order(patches), 0)
    pixels = jnp.pad(pixels, ((0, 0), (0, TOKENS - NPATCH), (0, 0)))
    around = jnp.concatenate([jnp.stack(around[::-1])] * 2)
    around = lax.dynamic_slice_in_dim(around, lines - 1 - rep // 2, lines, 0)
    tables = jnp.stack(in_order(around))
    tables = tables.transpose(2, 1, 0, 3, 4).reshape(2, B, -1).astype(F32)
    places = in_order(partner.astype(F32))

    def columns_of(values):
        scale = lax.rsqrt(jnp.sum(values * values, 0, keepdims=True) + 1e-06)
        return (values * scale).astype(BF16), scale

    columns, column_scale = columns_of(tables[0])
    teacher_columns = columns_of(tables[1])[0]

    here = jnp.arange(views)
    source = jnp.concatenate([places[0], places[1] + own_views]).astype(jnp.int32)
    source = jnp.where(low, here, source)
    turn = (source[:, None] == here[None, :]).astype(BF16)

    turn, columns, teacher_columns = lax.optimization_barrier((turn, columns, teacher_columns))
    kept = forward(plan, gathered, pixels, turn)
    unit, scale, probs, mixed, looked, classes, qkv_w, second = kept[:8]
    received = lax.all_to_all(kept[-1], BOTH, 0, 0)
    received = received.reshape(reps // 2, 2, groups * views, -1)
    all_rows = received[..., :B]
    ahead = received[:, 0, :, B:].reshape(half * views, -1)

    def gather_rows(values):
        return lax.all_gather(values, BOTH, axis=0, axis_index_groups=halves).reshape(
            half * views, -1
        )

    common = [mixed[:, :HEADS].reshape(views, -1), second]
    common.append(jnp.pad(classes[1:3], ((0, views - 2), (0, 0))).astype(BF16))
    common = jnp.concatenate(common, 1)
    other = trade(common)
    all_rows, ahead, other = lax.optimization_barrier((all_rows, ahead, other))
    common = jnp.where(low, common, other)

    all_rows = all_rows.transpose(1, 0, 2, 3).reshape(2, -1, B)
    start = (rep // 2 * groups * views).astype(jnp.int32)[None]
    note, new_center = prototypes(
        start, all_rows, columns, teacher_columns, center[None], groups, views
    )
    common = gather_rows(common)
    new_center = new_center[0]
    note = lax.all_to_all(note, "grp", 0, 0)
    totals = jnp.sum(note[:, 3 * views :], 0)
    totals = totals.reshape(-1, 8, B).transpose(1, 0, 2).reshape(8, -1)[:, : half * views]
    loss_value = jnp.sum(jnp.log(totals[0]) - totals[2] / totals[1])
    depth = protos.shape[0]
    grad_protos, proto_squares = prototypes_back(
        (rep * depth).astype(jnp.int32)[None],
        depth,
        all_rows,
        columns,
        teacher_columns,
        center[None],
        totals,
        tables[0],
        column_scale,
    )
    behind, grad_middle, ends = rows_back(
        plan, low.astype(jnp.int32)[None], gathered, note, (classes,) + tuple(kept[8:13])
    )
    odd, far = grp % 2 == 1, grp // 2 % 2 == 1
    behind_rows = trade_low(behind)
    kept_rows, sent_rows = tokens_back(
        odd.astype(jnp.int32)[None],
        behind,
        grad_middle,
        ends,
        (unit, scale, probs, looked, classes, qkv_w),
        pixels.transpose(0, 2, 1),
        behind_rows,
        grad_protos,
    )

    def across(bit, values):
        return lax.ppermute(values, "grp", [(g, g ^ bit) for g in range(groups)])

    partial = kept_rows + across(1, sent_rows).astype(F32)
    first, second = partial[:SET], partial[SET : 2 * SET]
    shared = partial[2 * SET :]
    other = jnp.concatenate([jnp.where(far, first, second), shared], 0).astype(BF16)
    partial = jnp.concatenate([jnp.where(far, second, first), shared], 0)
    partial = partial + across(2, other).astype(F32)
    behind_rows, partial = lax.optimization_barrier((behind_rows, partial))
    behind_rows = gather_rows(behind_rows)
    if plan.near:
        step = 1
        while step < lines:
            hops = [(r, r - 2 * step) for r in range(reps) if r // 2 % (2 * step) == step]
            partial = partial + lax.ppermute(partial.astype(BF16), "rep", hops).astype(F32)
            step *= 2
    else:
        depth = partial.shape[0] // lines
        partial = lax.all_to_all(
            partial.astype(BF16).reshape(lines, depth, D), "rep", 0, 0, axis_index_groups=pairs
        )
        partial = jnp.sum(partial.astype(F32), 0)
    class_rows = common[:2, CLASS:].astype(F32)
    class_normed, query = class_rows[0:1], class_rows[1:2]
    by_head = jnp.where(head_mask()[:HEADS], query, 0.0)
    values = (proto_squares, partial)
    if not plan.near:
        twice = odd & ~far & (jnp.arange(SET) < 8)
        weights = jnp.concatenate(
            [
                jnp.where(twice, 0.0, 1.0),
                jnp.sum(by_head * by_head, 1) / groups,
                jnp.zeros((HEADROWS - HEADS,), F32),
                jnp.sum(class_normed * class_normed)[None] / groups,
                jnp.full((2,), 1.0 / groups, F32),
                jnp.zeros((SHARED - HEADROWS - 3,), F32),
            ]
        )
        weights = lax.dynamic_slice_in_dim(weights, rep // 2 * depth, depth)
        pieces = jnp.sum(weights * jnp.sum(partial * partial, 1))
        values = (proto_squares + jnp.where(low, pieces, 0.0),)
    early, squares = early_gradient(
        plan, jnp.asarray(plan.grad_table)[device], ahead, common, behind_rows, *values
    )
    summed = partial.astype(BF16)
    if not plan.near:
        summed = lax.all_to_all(
            jnp.broadcast_to(summed[None], (lines, depth, D)), "rep", 0, 0, axis_index_groups=pairs
        ).reshape(-1, D)
    shared, summed = summed[SET:], summed[:SET]
    other, squares = lax.optimization_barrier((across(2, summed), squares))
    squares = lax.all_to_all(squares, BOTH, 0, 0)
    grad_norm = jnp.sqrt(jnp.sum(squares[:, 0, 0]))
    factor = jnp.minimum(1.0, CLIP_NORM / (grad_norm + 1e-06))
    summed = jnp.concatenate([jnp.where(far, other, summed), jnp.where(far, summed, other)], 0)
    if plan.all_sets:
        other = across(1, summed)
        summed = jnp.concatenate([jnp.where(odd, other, summed), jnp.where(odd, summed, other)], 0)
    if plan.odd_owner:
        summed = trade_low(summed)
    wide_grad = jnp.pad(summed.astype(F32), ((0, CHUNK), (0, 0)))

    ends = shared[HEADROWS + 1 : HEADROWS + 3]
    shared = trade_low(shared).astype(F32)
    if plan.near:
        for owner in plan.final_reps:
            moved = lax.ppermute(ends, "rep", [(0, owner)]) if owner else ends
            ends = jnp.where(rep == owner, moved, ends)
        ends = ends.astype(F32)
    else:
        ends = shared[HEADROWS + 1 : HEADROWS + 3]
    ends = jnp.pad(ends, ((0, 6), (0, 0)))
    sum_query, reach = shared[HEADROWS : HEADROWS + 1], shared[:HEADS]
    left = jnp.concatenate([class_normed, reach, jnp.zeros((LANES - 1 - HEADS, D), F32)], 0)
    left = jnp.pad(left.T, ((0, CHUNK), (0, 0)))
    right = jnp.concatenate(
        [
            jnp.pad(sum_query, ((0, 0), (0, D))),
            jnp.pad(by_head, ((0, 0), (D, 0))),
            jnp.zeros((LANES - 1 - HEADS, 2 * D), F32),
        ],
        0,
    )
    grad_flat = late_gradient(
        plan, jnp.asarray(plan.late_table)[device], early, wide_grad, left, right, ends
    )
    new_params, new_first, new_second = adam_update(
        params, grad_flat * factor, first_moment, second_moment, LEARNING_RATE
    )
    new_protos, new_proto_first, new_proto_second = adam_update(
        protos, grad_protos * factor, proto_first, proto_second, PROTO_RATE
    )
    new_teacher = TEACHER_MOMENTUM * teacher + (1.0 - TEACHER_MOMENTUM) * new_params
    new_teacher_protos = TEACHER_MOMENTUM * teacher_protos + (1.0 - TEACHER_MOMENTUM) * new_protos
    return (
        new_params,
        new_first,
        new_second,
        new_teacher,
        new_protos,
        new_proto_first,
        new_proto_second,
        new_teacher_protos,
        new_center,
        loss_value,
        grad_norm,
    )


def solution(mesh):
    placed = (
        P(BOTH),
        P(BOTH),
        P(BOTH),
        P(BOTH),
        P("rep", "grp"),
        P("rep", "grp"),
        P("rep", "grp"),
        P("rep", "grp"),
        P("grp"),
        P(BOTH, None, None),
        P(BOTH),
    )
    plan = Plan(mesh.shape["rep"], mesh.shape["grp"])
    return jax.shard_map(
        functools.partial(per_device, plan),
        mesh=mesh,
        in_specs=placed,
        out_specs=placed[:9] + (P(), P()),
        check_vma=False,
    )
```

```python
import functools

import jax
import jax.numpy as jnp
import numpy as np
from jax import lax
from jax.experimental import pallas as pl
from jax.experimental.pallas import tpu as pltpu
from jax.sharding import PartitionSpec as P

D = 768
HEADS = 12
HDIM = 64
F = 3072
PD = 768
NTOK = 197
H = 2048
B = 256
STEP = 10
NPATCH = NTOK - 1

PRECISE = lax.Precision.HIGHEST
STUDENT_TEMP = 0.1
TEACHER_TEMP = 0.04
CENTER_MOMENTUM = 0.9
TEACHER_MOMENTUM = 0.8
CLIP_NORM = 0.05
LEARNING_RATE = 0.03
PROTO_RATE = 0.6
BETA_FIRST = 0.9
BETA_SECOND = 0.999
ADAM_EPSILON = 1e-08
WEIGHT_DECAY = 0.04
BOTH = ("rep", "grp")
LANES = 128
F32 = jnp.float32
BF16 = jnp.bfloat16

SEGMENTS = []
_offset = 0
for _rows, _cols in ((PD + NTOK + 4, D), (D, 3 * D), (D, D), (D, F), (F + 2, D), (D + H, H), (H, B)):
    SEGMENTS.append((_offset, _rows, _cols))
    _offset += _rows * _cols
PFLAT = _offset
WIDTHS = sorted({cols // LANES for _, _, cols in SEGMENTS})

PIECES = []
_offset = 0
for _rows, _cols in (
    (PD + NTOK + 4, D),
    (D, 3 * D),
    (D, D),
    (D, F),
    (F, D),
    (2, D),
    (D, H),
    (H, H),
    (H, B),
):
    PIECES.append((_offset, _rows, _cols))
    _offset += _rows * _cols
FRONT = 192
CHUNK = 128
SET = 288
SHARED = 32
STEPS = 64
AHEAD = 3 * D + F + H
TILE = 16
TOKENS = 208
HEADROWS = 16
VMEM_LIMIT = 62 * 1024 * 1024


SPANS = {
    2: (0, 0),
    3: (D, D),
    4: (2 * D, D + F),
    6: (2 * D + F, 2 * D + F + B + H),
    7: (3 * D + F, 2 * D + F + B),
}
ATT_COLUMN = 2 * D + F + B + 2 * H
SECOND = HEADS * D
CLASS = SECOND + H
ROWS = CLASS + D


def round_up(value, step):
    return -(-value // step) * step


def steps_at_once(count):
    return max(size for size in range(1, 8) if count % size == 0)


def shard_parts(start, stop, table):
    parts = []
    line0 = start // LANES
    for index, (offset, rows, cols) in enumerate(table):
        low, high = max(start, offset), min(stop, offset + rows * cols)
        if low >= high:
            continue
        row0 = (low - offset) // cols
        row1 = -(-(high - offset) // cols)
        parts.append((index, row0, row1 - row0, (offset + row0 * cols) // LANES - line0))
    return parts


FINAL_ROW = round_up(PD + NTOK + 4, 8)


class Plan:
    def __init__(self, reps, groups):
        count = reps * groups
        self.count, self.groups = count, groups
        self.size = PFLAT // count
        self.lines = round_up(-(-self.size // LANES) + 1, STEPS)
        self.steps = self.lines // STEPS
        self.scratch = FRONT + self.lines + 8 * max(WIDTHS) + 16
        table = []
        self.blocks = [[] for _ in SEGMENTS]
        longest = 0
        for device in range(count):
            start = device * self.size
            entry = [start % LANES]
            target = 0
            for index, row0, rows, line in shard_parts(start, start + self.size, SEGMENTS):
                width = SEGMENTS[index][2] // LANES
                skew = row0 % 8
                tiles = -(-(rows + skew) // 8)
                self.blocks[index].append((device, target // TILE, row0 // 8, tiles))
                entry += [
                    WIDTHS.index(width),
                    FRONT + line - skew * width,
                    tiles // 2,
                    tiles % 2,
                    target // TILE,
                ]
                target += tiles * 8 * width
            longest = max(longest, target)
            entry += [-1, 0, 0, 0, 0] * (2 - len(entry) // 5)
            table.append(entry)
        self.buffer = round_up(longest, 16)
        self.lay_table = np.array(table, np.int32)
        edge = SEGMENTS[0][1] * SEGMENTS[0][2]
        owners = [device for device in range(count) if device * self.size < edge]
        self.odd_owner = any(self.place(device)[1] for device in owners)
        self.all_sets = len(owners) > 2
        edge = sum(rows * cols for _, rows, cols in SEGMENTS[:2])
        self.near = all(
            device < 2 * groups for device in range(count) if device * self.size < edge
        )
        offset, rows, cols = PIECES[5]
        self.final_reps = sorted(
            {
                device // groups
                for device in range(count)
                if device * self.size < offset + rows * cols and (device + 1) * self.size > offset
            }
        )
        self.grad_table = self.tabulate(lambda index: index, lambda device, index, row0, chunks: row0)
        self.most_chunks = {
            index: max(
                [1]
                + [
                    entry[3 + place]
                    for entry in self.grad_table
                    for place in range(0, len(entry) - 3, 4)
                    if entry[1 + place] == index
                ]
            )
            for index in SPANS
        }
        self.late_table = self.tabulate(lambda index: index in (0, 1, 5), self.wide_row)
        self.grad_scratch = FRONT + self.lines + CHUNK * max(WIDTHS) + 16


    def largest(self):
        longest = max(8 * block[3] for blocks in self.blocks for block in blocks)
        return max(len(blocks) for blocks in self.blocks), round_up(longest, LANES) + 2 * LANES

    def place(self, device):
        rep, grp = divmod(device, self.groups)
        return rep // 2 * self.groups + grp, rep % 2

    def tabulate(self, chosen, rows_of):
        table = []
        for device in range(self.count):
            start = device * self.size
            entry = []
            for index, row0, rows, line in shard_parts(start, start + self.size, PIECES):
                if not chosen(index):
                    continue
                skew = row0 % 8
                line -= skew * (PIECES[index][2] // LANES)
                chunks = -(-(rows + skew) // CHUNK)
                entry += [index, FRONT + line, chunks, rows_of(device, index, row0 - skew, chunks)]
            table.append(entry)
        most = max(len(entry) for entry in table) // 4
        for device, entry in enumerate(table):
            entry += [-1, 0, 0, 0] * (most - len(entry) // 4)
            entry.insert(0, device * self.size % LANES)
            entry += [device < self.groups, device % 4 == 1]
        return np.array(table, np.int32)

    def wide_row(self, device, index, row0, chunks):
        if index:
            return row0
        late = row0 >= 2 * SET - 8
        if not self.all_sets:
            if late != device % 2:
                raise ValueError("owner")
            return row0 - (2 * SET - 8) * late
        return row0 + 8 * late


def lay_kernel(plan, tab_ref, x_ref, out_ref, line_ref):
    shift = tab_ref[0]
    lane = lax.broadcasted_iota(jnp.int32, (STEPS + 8, LANES), 1)
    line_ref[pl.ds(0, FRONT), :] = jnp.zeros((FRONT, LANES), F32)
    tail = plan.scratch - FRONT - plan.lines
    line_ref[pl.ds(FRONT + plan.lines, tail), :] = jnp.zeros((tail, LANES), F32)

    def align(step, carry):
        base = pl.multiple_of(step * STEPS, 8)
        here = pltpu.roll(x_ref[pl.ds(base, STEPS + 8), :], shift, 1)
        above = pltpu.roll(here, 1, 0)
        both = jnp.where(lane >= shift, here, above)
        line_ref[pl.ds(pl.multiple_of(FRONT + base, 8), STEPS), :] = both[8:]
        return carry

    lax.fori_loop(0, plan.steps, align, 0, unroll=steps_at_once(plan.steps))
    for part in range(2):
        kind, base, pairs, odd, target = (tab_ref[1 + 5 * part + i] for i in range(5))
        for index, width in enumerate(WIDTHS):

            @pl.when(kind == index)
            def _(width=width):
                def move(step, carry):
                    row = base + step * (TILE * width)
                    goal = (target + step * width) * TILE
                    for tile in range(width):
                        both = line_ref[pl.ds(row + tile, TILE, stride=width), :]
                        place = pl.multiple_of(goal + TILE * tile, TILE)
                        out_ref[pl.ds(place, TILE), :] = both.astype(BF16)
                    return carry

                def last(step, carry):
                    row = base + pairs * (TILE * width)
                    goal = (target + pairs * width) * TILE
                    for tile in range(0, width, 2):
                        both = [
                            line_ref[pl.ds(row + tile + side, 8, stride=width), :]
                            for side in range(2)
                        ]
                        place = pl.multiple_of(goal + 8 * tile, TILE)
                        out_ref[pl.ds(place, TILE), :] = jnp.concatenate(both, 0).astype(BF16)
                    return carry

                lax.fori_loop(0, pairs, move, 0)
                lax.fori_loop(0, odd, last, 0)


def lay_out(plan, table, flat):
    padded = jnp.pad(flat, (8 * LANES, plan.lines * LANES - plan.size))
    lines = padded.reshape(8 + plan.lines, LANES)
    return pl.pallas_call(
        functools.partial(lay_kernel, plan),
        out_shape=jax.ShapeDtypeStruct((plan.buffer, LANES), BF16),
        in_specs=[
            pl.BlockSpec(memory_space=pltpu.SMEM),
            pl.BlockSpec(memory_space=pltpu.VMEM),
        ],
        out_specs=pl.BlockSpec(memory_space=pltpu.VMEM),
        scratch_shapes=[pltpu.VMEM((plan.scratch, LANES), F32)],
        compiler_params=pltpu.CompilerParams(vmem_limit_bytes=24 * 1024 * 1024),
    )(table, lines)


class Shards:
    def __init__(self, plan, gathered_ref, ref, sems, order):
        self.plan, self.ref, self.sems, self.waited = plan, ref, sems, set()
        self.copies = {}
        for device in order:
            place, side = plan.place(device)
            copy = pltpu.make_async_copy(
                gathered_ref.at[place, side], ref.at[device], sems.at[device]
            )
            copy.start()
            self.copies[device] = copy

    def wait(self, device):
        if device in self.copies:
            self.copies.pop(device).wait()

    def finish(self):
        for device in list(self.copies):
            self.wait(device)

    def blocks(self, index, first, count):
        found = [
            block
            for block in self.plan.blocks[index]
            if 8 * block[2] < first + count and 8 * (block[2] + block[3]) > first
        ]
        for block in found:
            self.wait(block[0])
        return found

    def eight(self, index, tile, pair, side):
        width = SEGMENTS[index][2] // LANES
        total = None
        for device, target, tile0, tiles in self.plan.blocks[index]:
            own = tile - tile0
            if not 0 <= own < tiles:
                continue
            if own < tiles // 2 * 2:
                both = self.ref[device, target + own // 2 * width + 2 * pair + side]
                half = own % 2
            else:
                both = self.ref[device, target + tiles // 2 * width + pair]
                half = side
            piece = both.astype(F32)[8 * half : 8 * half + 8]
            total = piece if total is None else total + piece
        return total

    def assemble(self, index, out_ref):
        width = SEGMENTS[index][2] // LANES
        rows = out_ref.shape[0]
        self.blocks(index, 0, rows)

        def column(pair, carry):
            for side in range(2):
                lanes = pl.ds(pl.multiple_of(pair * 2 * LANES + side * LANES, LANES), LANES)
                for group in range(rows // TILE):
                    both = [
                        self.eight(index, 2 * group + half, pair, side) for half in range(2)
                    ]
                    out_ref[TILE * group : TILE * (group + 1), lanes] = jnp.concatenate(
                        both, 0
                    ).astype(BF16)
            return carry

        lax.fori_loop(0, width // 2, column, 0)

    def columns(self, index, block, pair):
        width = SEGMENTS[index][2] // LANES
        device, target, _, tiles = block
        sides = []
        for side in range(2):
            pieces = [
                self.ref[device, target + step * width + 2 * pair + side]
                for step in range(tiles // 2)
            ]
            if tiles % 2:
                both = self.ref[device, target + tiles // 2 * width + pair].astype(F32)
                pieces.append(both[8 * side : 8 * side + 8].astype(BF16))
            sides.append(jnp.concatenate(pieces, 0))
        return jnp.concatenate(sides, 1)

    def times(self, index, first, values, left_ref, out_ref):
        views, count = values.shape
        blocks = self.blocks(index, first, count)
        top = max([first + count] + [8 * (tile0 + tiles) for _, _, tile0, tiles in blocks])
        top = round_up(top, LANES) + LANES
        parts = [values, jnp.zeros((views, top - first - count), F32)]
        if first:
            parts.insert(0, jnp.zeros((views, first), F32))
        wide = jnp.concatenate(parts, 1)
        for number, (_, _, tile0, tiles) in enumerate(blocks):
            start = 8 * tile0 // LANES * LANES
            turn = 8 * tile0 - start
            piece = wide[:, start : start + round_up(turn + 8 * tiles, LANES)]
            if turn:
                piece = pltpu.roll(piece, piece.shape[1] - turn, 1)
            left_ref[number, :, : 8 * tiles] = piece[:, : 8 * tiles]

        def column(pair, carry):
            total = jnp.zeros((views, 2 * LANES), F32)
            for number, block in enumerate(blocks):
                left = left_ref[number, :, : 8 * block[3]].astype(BF16)
                total += product(left, self.columns(index, block, pair))
            out_ref[:, pl.ds(pl.multiple_of(pair * 2 * LANES, LANES), 2 * LANES)] = total
            return carry

        lax.fori_loop(0, SEGMENTS[index][2] // LANES // 2, column, 0, unroll=2)


    def back(self, index, first, count, values, grad_ref, left_ref, wide_ref):
        views, cols = values.shape
        grad_ref[:, :cols] = values
        blocks = self.blocks(index, first, count)
        top = max([first + count] + [8 * (tile0 + tiles) for _, _, tile0, tiles in blocks])
        wide_ref[:, : round_up(top, LANES) + LANES] = jnp.zeros(
            (views, round_up(top, LANES) + LANES), F32
        )
        for number, (_, _, _, tiles) in enumerate(blocks):
            size = round_up(8 * tiles, LANES) + LANES
            left_ref[number, :, :size] = jnp.zeros((views, size), F32)

        def column(pair, carry):
            lanes = pl.ds(pl.multiple_of(pair * 2 * LANES, LANES), 2 * LANES)
            left = grad_ref[:, lanes].astype(BF16)
            for number, block in enumerate(blocks):
                size = 8 * block[3]
                left_ref[number, :, :size] += product_t(left, self.columns(index, block, pair))
            return carry

        lax.fori_loop(0, cols // LANES // 2, column, 0, unroll=2)
        for number, (_, _, tile0, tiles) in enumerate(blocks):
            start = 8 * tile0 // LANES * LANES
            turn = 8 * tile0 - start
            size = round_up(turn + 8 * tiles, LANES)
            piece = left_ref[number, :, :size]
            if turn:
                piece = pltpu.roll(piece, turn, 1)
            wide_ref[:, start : start + size] += piece
        return wide_ref[:, first : first + count]


def product(left, right):
    return jnp.dot(left, right, preferred_element_type=F32)


def product_t(left, right):
    return lax.dot_general(
        left, right, (((left.ndim - 1,), (1,)), ((), ())), preferred_element_type=F32
    )


def normal_share(values):
    return 0.5 + 0.5 * lax.erf(values * 2**-0.5)


def activate(values):
    return values * normal_share(values)


def gelu_back(values, grad):
    density = jnp.exp(-0.5 * values * values) * (2 * np.pi) ** -0.5
    return grad * (normal_share(values) + values * density)


def normalised(values):
    centred = values - jnp.mean(values, -1, keepdims=True)
    scale = lax.rsqrt(jnp.mean(centred * centred, -1, keepdims=True) + 1e-06)
    return centred * scale, scale


def norm_back(grad, gain, unit, scale):
    inner = grad * gain
    return scale * (
        inner
        - jnp.mean(inner, -1, keepdims=True)
        - unit * jnp.mean(inner * unit, -1, keepdims=True)
    )


def head_mask():
    shape = (HEADROWS, D)
    return lax.broadcasted_iota(jnp.int32, shape, 0) == (
        lax.broadcasted_iota(jnp.int32, shape, 1) // HDIM
    )


def token_norms(unit, norms, class_normed):
    token = lax.broadcasted_iota(jnp.int32, (TOKENS, D), 0)
    normed = unit * norms[0:1] + norms[1:2]
    return jnp.where(
        token < NPATCH, normed, jnp.where(token == NPATCH, class_normed, 0.0)
    ).astype(BF16)


def forward_kernel(
    plan,
    gathered_ref,
    pixels_ref,
    turn_ref,
    unit_out,
    scale_out,
    probs_ref,
    mixed_ref,
    looked_ref,
    class_ref,
    qkv_out,
    hidden_ref,
    one_ref,
    two_ref,
    bottle_ref,
    middle_ref,
    rows_ref,
    pack_out,
    shards_ref,
    wide_ref,
    place_ref,
    left_ref,
    sums_ref,
    pack_ref,
    unit_ref,
    scale_ref,
    qkv_ref,
    out_sems,
    sems,
):
    shards = Shards(plan, gathered_ref, shards_ref, sems, range(plan.count))
    views = pixels_ref.shape[0]
    temper = HDIM ** (-0.5)
    shards.assemble(0, wide_ref)
    position = wide_ref[PD : PD + TOKENS].astype(F32)
    place_ref[...] = pltpu.roll(position, TOKENS - 1, 0)
    class_place = position[0:1]
    norms = position[NTOK : NTOK + 4]
    class_unit, class_scale = normalised(class_place)
    class_normed = (class_unit * norms[0:1] + norms[1:2]).astype(BF16).astype(F32)
    shards.assemble(1, qkv_ref)
    qkv_copy = pltpu.make_async_copy(qkv_ref, qkv_out, out_sems.at[4])
    qkv_copy.start()
    mask = head_mask()
    query = jnp.broadcast_to(class_normed, (HEADROWS, D)).astype(BF16)
    query = product(query, qkv_ref[:, :D]).astype(BF16).astype(F32)
    by_head = jnp.where(mask, query, 0.0).astype(BF16)
    looked = product_t(by_head, qkv_ref[:, D : 2 * D]).astype(BF16)
    looked_ref[...] = looked

    def copies(v):
        slot = lax.rem(v, 2)
        return (
            pltpu.make_async_copy(unit_ref.at[slot], unit_out.at[v], out_sems.at[slot]),
            pltpu.make_async_copy(scale_ref.at[slot], scale_out.at[v], out_sems.at[2 + slot]),
        )

    def view(v, carry):
        embedded = product(pixels_ref[v], wide_ref[:PD]) + place_ref[...]
        unit, scale = normalised(embedded)

        @pl.when(v >= 2)
        def _():
            for copy in copies(v - 2):
                copy.wait()

        unit_ref[lax.rem(v, 2)] = unit
        scale_ref[lax.rem(v, 2)] = jnp.broadcast_to(scale, (TOKENS, LANES))
        for copy in copies(v):
            copy.start()
        normed = token_norms(unit, norms, class_normed)
        scores = product_t(looked, normed) * temper
        token = lax.broadcasted_iota(jnp.int32, scores.shape, 1)
        scores = jnp.where(token < NTOK, scores, -1e30)
        top = jnp.max(scores, -1, keepdims=True)
        top = top + jnp.log(jnp.sum(jnp.exp(scores - top), -1, keepdims=True))
        head = lax.broadcasted_iota(jnp.int32, scores.shape, 0)
        probs = jnp.where(head < HEADS, jnp.exp(scores - top), 0.0)
        probs_ref[v] = probs
        mixed_ref[v] = product(probs.astype(BF16), normed).astype(BF16)
        return carry

    lax.fori_loop(0, views, view, 0, unroll=2)
    mixed = mixed_ref[...].reshape(views * HEADROWS, D)
    valued = product(mixed, qkv_ref[:, 2 * D :]).reshape(views, HEADROWS, D)
    attended = jnp.sum(jnp.where(mask[None], valued, 0.0), 1).astype(BF16)
    pack_ref[:, :D] = attended.astype(F32)
    shards.times(2, 0, pack_ref[:, :D], left_ref, sums_ref)
    middle = class_place + sums_ref[...]
    unit, scale = normalised(middle)
    middle_ref[0], middle_ref[1] = unit, jnp.broadcast_to(scale, (views, D))
    normed = (unit * norms[2:3] + norms[3:4]).astype(BF16)
    pack_ref[:, D : 2 * D] = normed.astype(F32)
    shards.times(3, 0, pack_ref[:, D : 2 * D], left_ref, hidden_ref)
    act = activate(hidden_ref[...]).astype(BF16)
    pack_ref[:, 2 * D : 2 * D + F] = act.astype(F32)
    shards.times(4, 0, act.astype(F32), left_ref, sums_ref)
    unit, scale = normalised(middle + sums_ref[...])
    middle_ref[2], middle_ref[3] = unit, jnp.broadcast_to(scale, (views, D))
    final = jnp.concatenate(
        [shards.eight(4, F // 8, tile // 2, tile % 2) for tile in range(D // LANES)], 1
    )
    cls = (unit * final[0:1] + final[1:2]).astype(BF16)
    place = 2 * D + F
    pack_ref[:, place : place + D] = cls.astype(F32)
    shards.times(5, 0, cls.astype(F32), left_ref, one_ref)
    first = activate(one_ref[...]).astype(BF16)
    pack_ref[:, place + D : AHEAD] = first.astype(F32)
    shards.times(5, D, first.astype(F32), left_ref, two_ref)
    second = activate(two_ref[...]).astype(BF16)
    shards.times(6, 0, second.astype(F32), left_ref, bottle_ref)
    bottle = bottle_ref[...]
    scale = lax.rsqrt(jnp.sum(bottle * bottle, -1, keepdims=True) + 1e-06)
    rows = product(turn_ref[...], (bottle * scale).astype(BF16)).astype(BF16)
    rows_ref[...] = jnp.broadcast_to(rows[None], rows_ref.shape)
    mixed = mixed_ref[...].astype(F32)
    for head in range(HEADS):
        pack_out[:, head * D : (head + 1) * D] = mixed[:, head, :].astype(BF16)
    pack_out[:, SECOND:CLASS] = second
    row = lax.broadcasted_iota(jnp.int32, (views, D), 0)
    pack_out[:, CLASS:ROWS] = jnp.where(
        row == 0, class_normed, jnp.where(row == 1, query[0:1], 0.0)
    ).astype(BF16)
    pack_out[:, ROWS : ROWS + AHEAD] = pack_ref[...].astype(BF16)
    pack_out[:, ROWS + AHEAD :] = jnp.zeros((views, pack_out.shape[1] - ROWS - AHEAD), BF16)
    class_ref[...] = jnp.concatenate(
        [
            class_unit,
            class_normed,
            query[0:1],
            jnp.broadcast_to(class_scale, (1, D)),
            norms,
            final,
        ],
        0,
    )
    for v in range(max(0, views - 2), views):
        for copy in copies(v):
            copy.wait()
    qkv_copy.wait()
    shards.finish()


def forward(plan, gathered, pixels, turn):
    views = pixels.shape[0]
    shapes = [
        ((views, TOKENS, D), F32),
        ((views, TOKENS, LANES), F32),
        ((views, HEADROWS, TOKENS), F32),
        ((views, HEADROWS, D), BF16),
        ((HEADROWS, D), BF16),
        ((16, D), F32),
        ((D, 3 * D), BF16),
        ((views, F), F32),
        ((views, H), F32),
        ((views, H), F32),
        ((views, B), F32),
        ((4, views, D), F32),
        ((plan.count, views, B), BF16),
        ((views, ROWS + AHEAD + (max(plan.most_chunks.values()) + 1) * CHUNK), BF16),
    ]
    most, longest = plan.largest()
    return pl.pallas_call(
        functools.partial(forward_kernel, plan),
        out_shape=[jax.ShapeDtypeStruct(shape, dtype) for shape, dtype in shapes],
        in_specs=[pl.BlockSpec(memory_space=pl.ANY)]
        + [pl.BlockSpec(memory_space=pltpu.VMEM)] * 2,
        out_specs=[
            pl.BlockSpec(memory_space=pl.ANY if index in (0, 1, 6) else pltpu.VMEM)
            for index in range(len(shapes))
        ],
        scratch_shapes=[
            pltpu.VMEM((plan.count, plan.buffer // TILE, TILE, LANES), BF16),
            pltpu.VMEM((round_up(PD + NTOK + 4, TILE), D), BF16),
            pltpu.VMEM((TOKENS, D), F32),
            pltpu.VMEM((most, views, longest), F32),
            pltpu.VMEM((views, D), F32),
            pltpu.VMEM((views, AHEAD), F32),
            pltpu.VMEM((2, TOKENS, D), F32),
            pltpu.VMEM((2, TOKENS, LANES), F32),
            pltpu.VMEM((D, 3 * D), BF16),
            pltpu.SemaphoreType.DMA((5,)),
            pltpu.SemaphoreType.DMA((plan.count,)),
        ],
        compiler_params=pltpu.CompilerParams(vmem_limit_bytes=VMEM_LIMIT),
        cost_estimate=pl.CostEstimate(
            flops=60 * 10**9, bytes_accessed=40 * 10**6, transcendentals=10**5
        ),
    )(gathered, pixels, turn)


def proto_kernel(
    start_ref,
    rows_ref,
    columns_ref,
    others_ref,
    center_ref,
    note_ref,
    center_out_ref,
    student_ref,
    teacher_ref,
    sums_ref,
):
    count, groups = rows_ref.shape[1], note_ref.shape[0]
    views = (note_ref.shape[1] - 8 * -(-count // B)) // 3
    logits = product(rows_ref[1], others_ref[...])
    center = center_ref[...]
    center_out_ref[...] = CENTER_MOMENTUM * center + (1.0 - CENTER_MOMENTUM) * jnp.mean(
        logits, 0, keepdims=True
    )
    exp_teacher = jnp.exp((logits - center) / TEACHER_TEMP)
    teacher_ref[...] = exp_teacher
    scaled = product(rows_ref[0], columns_ref[...]) / STUDENT_TEMP
    exp_student = jnp.exp(scaled)
    student_ref[...] = exp_student
    turned = []
    for which, values in enumerate((exp_student, exp_teacher, exp_teacher * scaled)):
        total = jnp.broadcast_to(jnp.sum(values, 1, keepdims=True), (count, LANES))
        turned.append(total.T[0:1])
        if which < 2:
            sums_ref[:, which * LANES : (which + 1) * LANES] = total
    turned = jnp.concatenate(turned + [jnp.zeros((5, count), F32)], 0)
    for step in range(-(-count // B)):
        part = turned[:, step * B : (step + 1) * B]
        lines = slice(3 * views + 8 * step, 3 * views + 8 * (step + 1))
        note_ref[:, lines, : part.shape[1]] = jnp.broadcast_to(part[None], (groups,) + part.shape)
        if part.shape[1] < B:
            note_ref[:, lines, part.shape[1] :] = jnp.zeros((groups, 8, B - part.shape[1]), F32)
    start = pl.multiple_of(start_ref[0], 8)
    columns = columns_ref[...].astype(F32)
    for which, source in enumerate((student_ref, teacher_ref)):
        pulls = lax.dot_general(
            source[pl.ds(start, groups * views), :],
            columns,
            (((1,), (1,)), ((), ())),
            precision=PRECISE,
            preferred_element_type=F32,
        )
        note_ref[:, which * views : (which + 1) * views, :] = pulls.reshape(groups, views, B)
    own = sums_ref[pl.ds(start, groups * views), :]
    note_ref[:, 2 * views : 3 * views, :] = own.reshape(groups, views, B)


def prototypes(start, rows, columns, others, center, groups, views):
    count, width = rows.shape[1], columns.shape[1]
    shapes = [(groups, 3 * views + 8 * -(-count // B), B), (1, width)]
    return pl.pallas_call(
        proto_kernel,
        out_shape=[jax.ShapeDtypeStruct(shape, F32) for shape in shapes],
        in_specs=[pl.BlockSpec(memory_space=pltpu.SMEM)]
        + [pl.BlockSpec(memory_space=pltpu.VMEM)] * 4,
        out_specs=[pl.BlockSpec(memory_space=pltpu.VMEM)] * len(shapes),
        scratch_shapes=[pltpu.VMEM((count, width), F32)] * 2
        + [pltpu.VMEM((count, 2 * LANES), F32)],
        compiler_params=pltpu.CompilerParams(vmem_limit_bytes=32 * 1024 * 1024),
        cost_estimate=pl.CostEstimate(
            flops=3 * 10**9, bytes_accessed=6 * 10**6, transcendentals=10**6
        ),
    )(start, rows, columns, others, center)


def proto_back_kernel(
    start_ref,
    rows_ref,
    columns_ref,
    others_ref,
    center_ref,
    totals_ref,
    table_ref,
    scale_ref,
    grad_ref,
    square_ref,
    work_ref,
):
    count = rows_ref.shape[1]
    totals = jnp.broadcast_to(totals_ref[0:2][:, None, :], (2, 8, count))
    student, teacher = (totals[which].T[:, :1] for which in range(2))
    logits = product(rows_ref[1], others_ref[...])
    targets = jnp.exp((logits - center_ref[...]) / TEACHER_TEMP) / teacher
    scaled = product(rows_ref[0], columns_ref[...]) / STUDENT_TEMP
    grad = (jnp.exp(scaled) / student - targets) / STUDENT_TEMP
    work_ref[...] = jnp.dot(
        rows_ref[0].astype(F32).T, grad, precision=PRECISE, preferred_element_type=F32
    )
    scale = scale_ref[...]
    inner = jnp.sum(work_ref[...] * table_ref[...], 0, keepdims=True)
    start = pl.multiple_of(start_ref[0], 8)
    lines = pl.ds(start, grad_ref.shape[0])
    grad = work_ref[lines, :] * scale - table_ref[lines, :] * (scale * scale * scale * inner)
    grad_ref[...] = grad
    square_ref[...] = jnp.broadcast_to(jnp.sum(grad * grad, keepdims=True), square_ref.shape)


def prototypes_back(start, depth, *values):
    count, width = values[0].shape[1], values[1].shape[1]
    shapes = [(depth, width), (8, LANES)]
    return pl.pallas_call(
        proto_back_kernel,
        out_shape=[jax.ShapeDtypeStruct(shape, F32) for shape in shapes],
        in_specs=[pl.BlockSpec(memory_space=pltpu.SMEM)]
        + [pl.BlockSpec(memory_space=pltpu.VMEM)] * len(values),
        out_specs=[pl.BlockSpec(memory_space=pltpu.VMEM)] * len(shapes),
        scratch_shapes=[pltpu.VMEM((B, width), F32)],
        compiler_params=pltpu.CompilerParams(vmem_limit_bytes=32 * 1024 * 1024),
        cost_estimate=pl.CostEstimate(
            flops=3 * 10**9, bytes_accessed=6 * 10**6, transcendentals=10**6
        ),
    )(start, *values)


def rows_back_kernel(
    plan,
    low_ref,
    gathered_ref,
    note_ref,
    class_ref,
    hidden_ref,
    one_ref,
    two_ref,
    bottle_ref,
    middle_ref,
    pack_ref,
    stream_ref,
    extra_ref,
    shards_ref,
    left_ref,
    values_ref,
    wide_ref,
    sems,
):
    used = {block[0] for blocks in plan.blocks[2:] for block in blocks}
    shards = Shards(plan, gathered_ref, shards_ref, sems, sorted(used, reverse=True))
    work = (values_ref, left_ref, wide_ref)
    norms, final = class_ref[4:8], class_ref[8:10]

    views = bottle_ref.shape[0]
    note = jnp.sum(note_ref[...], 0)
    sums = note[2 * views : 3 * views]
    student, teacher = sums[:, :1], sums[:, LANES : LANES + 1]
    grad_rows = (note[:views] / student - note[views : 2 * views] / teacher) / STUDENT_TEMP
    grad_rows = jnp.where(low_ref[0] == 0, 0.0, grad_rows).astype(BF16).astype(F32)
    bottle = bottle_ref[...]
    scale = lax.rsqrt(jnp.sum(bottle * bottle, -1, keepdims=True) + 1e-06)
    grad_bottle = (
        grad_rows * scale - bottle * scale**3 * jnp.sum(grad_rows * bottle, -1, keepdims=True)
    ).astype(BF16)
    place = 2 * D + F
    pack_ref[:, place : place + B] = grad_bottle
    grad_two = shards.back(6, 0, H, grad_bottle.astype(F32), *work)
    grad_two = gelu_back(two_ref[...], grad_two).astype(BF16)
    pack_ref[:, place + B : place + B + H] = grad_two
    grad_one = shards.back(5, D, H, grad_two.astype(F32), *work)
    grad_one = gelu_back(one_ref[...], grad_one).astype(BF16)
    pack_ref[:, place + B + H : place + B + 2 * H] = grad_one
    grad_cls = shards.back(5, 0, D, grad_one.astype(F32), *work)
    unit, scale = middle_ref[2], middle_ref[3]
    gain_last = jnp.sum(grad_cls * unit, 0, keepdims=True)
    shift_last = jnp.sum(grad_cls, 0, keepdims=True)
    grad_stream = norm_back(grad_cls, final[0:1], unit, scale)
    grad_branch = grad_stream.astype(BF16)
    pack_ref[:, D + F : 2 * D + F] = grad_branch
    grad_hidden = shards.back(4, 0, F, grad_branch.astype(F32), *work)
    grad_hidden = gelu_back(hidden_ref[...], grad_hidden).astype(BF16)
    pack_ref[:, D : D + F] = grad_hidden
    grad_normed = shards.back(3, 0, D, grad_hidden.astype(F32), *work)
    unit, scale = middle_ref[0], middle_ref[1]
    extra_ref[...] = jnp.concatenate(
        [
            jnp.sum(grad_normed * unit, 0, keepdims=True),
            jnp.sum(grad_normed, 0, keepdims=True),
            gain_last,
            shift_last,
            jnp.zeros((4, D), F32),
        ],
        0,
    )
    grad_middle = grad_stream + norm_back(grad_normed, norms[2:3], unit, scale)
    stream_ref[...] = grad_middle
    grad_mixed = grad_middle.astype(BF16)
    pack_ref[:, :D] = grad_mixed
    grad_att = shards.back(2, 0, D, grad_mixed.astype(F32), *work).astype(BF16)
    pack_ref[:, place + B + 2 * H : place + B + 2 * H + D] = grad_att
    shards.finish()


def rows_back(plan, low, gathered, note, kept):
    views = kept[-1].shape[1]
    shapes = [((views, 3 * D + F + B + 2 * H), BF16), ((views, D), F32), ((8, D), F32)]
    most, longest = plan.largest()
    return pl.pallas_call(
        functools.partial(rows_back_kernel, plan),
        out_shape=[jax.ShapeDtypeStruct(shape, dtype) for shape, dtype in shapes],
        in_specs=[pl.BlockSpec(memory_space=pltpu.SMEM), pl.BlockSpec(memory_space=pl.ANY)]
        + [pl.BlockSpec(memory_space=pltpu.VMEM)] * (1 + len(kept)),
        out_specs=[pl.BlockSpec(memory_space=pltpu.VMEM)] * len(shapes),
        scratch_shapes=[
            pltpu.VMEM((plan.count, plan.buffer // TILE, TILE, LANES), BF16),
            pltpu.VMEM((most, views, longest), F32),
            pltpu.VMEM((views, F), F32),
            pltpu.VMEM((views, F + 2 * LANES), F32),
            pltpu.SemaphoreType.DMA((plan.count,)),
        ],
        compiler_params=pltpu.CompilerParams(vmem_limit_bytes=40 * 1024 * 1024),
        cost_estimate=pl.CostEstimate(
            flops=30 * 10**9, bytes_accessed=30 * 10**6, transcendentals=10**5
        ),
    )(low, gathered, note, *kept)


def tokens_back_kernel(
    odd_ref,
    behind_ref,
    stream_ref,
    ends_ref,
    unit_ref,
    scale_ref,
    probs_ref,
    looked_ref,
    class_ref,
    qkv_ref,
    pixels_ref,
    first_ref,
    second_ref,
    kept_ref,
    sent_ref,
    patch_ref,
    place_ref,
    reach_ref,
    back_ref,
    mixed_ref,
    rows_ref,
):
    v = pl.program_id(0)
    views = stream_ref.shape[0]
    temper = HDIM ** (-0.5)
    norms = class_ref[4:8]
    class_unit, class_normed, class_scale = (class_ref[row : row + 1] for row in (0, 1, 3))

    @pl.when(v == 0)
    def _():
        place = 2 * D + F + B + 2 * H
        grad_att = behind_ref[:, place : place + D].astype(F32)
        spread = jnp.where(head_mask()[None], grad_att[:, None, :], 0.0).astype(BF16)
        back = product_t(spread.reshape(views * HEADROWS, D), qkv_ref[:, 2 * D :])
        back_ref[...] = back.astype(BF16).reshape(views, HEADROWS, D)
        patch_ref[...] = jnp.zeros(patch_ref.shape, F32)
        place_ref[...] = jnp.zeros(place_ref.shape, F32)
        reach_ref[...] = jnp.zeros(reach_ref.shape, F32)
        rows_ref[...] = jnp.zeros(rows_ref.shape, F32)

    unit = unit_ref[0]
    scale = scale_ref[0][:, :1]
    normed = token_norms(unit, norms, class_normed)
    back = back_ref[v]
    probs = probs_ref[0]
    grad_probs = product_t(back, normed)
    delta = jnp.sum(probs * grad_probs, -1, keepdims=True)
    grad_scores = (probs * (grad_probs - delta)).astype(BF16)
    reach = product(grad_scores, normed) * temper
    mixed_ref[v] = reach.astype(BF16)
    reach_ref[...] += reach
    left = jnp.concatenate([grad_scores.astype(F32), probs.astype(BF16).astype(F32)], 0)
    looked = (looked_ref[...].astype(F32) * temper).astype(BF16)
    grad = product(left.T.astype(BF16), jnp.concatenate([looked, back], 0))
    row = lax.broadcasted_iota(jnp.int32, (8, D), 0)
    rows_ref[0] += jnp.where(row == v, grad[NPATCH : NPATCH + 1], 0.0)
    token = lax.broadcasted_iota(jnp.int32, (TOKENS, D), 0)
    grad = jnp.where(token < NPATCH, grad, 0.0)
    rows_ref[1, 0:1] += jnp.sum(grad * unit, 0, keepdims=True)
    rows_ref[2, 0:1] += jnp.sum(grad, 0, keepdims=True)
    stream = norm_back(grad, norms[0:1], unit, scale)
    place_ref[...] += stream
    patch_ref[...] += product(pixels_ref[0], stream.astype(BF16))

    @pl.when(v == views - 1)
    def _():
        keyed = product(mixed_ref[...].reshape(views * HEADROWS, D), qkv_ref[:, D : 2 * D])
        keyed = jnp.where(head_mask()[None], keyed.reshape(views, HEADROWS, D), 0.0)
        grad_query = jnp.sum(keyed, 1).astype(BF16)
        class_row = rows_ref[0][:views] + product_t(grad_query, qkv_ref[:, :D])
        class_stream = norm_back(class_row, norms[0:1], class_unit, class_scale)
        class_stream = class_stream + stream_ref[...]
        ends = [
            (0, jnp.sum(class_stream, 0, keepdims=True)),
            (NTOK, rows_ref[1, 0:1] + jnp.sum(class_row * class_unit, 0, keepdims=True)),
            (NTOK + 1, rows_ref[2, 0:1] + jnp.sum(class_row, 0, keepdims=True)),
            (NTOK + 2, ends_ref[0:1]),
            (NTOK + 3, ends_ref[1:2]),
        ]
        tail = pltpu.roll(place_ref[...], 1, 0)
        for row, value in ends:
            tail = jnp.where(token == row, value, tail)
        upper = 2 * SET - 8
        rest = jnp.zeros((2 * SET - (PD - upper) - TOKENS, D), F32)
        query_row = lax.broadcasted_iota(jnp.int32, (8, D), 0) == 0
        total = jnp.sum(grad_query.astype(F32), 0, keepdims=True)
        shared = [reach_ref[...], jnp.where(query_row, total, pltpu.roll(ends_ref[...], 7, 0))]
        shared = jnp.concatenate(shared + [jnp.zeros((SHARED - HEADROWS - 8, D), F32)], 0)
        kept_ref[2 * SET :] = shared
        sent_ref[2 * SET :] = shared.astype(BF16)
        last = jnp.concatenate([patch_ref[upper:], tail, rest], 0)

        @pl.when(odd_ref[0] == 0)
        def _():
            kept_ref[: 2 * SET] = patch_ref[: 2 * SET]
            sent_ref[: 2 * SET] = last.astype(BF16)

        @pl.when(odd_ref[0] != 0)
        def _():
            kept_ref[: 2 * SET] = last
            sent_ref[: 2 * SET] = patch_ref[: 2 * SET].astype(BF16)


def tokens_back(odd, behind, grad_middle, ends, kept, pixels, *before):
    views = grad_middle.shape[0]

    def whole(values):
        return pl.BlockSpec(values.shape, lambda v: (0,) * values.ndim)

    def by_view(values):
        return pl.BlockSpec((1,) + values.shape[1:], lambda v: (v,) + (0,) * (values.ndim - 1))

    unit, scale, probs, looked, classes, qkv_w = kept
    shape = (2 * SET + SHARED, D)
    return pl.pallas_call(
        tokens_back_kernel,
        grid=(views,),
        out_shape=[jax.ShapeDtypeStruct(shape, F32), jax.ShapeDtypeStruct(shape, BF16)],
        in_specs=[
            pl.BlockSpec(memory_space=pltpu.SMEM),
            whole(behind),
            whole(grad_middle),
            whole(ends),
            by_view(unit),
            by_view(scale),
            by_view(probs),
            whole(looked),
            whole(classes),
            whole(qkv_w),
            by_view(pixels),
        ]
        + [pl.BlockSpec(memory_space=pl.ANY)] * len(before),
        out_specs=[pl.BlockSpec(shape, lambda v: (0, 0))] * 2,
        scratch_shapes=[
            pltpu.VMEM((PD, D), F32),
            pltpu.VMEM((TOKENS, D), F32),
            pltpu.VMEM((HEADROWS, D), F32),
            pltpu.VMEM((views, HEADROWS, D), BF16),
            pltpu.VMEM((views, HEADROWS, D), BF16),
            pltpu.VMEM((3, 8, D), F32),
        ],
        compiler_params=pltpu.CompilerParams(vmem_limit_bytes=60 * 1024 * 1024),
        cost_estimate=pl.CostEstimate(
            flops=15 * 10**9, bytes_accessed=15 * 10**6, transcendentals=10**5
        ),
    )(odd, behind, grad_middle, ends, unit, scale, probs, looked, classes, qkv_w, pixels, *before)


def early_kernel(
    plan,
    most,
    tab_ref,
    common_hbm,
    behind_hbm,
    rest_ref,
    *refs,
):
    line_ref, square_ref, common_ref, behind_ref, class_ref, sem, class_sem = refs[-7:]
    class_copy = pltpu.make_async_copy(
        common_hbm.at[pl.ds(0, TILE), pl.ds(CLASS, D)], class_ref, class_sem
    )
    class_copy.start()
    line_ref[...] = jnp.zeros(line_ref.shape, F32)

    def fetch(source, target, column, size):
        copy = pltpu.make_async_copy(
            source.at[:, pl.ds(column, size)], target.at[:, pl.ds(0, size)], sem
        )
        copy.start()
        copy.wait()

    def turned(lane):
        start = pl.multiple_of(lane // LANES * LANES, LANES)
        both = common_ref[:, pl.ds(start, 2 * LANES)].astype(F32)
        both = pltpu.roll(both, lax.rem(2 * LANES - (lane - start), 2 * LANES), 1)
        return both[:, :LANES].T.astype(BF16)

    def store(goal, width, tile, block):
        line_ref[pl.ds(goal + tile, block.shape[0], stride=width), :] = block

    for part in range(most):
        kind, base, chunks, row0 = (tab_ref[1 + 4 * part + i] for i in range(4))
        for index, (lane, column) in SPANS.items():
            cols = PIECES[index][2]
            width = cols // LANES
            size = (plan.most_chunks[index] + 1) * CHUNK

            @pl.when(kind == index)
            def _(lane=lane, column=column, cols=cols, width=width, size=size):
                skew = lax.rem(row0, LANES)
                fetch(common_hbm, common_ref, pl.multiple_of(ROWS + lane + row0 - skew, LANES), size)
                fetch(behind_hbm, behind_ref, column, cols)

                def move(step, carry):
                    goal = base + step * (CHUNK * width)
                    block = product(turned(skew + step * CHUNK), behind_ref[:, :cols])
                    for tile in range(width):
                        store(goal, width, tile, block[:, tile * LANES : (tile + 1) * LANES])
                    return carry

                lax.fori_loop(0, chunks, move, 0)

        @pl.when(kind == 8)
        def _():
            fetch(behind_hbm, behind_ref, 2 * D + F, B)
            fetch(common_hbm, common_ref, SECOND, H + D)

            def move(step, carry):
                left = turned(row0 + step * CHUNK)
                block = product(left, behind_ref[:, :B])
                for tile in range(B // LANES):
                    piece = block[:, tile * LANES : (tile + 1) * LANES]
                    store(base + step * (CHUNK * B // LANES), B // LANES, tile, piece)
                return carry

            lax.fori_loop(0, chunks, move, 0)

        @pl.when(kind == 5)
        def _():
            for tile in range(D // LANES):
                store(base, D // LANES, tile, jnp.zeros((8, LANES), F32))

        @pl.when(kind == 1)
        def _():
            fetch(behind_hbm, behind_ref, ATT_COLUMN, D)
            fetch(common_hbm, common_ref, 0, ROWS)

            def move(step, carry):
                width = 3 * D // LANES
                goal = base + step * (CHUNK * width)
                side = lax.broadcasted_iota(jnp.int32, (CHUNK, LANES), 1)
                for pair in range(HEADS // 2):
                    right = behind_ref[:, pair * LANES : (pair + 1) * LANES]
                    lane = 2 * pair * D + row0 + step * CHUNK
                    first, second = (product(turned(lane + D * head), right) for head in range(2))
                    block = jnp.where(side < HDIM, first, second)
                    store(goal, width, 2 * D // LANES + pair, block)
                return carry

            lax.fori_loop(0, chunks, move, 0)

    shift = tab_ref[0]
    shape = (STEPS, LANES)
    place = lax.broadcasted_iota(jnp.int32, shape, 0) * LANES
    place = place + lax.broadcasted_iota(jnp.int32, shape, 1) - shift

    def clear(step, total):
        start = pl.multiple_of(step * STEPS, 8)
        entry = place + start * LANES
        lines = pl.ds(pl.multiple_of(FRONT + start, 8), STEPS)
        kept = jnp.where((entry >= 0) & (entry < plan.size), line_ref[lines, :], 0.0)
        line_ref[lines, :] = kept
        return total + kept * kept

    total = lax.fori_loop(
        0, plan.steps, clear, jnp.zeros(shape, F32), unroll=steps_at_once(plan.steps)
    )
    total = jnp.sum(total, keepdims=True) + rest_ref[0:1, 0:1]
    class_copy.wait()
    if len(refs) > 7:
        holds, twice = (tab_ref[1 + 4 * most + which] for which in range(2))
        rows = jnp.sum(refs[0][...] * refs[0][...], 1, keepdims=True)
        place = lax.broadcasted_iota(jnp.int32, (SET, 1), 0)
        pieces = jnp.sum(jnp.where((place < 8) & (twice != 0), 0.0, rows[:SET]), keepdims=True)
        classes = class_ref[...].astype(F32)
        by_head = jnp.where(head_mask(), classes[1:2], 0.0)
        by_head = jnp.sum(by_head * by_head, 1, keepdims=True)
        normed = jnp.sum(classes[0:1] * classes[0:1], 1, keepdims=True)
        outer = jnp.sum(rows[SET : SET + HEADROWS] * by_head, keepdims=True)
        outer = outer + rows[SET + HEADROWS : SET + HEADROWS + 1] * normed
        outer = outer + rows[SET + HEADROWS + 1 : SET + HEADROWS + 2]
        outer = outer + rows[SET + HEADROWS + 2 : SET + HEADROWS + 3]
        total = total + jnp.where(holds != 0, pieces + outer / plan.groups, 0.0)
    square_ref[...] = jnp.broadcast_to(total[None], square_ref.shape)


def early_gradient(plan, table, common, behind, *values):
    return pl.pallas_call(
        functools.partial(early_kernel, plan, (table.shape[0] - 3) // 4),
        out_shape=[
            jax.ShapeDtypeStruct((plan.grad_scratch, LANES), F32),
            jax.ShapeDtypeStruct((plan.count, 1, LANES), F32),
        ],
        in_specs=[
            pl.BlockSpec(memory_space=pltpu.SMEM),
            pl.BlockSpec(memory_space=pl.ANY),
            pl.BlockSpec(memory_space=pl.ANY),
        ]
        + [pl.BlockSpec(memory_space=pltpu.VMEM)] * len(values),
        out_specs=[pl.BlockSpec(memory_space=pltpu.VMEM)] * 2,
        scratch_shapes=[
            pltpu.VMEM((common.shape[0], ROWS), BF16),
            pltpu.VMEM((behind.shape[0], F), BF16),
            pltpu.VMEM((TILE, D), BF16),
            pltpu.SemaphoreType.DMA,
            pltpu.SemaphoreType.DMA,
        ],
        compiler_params=pltpu.CompilerParams(vmem_limit_bytes=60 * 1024 * 1024),
        cost_estimate=pl.CostEstimate(
            flops=10 * 10**9, bytes_accessed=10 * 10**6, transcendentals=0
        ),
    )(table, common, behind, *values)


def late_kernel(
    plan,
    most,
    tab_ref,
    lines_ref,
    wide_ref,
    left_ref,
    right_ref,
    ends_ref,
    out_ref,
    line_ref,
    sem,
):
    used = FRONT + plan.lines + 8
    copy = pltpu.make_async_copy(lines_ref.at[pl.ds(0, used)], line_ref.at[pl.ds(0, used)], sem)
    copy.start()
    copy.wait()

    def add(goal, width, tile, block):
        lines = pl.ds(goal + tile, CHUNK, stride=width)
        line_ref[lines, :] = line_ref[lines, :] + block

    for part in range(most):
        kind, base, chunks, row0 = (tab_ref[1 + 4 * part + i] for i in range(4))

        @pl.when(kind == 0)
        def _():
            def move(step, carry):
                width = D // LANES
                rows = pl.ds(pl.multiple_of(row0 + step * CHUNK, 8), CHUNK)
                for tile in range(width):
                    block = wide_ref[rows, tile * LANES : (tile + 1) * LANES]
                    add(base + step * (CHUNK * width), width, tile, block)
                return carry

            lax.fori_loop(0, chunks, move, 0)

        @pl.when(kind == 1)
        def _():
            def move(step, carry):
                width = 3 * D // LANES
                rows = pl.ds(pl.multiple_of(row0 + step * CHUNK, 8), CHUNK)
                block = jnp.dot(
                    left_ref[rows, :],
                    right_ref[...],
                    precision=PRECISE,
                    preferred_element_type=F32,
                )
                for tile in range(2 * D // LANES):
                    piece = block[:, tile * LANES : (tile + 1) * LANES]
                    add(base + step * (CHUNK * width), width, tile, piece)
                return carry

            lax.fori_loop(0, chunks, move, 0)

        @pl.when(kind == 5)
        def _():
            width = D // LANES
            for tile in range(width):
                lines = pl.ds(base + tile, 8, stride=width)
                block = ends_ref[:, tile * LANES : (tile + 1) * LANES]
                line_ref[lines, :] = line_ref[lines, :] + block

    shift = tab_ref[0]
    turn = lax.rem(LANES - shift, LANES)
    lane = lax.broadcasted_iota(jnp.int32, (STEPS + 8, LANES), 1)

    def align(step, carry):
        start = pl.multiple_of(step * STEPS, 8)
        lines = pl.ds(pl.multiple_of(FRONT + start, 8), STEPS + 8)
        here = pltpu.roll(line_ref[lines, :], turn, 1)
        below = pltpu.roll(here, STEPS + 7, 0)
        both = jnp.where(lane < LANES - shift, here, below)
        out_ref[pl.ds(start, STEPS), :] = both[:STEPS]
        return carry

    lax.fori_loop(0, plan.steps, align, 0, unroll=steps_at_once(plan.steps))


def late_gradient(plan, table, lines, *values):
    return pl.pallas_call(
        functools.partial(late_kernel, plan, (table.shape[0] - 3) // 4),
        out_shape=jax.ShapeDtypeStruct((plan.lines, LANES), F32),
        in_specs=[pl.BlockSpec(memory_space=pltpu.SMEM), pl.BlockSpec(memory_space=pl.ANY)]
        + [pl.BlockSpec(memory_space=pltpu.VMEM)] * len(values),
        out_specs=pl.BlockSpec(memory_space=pltpu.VMEM),
        scratch_shapes=[
            pltpu.VMEM((plan.grad_scratch, LANES), F32),
            pltpu.SemaphoreType.DMA,
        ],
        compiler_params=pltpu.CompilerParams(vmem_limit_bytes=24 * 1024 * 1024),
    )(table, lines, *values).reshape(-1)[: plan.size]


def adam_update(weight, grad, first, second, rate):
    first = BETA_FIRST * first + (1.0 - BETA_FIRST) * grad
    second = BETA_SECOND * second + (1.0 - BETA_SECOND) * grad * grad
    stepped = (
        first
        / (1.0 - BETA_FIRST**STEP)
        / (jnp.sqrt(second / (1.0 - BETA_SECOND**STEP)) + ADAM_EPSILON)
    )
    return (weight - rate * (stepped + WEIGHT_DECAY * weight), first, second)


def per_device(
    plan,
    params,
    first_moment,
    second_moment,
    teacher,
    protos,
    proto_first,
    proto_second,
    teacher_protos,
    center,
    patches,
    partner,
):
    reps, groups = lax.axis_size("rep"), lax.axis_size("grp")
    count, half = reps * groups, reps * groups // 2
    rep, grp = lax.axis_index("rep"), lax.axis_index("grp")
    device = rep * groups + grp
    low = rep % 2 == 0
    place = rep // 2 * groups + grp
    halves = [
        [r * groups + g for r in range(parity, reps, 2) for g in range(groups)] for parity in (0, 1)
    ]
    swap = [(r, r ^ 1) for r in range(reps)]
    own_views = patches.shape[0]
    views = 2 * own_views

    def trade(values):
        return lax.ppermute(values, "rep", swap)

    def trade_low(values):
        return jnp.where(low, values, trade(values))

    def in_order(values):
        other = trade(values)
        return jnp.where(low, values, other), jnp.where(low, other, values)

    pairs = [list(range(parity, reps, 2)) for parity in (0, 1)]
    lines = reps // 2
    tables = jnp.stack([protos, teacher_protos]).astype(BF16)
    around = [tables]
    for step in range(2, reps, 2):
        around.append(lax.ppermute(tables, "rep", [(r, (r + step) % reps) for r in range(reps)]))

    table = jnp.asarray(plan.lay_table)[device]
    given = trade(lay_out(plan, table, jnp.where(low, teacher, params)))
    kept = lay_out(plan, table, jnp.where(low, params, teacher))
    given, around = lax.optimization_barrier((given, around))
    shards = jnp.stack([jnp.where(low, kept, given), jnp.where(low, given, kept)])
    gathered = lax.all_gather(shards, BOTH, axis=0, axis_index_groups=halves)
    gathered = gathered.reshape(half, 2, -1, TILE, LANES)
    patches, partner, given = lax.optimization_barrier((patches, partner, given))
    pixels = jnp.concatenate(in_order(patches), 0)
    pixels = jnp.pad(pixels, ((0, 0), (0, TOKENS - NPATCH), (0, 0)))
    around = jnp.concatenate([jnp.stack(around[::-1])] * 2)
    around = lax.dynamic_slice_in_dim(around, lines - 1 - rep // 2, lines, 0)
    tables = jnp.stack(in_order(around))
    tables = tables.transpose(2, 1, 0, 3, 4).reshape(2, B, -1).astype(F32)
    places = in_order(partner.astype(F32))

    def columns_of(values):
        scale = lax.rsqrt(jnp.sum(values * values, 0, keepdims=True) + 1e-06)
        return (values * scale).astype(BF16), scale

    columns, column_scale = columns_of(tables[0])
    teacher_columns = columns_of(tables[1])[0]

    here = jnp.arange(views)
    source = jnp.concatenate([places[0], places[1] + own_views]).astype(jnp.int32)
    source = jnp.where(low, here, source)
    turn = (source[:, None] == here[None, :]).astype(BF16)

    turn, columns, teacher_columns = lax.optimization_barrier((turn, columns, teacher_columns))
    kept = forward(plan, gathered, pixels, turn)
    unit, scale, probs, _, looked, classes, qkv_w = kept[:7]
    all_rows, common = lax.all_to_all(kept[12], BOTH, 0, 0), kept[13]

    def gather_rows(values):
        return lax.all_gather(values, BOTH, axis=0, axis_index_groups=halves).reshape(
            half * views, -1
        )

    other = trade(common)
    all_rows, other = lax.optimization_barrier((all_rows, other))
    common = jnp.where(low, common, other)

    all_rows = all_rows.reshape(reps // 2, 2, -1, B).transpose(1, 0, 2, 3).reshape(2, -1, B)
    start = (rep // 2 * groups * views).astype(jnp.int32)[None]
    note, new_center = prototypes(
        start, all_rows, columns, teacher_columns, center[None], groups, views
    )
    common = gather_rows(common)
    new_center = new_center[0]
    note = lax.all_to_all(note, "grp", 0, 0)
    totals = jnp.sum(note[:, 3 * views :], 0)
    totals = totals.reshape(-1, 8, B).transpose(1, 0, 2).reshape(8, -1)[:, : half * views]
    loss_value = jnp.sum(jnp.log(totals[0]) - totals[2] / totals[1])
    depth = protos.shape[0]
    grad_protos, proto_squares = prototypes_back(
        (rep * depth).astype(jnp.int32)[None],
        depth,
        all_rows,
        columns,
        teacher_columns,
        center[None],
        totals,
        tables[0],
        column_scale,
    )
    behind, grad_middle, ends = rows_back(
        plan, low.astype(jnp.int32)[None], gathered, note, (classes,) + tuple(kept[7:12])
    )
    odd, far = grp % 2 == 1, grp // 2 % 2 == 1
    behind_rows = trade_low(behind)
    kept_rows, sent_rows = tokens_back(
        odd.astype(jnp.int32)[None],
        behind,
        grad_middle,
        ends,
        (unit, scale, probs, looked, classes, qkv_w),
        pixels.transpose(0, 2, 1),
        behind_rows,
        grad_protos,
    )

    def across(bit, values):
        return lax.ppermute(values, "grp", [(g, g ^ bit) for g in range(groups)])

    partial = kept_rows + across(1, sent_rows).astype(F32)
    first, second = partial[:SET], partial[SET : 2 * SET]
    shared = partial[2 * SET :]
    other = jnp.concatenate([jnp.where(far, first, second), shared], 0).astype(BF16)
    partial = jnp.concatenate([jnp.where(far, second, first), shared], 0)
    partial = partial + across(2, other).astype(F32)
    behind_rows, common, partial = lax.optimization_barrier((behind_rows, common, partial))
    behind_rows = gather_rows(behind_rows)
    if plan.near:
        step = 1
        while step < lines:
            hops = [(r, r - 2 * step) for r in range(reps) if r // 2 % (2 * step) == step]
            partial = partial + lax.ppermute(partial.astype(BF16), "rep", hops).astype(F32)
            step *= 2
    else:
        depth = partial.shape[0] // lines
        partial = lax.all_to_all(
            partial.astype(BF16).reshape(lines, depth, D), "rep", 0, 0, axis_index_groups=pairs
        )
        partial = jnp.sum(partial.astype(F32), 0)
    class_rows = common[:2, CLASS:ROWS].astype(F32)
    class_normed, query = class_rows[0:1], class_rows[1:2]
    by_head = jnp.where(head_mask()[:HEADS], query, 0.0)
    values = (proto_squares, partial)
    if not plan.near:
        twice = odd & ~far & (jnp.arange(SET) < 8)
        weights = jnp.concatenate(
            [
                jnp.where(twice, 0.0, 1.0),
                jnp.sum(by_head * by_head, 1) / groups,
                jnp.zeros((HEADROWS - HEADS,), F32),
                jnp.sum(class_normed * class_normed)[None] / groups,
                jnp.full((2,), 1.0 / groups, F32),
                jnp.zeros((SHARED - HEADROWS - 3,), F32),
            ]
        )
        weights = lax.dynamic_slice_in_dim(weights, rep // 2 * depth, depth)
        pieces = jnp.sum(weights * jnp.sum(partial * partial, 1))
        values = (proto_squares + jnp.where(low, pieces, 0.0),)
    early, squares = early_gradient(
        plan, jnp.asarray(plan.grad_table)[device], common, behind_rows, *values
    )
    summed = partial.astype(BF16)
    if not plan.near:
        summed = lax.all_to_all(
            jnp.broadcast_to(summed[None], (lines, depth, D)), "rep", 0, 0, axis_index_groups=pairs
        ).reshape(-1, D)
    shared, summed = summed[SET:], summed[:SET]
    other, squares = lax.optimization_barrier((across(2, summed), squares))
    squares = lax.all_to_all(squares, BOTH, 0, 0)
    grad_norm = jnp.sqrt(jnp.sum(squares[:, 0, 0]))
    factor = jnp.minimum(1.0, CLIP_NORM / (grad_norm + 1e-06))
    summed = jnp.concatenate([jnp.where(far, other, summed), jnp.where(far, summed, other)], 0)
    if plan.all_sets:
        other = across(1, summed)
        summed = jnp.concatenate([jnp.where(odd, other, summed), jnp.where(odd, summed, other)], 0)
    if plan.odd_owner:
        summed = trade_low(summed)
    wide_grad = jnp.pad(summed.astype(F32), ((0, CHUNK), (0, 0)))

    ends = shared[HEADROWS + 1 : HEADROWS + 3]
    shared = trade_low(shared).astype(F32)
    if plan.near:
        for owner in plan.final_reps:
            moved = lax.ppermute(ends, "rep", [(0, owner)]) if owner else ends
            ends = jnp.where(rep == owner, moved, ends)
        ends = ends.astype(F32)
    else:
        ends = shared[HEADROWS + 1 : HEADROWS + 3]
    ends = jnp.pad(ends, ((0, 6), (0, 0)))
    sum_query, reach = shared[HEADROWS : HEADROWS + 1], shared[:HEADS]
    left = jnp.concatenate([class_normed, reach, jnp.zeros((LANES - 1 - HEADS, D), F32)], 0)
    left = jnp.pad(left.T, ((0, CHUNK), (0, 0)))
    right = jnp.concatenate(
        [
            jnp.pad(sum_query, ((0, 0), (0, D))),
            jnp.pad(by_head, ((0, 0), (D, 0))),
            jnp.zeros((LANES - 1 - HEADS, 2 * D), F32),
        ],
        0,
    )
    grad_flat = late_gradient(
        plan, jnp.asarray(plan.late_table)[device], early, wide_grad, left, right, ends
    )
    new_params, new_first, new_second = adam_update(
        params, grad_flat * factor, first_moment, second_moment, LEARNING_RATE
    )
    new_protos, new_proto_first, new_proto_second = adam_update(
        protos, grad_protos * factor, proto_first, proto_second, PROTO_RATE
    )
    new_teacher = TEACHER_MOMENTUM * teacher + (1.0 - TEACHER_MOMENTUM) * new_params
    new_teacher_protos = TEACHER_MOMENTUM * teacher_protos + (1.0 - TEACHER_MOMENTUM) * new_protos
    return (
        new_params,
        new_first,
        new_second,
        new_teacher,
        new_protos,
        new_proto_first,
        new_proto_second,
        new_teacher_protos,
        new_center,
        loss_value,
        grad_norm,
    )


def solution(mesh):
    placed = (
        P(BOTH),
        P(BOTH),
        P(BOTH),
        P(BOTH),
        P("rep", "grp"),
        P("rep", "grp"),
        P("rep", "grp"),
        P("rep", "grp"),
        P("grp"),
        P(BOTH, None, None),
        P(BOTH),
    )
    plan = Plan(mesh.shape["rep"], mesh.shape["grp"])
    return jax.shard_map(
        functools.partial(per_device, plan),
        mesh=mesh,
        in_specs=placed,
        out_specs=placed[:9] + (P(), P()),
        check_vma=False,
    )
```

```python
import functools

import jax
import jax.numpy as jnp
import numpy as np
from jax import lax
from jax.experimental import pallas as pl
from jax.experimental.pallas import tpu as pltpu
from jax.sharding import PartitionSpec as P

D = 768
HEADS = 12
HDIM = 64
F = 3072
PD = 768
NTOK = 197
H = 2048
B = 256
STEP = 10
NPATCH = NTOK - 1

PRECISE = lax.Precision.HIGHEST
STUDENT_TEMP = 0.1
TEACHER_TEMP = 0.04
CENTER_MOMENTUM = 0.9
TEACHER_MOMENTUM = 0.8
CLIP_NORM = 0.05
LEARNING_RATE = 0.03
PROTO_RATE = 0.6
BETA_FIRST = 0.9
BETA_SECOND = 0.999
ADAM_EPSILON = 1e-08
WEIGHT_DECAY = 0.04
BOTH = ("rep", "grp")
LANES = 128
F32 = jnp.float32
BF16 = jnp.bfloat16

SEGMENTS = []
_offset = 0
for _rows, _cols in ((PD + NTOK + 4, D), (D, 3 * D), (D, D), (D, F), (F + 2, D), (D + H, H), (H, B)):
    SEGMENTS.append((_offset, _rows, _cols))
    _offset += _rows * _cols
PFLAT = _offset
WIDTHS = sorted({cols // LANES for _, _, cols in SEGMENTS})

PIECES = []
_offset = 0
for _rows, _cols in (
    (PD + NTOK + 4, D),
    (D, 3 * D),
    (D, D),
    (D, F),
    (F, D),
    (2, D),
    (D, H),
    (H, H),
    (H, B),
):
    PIECES.append((_offset, _rows, _cols))
    _offset += _rows * _cols
FRONT = 192
CHUNK = 128
SET = 288
SHARED = 32
STEPS = 64
AHEAD = 3 * D + F + H
TILE = 16
TOKENS = 208
HEADROWS = 16
VMEM_LIMIT = 62 * 1024 * 1024


SPANS = {
    2: (0, 0),
    3: (D, D),
    4: (2 * D, D + F),
    6: (2 * D + F, 2 * D + F + B + H),
    7: (3 * D + F, 2 * D + F + B),
}
ATT_COLUMN = 2 * D + F + B + 2 * H
SECOND = HEADS * D
CLASS = SECOND + H
ROWS = CLASS + D


def round_up(value, step):
    return -(-value // step) * step


def steps_at_once(count):
    return max(size for size in range(1, 8) if count % size == 0)


def shard_parts(start, stop, table):
    parts = []
    line0 = start // LANES
    for index, (offset, rows, cols) in enumerate(table):
        low, high = max(start, offset), min(stop, offset + rows * cols)
        if low >= high:
            continue
        row0 = (low - offset) // cols
        row1 = -(-(high - offset) // cols)
        parts.append((index, row0, row1 - row0, (offset + row0 * cols) // LANES - line0))
    return parts


FINAL_ROW = round_up(PD + NTOK + 4, 8)


class Plan:
    def __init__(self, reps, groups):
        count = reps * groups
        self.count, self.groups = count, groups
        self.size = PFLAT // count
        self.lines = round_up(-(-self.size // LANES) + 1, STEPS)
        self.steps = self.lines // STEPS
        self.scratch = FRONT + self.lines + 8 * max(WIDTHS) + 16
        table = []
        self.blocks = [[] for _ in SEGMENTS]
        longest = 0
        for device in range(count):
            start = device * self.size
            entry = [start % LANES]
            target = 0
            for index, row0, rows, line in shard_parts(start, start + self.size, SEGMENTS):
                width = SEGMENTS[index][2] // LANES
                skew = row0 % 8
                tiles = -(-(rows + skew) // 8)
                self.blocks[index].append((device, target // TILE, row0 // 8, tiles))
                entry += [
                    WIDTHS.index(width),
                    FRONT + line - skew * width,
                    tiles // 2,
                    tiles % 2,
                    target // TILE,
                ]
                target += tiles * 8 * width
            longest = max(longest, target)
            entry += [-1, 0, 0, 0, 0] * (2 - len(entry) // 5)
            table.append(entry)
        self.buffer = round_up(longest, 16)
        self.lay_table = np.array(table, np.int32)
        edge = SEGMENTS[0][1] * SEGMENTS[0][2]
        owners = [device for device in range(count) if device * self.size < edge]
        self.odd_owner = any(self.place(device)[1] for device in owners)
        self.all_sets = len(owners) > 2
        edge = sum(rows * cols for _, rows, cols in SEGMENTS[:2])
        self.near = all(
            device < 2 * groups for device in range(count) if device * self.size < edge
        )
        offset, rows, cols = PIECES[5]
        self.final_reps = sorted(
            {
                device // groups
                for device in range(count)
                if device * self.size < offset + rows * cols and (device + 1) * self.size > offset
            }
        )
        self.grad_table = self.tabulate(lambda index: index, lambda device, index, row0, chunks: row0)
        self.most_chunks = {
            index: max(
                [1]
                + [
                    entry[3 + place]
                    for entry in self.grad_table
                    for place in range(0, len(entry) - 3, 4)
                    if entry[1 + place] == index
                ]
            )
            for index in (1,) + tuple(SPANS)
        }
        self.fetched = max(
            [HEADS * (self.most_chunks[1] + 1) * CHUNK, H + D]
            + [(chunks + 1) * CHUNK for chunks in self.most_chunks.values()]
        )
        self.late_table = self.tabulate(lambda index: index in (0, 1, 5), self.wide_row)
        self.grad_scratch = FRONT + self.lines + CHUNK * max(WIDTHS) + 16
        self.used = FRONT + self.lines + 8


    def largest(self):
        longest = max(8 * block[3] for blocks in self.blocks for block in blocks)
        return max(len(blocks) for blocks in self.blocks), round_up(longest, LANES) + 2 * LANES

    def place(self, device):
        rep, grp = divmod(device, self.groups)
        return rep // 2 * self.groups + grp, rep % 2

    def tabulate(self, chosen, rows_of):
        table = []
        for device in range(self.count):
            start = device * self.size
            entry = []
            for index, row0, rows, line in shard_parts(start, start + self.size, PIECES):
                if not chosen(index):
                    continue
                skew = row0 % 8
                line -= skew * (PIECES[index][2] // LANES)
                chunks = -(-(rows + skew) // CHUNK)
                entry += [index, FRONT + line, chunks, rows_of(device, index, row0 - skew, chunks)]
            table.append(entry)
        most = max(len(entry) for entry in table) // 4
        for device, entry in enumerate(table):
            entry += [-1, 0, 0, 0] * (most - len(entry) // 4)
            entry.insert(0, device * self.size % LANES)
            entry += [device < self.groups, device % 4 == 1]
        return np.array(table, np.int32)

    def wide_row(self, device, index, row0, chunks):
        if index:
            return row0
        late = row0 >= 2 * SET - 8
        if not self.all_sets:
            if late != device % 2:
                raise ValueError("owner")
            return row0 - (2 * SET - 8) * late
        return row0 + 8 * late


def lay_kernel(plan, tab_ref, x_ref, out_ref, line_ref):
    shift = tab_ref[0]
    lane = lax.broadcasted_iota(jnp.int32, (STEPS + 8, LANES), 1)
    line_ref[pl.ds(0, FRONT), :] = jnp.zeros((FRONT, LANES), F32)
    tail = plan.scratch - FRONT - plan.lines
    line_ref[pl.ds(FRONT + plan.lines, tail), :] = jnp.zeros((tail, LANES), F32)

    def align(step, carry):
        base = pl.multiple_of(step * STEPS, 8)
        here = pltpu.roll(x_ref[pl.ds(base, STEPS + 8), :], shift, 1)
        above = pltpu.roll(here, 1, 0)
        both = jnp.where(lane >= shift, here, above)
        line_ref[pl.ds(pl.multiple_of(FRONT + base, 8), STEPS), :] = both[8:]
        return carry

    lax.fori_loop(0, plan.steps, align, 0, unroll=steps_at_once(plan.steps))
    for part in range(2):
        kind, base, pairs, odd, target = (tab_ref[1 + 5 * part + i] for i in range(5))
        for index, width in enumerate(WIDTHS):

            @pl.when(kind == index)
            def _(width=width):
                def move(step, carry):
                    row = base + step * (TILE * width)
                    goal = (target + step * width) * TILE
                    for tile in range(width):
                        both = line_ref[pl.ds(row + tile, TILE, stride=width), :]
                        place = pl.multiple_of(goal + TILE * tile, TILE)
                        out_ref[pl.ds(place, TILE), :] = both.astype(BF16)
                    return carry

                def last(step, carry):
                    row = base + pairs * (TILE * width)
                    goal = (target + pairs * width) * TILE
                    for tile in range(0, width, 2):
                        both = [
                            line_ref[pl.ds(row + tile + side, 8, stride=width), :]
                            for side in range(2)
                        ]
                        place = pl.multiple_of(goal + 8 * tile, TILE)
                        out_ref[pl.ds(place, TILE), :] = jnp.concatenate(both, 0).astype(BF16)
                    return carry

                lax.fori_loop(0, pairs, move, 0)
                lax.fori_loop(0, odd, last, 0)


def lay_out(plan, table, flat):
    padded = jnp.pad(flat, (8 * LANES, plan.lines * LANES - plan.size))
    lines = padded.reshape(8 + plan.lines, LANES)
    return pl.pallas_call(
        functools.partial(lay_kernel, plan),
        out_shape=jax.ShapeDtypeStruct((plan.buffer, LANES), BF16),
        in_specs=[
            pl.BlockSpec(memory_space=pltpu.SMEM),
            pl.BlockSpec(memory_space=pltpu.VMEM),
        ],
        out_specs=pl.BlockSpec(memory_space=pltpu.VMEM),
        scratch_shapes=[pltpu.VMEM((plan.scratch, LANES), F32)],
        compiler_params=pltpu.CompilerParams(vmem_limit_bytes=24 * 1024 * 1024),
    )(table, lines)


class Shards:
    def __init__(self, plan, gathered_ref, ref, sems, order):
        self.plan, self.ref, self.sems, self.waited = plan, ref, sems, set()
        self.copies = {}
        for device in order:
            place, side = plan.place(device)
            copy = pltpu.make_async_copy(
                gathered_ref.at[place, side], ref.at[device], sems.at[device]
            )
            copy.start()
            self.copies[device] = copy

    def wait(self, device):
        if device in self.copies:
            self.copies.pop(device).wait()

    def finish(self):
        for device in list(self.copies):
            self.wait(device)

    def blocks(self, index, first, count):
        found = [
            block
            for block in self.plan.blocks[index]
            if 8 * block[2] < first + count and 8 * (block[2] + block[3]) > first
        ]
        for block in found:
            self.wait(block[0])
        return found

    def eight(self, index, tile, pair, side):
        width = SEGMENTS[index][2] // LANES
        total = None
        for device, target, tile0, tiles in self.plan.blocks[index]:
            own = tile - tile0
            if not 0 <= own < tiles:
                continue
            if own < tiles // 2 * 2:
                both = self.ref[device, target + own // 2 * width + 2 * pair + side]
                half = own % 2
            else:
                both = self.ref[device, target + tiles // 2 * width + pair]
                half = side
            piece = both.astype(F32)[8 * half : 8 * half + 8]
            total = piece if total is None else total + piece
        return total

    def assemble(self, index, out_ref):
        width = SEGMENTS[index][2] // LANES
        rows = out_ref.shape[0]
        self.blocks(index, 0, rows)

        def column(pair, carry):
            for side in range(2):
                lanes = pl.ds(pl.multiple_of(pair * 2 * LANES + side * LANES, LANES), LANES)
                for group in range(rows // TILE):
                    both = [
                        self.eight(index, 2 * group + half, pair, side) for half in range(2)
                    ]
                    out_ref[TILE * group : TILE * (group + 1), lanes] = jnp.concatenate(
                        both, 0
                    ).astype(BF16)
            return carry

        lax.fori_loop(0, width // 2, column, 0)

    def columns(self, index, block, pair):
        width = SEGMENTS[index][2] // LANES
        device, target, _, tiles = block
        sides = []
        for side in range(2):
            pieces = [
                self.ref[device, target + step * width + 2 * pair + side]
                for step in range(tiles // 2)
            ]
            if tiles % 2:
                both = self.ref[device, target + tiles // 2 * width + pair].astype(F32)
                pieces.append(both[8 * side : 8 * side + 8].astype(BF16))
            sides.append(jnp.concatenate(pieces, 0))
        return jnp.concatenate(sides, 1)

    def times(self, index, first, values, left_ref, out_ref):
        views, count = values.shape
        blocks = self.blocks(index, first, count)
        top = max([first + count] + [8 * (tile0 + tiles) for _, _, tile0, tiles in blocks])
        top = round_up(top, LANES) + LANES
        parts = [values, jnp.zeros((views, top - first - count), F32)]
        if first:
            parts.insert(0, jnp.zeros((views, first), F32))
        wide = jnp.concatenate(parts, 1)
        for number, (_, _, tile0, tiles) in enumerate(blocks):
            start = 8 * tile0 // LANES * LANES
            turn = 8 * tile0 - start
            piece = wide[:, start : start + round_up(turn + 8 * tiles, LANES)]
            if turn:
                piece = pltpu.roll(piece, piece.shape[1] - turn, 1)
            left_ref[number, :, : 8 * tiles] = piece[:, : 8 * tiles]

        def column(pair, carry):
            total = jnp.zeros((views, 2 * LANES), F32)
            for number, block in enumerate(blocks):
                left = left_ref[number, :, : 8 * block[3]].astype(BF16)
                total += product(left, self.columns(index, block, pair))
            out_ref[:, pl.ds(pl.multiple_of(pair * 2 * LANES, LANES), 2 * LANES)] = total
            return carry

        lax.fori_loop(0, SEGMENTS[index][2] // LANES // 2, column, 0, unroll=4)


    def back(self, index, first, count, values, grad_ref, left_ref, wide_ref):
        views, cols = values.shape
        grad_ref[:, :cols] = values
        blocks = self.blocks(index, first, count)
        top = max([first + count] + [8 * (tile0 + tiles) for _, _, tile0, tiles in blocks])
        wide_ref[:, : round_up(top, LANES) + LANES] = jnp.zeros(
            (views, round_up(top, LANES) + LANES), F32
        )
        for number, (_, _, _, tiles) in enumerate(blocks):
            size = round_up(8 * tiles, LANES) + LANES
            left_ref[number, :, :size] = jnp.zeros((views, size), F32)

        def column(pair, carry):
            lanes = pl.ds(pl.multiple_of(pair * 2 * LANES, LANES), 2 * LANES)
            left = grad_ref[:, lanes].astype(BF16)
            for number, block in enumerate(blocks):
                size = 8 * block[3]
                left_ref[number, :, :size] += product_t(left, self.columns(index, block, pair))
            return carry

        lax.fori_loop(0, cols // LANES // 2, column, 0, unroll=4)
        for number, (_, _, tile0, tiles) in enumerate(blocks):
            start = 8 * tile0 // LANES * LANES
            turn = 8 * tile0 - start
            size = round_up(turn + 8 * tiles, LANES)
            piece = left_ref[number, :, :size]
            if turn:
                piece = pltpu.roll(piece, turn, 1)
            wide_ref[:, start : start + size] += piece
        return wide_ref[:, first : first + count]


def product(left, right):
    return jnp.dot(left, right, preferred_element_type=F32)


def product_t(left, right):
    return lax.dot_general(
        left, right, (((left.ndim - 1,), (1,)), ((), ())), preferred_element_type=F32
    )


def normal_share(values):
    return 0.5 + 0.5 * lax.erf(values * 2**-0.5)


def activate(values):
    return values * normal_share(values)


def gelu_back(values, grad):
    density = jnp.exp(-0.5 * values * values) * (2 * np.pi) ** -0.5
    return grad * (normal_share(values) + values * density)


def normalised(values):
    centred = values - jnp.mean(values, -1, keepdims=True)
    scale = lax.rsqrt(jnp.mean(centred * centred, -1, keepdims=True) + 1e-06)
    return centred * scale, scale


def norm_back(grad, gain, unit, scale):
    inner = grad * gain
    return scale * (
        inner
        - jnp.mean(inner, -1, keepdims=True)
        - unit * jnp.mean(inner * unit, -1, keepdims=True)
    )


def head_mask():
    shape = (HEADROWS, D)
    return lax.broadcasted_iota(jnp.int32, shape, 0) == (
        lax.broadcasted_iota(jnp.int32, shape, 1) // HDIM
    )


def token_norms(unit, norms, class_normed):
    token = lax.broadcasted_iota(jnp.int32, (TOKENS, D), 0)
    normed = unit * norms[0:1] + norms[1:2]
    return jnp.where(
        token < NPATCH, normed, jnp.where(token == NPATCH, class_normed, 0.0)
    ).astype(BF16)


def forward_kernel(
    plan,
    gathered_ref,
    pixels_ref,
    turn_ref,
    unit_out,
    scale_out,
    probs_ref,
    mixed_ref,
    looked_ref,
    class_ref,
    qkv_out,
    hidden_ref,
    one_ref,
    two_ref,
    bottle_ref,
    middle_ref,
    rows_ref,
    pack_out,
    shards_ref,
    wide_ref,
    place_ref,
    left_ref,
    sums_ref,
    pack_ref,
    unit_ref,
    scale_ref,
    qkv_ref,
    out_sems,
    sems,
):
    shards = Shards(plan, gathered_ref, shards_ref, sems, range(plan.count))
    views = pixels_ref.shape[0]
    temper = HDIM ** (-0.5)
    shards.assemble(0, wide_ref)
    position = wide_ref[PD : PD + TOKENS].astype(F32)
    place_ref[...] = pltpu.roll(position, TOKENS - 1, 0)
    class_place = position[0:1]
    norms = position[NTOK : NTOK + 4]
    class_unit, class_scale = normalised(class_place)
    class_normed = (class_unit * norms[0:1] + norms[1:2]).astype(BF16).astype(F32)
    shards.assemble(1, qkv_ref)
    qkv_copy = pltpu.make_async_copy(qkv_ref, qkv_out, out_sems.at[4])
    qkv_copy.start()
    mask = head_mask()
    query = jnp.broadcast_to(class_normed, (HEADROWS, D)).astype(BF16)
    query = product(query, qkv_ref[:, :D]).astype(BF16).astype(F32)
    by_head = jnp.where(mask, query, 0.0).astype(BF16)
    looked = product_t(by_head, qkv_ref[:, D : 2 * D]).astype(BF16)
    looked_ref[...] = looked

    def copies(v):
        slot = lax.rem(v, 2)
        return (
            pltpu.make_async_copy(unit_ref.at[slot], unit_out.at[v], out_sems.at[slot]),
            pltpu.make_async_copy(scale_ref.at[slot], scale_out.at[v], out_sems.at[2 + slot]),
        )

    def view(v, carry):
        embedded = product(pixels_ref[v], wide_ref[:PD]) + place_ref[...]
        unit, scale = normalised(embedded)

        @pl.when(v >= 2)
        def _():
            for copy in copies(v - 2):
                copy.wait()

        unit_ref[lax.rem(v, 2)] = unit
        scale_ref[lax.rem(v, 2)] = jnp.broadcast_to(scale, (TOKENS, LANES))
        for copy in copies(v):
            copy.start()
        normed = token_norms(unit, norms, class_normed)
        scores = product_t(looked, normed) * temper
        token = lax.broadcasted_iota(jnp.int32, scores.shape, 1)
        scores = jnp.where(token < NTOK, scores, -1e30)
        top = jnp.max(scores, -1, keepdims=True)
        top = top + jnp.log(jnp.sum(jnp.exp(scores - top), -1, keepdims=True))
        head = lax.broadcasted_iota(jnp.int32, scores.shape, 0)
        probs = jnp.where(head < HEADS, jnp.exp(scores - top), 0.0)
        probs_ref[v] = probs
        mixed_ref[v] = product(probs.astype(BF16), normed).astype(BF16)
        return carry

    lax.fori_loop(0, views, view, 0, unroll=2)
    mixed = mixed_ref[...].reshape(views * HEADROWS, D)
    valued = product(mixed, qkv_ref[:, 2 * D :]).reshape(views, HEADROWS, D)
    attended = jnp.sum(jnp.where(mask[None], valued, 0.0), 1).astype(BF16)
    pack_ref[:, :D] = attended.astype(F32)
    shards.times(2, 0, pack_ref[:, :D], left_ref, sums_ref)
    middle = class_place + sums_ref[...]
    unit, scale = normalised(middle)
    middle_ref[0], middle_ref[1] = unit, jnp.broadcast_to(scale, (views, D))
    normed = (unit * norms[2:3] + norms[3:4]).astype(BF16)
    pack_ref[:, D : 2 * D] = normed.astype(F32)
    shards.times(3, 0, pack_ref[:, D : 2 * D], left_ref, hidden_ref)
    act = activate(hidden_ref[...]).astype(BF16)
    pack_ref[:, 2 * D : 2 * D + F] = act.astype(F32)
    shards.times(4, 0, act.astype(F32), left_ref, sums_ref)
    unit, scale = normalised(middle + sums_ref[...])
    middle_ref[2], middle_ref[3] = unit, jnp.broadcast_to(scale, (views, D))
    final = jnp.concatenate(
        [shards.eight(4, F // 8, tile // 2, tile % 2) for tile in range(D // LANES)], 1
    )
    cls = (unit * final[0:1] + final[1:2]).astype(BF16)
    place = 2 * D + F
    pack_ref[:, place : place + D] = cls.astype(F32)
    shards.times(5, 0, cls.astype(F32), left_ref, one_ref)
    first = activate(one_ref[...]).astype(BF16)
    pack_ref[:, place + D : AHEAD] = first.astype(F32)
    shards.times(5, D, first.astype(F32), left_ref, two_ref)
    second = activate(two_ref[...]).astype(BF16)
    shards.times(6, 0, second.astype(F32), left_ref, bottle_ref)
    bottle = bottle_ref[...]
    scale = lax.rsqrt(jnp.sum(bottle * bottle, -1, keepdims=True) + 1e-06)
    rows = product(turn_ref[...], (bottle * scale).astype(BF16)).astype(BF16)
    rows_ref[...] = jnp.broadcast_to(rows[None], rows_ref.shape)
    mixed = mixed_ref[...].astype(F32)
    for head in range(HEADS):
        pack_out[:, head * D : (head + 1) * D] = mixed[:, head, :].astype(BF16)
    pack_out[:, SECOND:CLASS] = second
    row = lax.broadcasted_iota(jnp.int32, (views, D), 0)
    pack_out[:, CLASS:ROWS] = jnp.where(
        row == 0, class_normed, jnp.where(row == 1, query[0:1], 0.0)
    ).astype(BF16)
    pack_out[:, ROWS : ROWS + AHEAD] = pack_ref[...].astype(BF16)
    pack_out[:, ROWS + AHEAD :] = jnp.zeros((views, pack_out.shape[1] - ROWS - AHEAD), BF16)
    class_ref[...] = jnp.concatenate(
        [
            class_unit,
            class_normed,
            query[0:1],
            jnp.broadcast_to(class_scale, (1, D)),
            norms,
            final,
        ],
        0,
    )
    for v in range(max(0, views - 2), views):
        for copy in copies(v):
            copy.wait()
    qkv_copy.wait()
    shards.finish()


def forward(plan, gathered, pixels, turn):
    views = pixels.shape[0]
    shapes = [
        ((views, TOKENS, D), F32),
        ((views, TOKENS, LANES), F32),
        ((views, HEADROWS, TOKENS), F32),
        ((views, HEADROWS, D), BF16),
        ((HEADROWS, D), BF16),
        ((16, D), F32),
        ((D, 3 * D), BF16),
        ((views, F), F32),
        ((views, H), F32),
        ((views, H), F32),
        ((views, B), F32),
        ((4, views, D), F32),
        ((plan.count, views, B), BF16),
        ((views, ROWS + AHEAD + (max(plan.most_chunks.values()) + 1) * CHUNK), BF16),
    ]
    most, longest = plan.largest()
    return pl.pallas_call(
        functools.partial(forward_kernel, plan),
        out_shape=[jax.ShapeDtypeStruct(shape, dtype) for shape, dtype in shapes],
        in_specs=[pl.BlockSpec(memory_space=pl.ANY)]
        + [pl.BlockSpec(memory_space=pltpu.VMEM)] * 2,
        out_specs=[
            pl.BlockSpec(memory_space=pl.ANY if index in (0, 1, 6) else pltpu.VMEM)
            for index in range(len(shapes))
        ],
        scratch_shapes=[
            pltpu.VMEM((plan.count, plan.buffer // TILE, TILE, LANES), BF16),
            pltpu.VMEM((round_up(PD + NTOK + 4, TILE), D), BF16),
            pltpu.VMEM((TOKENS, D), F32),
            pltpu.VMEM((most, views, longest), F32),
            pltpu.VMEM((views, D), F32),
            pltpu.VMEM((views, AHEAD), F32),
            pltpu.VMEM((2, TOKENS, D), F32),
            pltpu.VMEM((2, TOKENS, LANES), F32),
            pltpu.VMEM((D, 3 * D), BF16),
            pltpu.SemaphoreType.DMA((5,)),
            pltpu.SemaphoreType.DMA((plan.count,)),
        ],
        compiler_params=pltpu.CompilerParams(vmem_limit_bytes=VMEM_LIMIT),
        cost_estimate=pl.CostEstimate(
            flops=60 * 10**9, bytes_accessed=40 * 10**6, transcendentals=10**5
        ),
    )(gathered, pixels, turn)


def proto_kernel(
    start_ref,
    rows_ref,
    columns_ref,
    others_ref,
    center_ref,
    note_ref,
    center_out_ref,
    student_ref,
    teacher_ref,
    sums_ref,
):
    count, groups = rows_ref.shape[1], note_ref.shape[0]
    views = (note_ref.shape[1] - 8 * -(-count // B)) // 3
    logits = product(rows_ref[1], others_ref[...])
    center = center_ref[...]
    center_out_ref[...] = CENTER_MOMENTUM * center + (1.0 - CENTER_MOMENTUM) * jnp.mean(
        logits, 0, keepdims=True
    )
    exp_teacher = jnp.exp((logits - center) / TEACHER_TEMP)
    teacher_ref[...] = exp_teacher
    scaled = product(rows_ref[0], columns_ref[...]) / STUDENT_TEMP
    exp_student = jnp.exp(scaled)
    student_ref[...] = exp_student
    turned = []
    for which, values in enumerate((exp_student, exp_teacher, exp_teacher * scaled)):
        total = jnp.broadcast_to(jnp.sum(values, 1, keepdims=True), (count, LANES))
        turned.append(total.T[0:1])
        if which < 2:
            sums_ref[:, which * LANES : (which + 1) * LANES] = total
    turned = jnp.concatenate(turned + [jnp.zeros((5, count), F32)], 0)
    for step in range(-(-count // B)):
        part = turned[:, step * B : (step + 1) * B]
        lines = slice(3 * views + 8 * step, 3 * views + 8 * (step + 1))
        note_ref[:, lines, : part.shape[1]] = jnp.broadcast_to(part[None], (groups,) + part.shape)
        if part.shape[1] < B:
            note_ref[:, lines, part.shape[1] :] = jnp.zeros((groups, 8, B - part.shape[1]), F32)
    start = pl.multiple_of(start_ref[0], 8)
    band, parts = groups * views, []
    for source in (student_ref, teacher_ref):
        rest = source[pl.ds(start, band), :]
        for _ in range(3):
            parts.append(rest.astype(BF16))
            rest = rest - parts[-1].astype(F32)
    pulls = product_t(jnp.concatenate(parts, 0), columns_ref[...])
    for which in range(2):
        first = 3 * which * band
        total = pulls[first : first + band] + pulls[first + band : first + 2 * band]
        total = total + pulls[first + 2 * band : first + 3 * band]
        note_ref[:, which * views : (which + 1) * views, :] = total.reshape(groups, views, B)
    own = sums_ref[pl.ds(start, groups * views), :]
    note_ref[:, 2 * views : 3 * views, :] = own.reshape(groups, views, B)


def prototypes(start, rows, columns, others, center, groups, views):
    count, width = rows.shape[1], columns.shape[1]
    shapes = [(groups, 3 * views + 8 * -(-count // B), B), (1, width)]
    return pl.pallas_call(
        proto_kernel,
        out_shape=[jax.ShapeDtypeStruct(shape, F32) for shape in shapes],
        in_specs=[pl.BlockSpec(memory_space=pltpu.SMEM)]
        + [pl.BlockSpec(memory_space=pltpu.VMEM)] * 4,
        out_specs=[pl.BlockSpec(memory_space=pltpu.VMEM)] * len(shapes),
        scratch_shapes=[pltpu.VMEM((count, width), F32)] * 2
        + [pltpu.VMEM((count, 2 * LANES), F32)],
        compiler_params=pltpu.CompilerParams(vmem_limit_bytes=32 * 1024 * 1024),
        cost_estimate=pl.CostEstimate(
            flops=3 * 10**9, bytes_accessed=6 * 10**6, transcendentals=10**6
        ),
    )(start, rows, columns, others, center)


def proto_back_kernel(
    start_ref,
    rows_ref,
    columns_ref,
    others_ref,
    center_ref,
    totals_ref,
    table_ref,
    scale_ref,
    grad_ref,
    square_ref,
    work_ref,
):
    count = rows_ref.shape[1]
    totals = jnp.broadcast_to(totals_ref[0:2][:, None, :], (2, 8, count))
    student, teacher = (totals[which].T[:, :1] for which in range(2))
    logits = product(rows_ref[1], others_ref[...])
    targets = jnp.exp((logits - center_ref[...]) / TEACHER_TEMP) / teacher
    scaled = product(rows_ref[0], columns_ref[...]) / STUDENT_TEMP
    grad = (jnp.exp(scaled) / student - targets) / STUDENT_TEMP
    work_ref[...] = jnp.dot(
        rows_ref[0].astype(F32).T, grad, precision=PRECISE, preferred_element_type=F32
    )
    scale = scale_ref[...]
    inner = jnp.sum(work_ref[...] * table_ref[...], 0, keepdims=True)
    start = pl.multiple_of(start_ref[0], 8)
    lines = pl.ds(start, grad_ref.shape[0])
    grad = work_ref[lines, :] * scale - table_ref[lines, :] * (scale * scale * scale * inner)
    grad_ref[...] = grad
    square_ref[...] = jnp.broadcast_to(jnp.sum(grad * grad, keepdims=True), square_ref.shape)


def prototypes_back(start, depth, *values):
    count, width = values[0].shape[1], values[1].shape[1]
    shapes = [(depth, width), (8, LANES)]
    return pl.pallas_call(
        proto_back_kernel,
        out_shape=[jax.ShapeDtypeStruct(shape, F32) for shape in shapes],
        in_specs=[pl.BlockSpec(memory_space=pltpu.SMEM)]
        + [pl.BlockSpec(memory_space=pltpu.VMEM)] * len(values),
        out_specs=[pl.BlockSpec(memory_space=pltpu.VMEM)] * len(shapes),
        scratch_shapes=[pltpu.VMEM((B, width), F32)],
        compiler_params=pltpu.CompilerParams(vmem_limit_bytes=32 * 1024 * 1024),
        cost_estimate=pl.CostEstimate(
            flops=3 * 10**9, bytes_accessed=6 * 10**6, transcendentals=10**6
        ),
    )(start, *values)


def rows_back_kernel(
    plan,
    low_ref,
    gathered_ref,
    note_ref,
    class_ref,
    hidden_ref,
    one_ref,
    two_ref,
    bottle_ref,
    middle_ref,
    pack_ref,
    stream_ref,
    extra_ref,
    shards_ref,
    left_ref,
    values_ref,
    wide_ref,
    sems,
):
    used = {block[0] for blocks in plan.blocks[2:] for block in blocks}
    shards = Shards(plan, gathered_ref, shards_ref, sems, sorted(used, reverse=True))
    work = (values_ref, left_ref, wide_ref)
    norms, final = class_ref[4:8], class_ref[8:10]

    views = bottle_ref.shape[0]
    note = jnp.sum(note_ref[...], 0)
    sums = note[2 * views : 3 * views]
    student, teacher = sums[:, :1], sums[:, LANES : LANES + 1]
    grad_rows = (note[:views] / student - note[views : 2 * views] / teacher) / STUDENT_TEMP
    grad_rows = jnp.where(low_ref[0] == 0, 0.0, grad_rows).astype(BF16).astype(F32)
    bottle = bottle_ref[...]
    scale = lax.rsqrt(jnp.sum(bottle * bottle, -1, keepdims=True) + 1e-06)
    grad_bottle = (
        grad_rows * scale - bottle * scale**3 * jnp.sum(grad_rows * bottle, -1, keepdims=True)
    ).astype(BF16)
    place = 2 * D + F
    pack_ref[:, place : place + B] = grad_bottle
    grad_two = shards.back(6, 0, H, grad_bottle.astype(F32), *work)
    grad_two = gelu_back(two_ref[...], grad_two).astype(BF16)
    pack_ref[:, place + B : place + B + H] = grad_two
    grad_one = shards.back(5, D, H, grad_two.astype(F32), *work)
    grad_one = gelu_back(one_ref[...], grad_one).astype(BF16)
    pack_ref[:, place + B + H : place + B + 2 * H] = grad_one
    grad_cls = shards.back(5, 0, D, grad_one.astype(F32), *work)
    unit, scale = middle_ref[2], middle_ref[3]
    gain_last = jnp.sum(grad_cls * unit, 0, keepdims=True)
    shift_last = jnp.sum(grad_cls, 0, keepdims=True)
    grad_stream = norm_back(grad_cls, final[0:1], unit, scale)
    grad_branch = grad_stream.astype(BF16)
    pack_ref[:, D + F : 2 * D + F] = grad_branch
    grad_hidden = shards.back(4, 0, F, grad_branch.astype(F32), *work)
    grad_hidden = gelu_back(hidden_ref[...], grad_hidden).astype(BF16)
    pack_ref[:, D : D + F] = grad_hidden
    grad_normed = shards.back(3, 0, D, grad_hidden.astype(F32), *work)
    unit, scale = middle_ref[0], middle_ref[1]
    extra_ref[...] = jnp.concatenate(
        [
            jnp.sum(grad_normed * unit, 0, keepdims=True),
            jnp.sum(grad_normed, 0, keepdims=True),
            gain_last,
            shift_last,
            jnp.zeros((4, D), F32),
        ],
        0,
    )
    grad_middle = grad_stream + norm_back(grad_normed, norms[2:3], unit, scale)
    stream_ref[...] = grad_middle
    grad_mixed = grad_middle.astype(BF16)
    pack_ref[:, :D] = grad_mixed
    grad_att = shards.back(2, 0, D, grad_mixed.astype(F32), *work).astype(BF16)
    pack_ref[:, place + B + 2 * H : place + B + 2 * H + D] = grad_att
    shards.finish()


def rows_back(plan, low, gathered, note, kept):
    views = kept[-1].shape[1]
    shapes = [((views, 3 * D + F + B + 2 * H), BF16), ((views, D), F32), ((8, D), F32)]
    most, longest = plan.largest()
    return pl.pallas_call(
        functools.partial(rows_back_kernel, plan),
        out_shape=[jax.ShapeDtypeStruct(shape, dtype) for shape, dtype in shapes],
        in_specs=[pl.BlockSpec(memory_space=pltpu.SMEM), pl.BlockSpec(memory_space=pl.ANY)]
        + [pl.BlockSpec(memory_space=pltpu.VMEM)] * (1 + len(kept)),
        out_specs=[pl.BlockSpec(memory_space=pltpu.VMEM)] * len(shapes),
        scratch_shapes=[
            pltpu.VMEM((plan.count, plan.buffer // TILE, TILE, LANES), BF16),
            pltpu.VMEM((most, views, longest), F32),
            pltpu.VMEM((views, F), F32),
            pltpu.VMEM((views, F + 2 * LANES), F32),
            pltpu.SemaphoreType.DMA((plan.count,)),
        ],
        compiler_params=pltpu.CompilerParams(vmem_limit_bytes=40 * 1024 * 1024),
        cost_estimate=pl.CostEstimate(
            flops=30 * 10**9, bytes_accessed=30 * 10**6, transcendentals=10**5
        ),
    )(low, gathered, note, *kept)


def tokens_back_kernel(
    odd_ref,
    behind_ref,
    stream_ref,
    ends_ref,
    unit_ref,
    scale_ref,
    probs_ref,
    looked_ref,
    class_ref,
    qkv_ref,
    pixels_ref,
    first_ref,
    second_ref,
    kept_ref,
    sent_ref,
    patch_ref,
    place_ref,
    reach_ref,
    back_ref,
    mixed_ref,
    rows_ref,
):
    v = pl.program_id(0)
    views = stream_ref.shape[0]
    temper = HDIM ** (-0.5)
    norms = class_ref[4:8]
    class_unit, class_normed, class_scale = (class_ref[row : row + 1] for row in (0, 1, 3))

    @pl.when(v == 0)
    def _():
        place = 2 * D + F + B + 2 * H
        grad_att = behind_ref[:, place : place + D].astype(F32)
        spread = jnp.where(head_mask()[None], grad_att[:, None, :], 0.0).astype(BF16)
        back = product_t(spread.reshape(views * HEADROWS, D), qkv_ref[:, 2 * D :])
        back_ref[...] = back.astype(BF16).reshape(views, HEADROWS, D)
        patch_ref[...] = jnp.zeros(patch_ref.shape, F32)
        place_ref[...] = jnp.zeros(place_ref.shape, F32)
        reach_ref[...] = jnp.zeros(reach_ref.shape, F32)
        rows_ref[...] = jnp.zeros(rows_ref.shape, F32)

    unit = unit_ref[0]
    scale = scale_ref[0][:, :1]
    normed = token_norms(unit, norms, class_normed)
    back = back_ref[v]
    probs = probs_ref[0]
    grad_probs = product_t(back, normed)
    delta = jnp.sum(probs * grad_probs, -1, keepdims=True)
    grad_scores = (probs * (grad_probs - delta)).astype(BF16)
    reach = product(grad_scores, normed) * temper
    mixed_ref[v] = reach.astype(BF16)
    reach_ref[...] += reach
    left = jnp.concatenate([grad_scores.astype(F32), probs.astype(BF16).astype(F32)], 0)
    looked = (looked_ref[...].astype(F32) * temper).astype(BF16)
    grad = product(left.T.astype(BF16), jnp.concatenate([looked, back], 0))
    row = lax.broadcasted_iota(jnp.int32, (8, D), 0)
    rows_ref[0] += jnp.where(row == v, grad[NPATCH : NPATCH + 1], 0.0)
    token = lax.broadcasted_iota(jnp.int32, (TOKENS, D), 0)
    grad = jnp.where(token < NPATCH, grad, 0.0)
    rows_ref[1, 0:1] += jnp.sum(grad * unit, 0, keepdims=True)
    rows_ref[2, 0:1] += jnp.sum(grad, 0, keepdims=True)
    stream = norm_back(grad, norms[0:1], unit, scale)
    place_ref[...] += stream
    patch_ref[...] += product(pixels_ref[0], stream.astype(BF16))

    @pl.when(v == views - 1)
    def _():
        keyed = product(mixed_ref[...].reshape(views * HEADROWS, D), qkv_ref[:, D : 2 * D])
        keyed = jnp.where(head_mask()[None], keyed.reshape(views, HEADROWS, D), 0.0)
        grad_query = jnp.sum(keyed, 1).astype(BF16)
        class_row = rows_ref[0][:views] + product_t(grad_query, qkv_ref[:, :D])
        class_stream = norm_back(class_row, norms[0:1], class_unit, class_scale)
        class_stream = class_stream + stream_ref[...]
        ends = [
            (0, jnp.sum(class_stream, 0, keepdims=True)),
            (NTOK, rows_ref[1, 0:1] + jnp.sum(class_row * class_unit, 0, keepdims=True)),
            (NTOK + 1, rows_ref[2, 0:1] + jnp.sum(class_row, 0, keepdims=True)),
            (NTOK + 2, ends_ref[0:1]),
            (NTOK + 3, ends_ref[1:2]),
        ]
        tail = pltpu.roll(place_ref[...], 1, 0)
        for row, value in ends:
            tail = jnp.where(token == row, value, tail)
        upper = 2 * SET - 8
        rest = jnp.zeros((2 * SET - (PD - upper) - TOKENS, D), F32)
        query_row = lax.broadcasted_iota(jnp.int32, (8, D), 0) == 0
        total = jnp.sum(grad_query.astype(F32), 0, keepdims=True)
        shared = [reach_ref[...], jnp.where(query_row, total, pltpu.roll(ends_ref[...], 7, 0))]
        shared = jnp.concatenate(shared + [jnp.zeros((SHARED - HEADROWS - 8, D), F32)], 0)
        kept_ref[2 * SET :] = shared
        sent_ref[2 * SET :] = shared.astype(BF16)
        last = jnp.concatenate([patch_ref[upper:], tail, rest], 0)

        @pl.when(odd_ref[0] == 0)
        def _():
            kept_ref[: 2 * SET] = patch_ref[: 2 * SET]
            sent_ref[: 2 * SET] = last.astype(BF16)

        @pl.when(odd_ref[0] != 0)
        def _():
            kept_ref[: 2 * SET] = last
            sent_ref[: 2 * SET] = patch_ref[: 2 * SET].astype(BF16)


def tokens_back(odd, behind, grad_middle, ends, kept, pixels, *before):
    views = grad_middle.shape[0]

    def whole(values):
        return pl.BlockSpec(values.shape, lambda v: (0,) * values.ndim)

    def by_view(values):
        return pl.BlockSpec((1,) + values.shape[1:], lambda v: (v,) + (0,) * (values.ndim - 1))

    unit, scale, probs, looked, classes, qkv_w = kept
    shape = (2 * SET + SHARED, D)
    return pl.pallas_call(
        tokens_back_kernel,
        grid=(views,),
        out_shape=[jax.ShapeDtypeStruct(shape, F32), jax.ShapeDtypeStruct(shape, BF16)],
        in_specs=[
            pl.BlockSpec(memory_space=pltpu.SMEM),
            whole(behind),
            whole(grad_middle),
            whole(ends),
            by_view(unit),
            by_view(scale),
            by_view(probs),
            whole(looked),
            whole(classes),
            whole(qkv_w),
            by_view(pixels),
        ]
        + [pl.BlockSpec(memory_space=pl.ANY)] * len(before),
        out_specs=[pl.BlockSpec(shape, lambda v: (0, 0))] * 2,
        scratch_shapes=[
            pltpu.VMEM((PD, D), F32),
            pltpu.VMEM((TOKENS, D), F32),
            pltpu.VMEM((HEADROWS, D), F32),
            pltpu.VMEM((views, HEADROWS, D), BF16),
            pltpu.VMEM((views, HEADROWS, D), BF16),
            pltpu.VMEM((3, 8, D), F32),
        ],
        compiler_params=pltpu.CompilerParams(vmem_limit_bytes=60 * 1024 * 1024),
        cost_estimate=pl.CostEstimate(
            flops=15 * 10**9, bytes_accessed=15 * 10**6, transcendentals=10**5
        ),
    )(odd, behind, grad_middle, ends, unit, scale, probs, looked, classes, qkv_w, pixels, *before)


def early_kernel(
    plan,
    most,
    tab_ref,
    common_hbm,
    behind_hbm,
    rest_ref,
    *refs,
):
    line_out, square_ref, common_ref, behind_ref, class_ref, line_ref, sem, class_sem = refs[-8:]
    slab = (plan.most_chunks[1] + 1) * CHUNK
    class_copy = pltpu.make_async_copy(
        common_hbm.at[pl.ds(0, TILE), pl.ds(CLASS, D)], class_ref, class_sem
    )
    class_copy.start()
    line_ref[...] = jnp.zeros(line_ref.shape, F32)

    def fetch(source, target, column, size):
        which = 0 if target is common_ref else 1
        copy = pltpu.make_async_copy(
            source.at[:, pl.ds(column, size)], target.at[:, pl.ds(0, size)], sem.at[which]
        )
        copy.start()
        return copy

    def turned(lane):
        start = pl.multiple_of(lane // LANES * LANES, LANES)
        both = common_ref[:, pl.ds(start, 2 * LANES)].astype(F32)
        both = pltpu.roll(both, lax.rem(2 * LANES - (lane - start), 2 * LANES), 1)
        return both[:, :LANES].T.astype(BF16)

    def store(goal, width, tile, block):
        line_ref[pl.ds(goal + tile, block.shape[0], stride=width), :] = block

    for part in range(most):
        kind, base, chunks, row0 = (tab_ref[1 + 4 * part + i] for i in range(4))
        for index, (lane, column) in SPANS.items():
            cols = PIECES[index][2]
            width = cols // LANES
            size = (plan.most_chunks[index] + 1) * CHUNK

            @pl.when(kind == index)
            def _(lane=lane, column=column, cols=cols, width=width, size=size):
                skew = lax.rem(row0, LANES)
                place = pl.multiple_of(ROWS + lane + row0 - skew, LANES)
                copies = [
                    fetch(common_hbm, common_ref, place, size),
                    fetch(behind_hbm, behind_ref, column, cols),
                ]
                for copy in copies:
                    copy.wait()

                def move(step, carry):
                    goal = base + step * (CHUNK * width)
                    block = product(turned(skew + step * CHUNK), behind_ref[:, :cols])
                    for tile in range(width):
                        store(goal, width, tile, block[:, tile * LANES : (tile + 1) * LANES])
                    return carry

                lax.fori_loop(0, chunks, move, 0)

        @pl.when(kind == 8)
        def _():
            copies = [
                fetch(behind_hbm, behind_ref, 2 * D + F, B),
                fetch(common_hbm, common_ref, SECOND, H + D),
            ]
            for copy in copies:
                copy.wait()

            def move(step, carry):
                for own in range(2):
                    place = 2 * step + own
                    block = product(turned(row0 + place * CHUNK), behind_ref[:, :B])
                    for tile in range(B // LANES):
                        piece = block[:, tile * LANES : (tile + 1) * LANES]
                        store(base + place * (CHUNK * B // LANES), B // LANES, tile, piece)
                return carry

            lax.fori_loop(0, (chunks + 1) // 2, move, 0)

        @pl.when(kind == 5)
        def _():
            for tile in range(D // LANES):
                store(base, D // LANES, tile, jnp.zeros((8, LANES), F32))

        @pl.when(kind == 1)
        def _():
            skew = lax.rem(row0, LANES)
            first = pl.multiple_of(row0 - skew, LANES)
            copies = [fetch(behind_hbm, behind_ref, ATT_COLUMN, D)]
            for head in range(HEADS):
                copies.append(
                    pltpu.make_async_copy(
                        common_hbm.at[:, pl.ds(pl.multiple_of(head * D + first, LANES), slab)],
                        common_ref.at[:, pl.ds(head * slab, slab)],
                        sem.at[2 + head],
                    )
                )
                copies[-1].start()
            for copy in copies:
                copy.wait()

            def move(step, carry):
                width = 3 * D // LANES
                goal = base + step * (CHUNK * width)
                side = lax.broadcasted_iota(jnp.int32, (CHUNK, LANES), 1)
                for pair in range(HEADS // 2):
                    right = behind_ref[:, pair * LANES : (pair + 1) * LANES]
                    lane = 2 * pair * slab + skew + step * CHUNK
                    left, other = (product(turned(lane + slab * head), right) for head in range(2))
                    block = jnp.where(side < HDIM, left, other)
                    store(goal, width, 2 * D // LANES + pair, block)
                return carry

            lax.fori_loop(0, chunks, move, 0)

    shift = tab_ref[0]
    shape = (STEPS, LANES)
    place = lax.broadcasted_iota(jnp.int32, shape, 0) * LANES
    place = place + lax.broadcasted_iota(jnp.int32, shape, 1) - shift

    def clear(step, total):
        start = pl.multiple_of(step * STEPS, 8)
        entry = place + start * LANES
        lines = pl.ds(pl.multiple_of(FRONT + start, 8), STEPS)
        kept = jnp.where((entry >= 0) & (entry < plan.size), line_ref[lines, :], 0.0)
        line_ref[lines, :] = kept
        return total + kept * kept

    total = lax.fori_loop(
        0, plan.steps, clear, jnp.zeros(shape, F32), unroll=steps_at_once(plan.steps)
    )
    line_copy = pltpu.make_async_copy(line_ref.at[pl.ds(0, plan.used)], line_out, sem.at[0])
    line_copy.start()
    total = jnp.sum(total, keepdims=True) + rest_ref[0:1, 0:1]
    class_copy.wait()
    if len(refs) > 8:
        holds, twice = (tab_ref[1 + 4 * most + which] for which in range(2))
        rows = jnp.sum(refs[0][...] * refs[0][...], 1, keepdims=True)
        place = lax.broadcasted_iota(jnp.int32, (SET, 1), 0)
        pieces = jnp.sum(jnp.where((place < 8) & (twice != 0), 0.0, rows[:SET]), keepdims=True)
        classes = class_ref[...].astype(F32)
        by_head = jnp.where(head_mask(), classes[1:2], 0.0)
        by_head = jnp.sum(by_head * by_head, 1, keepdims=True)
        normed = jnp.sum(classes[0:1] * classes[0:1], 1, keepdims=True)
        outer = jnp.sum(rows[SET : SET + HEADROWS] * by_head, keepdims=True)
        outer = outer + rows[SET + HEADROWS : SET + HEADROWS + 1] * normed
        outer = outer + rows[SET + HEADROWS + 1 : SET + HEADROWS + 2]
        outer = outer + rows[SET + HEADROWS + 2 : SET + HEADROWS + 3]
        total = total + jnp.where(holds != 0, pieces + outer / plan.groups, 0.0)
    square_ref[...] = jnp.broadcast_to(total[None], square_ref.shape)
    line_copy.wait()


def early_gradient(plan, table, common, behind, *values):
    return pl.pallas_call(
        functools.partial(early_kernel, plan, (table.shape[0] - 3) // 4),
        out_shape=[
            jax.ShapeDtypeStruct((plan.used, LANES), F32),
            jax.ShapeDtypeStruct((plan.count, 1, LANES), F32),
        ],
        in_specs=[
            pl.BlockSpec(memory_space=pltpu.SMEM),
            pl.BlockSpec(memory_space=pl.ANY),
            pl.BlockSpec(memory_space=pl.ANY),
        ]
        + [pl.BlockSpec(memory_space=pltpu.VMEM)] * len(values),
        out_specs=[
            pl.BlockSpec(memory_space=pl.ANY),
            pl.BlockSpec(memory_space=pltpu.VMEM),
        ],
        scratch_shapes=[
            pltpu.VMEM((common.shape[0], plan.fetched), BF16),
            pltpu.VMEM((behind.shape[0], F), BF16),
            pltpu.VMEM((TILE, D), BF16),
            pltpu.VMEM((plan.grad_scratch, LANES), F32),
            pltpu.SemaphoreType.DMA((2 + HEADS,)),
            pltpu.SemaphoreType.DMA,
        ],
        compiler_params=pltpu.CompilerParams(vmem_limit_bytes=60 * 1024 * 1024),
        cost_estimate=pl.CostEstimate(
            flops=10 * 10**9, bytes_accessed=10 * 10**6, transcendentals=0
        ),
    )(table, common, behind, *values)


def late_kernel(
    plan,
    most,
    tab_ref,
    lines_ref,
    wide_ref,
    left_ref,
    right_ref,
    ends_ref,
    out_ref,
    line_ref,
    sem,
):
    copy = pltpu.make_async_copy(lines_ref, line_ref.at[pl.ds(0, plan.used)], sem)
    copy.start()
    copy.wait()

    def add(goal, width, tile, block):
        lines = pl.ds(goal + tile, CHUNK, stride=width)
        line_ref[lines, :] = line_ref[lines, :] + block

    for part in range(most):
        kind, base, chunks, row0 = (tab_ref[1 + 4 * part + i] for i in range(4))

        @pl.when(kind == 0)
        def _():
            def move(step, carry):
                width = D // LANES
                rows = pl.ds(pl.multiple_of(row0 + step * CHUNK, 8), CHUNK)
                for tile in range(width):
                    block = wide_ref[rows, tile * LANES : (tile + 1) * LANES]
                    add(base + step * (CHUNK * width), width, tile, block)
                return carry

            lax.fori_loop(0, chunks, move, 0)

        @pl.when(kind == 1)
        def _():
            def move(step, carry):
                width = 3 * D // LANES
                rows = pl.ds(pl.multiple_of(row0 + step * CHUNK, 8), CHUNK)
                block = jnp.dot(
                    left_ref[rows, :],
                    right_ref[...],
                    precision=PRECISE,
                    preferred_element_type=F32,
                )
                for tile in range(2 * D // LANES):
                    piece = block[:, tile * LANES : (tile + 1) * LANES]
                    add(base + step * (CHUNK * width), width, tile, piece)
                return carry

            lax.fori_loop(0, chunks, move, 0)

        @pl.when(kind == 5)
        def _():
            width = D // LANES
            for tile in range(width):
                lines = pl.ds(base + tile, 8, stride=width)
                block = ends_ref[:, tile * LANES : (tile + 1) * LANES]
                line_ref[lines, :] = line_ref[lines, :] + block

    shift = tab_ref[0]
    turn = lax.rem(LANES - shift, LANES)
    lane = lax.broadcasted_iota(jnp.int32, (STEPS + 8, LANES), 1)

    def align(step, carry):
        start = pl.multiple_of(step * STEPS, 8)
        lines = pl.ds(pl.multiple_of(FRONT + start, 8), STEPS + 8)
        here = pltpu.roll(line_ref[lines, :], turn, 1)
        below = pltpu.roll(here, STEPS + 7, 0)
        both = jnp.where(lane < LANES - shift, here, below)
        out_ref[pl.ds(start, STEPS), :] = both[:STEPS]
        return carry

    lax.fori_loop(0, plan.steps, align, 0, unroll=steps_at_once(plan.steps))


def late_gradient(plan, table, lines, *values):
    return pl.pallas_call(
        functools.partial(late_kernel, plan, (table.shape[0] - 3) // 4),
        out_shape=jax.ShapeDtypeStruct((plan.lines, LANES), F32),
        in_specs=[pl.BlockSpec(memory_space=pltpu.SMEM), pl.BlockSpec(memory_space=pl.ANY)]
        + [pl.BlockSpec(memory_space=pltpu.VMEM)] * len(values),
        out_specs=pl.BlockSpec(memory_space=pltpu.VMEM),
        scratch_shapes=[
            pltpu.VMEM((plan.grad_scratch, LANES), F32),
            pltpu.SemaphoreType.DMA,
        ],
        compiler_params=pltpu.CompilerParams(vmem_limit_bytes=24 * 1024 * 1024),
    )(table, lines, *values).reshape(-1)[: plan.size]


def adam_update(weight, grad, first, second, rate):
    first = BETA_FIRST * first + (1.0 - BETA_FIRST) * grad
    second = BETA_SECOND * second + (1.0 - BETA_SECOND) * grad * grad
    stepped = (
        first
        / (1.0 - BETA_FIRST**STEP)
        / (jnp.sqrt(second / (1.0 - BETA_SECOND**STEP)) + ADAM_EPSILON)
    )
    return (weight - rate * (stepped + WEIGHT_DECAY * weight), first, second)


def per_device(
    plan,
    params,
    first_moment,
    second_moment,
    teacher,
    protos,
    proto_first,
    proto_second,
    teacher_protos,
    center,
    patches,
    partner,
):
    reps, groups = lax.axis_size("rep"), lax.axis_size("grp")
    count, half = reps * groups, reps * groups // 2
    rep, grp = lax.axis_index("rep"), lax.axis_index("grp")
    device = rep * groups + grp
    low = rep % 2 == 0
    place = rep // 2 * groups + grp
    halves = [
        [r * groups + g for r in range(parity, reps, 2) for g in range(groups)] for parity in (0, 1)
    ]
    swap = [(r, r ^ 1) for r in range(reps)]
    own_views = patches.shape[0]
    views = 2 * own_views

    def trade(values):
        return lax.ppermute(values, "rep", swap)

    def trade_low(values):
        return jnp.where(low, values, trade(values))

    def in_order(values):
        other = trade(values)
        return jnp.where(low, values, other), jnp.where(low, other, values)

    pairs = [list(range(parity, reps, 2)) for parity in (0, 1)]
    lines = reps // 2
    tables = jnp.stack([protos, teacher_protos]).astype(BF16)
    around = [tables]
    for step in range(2, reps, 2):
        around.append(lax.ppermute(tables, "rep", [(r, (r + step) % reps) for r in range(reps)]))

    table = jnp.asarray(plan.lay_table)[device]
    given = trade(lay_out(plan, table, jnp.where(low, teacher, params)))
    kept = lay_out(plan, table, jnp.where(low, params, teacher))
    given, around = lax.optimization_barrier((given, around))
    shards = jnp.stack([jnp.where(low, kept, given), jnp.where(low, given, kept)])
    gathered = lax.all_gather(shards, BOTH, axis=0, axis_index_groups=halves)
    gathered = gathered.reshape(half, 2, -1, TILE, LANES)
    patches, partner, given = lax.optimization_barrier((patches, partner, given))
    pixels = jnp.concatenate(in_order(patches), 0)
    pixels = jnp.pad(pixels, ((0, 0), (0, TOKENS - NPATCH), (0, 0)))
    around = jnp.concatenate([jnp.stack(around[::-1])] * 2)
    around = lax.dynamic_slice_in_dim(around, lines - 1 - rep // 2, lines, 0)
    tables = jnp.stack(in_order(around))
    tables = tables.transpose(2, 1, 0, 3, 4).reshape(2, B, -1).astype(F32)
    places = in_order(partner.astype(F32))

    def columns_of(values):
        scale = lax.rsqrt(jnp.sum(values * values, 0, keepdims=True) + 1e-06)
        return (values * scale).astype(BF16), scale

    columns, column_scale = columns_of(tables[0])
    teacher_columns = columns_of(tables[1])[0]

    here = jnp.arange(views)
    source = jnp.concatenate([places[0], places[1] + own_views]).astype(jnp.int32)
    source = jnp.where(low, here, source)
    turn = (source[:, None] == here[None, :]).astype(BF16)

    turn, columns, teacher_columns = lax.optimization_barrier((turn, columns, teacher_columns))
    kept = forward(plan, gathered, pixels, turn)
    unit, scale, probs, _, looked, classes, qkv_w = kept[:7]
    all_rows, common = lax.all_to_all(kept[12], BOTH, 0, 0), kept[13]

    def gather_rows(values):
        return lax.all_gather(values, BOTH, axis=0, axis_index_groups=halves).reshape(
            half * views, -1
        )

    other = trade(common)

    all_rows = all_rows.reshape(reps // 2, 2, -1, B).transpose(1, 0, 2, 3).reshape(2, -1, B)
    start = (rep // 2 * groups * views).astype(jnp.int32)[None]
    note, new_center = prototypes(
        start, all_rows, columns, teacher_columns, center[None], groups, views
    )
    note, other = lax.optimization_barrier((note, other))
    common = gather_rows(jnp.where(low, common, other))
    new_center = new_center[0]
    note = lax.all_to_all(note, "grp", 0, 0)
    totals = jnp.sum(note[:, 3 * views :], 0)
    totals = totals.reshape(-1, 8, B).transpose(1, 0, 2).reshape(8, -1)[:, : half * views]
    loss_value = jnp.sum(jnp.log(totals[0]) - totals[2] / totals[1])
    depth = protos.shape[0]
    grad_protos, proto_squares = prototypes_back(
        (rep * depth).astype(jnp.int32)[None],
        depth,
        all_rows,
        columns,
        teacher_columns,
        center[None],
        totals,
        tables[0],
        column_scale,
    )
    behind, grad_middle, ends = rows_back(
        plan, low.astype(jnp.int32)[None], gathered, note, (classes,) + tuple(kept[7:12])
    )
    odd, far = grp % 2 == 1, grp // 2 % 2 == 1
    behind_rows = trade_low(behind)
    kept_rows, sent_rows = tokens_back(
        odd.astype(jnp.int32)[None],
        behind,
        grad_middle,
        ends,
        (unit, scale, probs, looked, classes, qkv_w),
        pixels.transpose(0, 2, 1),
        behind_rows,
        grad_protos,
    )

    def across(bit, values):
        return lax.ppermute(values, "grp", [(g, g ^ bit) for g in range(groups)])

    partial = kept_rows + across(1, sent_rows).astype(F32)
    first, second = partial[:SET], partial[SET : 2 * SET]
    shared = partial[2 * SET :]
    other = jnp.concatenate([jnp.where(far, first, second), shared], 0).astype(BF16)
    partial = jnp.concatenate([jnp.where(far, second, first), shared], 0)
    partial = partial + across(2, other).astype(F32)
    behind_rows, common, partial = lax.optimization_barrier((behind_rows, common, partial))
    behind_rows = gather_rows(behind_rows)
    if plan.near:
        step = 1
        while step < lines:
            hops = [(r, r - 2 * step) for r in range(reps) if r // 2 % (2 * step) == step]
            partial = partial + lax.ppermute(partial.astype(BF16), "rep", hops).astype(F32)
            step *= 2
    else:
        depth = partial.shape[0] // lines
        partial = lax.all_to_all(
            partial.astype(BF16).reshape(lines, depth, D), "rep", 0, 0, axis_index_groups=pairs
        )
        partial = jnp.sum(partial.astype(F32), 0)
    class_rows = common[:2, CLASS:ROWS].astype(F32)
    class_normed, query = class_rows[0:1], class_rows[1:2]
    by_head = jnp.where(head_mask()[:HEADS], query, 0.0)
    values = (proto_squares, partial)
    if not plan.near:
        twice = odd & ~far & (jnp.arange(SET) < 8)
        weights = jnp.concatenate(
            [
                jnp.where(twice, 0.0, 1.0),
                jnp.sum(by_head * by_head, 1) / groups,
                jnp.zeros((HEADROWS - HEADS,), F32),
                jnp.sum(class_normed * class_normed)[None] / groups,
                jnp.full((2,), 1.0 / groups, F32),
                jnp.zeros((SHARED - HEADROWS - 3,), F32),
            ]
        )
        weights = lax.dynamic_slice_in_dim(weights, rep // 2 * depth, depth)
        pieces = jnp.sum(weights * jnp.sum(partial * partial, 1))
        values = (proto_squares + jnp.where(low, pieces, 0.0),)
    early, squares = early_gradient(
        plan, jnp.asarray(plan.grad_table)[device], common, behind_rows, *values
    )
    summed = partial.astype(BF16)
    if not plan.near:
        summed = lax.all_to_all(
            jnp.broadcast_to(summed[None], (lines, depth, D)), "rep", 0, 0, axis_index_groups=pairs
        ).reshape(-1, D)
    shared, summed = summed[SET:], summed[:SET]
    other, squares = lax.optimization_barrier((across(2, summed), squares))
    squares = lax.all_to_all(squares, BOTH, 0, 0)
    grad_norm = jnp.sqrt(jnp.sum(squares[:, 0, 0]))
    factor = jnp.minimum(1.0, CLIP_NORM / (grad_norm + 1e-06))
    summed = jnp.concatenate([jnp.where(far, other, summed), jnp.where(far, summed, other)], 0)
    if plan.all_sets:
        other = across(1, summed)
        summed = jnp.concatenate([jnp.where(odd, other, summed), jnp.where(odd, summed, other)], 0)
    if plan.odd_owner:
        summed = trade_low(summed)
    wide_grad = jnp.pad(summed.astype(F32), ((0, CHUNK), (0, 0)))

    ends = shared[HEADROWS + 1 : HEADROWS + 3]
    shared = trade_low(shared).astype(F32)
    if plan.near:
        for owner in plan.final_reps:
            moved = lax.ppermute(ends, "rep", [(0, owner)]) if owner else ends
            ends = jnp.where(rep == owner, moved, ends)
        ends = ends.astype(F32)
    else:
        ends = shared[HEADROWS + 1 : HEADROWS + 3]
    ends = jnp.pad(ends, ((0, 6), (0, 0)))
    sum_query, reach = shared[HEADROWS : HEADROWS + 1], shared[:HEADS]
    left = jnp.concatenate([class_normed, reach, jnp.zeros((LANES - 1 - HEADS, D), F32)], 0)
    left = jnp.pad(left.T, ((0, CHUNK), (0, 0)))
    right = jnp.concatenate(
        [
            jnp.pad(sum_query, ((0, 0), (0, D))),
            jnp.pad(by_head, ((0, 0), (D, 0))),
            jnp.zeros((LANES - 1 - HEADS, 2 * D), F32),
        ],
        0,
    )
    grad_flat = late_gradient(
        plan, jnp.asarray(plan.late_table)[device], early, wide_grad, left, right, ends
    )
    new_params, new_first, new_second = adam_update(
        params, grad_flat * factor, first_moment, second_moment, LEARNING_RATE
    )
    new_protos, new_proto_first, new_proto_second = adam_update(
        protos, grad_protos * factor, proto_first, proto_second, PROTO_RATE
    )
    new_teacher = TEACHER_MOMENTUM * teacher + (1.0 - TEACHER_MOMENTUM) * new_params
    new_teacher_protos = TEACHER_MOMENTUM * teacher_protos + (1.0 - TEACHER_MOMENTUM) * new_protos
    return (
        new_params,
        new_first,
        new_second,
        new_teacher,
        new_protos,
        new_proto_first,
        new_proto_second,
        new_teacher_protos,
        new_center,
        loss_value,
        grad_norm,
    )


def solution(mesh):
    placed = (
        P(BOTH),
        P(BOTH),
        P(BOTH),
        P(BOTH),
        P("rep", "grp"),
        P("rep", "grp"),
        P("rep", "grp"),
        P("rep", "grp"),
        P("grp"),
        P(BOTH, None, None),
        P(BOTH),
    )
    plan = Plan(mesh.shape["rep"], mesh.shape["grp"])
    return jax.shard_map(
        functools.partial(per_device, plan),
        mesh=mesh,
        in_specs=placed,
        out_specs=placed[:9] + (P(), P()),
        check_vma=False,
    )
```

```python
import functools

import jax
import jax.numpy as jnp
import numpy as np
from jax import lax
from jax.experimental import pallas as pl
from jax.experimental.pallas import tpu as pltpu
from jax.sharding import PartitionSpec as P

D = 768
HEADS = 12
HDIM = 64
F = 3072
PD = 768
NTOK = 197
H = 2048
B = 256
STEP = 10
NPATCH = NTOK - 1

PRECISE = lax.Precision.HIGHEST
STUDENT_TEMP = 0.1
TEACHER_TEMP = 0.04
CENTER_MOMENTUM = 0.9
TEACHER_MOMENTUM = 0.8
CLIP_NORM = 0.05
LEARNING_RATE = 0.03
PROTO_RATE = 0.6
BETA_FIRST = 0.9
BETA_SECOND = 0.999
ADAM_EPSILON = 1e-08
WEIGHT_DECAY = 0.04
BOTH = ("rep", "grp")
LANES = 128
F32 = jnp.float32
BF16 = jnp.bfloat16

SEGMENTS = []
_offset = 0
for _rows, _cols in ((PD + NTOK + 4, D), (D, 3 * D), (D, D), (D, F), (F + 2, D), (D + H, H), (H, B)):
    SEGMENTS.append((_offset, _rows, _cols))
    _offset += _rows * _cols
PFLAT = _offset
WIDTHS = sorted({cols // LANES for _, _, cols in SEGMENTS})

PIECES = []
_offset = 0
for _rows, _cols in (
    (PD + NTOK + 4, D),
    (D, 3 * D),
    (D, D),
    (D, F),
    (F, D),
    (2, D),
    (D, H),
    (H, H),
    (H, B),
):
    PIECES.append((_offset, _rows, _cols))
    _offset += _rows * _cols
FRONT = 192
CHUNK = 128
SET = 288
SHARED = 32
STEPS = 64
AHEAD = 3 * D + F + H
TILE = 16
TOKENS = 208
HEADROWS = 16
VMEM_LIMIT = 62 * 1024 * 1024


SPANS = {
    2: (0, 0),
    3: (D, D),
    4: (2 * D, D + F),
    6: (2 * D + F, 2 * D + F + B + H),
    7: (3 * D + F, 2 * D + F + B),
}
ATT_COLUMN = 2 * D + F + B + 2 * H
SECOND = HEADS * D
CLASS = SECOND + H
ROWS = CLASS + D


def round_up(value, step):
    return -(-value // step) * step


def steps_at_once(count):
    return max(size for size in range(1, 8) if count % size == 0)


def shard_parts(start, stop, table):
    parts = []
    line0 = start // LANES
    for index, (offset, rows, cols) in enumerate(table):
        low, high = max(start, offset), min(stop, offset + rows * cols)
        if low >= high:
            continue
        row0 = (low - offset) // cols
        row1 = -(-(high - offset) // cols)
        parts.append((index, row0, row1 - row0, (offset + row0 * cols) // LANES - line0))
    return parts


FINAL_ROW = round_up(PD + NTOK + 4, 8)


class Plan:
    def __init__(self, reps, groups):
        count = reps * groups
        self.count, self.groups = count, groups
        self.size = PFLAT // count
        self.lines = round_up(-(-self.size // LANES) + 1, STEPS)
        self.steps = self.lines // STEPS
        self.scratch = FRONT + self.lines + 8 * max(WIDTHS) + 16
        table = []
        self.blocks = [[] for _ in SEGMENTS]
        longest = 0
        for device in range(count):
            start = device * self.size
            entry = [start % LANES]
            target = 0
            for index, row0, rows, line in shard_parts(start, start + self.size, SEGMENTS):
                width = SEGMENTS[index][2] // LANES
                skew = row0 % 8
                tiles = -(-(rows + skew) // 8)
                self.blocks[index].append((device, target // TILE, row0 // 8, tiles))
                entry += [
                    WIDTHS.index(width),
                    FRONT + line - skew * width,
                    tiles // 2,
                    tiles % 2,
                    target // TILE,
                ]
                target += tiles * 8 * width
            longest = max(longest, target)
            entry += [-1, 0, 0, 0, 0] * (2 - len(entry) // 5)
            table.append(entry)
        self.buffer = round_up(longest, 16)
        self.lay_table = np.array(table, np.int32)
        edge = SEGMENTS[0][1] * SEGMENTS[0][2]
        owners = [device for device in range(count) if device * self.size < edge]
        self.odd_owner = any(self.place(device)[1] for device in owners)
        self.all_sets = len(owners) > 2
        edge = sum(rows * cols for _, rows, cols in SEGMENTS[:2])
        self.near = all(
            device < 2 * groups for device in range(count) if device * self.size < edge
        )
        offset, rows, cols = PIECES[5]
        self.final_reps = sorted(
            {
                device // groups
                for device in range(count)
                if device * self.size < offset + rows * cols and (device + 1) * self.size > offset
            }
        )
        self.grad_table = self.tabulate(lambda index: index, lambda device, index, row0, chunks: row0)
        self.most_chunks = {
            index: max(
                [1]
                + [
                    entry[3 + place]
                    for entry in self.grad_table
                    for place in range(0, len(entry) - 3, 4)
                    if entry[1 + place] == index
                ]
            )
            for index in (1,) + tuple(SPANS)
        }
        self.fetched = max(
            [HEADS * (self.most_chunks[1] + 1) * CHUNK, H + D]
            + [(chunks + 1) * CHUNK for chunks in self.most_chunks.values()]
        )
        self.late_table = self.tabulate(lambda index: index in (0, 1, 5), self.wide_row)
        self.grad_scratch = FRONT + self.lines + CHUNK * max(WIDTHS) + 16
        self.used = FRONT + self.lines + 8


    def largest(self):
        longest = max(8 * block[3] for blocks in self.blocks for block in blocks)
        return max(len(blocks) for blocks in self.blocks), round_up(longest, LANES) + 2 * LANES

    def place(self, device):
        rep, grp = divmod(device, self.groups)
        return rep // 2 * self.groups + grp, rep % 2

    def tabulate(self, chosen, rows_of):
        table = []
        for device in range(self.count):
            start = device * self.size
            entry = []
            for index, row0, rows, line in shard_parts(start, start + self.size, PIECES):
                if not chosen(index):
                    continue
                skew = row0 % 8
                line -= skew * (PIECES[index][2] // LANES)
                chunks = -(-(rows + skew) // CHUNK)
                entry += [index, FRONT + line, chunks, rows_of(device, index, row0 - skew, chunks)]
            table.append(entry)
        most = max(len(entry) for entry in table) // 4
        for device, entry in enumerate(table):
            entry += [-1, 0, 0, 0] * (most - len(entry) // 4)
            entry.insert(0, device * self.size % LANES)
            entry += [device < self.groups, device % 4 == 1]
        return np.array(table, np.int32)

    def wide_row(self, device, index, row0, chunks):
        if index:
            return row0
        late = row0 >= 2 * SET - 8
        if not self.all_sets:
            if late != device % 2:
                raise ValueError("owner")
            return row0 - (2 * SET - 8) * late
        return row0 + 8 * late


def lay_kernel(plan, tab_ref, x_ref, out_ref, line_ref):
    shift = tab_ref[0]
    lane = lax.broadcasted_iota(jnp.int32, (STEPS + 8, LANES), 1)
    line_ref[pl.ds(0, FRONT), :] = jnp.zeros((FRONT, LANES), F32)
    tail = plan.scratch - FRONT - plan.lines
    line_ref[pl.ds(FRONT + plan.lines, tail), :] = jnp.zeros((tail, LANES), F32)

    def align(step, carry):
        base = pl.multiple_of(step * STEPS, 8)
        here = pltpu.roll(x_ref[pl.ds(base, STEPS + 8), :], shift, 1)
        above = pltpu.roll(here, 1, 0)
        both = jnp.where(lane >= shift, here, above)
        line_ref[pl.ds(pl.multiple_of(FRONT + base, 8), STEPS), :] = both[8:]
        return carry

    lax.fori_loop(0, plan.steps, align, 0, unroll=steps_at_once(plan.steps))
    for part in range(2):
        kind, base, pairs, odd, target = (tab_ref[1 + 5 * part + i] for i in range(5))
        for index, width in enumerate(WIDTHS):

            @pl.when(kind == index)
            def _(width=width):
                def move(step, carry):
                    row = base + step * (TILE * width)
                    goal = (target + step * width) * TILE
                    for tile in range(width):
                        both = line_ref[pl.ds(row + tile, TILE, stride=width), :]
                        place = pl.multiple_of(goal + TILE * tile, TILE)
                        out_ref[pl.ds(place, TILE), :] = both.astype(BF16)
                    return carry

                def last(step, carry):
                    row = base + pairs * (TILE * width)
                    goal = (target + pairs * width) * TILE
                    for tile in range(0, width, 2):
                        both = [
                            line_ref[pl.ds(row + tile + side, 8, stride=width), :]
                            for side in range(2)
                        ]
                        place = pl.multiple_of(goal + 8 * tile, TILE)
                        out_ref[pl.ds(place, TILE), :] = jnp.concatenate(both, 0).astype(BF16)
                    return carry

                lax.fori_loop(0, pairs, move, 0)
                lax.fori_loop(0, odd, last, 0)


def lay_out(plan, table, flat):
    padded = jnp.pad(flat, (8 * LANES, plan.lines * LANES - plan.size))
    lines = padded.reshape(8 + plan.lines, LANES)
    return pl.pallas_call(
        functools.partial(lay_kernel, plan),
        out_shape=jax.ShapeDtypeStruct((plan.buffer, LANES), BF16),
        in_specs=[
            pl.BlockSpec(memory_space=pltpu.SMEM),
            pl.BlockSpec(memory_space=pltpu.VMEM),
        ],
        out_specs=pl.BlockSpec(memory_space=pltpu.VMEM),
        scratch_shapes=[pltpu.VMEM((plan.scratch, LANES), F32)],
        compiler_params=pltpu.CompilerParams(vmem_limit_bytes=24 * 1024 * 1024),
    )(table, lines)


class Shards:
    def __init__(self, plan, gathered_ref, ref, sems, order):
        self.plan, self.ref, self.sems, self.waited = plan, ref, sems, set()
        self.copies = {}
        for device in order:
            place, side = plan.place(device)
            copy = pltpu.make_async_copy(
                gathered_ref.at[place, side], ref.at[device], sems.at[device]
            )
            copy.start()
            self.copies[device] = copy

    def wait(self, device):
        if device in self.copies:
            self.copies.pop(device).wait()

    def finish(self):
        for device in list(self.copies):
            self.wait(device)

    def blocks(self, index, first, count):
        found = [
            block
            for block in self.plan.blocks[index]
            if 8 * block[2] < first + count and 8 * (block[2] + block[3]) > first
        ]
        for block in found:
            self.wait(block[0])
        return found

    def eight(self, index, tile, pair, side):
        width = SEGMENTS[index][2] // LANES
        total = None
        for device, target, tile0, tiles in self.plan.blocks[index]:
            own = tile - tile0
            if not 0 <= own < tiles:
                continue
            if own < tiles // 2 * 2:
                both = self.ref[device, target + own // 2 * width + 2 * pair + side]
                half = own % 2
            else:
                both = self.ref[device, target + tiles // 2 * width + pair]
                half = side
            piece = both.astype(F32)[8 * half : 8 * half + 8]
            total = piece if total is None else total + piece
        return total

    def assemble(self, index, out_ref):
        width = SEGMENTS[index][2] // LANES
        rows = out_ref.shape[0]
        self.blocks(index, 0, rows)

        def column(pair, carry):
            for side in range(2):
                lanes = pl.ds(pl.multiple_of(pair * 2 * LANES + side * LANES, LANES), LANES)
                for group in range(rows // TILE):
                    both = [
                        self.eight(index, 2 * group + half, pair, side) for half in range(2)
                    ]
                    out_ref[TILE * group : TILE * (group + 1), lanes] = jnp.concatenate(
                        both, 0
                    ).astype(BF16)
            return carry

        lax.fori_loop(0, width // 2, column, 0)

    def columns(self, index, block, pair):
        width = SEGMENTS[index][2] // LANES
        device, target, _, tiles = block
        sides = []
        for side in range(2):
            pieces = [
                self.ref[device, target + step * width + 2 * pair + side]
                for step in range(tiles // 2)
            ]
            if tiles % 2:
                both = self.ref[device, target + tiles // 2 * width + pair].astype(F32)
                pieces.append(both[8 * side : 8 * side + 8].astype(BF16))
            sides.append(jnp.concatenate(pieces, 0))
        return jnp.concatenate(sides, 1)

    def times(self, index, first, values, left_ref, out_ref):
        views, count = values.shape
        blocks = self.blocks(index, first, count)
        top = max([first + count] + [8 * (tile0 + tiles) for _, _, tile0, tiles in blocks])
        top = round_up(top, LANES) + LANES
        parts = [values, jnp.zeros((views, top - first - count), F32)]
        if first:
            parts.insert(0, jnp.zeros((views, first), F32))
        wide = jnp.concatenate(parts, 1)
        for number, (_, _, tile0, tiles) in enumerate(blocks):
            start = 8 * tile0 // LANES * LANES
            turn = 8 * tile0 - start
            piece = wide[:, start : start + round_up(turn + 8 * tiles, LANES)]
            if turn:
                piece = pltpu.roll(piece, piece.shape[1] - turn, 1)
            left_ref[number, :, : 8 * tiles] = piece[:, : 8 * tiles]

        def column(pair, carry):
            total = jnp.zeros((views, 2 * LANES), F32)
            for number, block in enumerate(blocks):
                left = left_ref[number, :, : 8 * block[3]].astype(BF16)
                total += product(left, self.columns(index, block, pair))
            out_ref[:, pl.ds(pl.multiple_of(pair * 2 * LANES, LANES), 2 * LANES)] = total
            return carry

        lax.fori_loop(0, SEGMENTS[index][2] // LANES // 2, column, 0, unroll=4)


    def back(self, index, first, count, values, grad_ref, left_ref, wide_ref):
        views, cols = values.shape
        grad_ref[:, :cols] = values
        blocks = self.blocks(index, first, count)
        top = max([first + count] + [8 * (tile0 + tiles) for _, _, tile0, tiles in blocks])
        wide_ref[:, : round_up(top, LANES) + LANES] = jnp.zeros(
            (views, round_up(top, LANES) + LANES), F32
        )
        for number, (_, _, _, tiles) in enumerate(blocks):
            size = round_up(8 * tiles, LANES) + LANES
            left_ref[number, :, :size] = jnp.zeros((views, size), F32)

        def column(pair, carry):
            lanes = pl.ds(pl.multiple_of(pair * 2 * LANES, LANES), 2 * LANES)
            left = grad_ref[:, lanes].astype(BF16)
            for number, block in enumerate(blocks):
                size = 8 * block[3]
                left_ref[number, :, :size] += product_t(left, self.columns(index, block, pair))
            return carry

        lax.fori_loop(0, cols // LANES // 2, column, 0, unroll=4)
        for number, (_, _, tile0, tiles) in enumerate(blocks):
            start = 8 * tile0 // LANES * LANES
            turn = 8 * tile0 - start
            size = round_up(turn + 8 * tiles, LANES)
            piece = left_ref[number, :, :size]
            if turn:
                piece = pltpu.roll(piece, turn, 1)
            wide_ref[:, start : start + size] += piece
        return wide_ref[:, first : first + count]


def product(left, right):
    return jnp.dot(left, right, preferred_element_type=F32)


def product_t(left, right):
    return lax.dot_general(
        left, right, (((left.ndim - 1,), (1,)), ((), ())), preferred_element_type=F32
    )


def normal_share(values):
    return 0.5 + 0.5 * lax.erf(values * 2**-0.5)


def activate(values):
    return values * normal_share(values)


def gelu_back(values, grad):
    density = jnp.exp(-0.5 * values * values) * (2 * np.pi) ** -0.5
    return grad * (normal_share(values) + values * density)


def normalised(values):
    centred = values - jnp.mean(values, -1, keepdims=True)
    scale = lax.rsqrt(jnp.mean(centred * centred, -1, keepdims=True) + 1e-06)
    return centred * scale, scale


def norm_back(grad, gain, unit, scale):
    inner = grad * gain
    return scale * (
        inner
        - jnp.mean(inner, -1, keepdims=True)
        - unit * jnp.mean(inner * unit, -1, keepdims=True)
    )


def head_mask():
    shape = (HEADROWS, D)
    return lax.broadcasted_iota(jnp.int32, shape, 0) == (
        lax.broadcasted_iota(jnp.int32, shape, 1) // HDIM
    )


def token_norms(unit, norms, class_normed):
    token = lax.broadcasted_iota(jnp.int32, (TOKENS, D), 0)
    normed = unit * norms[0:1] + norms[1:2]
    return jnp.where(
        token < NPATCH, normed, jnp.where(token == NPATCH, class_normed, 0.0)
    ).astype(BF16)


def forward_kernel(
    plan,
    gathered_ref,
    pixels_ref,
    turn_ref,
    unit_out,
    scale_out,
    probs_ref,
    mixed_ref,
    looked_ref,
    class_ref,
    qkv_out,
    hidden_ref,
    one_ref,
    two_ref,
    bottle_ref,
    middle_ref,
    rows_ref,
    pack_out,
    shards_ref,
    wide_ref,
    place_ref,
    left_ref,
    sums_ref,
    pack_ref,
    unit_ref,
    scale_ref,
    qkv_ref,
    out_sems,
    sems,
):
    shards = Shards(plan, gathered_ref, shards_ref, sems, range(plan.count))
    views = pixels_ref.shape[0]
    temper = HDIM ** (-0.5)
    shards.assemble(0, wide_ref)
    position = wide_ref[PD : PD + TOKENS].astype(F32)
    place_ref[...] = pltpu.roll(position, TOKENS - 1, 0)
    class_place = position[0:1]
    norms = position[NTOK : NTOK + 4]
    class_unit, class_scale = normalised(class_place)
    class_normed = (class_unit * norms[0:1] + norms[1:2]).astype(BF16).astype(F32)
    shards.assemble(1, qkv_ref)
    qkv_copy = pltpu.make_async_copy(qkv_ref, qkv_out, out_sems.at[4])
    qkv_copy.start()
    mask = head_mask()
    query = jnp.broadcast_to(class_normed, (HEADROWS, D)).astype(BF16)
    query = product(query, qkv_ref[:, :D]).astype(BF16).astype(F32)
    by_head = jnp.where(mask, query, 0.0).astype(BF16)
    looked = product_t(by_head, qkv_ref[:, D : 2 * D]).astype(BF16)
    looked_ref[...] = looked

    def copies(v):
        slot = lax.rem(v, 2)
        return (
            pltpu.make_async_copy(unit_ref.at[slot], unit_out.at[v], out_sems.at[slot]),
            pltpu.make_async_copy(scale_ref.at[slot], scale_out.at[v], out_sems.at[2 + slot]),
        )

    def view(v, carry):
        embedded = product(pixels_ref[v], wide_ref[:PD]) + place_ref[...]
        unit, scale = normalised(embedded)

        @pl.when(v >= 2)
        def _():
            for copy in copies(v - 2):
                copy.wait()

        unit_ref[lax.rem(v, 2)] = unit
        scale_ref[lax.rem(v, 2)] = jnp.broadcast_to(scale, (TOKENS, LANES))
        for copy in copies(v):
            copy.start()
        normed = token_norms(unit, norms, class_normed)
        scores = product_t(looked, normed) * temper
        token = lax.broadcasted_iota(jnp.int32, scores.shape, 1)
        scores = jnp.where(token < NTOK, scores, -1e30)
        top = jnp.max(scores, -1, keepdims=True)
        top = top + jnp.log(jnp.sum(jnp.exp(scores - top), -1, keepdims=True))
        head = lax.broadcasted_iota(jnp.int32, scores.shape, 0)
        probs = jnp.where(head < HEADS, jnp.exp(scores - top), 0.0)
        probs_ref[v] = probs
        mixed_ref[v] = product(probs.astype(BF16), normed).astype(BF16)
        return carry

    lax.fori_loop(0, views, view, 0, unroll=4)
    mixed = mixed_ref[...].reshape(views * HEADROWS, D)
    valued = product(mixed, qkv_ref[:, 2 * D :]).reshape(views, HEADROWS, D)
    attended = jnp.sum(jnp.where(mask[None], valued, 0.0), 1).astype(BF16)
    pack_ref[:, :D] = attended.astype(F32)
    shards.times(2, 0, pack_ref[:, :D], left_ref, sums_ref)
    middle = class_place + sums_ref[...]
    unit, scale = normalised(middle)
    middle_ref[0], middle_ref[1] = unit, jnp.broadcast_to(scale, (views, D))
    normed = (unit * norms[2:3] + norms[3:4]).astype(BF16)
    pack_ref[:, D : 2 * D] = normed.astype(F32)
    shards.times(3, 0, pack_ref[:, D : 2 * D], left_ref, hidden_ref)
    act = activate(hidden_ref[...]).astype(BF16)
    pack_ref[:, 2 * D : 2 * D + F] = act.astype(F32)
    shards.times(4, 0, act.astype(F32), left_ref, sums_ref)
    unit, scale = normalised(middle + sums_ref[...])
    middle_ref[2], middle_ref[3] = unit, jnp.broadcast_to(scale, (views, D))
    final = jnp.concatenate(
        [shards.eight(4, F // 8, tile // 2, tile % 2) for tile in range(D // LANES)], 1
    )
    cls = (unit * final[0:1] + final[1:2]).astype(BF16)
    place = 2 * D + F
    pack_ref[:, place : place + D] = cls.astype(F32)
    shards.times(5, 0, cls.astype(F32), left_ref, one_ref)
    first = activate(one_ref[...]).astype(BF16)
    pack_ref[:, place + D : AHEAD] = first.astype(F32)
    shards.times(5, D, first.astype(F32), left_ref, two_ref)
    second = activate(two_ref[...]).astype(BF16)
    shards.times(6, 0, second.astype(F32), left_ref, bottle_ref)
    bottle = bottle_ref[...]
    scale = lax.rsqrt(jnp.sum(bottle * bottle, -1, keepdims=True) + 1e-06)
    rows = product(turn_ref[...], (bottle * scale).astype(BF16)).astype(BF16)
    rows_ref[...] = jnp.broadcast_to(rows[None], rows_ref.shape)
    mixed = mixed_ref[...].astype(F32)
    for head in range(HEADS):
        pack_out[:, head * D : (head + 1) * D] = mixed[:, head, :].astype(BF16)
    pack_out[:, SECOND:CLASS] = second
    row = lax.broadcasted_iota(jnp.int32, (views, D), 0)
    pack_out[:, CLASS:ROWS] = jnp.where(
        row == 0, class_normed, jnp.where(row == 1, query[0:1], 0.0)
    ).astype(BF16)
    pack_out[:, ROWS : ROWS + AHEAD] = pack_ref[...].astype(BF16)
    pack_out[:, ROWS + AHEAD :] = jnp.zeros((views, pack_out.shape[1] - ROWS - AHEAD), BF16)
    class_ref[...] = jnp.concatenate(
        [
            class_unit,
            class_normed,
            query[0:1],
            jnp.broadcast_to(class_scale, (1, D)),
            norms,
            final,
        ],
        0,
    )
    for v in range(max(0, views - 2), views):
        for copy in copies(v):
            copy.wait()
    qkv_copy.wait()
    shards.finish()


def forward(plan, gathered, pixels, turn):
    views = pixels.shape[0]
    shapes = [
        ((views, TOKENS, D), F32),
        ((views, TOKENS, LANES), F32),
        ((views, HEADROWS, TOKENS), F32),
        ((views, HEADROWS, D), BF16),
        ((HEADROWS, D), BF16),
        ((16, D), F32),
        ((D, 3 * D), BF16),
        ((views, F), F32),
        ((views, H), F32),
        ((views, H), F32),
        ((views, B), F32),
        ((4, views, D), F32),
        ((plan.count, views, B), BF16),
        ((views, ROWS + AHEAD + (max(plan.most_chunks.values()) + 1) * CHUNK), BF16),
    ]
    most, longest = plan.largest()
    return pl.pallas_call(
        functools.partial(forward_kernel, plan),
        out_shape=[jax.ShapeDtypeStruct(shape, dtype) for shape, dtype in shapes],
        in_specs=[pl.BlockSpec(memory_space=pl.ANY)]
        + [pl.BlockSpec(memory_space=pltpu.VMEM)] * 2,
        out_specs=[
            pl.BlockSpec(memory_space=pl.ANY if index in (0, 1, 6) else pltpu.VMEM)
            for index in range(len(shapes))
        ],
        scratch_shapes=[
            pltpu.VMEM((plan.count, plan.buffer // TILE, TILE, LANES), BF16),
            pltpu.VMEM((round_up(PD + NTOK + 4, TILE), D), BF16),
            pltpu.VMEM((TOKENS, D), F32),
            pltpu.VMEM((most, views, longest), F32),
            pltpu.VMEM((views, D), F32),
            pltpu.VMEM((views, AHEAD), F32),
            pltpu.VMEM((2, TOKENS, D), F32),
            pltpu.VMEM((2, TOKENS, LANES), F32),
            pltpu.VMEM((D, 3 * D), BF16),
            pltpu.SemaphoreType.DMA((5,)),
            pltpu.SemaphoreType.DMA((plan.count,)),
        ],
        compiler_params=pltpu.CompilerParams(vmem_limit_bytes=VMEM_LIMIT),
        cost_estimate=pl.CostEstimate(
            flops=60 * 10**9, bytes_accessed=40 * 10**6, transcendentals=10**5
        ),
    )(gathered, pixels, turn)


def proto_kernel(
    start_ref,
    rows_ref,
    columns_ref,
    others_ref,
    center_ref,
    note_ref,
    center_out_ref,
    student_ref,
    teacher_ref,
    sums_ref,
):
    count, groups = rows_ref.shape[1], note_ref.shape[0]
    views = (note_ref.shape[1] - 8 * -(-count // B)) // 3
    logits = product(rows_ref[1], others_ref[...])
    center = center_ref[...]
    center_out_ref[...] = CENTER_MOMENTUM * center + (1.0 - CENTER_MOMENTUM) * jnp.mean(
        logits, 0, keepdims=True
    )
    exp_teacher = jnp.exp((logits - center) / TEACHER_TEMP)
    teacher_ref[...] = exp_teacher
    scaled = product(rows_ref[0], columns_ref[...]) / STUDENT_TEMP
    exp_student = jnp.exp(scaled)
    student_ref[...] = exp_student
    turned = []
    for which, values in enumerate((exp_student, exp_teacher, exp_teacher * scaled)):
        total = jnp.broadcast_to(jnp.sum(values, 1, keepdims=True), (count, LANES))
        turned.append(total.T[0:1])
        if which < 2:
            sums_ref[:, which * LANES : (which + 1) * LANES] = total
    turned = jnp.concatenate(turned + [jnp.zeros((5, count), F32)], 0)
    for step in range(-(-count // B)):
        part = turned[:, step * B : (step + 1) * B]
        lines = slice(3 * views + 8 * step, 3 * views + 8 * (step + 1))
        note_ref[:, lines, : part.shape[1]] = jnp.broadcast_to(part[None], (groups,) + part.shape)
        if part.shape[1] < B:
            note_ref[:, lines, part.shape[1] :] = jnp.zeros((groups, 8, B - part.shape[1]), F32)
    start = pl.multiple_of(start_ref[0], 8)
    band, parts = groups * views, []
    for source in (student_ref, teacher_ref):
        rest = source[pl.ds(start, band), :]
        for _ in range(3):
            parts.append(rest.astype(BF16))
            rest = rest - parts[-1].astype(F32)
    pulls = product_t(jnp.concatenate(parts, 0), columns_ref[...])
    for which in range(2):
        first = 3 * which * band
        total = pulls[first : first + band] + pulls[first + band : first + 2 * band]
        total = total + pulls[first + 2 * band : first + 3 * band]
        note_ref[:, which * views : (which + 1) * views, :] = total.reshape(groups, views, B)
    own = sums_ref[pl.ds(start, groups * views), :]
    note_ref[:, 2 * views : 3 * views, :] = own.reshape(groups, views, B)


def prototypes(start, rows, columns, others, center, groups, views):
    count, width = rows.shape[1], columns.shape[1]
    shapes = [(groups, 3 * views + 8 * -(-count // B), B), (1, width)]
    return pl.pallas_call(
        proto_kernel,
        out_shape=[jax.ShapeDtypeStruct(shape, F32) for shape in shapes],
        in_specs=[pl.BlockSpec(memory_space=pltpu.SMEM)]
        + [pl.BlockSpec(memory_space=pltpu.VMEM)] * 4,
        out_specs=[pl.BlockSpec(memory_space=pltpu.VMEM)] * len(shapes),
        scratch_shapes=[pltpu.VMEM((count, width), F32)] * 2
        + [pltpu.VMEM((count, 2 * LANES), F32)],
        compiler_params=pltpu.CompilerParams(vmem_limit_bytes=32 * 1024 * 1024),
        cost_estimate=pl.CostEstimate(
            flops=3 * 10**9, bytes_accessed=6 * 10**6, transcendentals=10**6
        ),
    )(start, rows, columns, others, center)


def proto_back_kernel(
    start_ref,
    rows_ref,
    columns_ref,
    others_ref,
    center_ref,
    totals_ref,
    table_ref,
    scale_ref,
    grad_ref,
    square_ref,
    work_ref,
):
    count = rows_ref.shape[1]
    totals = jnp.broadcast_to(totals_ref[0:2][:, None, :], (2, 8, count))
    student, teacher = (totals[which].T[:, :1] for which in range(2))
    logits = product(rows_ref[1], others_ref[...])
    targets = jnp.exp((logits - center_ref[...]) / TEACHER_TEMP) / teacher
    scaled = product(rows_ref[0], columns_ref[...]) / STUDENT_TEMP
    grad = (jnp.exp(scaled) / student - targets) / STUDENT_TEMP
    work_ref[...] = jnp.dot(
        rows_ref[0].astype(F32).T, grad, precision=PRECISE, preferred_element_type=F32
    )
    scale = scale_ref[...]
    inner = jnp.sum(work_ref[...] * table_ref[...], 0, keepdims=True)
    start = pl.multiple_of(start_ref[0], 8)
    lines = pl.ds(start, grad_ref.shape[0])
    grad = work_ref[lines, :] * scale - table_ref[lines, :] * (scale * scale * scale * inner)
    grad_ref[...] = grad
    square_ref[...] = jnp.broadcast_to(jnp.sum(grad * grad, keepdims=True), square_ref.shape)


def prototypes_back(start, depth, *values):
    count, width = values[0].shape[1], values[1].shape[1]
    shapes = [(depth, width), (8, LANES)]
    return pl.pallas_call(
        proto_back_kernel,
        out_shape=[jax.ShapeDtypeStruct(shape, F32) for shape in shapes],
        in_specs=[pl.BlockSpec(memory_space=pltpu.SMEM)]
        + [pl.BlockSpec(memory_space=pltpu.VMEM)] * len(values),
        out_specs=[pl.BlockSpec(memory_space=pltpu.VMEM)] * len(shapes),
        scratch_shapes=[pltpu.VMEM((B, width), F32)],
        compiler_params=pltpu.CompilerParams(vmem_limit_bytes=32 * 1024 * 1024),
        cost_estimate=pl.CostEstimate(
            flops=3 * 10**9, bytes_accessed=6 * 10**6, transcendentals=10**6
        ),
    )(start, *values)


def rows_back_kernel(
    plan,
    low_ref,
    gathered_ref,
    note_ref,
    class_ref,
    hidden_ref,
    one_ref,
    two_ref,
    bottle_ref,
    middle_ref,
    pack_ref,
    stream_ref,
    extra_ref,
    shards_ref,
    left_ref,
    values_ref,
    wide_ref,
    sems,
):
    used = {block[0] for blocks in plan.blocks[2:] for block in blocks}
    shards = Shards(plan, gathered_ref, shards_ref, sems, sorted(used, reverse=True))
    work = (values_ref, left_ref, wide_ref)
    norms, final = class_ref[4:8], class_ref[8:10]

    views = bottle_ref.shape[0]
    note = jnp.sum(note_ref[...], 0)
    sums = note[2 * views : 3 * views]
    student, teacher = sums[:, :1], sums[:, LANES : LANES + 1]
    grad_rows = (note[:views] / student - note[views : 2 * views] / teacher) / STUDENT_TEMP
    grad_rows = jnp.where(low_ref[0] == 0, 0.0, grad_rows).astype(BF16).astype(F32)
    bottle = bottle_ref[...]
    scale = lax.rsqrt(jnp.sum(bottle * bottle, -1, keepdims=True) + 1e-06)
    grad_bottle = (
        grad_rows * scale - bottle * scale**3 * jnp.sum(grad_rows * bottle, -1, keepdims=True)
    ).astype(BF16)
    place = 2 * D + F
    pack_ref[:, place : place + B] = grad_bottle
    grad_two = shards.back(6, 0, H, grad_bottle.astype(F32), *work)
    grad_two = gelu_back(two_ref[...], grad_two).astype(BF16)
    pack_ref[:, place + B : place + B + H] = grad_two
    grad_one = shards.back(5, D, H, grad_two.astype(F32), *work)
    grad_one = gelu_back(one_ref[...], grad_one).astype(BF16)
    pack_ref[:, place + B + H : place + B + 2 * H] = grad_one
    grad_cls = shards.back(5, 0, D, grad_one.astype(F32), *work)
    unit, scale = middle_ref[2], middle_ref[3]
    gain_last = jnp.sum(grad_cls * unit, 0, keepdims=True)
    shift_last = jnp.sum(grad_cls, 0, keepdims=True)
    grad_stream = norm_back(grad_cls, final[0:1], unit, scale)
    grad_branch = grad_stream.astype(BF16)
    pack_ref[:, D + F : 2 * D + F] = grad_branch
    grad_hidden = shards.back(4, 0, F, grad_branch.astype(F32), *work)
    grad_hidden = gelu_back(hidden_ref[...], grad_hidden).astype(BF16)
    pack_ref[:, D : D + F] = grad_hidden
    grad_normed = shards.back(3, 0, D, grad_hidden.astype(F32), *work)
    unit, scale = middle_ref[0], middle_ref[1]
    extra_ref[...] = jnp.concatenate(
        [
            jnp.sum(grad_normed * unit, 0, keepdims=True),
            jnp.sum(grad_normed, 0, keepdims=True),
            gain_last,
            shift_last,
            jnp.zeros((4, D), F32),
        ],
        0,
    )
    grad_middle = grad_stream + norm_back(grad_normed, norms[2:3], unit, scale)
    stream_ref[...] = grad_middle
    grad_mixed = grad_middle.astype(BF16)
    pack_ref[:, :D] = grad_mixed
    grad_att = shards.back(2, 0, D, grad_mixed.astype(F32), *work).astype(BF16)
    pack_ref[:, place + B + 2 * H : place + B + 2 * H + D] = grad_att
    shards.finish()


def rows_back(plan, low, gathered, note, kept):
    views = kept[-1].shape[1]
    shapes = [((views, 3 * D + F + B + 2 * H), BF16), ((views, D), F32), ((8, D), F32)]
    most, longest = plan.largest()
    return pl.pallas_call(
        functools.partial(rows_back_kernel, plan),
        out_shape=[jax.ShapeDtypeStruct(shape, dtype) for shape, dtype in shapes],
        in_specs=[pl.BlockSpec(memory_space=pltpu.SMEM), pl.BlockSpec(memory_space=pl.ANY)]
        + [pl.BlockSpec(memory_space=pltpu.VMEM)] * (1 + len(kept)),
        out_specs=[pl.BlockSpec(memory_space=pltpu.VMEM)] * len(shapes),
        scratch_shapes=[
            pltpu.VMEM((plan.count, plan.buffer // TILE, TILE, LANES), BF16),
            pltpu.VMEM((most, views, longest), F32),
            pltpu.VMEM((views, F), F32),
            pltpu.VMEM((views, F + 2 * LANES), F32),
            pltpu.SemaphoreType.DMA((plan.count,)),
        ],
        compiler_params=pltpu.CompilerParams(vmem_limit_bytes=40 * 1024 * 1024),
        cost_estimate=pl.CostEstimate(
            flops=30 * 10**9, bytes_accessed=30 * 10**6, transcendentals=10**5
        ),
    )(low, gathered, note, *kept)


def tokens_back_kernel(
    odd_ref,
    behind_ref,
    stream_ref,
    ends_ref,
    unit_ref,
    scale_ref,
    probs_ref,
    looked_ref,
    class_ref,
    qkv_ref,
    pixels_ref,
    first_ref,
    second_ref,
    kept_ref,
    sent_ref,
    patch_ref,
    place_ref,
    reach_ref,
    back_ref,
    mixed_ref,
    rows_ref,
):
    v = pl.program_id(0)
    views = stream_ref.shape[0]
    temper = HDIM ** (-0.5)
    norms = class_ref[4:8]
    class_unit, class_normed, class_scale = (class_ref[row : row + 1] for row in (0, 1, 3))

    @pl.when(v == 0)
    def _():
        place = 2 * D + F + B + 2 * H
        grad_att = behind_ref[:, place : place + D].astype(F32)
        spread = jnp.where(head_mask()[None], grad_att[:, None, :], 0.0).astype(BF16)
        back = product_t(spread.reshape(views * HEADROWS, D), qkv_ref[:, 2 * D :])
        back_ref[...] = back.astype(BF16).reshape(views, HEADROWS, D)
        patch_ref[...] = jnp.zeros(patch_ref.shape, F32)
        place_ref[...] = jnp.zeros(place_ref.shape, F32)
        reach_ref[...] = jnp.zeros(reach_ref.shape, F32)
        rows_ref[...] = jnp.zeros(rows_ref.shape, F32)

    unit = unit_ref[0]
    scale = scale_ref[0][:, :1]
    normed = token_norms(unit, norms, class_normed)
    back = back_ref[v]
    probs = probs_ref[0]
    grad_probs = product_t(back, normed)
    delta = jnp.sum(probs * grad_probs, -1, keepdims=True)
    grad_scores = (probs * (grad_probs - delta)).astype(BF16)
    reach = product(grad_scores, normed) * temper
    mixed_ref[v] = reach.astype(BF16)
    reach_ref[...] += reach
    left = jnp.concatenate([grad_scores.astype(F32), probs.astype(BF16).astype(F32)], 0)
    looked = (looked_ref[...].astype(F32) * temper).astype(BF16)
    grad = product(left.T.astype(BF16), jnp.concatenate([looked, back], 0))
    row = lax.broadcasted_iota(jnp.int32, (8, D), 0)
    rows_ref[0] += jnp.where(row == v, grad[NPATCH : NPATCH + 1], 0.0)
    token = lax.broadcasted_iota(jnp.int32, (TOKENS, D), 0)
    grad = jnp.where(token < NPATCH, grad, 0.0)
    rows_ref[1, 0:1] += jnp.sum(grad * unit, 0, keepdims=True)
    rows_ref[2, 0:1] += jnp.sum(grad, 0, keepdims=True)
    stream = norm_back(grad, norms[0:1], unit, scale)
    place_ref[...] += stream
    patch_ref[...] += product(pixels_ref[0], stream.astype(BF16))

    @pl.when(v == views - 1)
    def _():
        keyed = product(mixed_ref[...].reshape(views * HEADROWS, D), qkv_ref[:, D : 2 * D])
        keyed = jnp.where(head_mask()[None], keyed.reshape(views, HEADROWS, D), 0.0)
        grad_query = jnp.sum(keyed, 1).astype(BF16)
        class_row = rows_ref[0][:views] + product_t(grad_query, qkv_ref[:, :D])
        class_stream = norm_back(class_row, norms[0:1], class_unit, class_scale)
        class_stream = class_stream + stream_ref[...]
        ends = [
            (0, jnp.sum(class_stream, 0, keepdims=True)),
            (NTOK, rows_ref[1, 0:1] + jnp.sum(class_row * class_unit, 0, keepdims=True)),
            (NTOK + 1, rows_ref[2, 0:1] + jnp.sum(class_row, 0, keepdims=True)),
            (NTOK + 2, ends_ref[0:1]),
            (NTOK + 3, ends_ref[1:2]),
        ]
        tail = pltpu.roll(place_ref[...], 1, 0)
        for row, value in ends:
            tail = jnp.where(token == row, value, tail)
        upper = 2 * SET - 8
        rest = jnp.zeros((2 * SET - (PD - upper) - TOKENS, D), F32)
        query_row = lax.broadcasted_iota(jnp.int32, (8, D), 0) == 0
        total = jnp.sum(grad_query.astype(F32), 0, keepdims=True)
        shared = [reach_ref[...], jnp.where(query_row, total, pltpu.roll(ends_ref[...], 7, 0))]
        shared = jnp.concatenate(shared + [jnp.zeros((SHARED - HEADROWS - 8, D), F32)], 0)
        kept_ref[2 * SET :] = shared
        sent_ref[2 * SET :] = shared.astype(BF16)
        last = jnp.concatenate([patch_ref[upper:], tail, rest], 0)

        @pl.when(odd_ref[0] == 0)
        def _():
            kept_ref[: 2 * SET] = patch_ref[: 2 * SET]
            sent_ref[: 2 * SET] = last.astype(BF16)

        @pl.when(odd_ref[0] != 0)
        def _():
            kept_ref[: 2 * SET] = last
            sent_ref[: 2 * SET] = patch_ref[: 2 * SET].astype(BF16)


def tokens_back(odd, behind, grad_middle, ends, kept, pixels, *before):
    views = grad_middle.shape[0]

    def whole(values):
        return pl.BlockSpec(values.shape, lambda v: (0,) * values.ndim)

    def by_view(values):
        return pl.BlockSpec((1,) + values.shape[1:], lambda v: (v,) + (0,) * (values.ndim - 1))

    unit, scale, probs, looked, classes, qkv_w = kept
    shape = (2 * SET + SHARED, D)
    return pl.pallas_call(
        tokens_back_kernel,
        grid=(views,),
        out_shape=[jax.ShapeDtypeStruct(shape, F32), jax.ShapeDtypeStruct(shape, BF16)],
        in_specs=[
            pl.BlockSpec(memory_space=pltpu.SMEM),
            whole(behind),
            whole(grad_middle),
            whole(ends),
            by_view(unit),
            by_view(scale),
            by_view(probs),
            whole(looked),
            whole(classes),
            whole(qkv_w),
            by_view(pixels),
        ]
        + [pl.BlockSpec(memory_space=pl.ANY)] * len(before),
        out_specs=[pl.BlockSpec(shape, lambda v: (0, 0))] * 2,
        scratch_shapes=[
            pltpu.VMEM((PD, D), F32),
            pltpu.VMEM((TOKENS, D), F32),
            pltpu.VMEM((HEADROWS, D), F32),
            pltpu.VMEM((views, HEADROWS, D), BF16),
            pltpu.VMEM((views, HEADROWS, D), BF16),
            pltpu.VMEM((3, 8, D), F32),
        ],
        compiler_params=pltpu.CompilerParams(vmem_limit_bytes=60 * 1024 * 1024),
        cost_estimate=pl.CostEstimate(
            flops=15 * 10**9, bytes_accessed=15 * 10**6, transcendentals=10**5
        ),
    )(odd, behind, grad_middle, ends, unit, scale, probs, looked, classes, qkv_w, pixels, *before)


def early_kernel(
    plan,
    most,
    tab_ref,
    common_hbm,
    behind_hbm,
    rest_ref,
    *refs,
):
    line_out, square_ref, common_ref, behind_ref, class_ref, line_ref, sem, class_sem = refs[-8:]
    slab = (plan.most_chunks[1] + 1) * CHUNK
    class_copy = pltpu.make_async_copy(
        common_hbm.at[pl.ds(0, TILE), pl.ds(CLASS, D)], class_ref, class_sem
    )
    class_copy.start()
    line_ref[pl.ds(0, plan.used), :] = jnp.zeros((plan.used, LANES), F32)

    def fetch(source, target, column, size):
        which = 0 if target is common_ref else 1
        copy = pltpu.make_async_copy(
            source.at[:, pl.ds(column, size)], target.at[:, pl.ds(0, size)], sem.at[which]
        )
        copy.start()
        return copy

    def turned(lane):
        start = pl.multiple_of(lane // LANES * LANES, LANES)
        both = common_ref[:, pl.ds(start, 2 * LANES)].astype(F32)
        both = pltpu.roll(both, lax.rem(2 * LANES - (lane - start), 2 * LANES), 1)
        return both[:, :LANES].T.astype(BF16)

    def store(goal, width, tile, block):
        line_ref[pl.ds(goal + tile, block.shape[0], stride=width), :] = block

    for part in range(most):
        kind, base, chunks, row0 = (tab_ref[1 + 4 * part + i] for i in range(4))
        for index, (lane, column) in SPANS.items():
            cols = PIECES[index][2]
            width = cols // LANES
            size = (plan.most_chunks[index] + 1) * CHUNK

            @pl.when(kind == index)
            def _(lane=lane, column=column, cols=cols, width=width, size=size):
                skew = lax.rem(row0, LANES)
                place = pl.multiple_of(ROWS + lane + row0 - skew, LANES)
                copies = [
                    fetch(common_hbm, common_ref, place, size),
                    fetch(behind_hbm, behind_ref, column, cols),
                ]
                for copy in copies:
                    copy.wait()

                def move(step, carry):
                    goal = base + step * (CHUNK * width)
                    block = product(turned(skew + step * CHUNK), behind_ref[:, :cols])
                    for tile in range(width):
                        store(goal, width, tile, block[:, tile * LANES : (tile + 1) * LANES])
                    return carry

                lax.fori_loop(0, chunks, move, 0)

        @pl.when(kind == 8)
        def _():
            copies = [
                fetch(behind_hbm, behind_ref, 2 * D + F, B),
                fetch(common_hbm, common_ref, SECOND, H + D),
            ]
            for copy in copies:
                copy.wait()

            def move(step, carry):
                for own in range(2):
                    place = 2 * step + own
                    block = product(turned(row0 + place * CHUNK), behind_ref[:, :B])
                    for tile in range(B // LANES):
                        piece = block[:, tile * LANES : (tile + 1) * LANES]
                        store(base + place * (CHUNK * B // LANES), B // LANES, tile, piece)
                return carry

            lax.fori_loop(0, (chunks + 1) // 2, move, 0)

        @pl.when(kind == 5)
        def _():
            for tile in range(D // LANES):
                store(base, D // LANES, tile, jnp.zeros((8, LANES), F32))

        @pl.when(kind == 1)
        def _():
            skew = lax.rem(row0, LANES)
            first = pl.multiple_of(row0 - skew, LANES)
            copies = [fetch(behind_hbm, behind_ref, ATT_COLUMN, D)]
            for head in range(HEADS):
                copies.append(
                    pltpu.make_async_copy(
                        common_hbm.at[:, pl.ds(pl.multiple_of(head * D + first, LANES), slab)],
                        common_ref.at[:, pl.ds(head * slab, slab)],
                        sem.at[2 + head],
                    )
                )
                copies[-1].start()
            for copy in copies:
                copy.wait()

            def move(step, carry):
                width = 3 * D // LANES
                goal = base + step * (CHUNK * width)
                side = lax.broadcasted_iota(jnp.int32, (CHUNK, LANES), 1)
                for pair in range(HEADS // 2):
                    right = behind_ref[:, pair * LANES : (pair + 1) * LANES]
                    lane = 2 * pair * slab + skew + step * CHUNK
                    left, other = (product(turned(lane + slab * head), right) for head in range(2))
                    block = jnp.where(side < HDIM, left, other)
                    store(goal, width, 2 * D // LANES + pair, block)
                return carry

            lax.fori_loop(0, chunks, move, 0)

    shift = tab_ref[0]
    place = lax.broadcasted_iota(jnp.int32, (8, LANES), 0) * LANES
    place = place + lax.broadcasted_iota(jnp.int32, (8, LANES), 1)
    head = line_ref[FRONT : FRONT + 8, :]
    line_ref[FRONT : FRONT + 8, :] = jnp.where(place >= shift, head, 0.0)
    end = shift + plan.size
    block = pl.multiple_of(end // (8 * LANES) * 8, 8)
    lines = pl.ds(pl.multiple_of(FRONT + block, 8), 8)
    line_ref[lines, :] = jnp.where(place + block * LANES < end, line_ref[lines, :], 0.0)

    def clear(step, carry):
        start = pl.multiple_of(FRONT + block + 8 * step, 8)
        line_ref[pl.ds(start, 8), :] = jnp.zeros((8, LANES), F32)
        return carry

    lax.fori_loop(1, (plan.lines + 8 - block) // 8, clear, 0)

    def square(step, total):
        start = pl.multiple_of(FRONT + step * STEPS, 8)
        part = line_ref[pl.ds(start, STEPS), :]
        return total + part * part

    total = lax.fori_loop(
        0, plan.steps, square, jnp.zeros((STEPS, LANES), F32), unroll=steps_at_once(plan.steps)
    )
    line_copy = pltpu.make_async_copy(line_ref.at[pl.ds(0, plan.used)], line_out, sem.at[0])
    line_copy.start()
    total = jnp.sum(total, keepdims=True) + rest_ref[0:1, 0:1]
    class_copy.wait()
    if len(refs) > 8:
        holds, twice = (tab_ref[1 + 4 * most + which] for which in range(2))
        rows = jnp.sum(refs[0][...] * refs[0][...], 1, keepdims=True)
        place = lax.broadcasted_iota(jnp.int32, (SET, 1), 0)
        pieces = jnp.sum(jnp.where((place < 8) & (twice != 0), 0.0, rows[:SET]), keepdims=True)
        classes = class_ref[...].astype(F32)
        by_head = jnp.where(head_mask(), classes[1:2], 0.0)
        by_head = jnp.sum(by_head * by_head, 1, keepdims=True)
        normed = jnp.sum(classes[0:1] * classes[0:1], 1, keepdims=True)
        outer = jnp.sum(rows[SET : SET + HEADROWS] * by_head, keepdims=True)
        outer = outer + rows[SET + HEADROWS : SET + HEADROWS + 1] * normed
        outer = outer + rows[SET + HEADROWS + 1 : SET + HEADROWS + 2]
        outer = outer + rows[SET + HEADROWS + 2 : SET + HEADROWS + 3]
        total = total + jnp.where(holds != 0, pieces + outer / plan.groups, 0.0)
    square_ref[...] = jnp.broadcast_to(total[None], square_ref.shape)
    line_copy.wait()


def early_gradient(plan, table, common, behind, *values):
    return pl.pallas_call(
        functools.partial(early_kernel, plan, (table.shape[0] - 3) // 4),
        out_shape=[
            jax.ShapeDtypeStruct((plan.used, LANES), F32),
            jax.ShapeDtypeStruct((plan.count, 1, LANES), F32),
        ],
        in_specs=[
            pl.BlockSpec(memory_space=pltpu.SMEM),
            pl.BlockSpec(memory_space=pl.ANY),
            pl.BlockSpec(memory_space=pl.ANY),
        ]
        + [pl.BlockSpec(memory_space=pltpu.VMEM)] * len(values),
        out_specs=[
            pl.BlockSpec(memory_space=pl.ANY),
            pl.BlockSpec(memory_space=pltpu.VMEM),
        ],
        scratch_shapes=[
            pltpu.VMEM((common.shape[0], plan.fetched), BF16),
            pltpu.VMEM((behind.shape[0], F), BF16),
            pltpu.VMEM((TILE, D), BF16),
            pltpu.VMEM((plan.grad_scratch, LANES), F32),
            pltpu.SemaphoreType.DMA((2 + HEADS,)),
            pltpu.SemaphoreType.DMA,
        ],
        compiler_params=pltpu.CompilerParams(vmem_limit_bytes=60 * 1024 * 1024),
        cost_estimate=pl.CostEstimate(
            flops=10 * 10**9, bytes_accessed=10 * 10**6, transcendentals=0
        ),
    )(table, common, behind, *values)


def late_kernel(
    plan,
    most,
    tab_ref,
    lines_ref,
    wide_ref,
    left_ref,
    right_ref,
    ends_ref,
    out_ref,
    line_ref,
    sem,
):
    copy = pltpu.make_async_copy(lines_ref, line_ref.at[pl.ds(0, plan.used)], sem)
    copy.start()
    copy.wait()

    def add(goal, width, tile, block):
        lines = pl.ds(goal + tile, CHUNK, stride=width)
        line_ref[lines, :] = line_ref[lines, :] + block

    for part in range(most):
        kind, base, chunks, row0 = (tab_ref[1 + 4 * part + i] for i in range(4))

        @pl.when(kind == 0)
        def _():
            def move(step, carry):
                width = D // LANES
                rows = pl.ds(pl.multiple_of(row0 + step * CHUNK, 8), CHUNK)
                for tile in range(width):
                    block = wide_ref[rows, tile * LANES : (tile + 1) * LANES]
                    add(base + step * (CHUNK * width), width, tile, block)
                return carry

            lax.fori_loop(0, chunks, move, 0)

        @pl.when(kind == 1)
        def _():
            def move(step, carry):
                width = 3 * D // LANES
                rows = pl.ds(pl.multiple_of(row0 + step * CHUNK, 8), CHUNK)
                block = jnp.dot(
                    left_ref[rows, :],
                    right_ref[...],
                    precision=PRECISE,
                    preferred_element_type=F32,
                )
                for tile in range(2 * D // LANES):
                    piece = block[:, tile * LANES : (tile + 1) * LANES]
                    add(base + step * (CHUNK * width), width, tile, piece)
                return carry

            lax.fori_loop(0, chunks, move, 0)

        @pl.when(kind == 5)
        def _():
            width = D // LANES
            for tile in range(width):
                lines = pl.ds(base + tile, 8, stride=width)
                block = ends_ref[:, tile * LANES : (tile + 1) * LANES]
                line_ref[lines, :] = line_ref[lines, :] + block

    shift = tab_ref[0]
    turn = lax.rem(LANES - shift, LANES)
    lane = lax.broadcasted_iota(jnp.int32, (STEPS + 8, LANES), 1)

    def align(step, carry):
        start = pl.multiple_of(step * STEPS, 8)
        lines = pl.ds(pl.multiple_of(FRONT + start, 8), STEPS + 8)
        here = pltpu.roll(line_ref[lines, :], turn, 1)
        below = pltpu.roll(here, STEPS + 7, 0)
        both = jnp.where(lane < LANES - shift, here, below)
        out_ref[pl.ds(start, STEPS), :] = both[:STEPS]
        return carry

    lax.fori_loop(0, plan.steps, align, 0, unroll=steps_at_once(plan.steps))


def late_gradient(plan, table, lines, *values):
    return pl.pallas_call(
        functools.partial(late_kernel, plan, (table.shape[0] - 3) // 4),
        out_shape=jax.ShapeDtypeStruct((plan.lines, LANES), F32),
        in_specs=[pl.BlockSpec(memory_space=pltpu.SMEM), pl.BlockSpec(memory_space=pl.ANY)]
        + [pl.BlockSpec(memory_space=pltpu.VMEM)] * len(values),
        out_specs=pl.BlockSpec(memory_space=pltpu.VMEM),
        scratch_shapes=[
            pltpu.VMEM((plan.grad_scratch, LANES), F32),
            pltpu.SemaphoreType.DMA,
        ],
        compiler_params=pltpu.CompilerParams(vmem_limit_bytes=24 * 1024 * 1024),
    )(table, lines, *values).reshape(-1)[: plan.size]


def adam_update(weight, grad, first, second, rate):
    first = BETA_FIRST * first + (1.0 - BETA_FIRST) * grad
    second = BETA_SECOND * second + (1.0 - BETA_SECOND) * grad * grad
    stepped = (
        first
        / (1.0 - BETA_FIRST**STEP)
        / (jnp.sqrt(second / (1.0 - BETA_SECOND**STEP)) + ADAM_EPSILON)
    )
    return (weight - rate * (stepped + WEIGHT_DECAY * weight), first, second)


def per_device(
    plan,
    params,
    first_moment,
    second_moment,
    teacher,
    protos,
    proto_first,
    proto_second,
    teacher_protos,
    center,
    patches,
    partner,
):
    reps, groups = lax.axis_size("rep"), lax.axis_size("grp")
    count, half = reps * groups, reps * groups // 2
    rep, grp = lax.axis_index("rep"), lax.axis_index("grp")
    device = rep * groups + grp
    low = rep % 2 == 0
    place = rep // 2 * groups + grp
    halves = [
        [r * groups + g for r in range(parity, reps, 2) for g in range(groups)] for parity in (0, 1)
    ]
    swap = [(r, r ^ 1) for r in range(reps)]
    own_views = patches.shape[0]
    views = 2 * own_views

    def trade(values):
        return lax.ppermute(values, "rep", swap)

    def trade_low(values):
        return jnp.where(low, values, trade(values))

    def in_order(values):
        other = trade(values)
        return jnp.where(low, values, other), jnp.where(low, other, values)

    pairs = [list(range(parity, reps, 2)) for parity in (0, 1)]
    lines = reps // 2
    table = jnp.asarray(plan.lay_table)[device]
    given = lay_out(plan, table, jnp.where(low, teacher, params))
    later, given = lax.optimization_barrier(((params, teacher, protos, teacher_protos), given))
    given = trade(given)
    tables = jnp.stack(later[2:]).astype(BF16)
    around = [tables]
    for step in range(2, reps, 2):
        around.append(lax.ppermute(tables, "rep", [(r, (r + step) % reps) for r in range(reps)]))

    kept = lay_out(plan, table, jnp.where(low, later[0], later[1]))
    given, around = lax.optimization_barrier((given, around))
    shards = jnp.stack([jnp.where(low, kept, given), jnp.where(low, given, kept)])
    gathered = lax.all_gather(shards, BOTH, axis=0, axis_index_groups=halves)
    gathered = gathered.reshape(half, 2, -1, TILE, LANES)
    patches, partner, given = lax.optimization_barrier((patches, partner, given))
    pixels = jnp.concatenate(in_order(patches), 0)
    pixels = jnp.pad(pixels, ((0, 0), (0, TOKENS - NPATCH), (0, 0)))
    around = jnp.concatenate([jnp.stack(around[::-1])] * 2)
    around = lax.dynamic_slice_in_dim(around, lines - 1 - rep // 2, lines, 0)
    tables = jnp.stack(in_order(around))
    tables = tables.transpose(2, 1, 0, 3, 4).reshape(2, B, -1).astype(F32)
    places = in_order(partner.astype(F32))

    def columns_of(values):
        scale = lax.rsqrt(jnp.sum(values * values, 0, keepdims=True) + 1e-06)
        return (values * scale).astype(BF16), scale

    columns, column_scale = columns_of(tables[0])
    teacher_columns = columns_of(tables[1])[0]

    here = jnp.arange(views)
    source = jnp.concatenate([places[0], places[1] + own_views]).astype(jnp.int32)
    source = jnp.where(low, here, source)
    turn = (source[:, None] == here[None, :]).astype(BF16)

    turn, columns, teacher_columns = lax.optimization_barrier((turn, columns, teacher_columns))
    kept = forward(plan, gathered, pixels, turn)
    unit, scale, probs, _, looked, classes, qkv_w = kept[:7]
    all_rows, common = lax.all_to_all(kept[12], BOTH, 0, 0), kept[13]

    def gather_rows(values):
        return lax.all_gather(values, BOTH, axis=0, axis_index_groups=halves).reshape(
            half * views, -1
        )

    other = trade(common)

    all_rows = all_rows.reshape(reps // 2, 2, -1, B).transpose(1, 0, 2, 3).reshape(2, -1, B)
    start = (rep // 2 * groups * views).astype(jnp.int32)[None]
    note, new_center = prototypes(
        start, all_rows, columns, teacher_columns, center[None], groups, views
    )
    note, other = lax.optimization_barrier((note, other))
    common = gather_rows(jnp.where(low, common, other))
    new_center = new_center[0]
    note = lax.all_to_all(note, "grp", 0, 0)
    totals = jnp.sum(note[:, 3 * views :], 0)
    totals = totals.reshape(-1, 8, B).transpose(1, 0, 2).reshape(8, -1)[:, : half * views]
    loss_value = jnp.sum(jnp.log(totals[0]) - totals[2] / totals[1])
    depth = protos.shape[0]
    grad_protos, proto_squares = prototypes_back(
        (rep * depth).astype(jnp.int32)[None],
        depth,
        all_rows,
        columns,
        teacher_columns,
        center[None],
        totals,
        tables[0],
        column_scale,
    )
    behind, grad_middle, ends = rows_back(
        plan, low.astype(jnp.int32)[None], gathered, note, (classes,) + tuple(kept[7:12])
    )
    odd, far = grp % 2 == 1, grp // 2 % 2 == 1
    behind_rows = trade_low(behind)
    kept_rows, sent_rows = tokens_back(
        odd.astype(jnp.int32)[None],
        behind,
        grad_middle,
        ends,
        (unit, scale, probs, looked, classes, qkv_w),
        pixels.transpose(0, 2, 1),
        behind_rows,
        grad_protos,
    )

    def across(bit, values):
        return lax.ppermute(values, "grp", [(g, g ^ bit) for g in range(groups)])

    partial = kept_rows + across(1, sent_rows).astype(F32)
    first, second = partial[:SET], partial[SET : 2 * SET]
    shared = partial[2 * SET :]
    other = jnp.concatenate([jnp.where(far, first, second), shared], 0).astype(BF16)
    partial = jnp.concatenate([jnp.where(far, second, first), shared], 0)
    partial = partial + across(2, other).astype(F32)
    behind_rows, common, partial = lax.optimization_barrier((behind_rows, common, partial))
    behind_rows = gather_rows(behind_rows)
    if plan.near:
        step = 1
        while step < lines:
            hops = [(r, r - 2 * step) for r in range(reps) if r // 2 % (2 * step) == step]
            partial = partial + lax.ppermute(partial.astype(BF16), "rep", hops).astype(F32)
            step *= 2
    else:
        depth = partial.shape[0] // lines
        partial = lax.all_to_all(
            partial.astype(BF16).reshape(lines, depth, D), "rep", 0, 0, axis_index_groups=pairs
        )
        partial = jnp.sum(partial.astype(F32), 0)
    class_rows = common[:2, CLASS:ROWS].astype(F32)
    class_normed, query = class_rows[0:1], class_rows[1:2]
    by_head = jnp.where(head_mask()[:HEADS], query, 0.0)
    values = (proto_squares, partial)
    if not plan.near:
        twice = odd & ~far & (jnp.arange(SET) < 8)
        weights = jnp.concatenate(
            [
                jnp.where(twice, 0.0, 1.0),
                jnp.sum(by_head * by_head, 1) / groups,
                jnp.zeros((HEADROWS - HEADS,), F32),
                jnp.sum(class_normed * class_normed)[None] / groups,
                jnp.full((2,), 1.0 / groups, F32),
                jnp.zeros((SHARED - HEADROWS - 3,), F32),
            ]
        )
        weights = lax.dynamic_slice_in_dim(weights, rep // 2 * depth, depth)
        pieces = jnp.sum(weights * jnp.sum(partial * partial, 1))
        values = (proto_squares + jnp.where(low, pieces, 0.0),)
    early, squares = early_gradient(
        plan, jnp.asarray(plan.grad_table)[device], common, behind_rows, *values
    )
    summed = partial.astype(BF16)
    if not plan.near:
        summed = lax.all_to_all(
            jnp.broadcast_to(summed[None], (lines, depth, D)), "rep", 0, 0, axis_index_groups=pairs
        ).reshape(-1, D)
    shared, summed = summed[SET:], summed[:SET]
    other, squares = lax.optimization_barrier((across(2, summed), squares))
    squares = lax.all_to_all(squares, BOTH, 0, 0)
    grad_norm = jnp.sqrt(jnp.sum(squares[:, 0, 0]))
    factor = jnp.minimum(1.0, CLIP_NORM / (grad_norm + 1e-06))
    summed = jnp.concatenate([jnp.where(far, other, summed), jnp.where(far, summed, other)], 0)
    if plan.all_sets:
        other = across(1, summed)
        summed = jnp.concatenate([jnp.where(odd, other, summed), jnp.where(odd, summed, other)], 0)
    if plan.odd_owner:
        summed = trade_low(summed)
    wide_grad = jnp.pad(summed.astype(F32), ((0, CHUNK), (0, 0)))

    ends = shared[HEADROWS + 1 : HEADROWS + 3]
    shared = trade_low(shared).astype(F32)
    if plan.near:
        for owner in plan.final_reps:
            moved = lax.ppermute(ends, "rep", [(0, owner)]) if owner else ends
            ends = jnp.where(rep == owner, moved, ends)
        ends = ends.astype(F32)
    else:
        ends = shared[HEADROWS + 1 : HEADROWS + 3]
    ends = jnp.pad(ends, ((0, 6), (0, 0)))
    sum_query, reach = shared[HEADROWS : HEADROWS + 1], shared[:HEADS]
    left = jnp.concatenate([class_normed, reach, jnp.zeros((LANES - 1 - HEADS, D), F32)], 0)
    left = jnp.pad(left.T, ((0, CHUNK), (0, 0)))
    right = jnp.concatenate(
        [
            jnp.pad(sum_query, ((0, 0), (0, D))),
            jnp.pad(by_head, ((0, 0), (D, 0))),
            jnp.zeros((LANES - 1 - HEADS, 2 * D), F32),
        ],
        0,
    )
    grad_flat = late_gradient(
        plan, jnp.asarray(plan.late_table)[device], early, wide_grad, left, right, ends
    )
    new_params, new_first, new_second = adam_update(
        params, grad_flat * factor, first_moment, second_moment, LEARNING_RATE
    )
    new_protos, new_proto_first, new_proto_second = adam_update(
        protos, grad_protos * factor, proto_first, proto_second, PROTO_RATE
    )
    new_teacher = TEACHER_MOMENTUM * teacher + (1.0 - TEACHER_MOMENTUM) * new_params
    new_teacher_protos = TEACHER_MOMENTUM * teacher_protos + (1.0 - TEACHER_MOMENTUM) * new_protos
    return (
        new_params,
        new_first,
        new_second,
        new_teacher,
        new_protos,
        new_proto_first,
        new_proto_second,
        new_teacher_protos,
        new_center,
        loss_value,
        grad_norm,
    )


def solution(mesh):
    placed = (
        P(BOTH),
        P(BOTH),
        P(BOTH),
        P(BOTH),
        P("rep", "grp"),
        P("rep", "grp"),
        P("rep", "grp"),
        P("rep", "grp"),
        P("grp"),
        P(BOTH, None, None),
        P(BOTH),
    )
    plan = Plan(mesh.shape["rep"], mesh.shape["grp"])
    return jax.shard_map(
        functools.partial(per_device, plan),
        mesh=mesh,
        in_specs=placed,
        out_specs=placed[:9] + (P(), P()),
        check_vma=False,
    )
```

```python
import functools

import jax
import jax.numpy as jnp
import numpy as np
from jax import lax
from jax.experimental import pallas as pl
from jax.experimental.pallas import tpu as pltpu
from jax.sharding import PartitionSpec as P

D = 768
HEADS = 12
HDIM = 64
F = 3072
PD = 768
NTOK = 197
H = 2048
B = 256
STEP = 10
NPATCH = NTOK - 1

PRECISE = lax.Precision.HIGHEST
STUDENT_TEMP = 0.1
TEACHER_TEMP = 0.04
CENTER_MOMENTUM = 0.9
TEACHER_MOMENTUM = 0.8
CLIP_NORM = 0.05
LEARNING_RATE = 0.03
PROTO_RATE = 0.6
BETA_FIRST = 0.9
BETA_SECOND = 0.999
ADAM_EPSILON = 1e-08
WEIGHT_DECAY = 0.04
BOTH = ("rep", "grp")
LANES = 128
F32 = jnp.float32
BF16 = jnp.bfloat16

SEGMENTS = []
_offset = 0
for _rows, _cols in ((PD + NTOK + 4, D), (D, 3 * D), (D, D), (D, F), (F + 2, D), (D + H, H), (H, B)):
    SEGMENTS.append((_offset, _rows, _cols))
    _offset += _rows * _cols
PFLAT = _offset
WIDTHS = sorted({cols // LANES for _, _, cols in SEGMENTS})

PIECES = []
_offset = 0
for _rows, _cols in (
    (PD + NTOK + 4, D),
    (D, 3 * D),
    (D, D),
    (D, F),
    (F, D),
    (2, D),
    (D, H),
    (H, H),
    (H, B),
):
    PIECES.append((_offset, _rows, _cols))
    _offset += _rows * _cols
FRONT = 192
CHUNK = 128
SET = 288
SHARED = 32
STEPS = 64
AHEAD = 3 * D + F + H
TILE = 16
TOKENS = 208
HEADROWS = 16
VMEM_LIMIT = 62 * 1024 * 1024


SPANS = {
    2: (0, 0),
    3: (D, D),
    4: (2 * D, D + F),
    6: (2 * D + F, 2 * D + F + B + H),
    7: (3 * D + F, 2 * D + F + B),
}
ATT_COLUMN = 2 * D + F + B + 2 * H
SECOND = HEADS * D
CLASS = SECOND + H
ROWS = CLASS + D


def round_up(value, step):
    return -(-value // step) * step


def steps_at_once(count):
    return max(size for size in range(1, 8) if count % size == 0)


def shard_parts(start, stop, table):
    parts = []
    line0 = start // LANES
    for index, (offset, rows, cols) in enumerate(table):
        low, high = max(start, offset), min(stop, offset + rows * cols)
        if low >= high:
            continue
        row0 = (low - offset) // cols
        row1 = -(-(high - offset) // cols)
        parts.append((index, row0, row1 - row0, (offset + row0 * cols) // LANES - line0))
    return parts


FINAL_ROW = round_up(PD + NTOK + 4, 8)


class Plan:
    def __init__(self, reps, groups):
        count = reps * groups
        self.count, self.groups = count, groups
        self.size = PFLAT // count
        self.lines = round_up(-(-self.size // LANES) + 1, STEPS)
        self.steps = self.lines // STEPS
        self.scratch = FRONT + self.lines + 8 * max(WIDTHS) + 16
        table = []
        self.blocks = [[] for _ in SEGMENTS]
        longest = 0
        for device in range(count):
            start = device * self.size
            entry = [start % LANES]
            target = 0
            for index, row0, rows, line in shard_parts(start, start + self.size, SEGMENTS):
                width = SEGMENTS[index][2] // LANES
                skew = row0 % 8
                tiles = -(-(rows + skew) // 8)
                self.blocks[index].append((device, target // TILE, row0 // 8, tiles))
                entry += [
                    WIDTHS.index(width),
                    FRONT + line - skew * width,
                    tiles // 2,
                    tiles % 2,
                    target // TILE,
                ]
                target += tiles * 8 * width
            longest = max(longest, target)
            entry += [-1, 0, 0, 0, 0] * (2 - len(entry) // 5)
            table.append(entry)
        self.buffer = round_up(longest, 16)
        self.lay_table = np.array(table, np.int32)
        edge = SEGMENTS[0][1] * SEGMENTS[0][2]
        owners = [device for device in range(count) if device * self.size < edge]
        self.odd_owner = any(self.place(device)[1] for device in owners)
        self.all_sets = len(owners) > 2
        edge = sum(rows * cols for _, rows, cols in SEGMENTS[:2])
        self.near = all(
            device < 2 * groups for device in range(count) if device * self.size < edge
        )
        offset, rows, cols = PIECES[5]
        self.final_reps = sorted(
            {
                device // groups
                for device in range(count)
                if device * self.size < offset + rows * cols and (device + 1) * self.size > offset
            }
        )
        self.grad_table = self.tabulate(lambda index: index, lambda device, index, row0, chunks: row0)
        self.most_chunks = {
            index: max(
                [1]
                + [
                    entry[3 + place]
                    for entry in self.grad_table
                    for place in range(0, len(entry) - 3, 4)
                    if entry[1 + place] == index
                ]
            )
            for index in (1,) + tuple(SPANS)
        }
        self.fetched = max(
            [HEADS * (self.most_chunks[1] + 1) * CHUNK, H + D]
            + [(chunks + 1) * CHUNK for chunks in self.most_chunks.values()]
        )
        self.late_table = self.tabulate(lambda index: index in (0, 1, 5), self.wide_row)
        self.grad_scratch = FRONT + self.lines + CHUNK * max(WIDTHS) + 16
        self.used = FRONT + self.lines + 8


    def largest(self):
        longest = max(8 * block[3] for blocks in self.blocks for block in blocks)
        return max(len(blocks) for blocks in self.blocks), round_up(longest, LANES) + 2 * LANES

    def place(self, device):
        rep, grp = divmod(device, self.groups)
        return rep // 2 * self.groups + grp, rep % 2

    def tabulate(self, chosen, rows_of):
        table = []
        for device in range(self.count):
            start = device * self.size
            entry = []
            for index, row0, rows, line in shard_parts(start, start + self.size, PIECES):
                if not chosen(index):
                    continue
                skew = row0 % 8
                line -= skew * (PIECES[index][2] // LANES)
                chunks = -(-(rows + skew) // CHUNK)
                entry += [index, FRONT + line, chunks, rows_of(device, index, row0 - skew, chunks)]
            table.append(entry)
        most = max(len(entry) for entry in table) // 4
        for device, entry in enumerate(table):
            entry += [-1, 0, 0, 0] * (most - len(entry) // 4)
            entry.insert(0, device * self.size % LANES)
            entry += [device < self.groups, device % 4 == 1]
        return np.array(table, np.int32)

    def wide_row(self, device, index, row0, chunks):
        if index:
            return row0
        late = row0 >= 2 * SET - 8
        if not self.all_sets:
            if late != device % 2:
                raise ValueError("owner")
            return row0 - (2 * SET - 8) * late
        return row0 + 8 * late


def lay_kernel(plan, tab_ref, x_ref, out_ref, line_ref):
    shift = tab_ref[0]
    lane = lax.broadcasted_iota(jnp.int32, (STEPS + 8, LANES), 1)
    line_ref[pl.ds(0, FRONT), :] = jnp.zeros((FRONT, LANES), F32)
    tail = plan.scratch - FRONT - plan.lines
    line_ref[pl.ds(FRONT + plan.lines, tail), :] = jnp.zeros((tail, LANES), F32)

    def align(step, carry):
        base = pl.multiple_of(step * STEPS, 8)
        here = pltpu.roll(x_ref[pl.ds(base, STEPS + 8), :], shift, 1)
        above = pltpu.roll(here, 1, 0)
        both = jnp.where(lane >= shift, here, above)
        line_ref[pl.ds(pl.multiple_of(FRONT + base, 8), STEPS), :] = both[8:]
        return carry

    lax.fori_loop(0, plan.steps, align, 0, unroll=steps_at_once(plan.steps))
    for part in range(2):
        kind, base, pairs, odd, target = (tab_ref[1 + 5 * part + i] for i in range(5))
        for index, width in enumerate(WIDTHS):

            @pl.when(kind == index)
            def _(width=width):
                def move(step, carry):
                    row = base + step * (TILE * width)
                    goal = (target + step * width) * TILE
                    for tile in range(width):
                        both = line_ref[pl.ds(row + tile, TILE, stride=width), :]
                        place = pl.multiple_of(goal + TILE * tile, TILE)
                        out_ref[pl.ds(place, TILE), :] = both.astype(BF16)
                    return carry

                def last(step, carry):
                    row = base + pairs * (TILE * width)
                    goal = (target + pairs * width) * TILE
                    for tile in range(0, width, 2):
                        both = [
                            line_ref[pl.ds(row + tile + side, 8, stride=width), :]
                            for side in range(2)
                        ]
                        place = pl.multiple_of(goal + 8 * tile, TILE)
                        out_ref[pl.ds(place, TILE), :] = jnp.concatenate(both, 0).astype(BF16)
                    return carry

                lax.fori_loop(0, pairs, move, 0)
                lax.fori_loop(0, odd, last, 0)


def lay_out(plan, table, flat):
    padded = jnp.pad(flat, (8 * LANES, plan.lines * LANES - plan.size))
    lines = padded.reshape(8 + plan.lines, LANES)
    return pl.pallas_call(
        functools.partial(lay_kernel, plan),
        out_shape=jax.ShapeDtypeStruct((plan.buffer, LANES), BF16),
        in_specs=[
            pl.BlockSpec(memory_space=pltpu.SMEM),
            pl.BlockSpec(memory_space=pltpu.VMEM),
        ],
        out_specs=pl.BlockSpec(memory_space=pltpu.VMEM),
        scratch_shapes=[pltpu.VMEM((plan.scratch, LANES), F32)],
        compiler_params=pltpu.CompilerParams(vmem_limit_bytes=24 * 1024 * 1024),
    )(table, lines)


class Shards:
    def __init__(self, plan, gathered_ref, ref, sems, order):
        self.plan, self.ref, self.sems, self.waited = plan, ref, sems, set()
        self.copies = {}
        for device in order:
            place, side = plan.place(device)
            copy = pltpu.make_async_copy(
                gathered_ref.at[place, side], ref.at[device], sems.at[device]
            )
            copy.start()
            self.copies[device] = copy

    def wait(self, device):
        if device in self.copies:
            self.copies.pop(device).wait()

    def finish(self):
        for device in list(self.copies):
            self.wait(device)

    def blocks(self, index, first, count):
        found = [
            block
            for block in self.plan.blocks[index]
            if 8 * block[2] < first + count and 8 * (block[2] + block[3]) > first
        ]
        for block in found:
            self.wait(block[0])
        return found

    def eight(self, index, tile, pair, side):
        width = SEGMENTS[index][2] // LANES
        total = None
        for device, target, tile0, tiles in self.plan.blocks[index]:
            own = tile - tile0
            if not 0 <= own < tiles:
                continue
            if own < tiles // 2 * 2:
                both = self.ref[device, target + own // 2 * width + 2 * pair + side]
                half = own % 2
            else:
                both = self.ref[device, target + tiles // 2 * width + pair]
                half = side
            piece = both.astype(F32)[8 * half : 8 * half + 8]
            total = piece if total is None else total + piece
        return total

    def assemble(self, index, out_ref):
        width = SEGMENTS[index][2] // LANES
        rows = out_ref.shape[0]
        self.blocks(index, 0, rows)

        def column(pair, carry):
            for side in range(2):
                lanes = pl.ds(pl.multiple_of(pair * 2 * LANES + side * LANES, LANES), LANES)
                for group in range(rows // TILE):
                    both = [
                        self.eight(index, 2 * group + half, pair, side) for half in range(2)
                    ]
                    out_ref[TILE * group : TILE * (group + 1), lanes] = jnp.concatenate(
                        both, 0
                    ).astype(BF16)
            return carry

        lax.fori_loop(0, width // 2, column, 0)

    def columns(self, index, block, pair):
        width = SEGMENTS[index][2] // LANES
        device, target, _, tiles = block
        sides = []
        for side in range(2):
            pieces = [
                self.ref[device, target + step * width + 2 * pair + side]
                for step in range(tiles // 2)
            ]
            if tiles % 2:
                both = self.ref[device, target + tiles // 2 * width + pair].astype(F32)
                pieces.append(both[8 * side : 8 * side + 8].astype(BF16))
            sides.append(jnp.concatenate(pieces, 0))
        return jnp.concatenate(sides, 1)

    def times(self, index, first, values, left_ref, out_ref):
        views, count = values.shape
        blocks = self.blocks(index, first, count)
        top = max([first + count] + [8 * (tile0 + tiles) for _, _, tile0, tiles in blocks])
        top = round_up(top, LANES) + LANES
        parts = [values, jnp.zeros((views, top - first - count), F32)]
        if first:
            parts.insert(0, jnp.zeros((views, first), F32))
        wide = jnp.concatenate(parts, 1)
        for number, (_, _, tile0, tiles) in enumerate(blocks):
            start = 8 * tile0 // LANES * LANES
            turn = 8 * tile0 - start
            piece = wide[:, start : start + round_up(turn + 8 * tiles, LANES)]
            if turn:
                piece = pltpu.roll(piece, piece.shape[1] - turn, 1)
            left_ref[number, :, : 8 * tiles] = piece[:, : 8 * tiles]

        def column(pair, carry):
            total = jnp.zeros((views, 2 * LANES), F32)
            for number, block in enumerate(blocks):
                left = left_ref[number, :, : 8 * block[3]].astype(BF16)
                total += product(left, self.columns(index, block, pair))
            out_ref[:, pl.ds(pl.multiple_of(pair * 2 * LANES, LANES), 2 * LANES)] = total
            return carry

        lax.fori_loop(0, SEGMENTS[index][2] // LANES // 2, column, 0, unroll=4)


    def back(self, index, first, count, values, grad_ref, left_ref, wide_ref):
        views, cols = values.shape
        grad_ref[:, :cols] = values
        blocks = self.blocks(index, first, count)
        top = max([first + count] + [8 * (tile0 + tiles) for _, _, tile0, tiles in blocks])
        wide_ref[:, : round_up(top, LANES) + LANES] = jnp.zeros(
            (views, round_up(top, LANES) + LANES), F32
        )
        for number, (_, _, _, tiles) in enumerate(blocks):
            size = round_up(8 * tiles, LANES) + LANES
            left_ref[number, :, :size] = jnp.zeros((views, size), F32)

        def column(pair, carry):
            lanes = pl.ds(pl.multiple_of(pair * 2 * LANES, LANES), 2 * LANES)
            left = grad_ref[:, lanes].astype(BF16)
            for number, block in enumerate(blocks):
                size = 8 * block[3]
                left_ref[number, :, :size] += product_t(left, self.columns(index, block, pair))
            return carry

        lax.fori_loop(0, cols // LANES // 2, column, 0, unroll=4)
        for number, (_, _, tile0, tiles) in enumerate(blocks):
            start = 8 * tile0 // LANES * LANES
            turn = 8 * tile0 - start
            size = round_up(turn + 8 * tiles, LANES)
            piece = left_ref[number, :, :size]
            if turn:
                piece = pltpu.roll(piece, turn, 1)
            wide_ref[:, start : start + size] += piece
        return wide_ref[:, first : first + count]


def product(left, right):
    return jnp.dot(left, right, preferred_element_type=F32)


def product_t(left, right):
    return lax.dot_general(
        left, right, (((left.ndim - 1,), (1,)), ((), ())), preferred_element_type=F32
    )


def normal_share(values):
    return 0.5 + 0.5 * lax.erf(values * 2**-0.5)


def activate(values):
    return values * normal_share(values)


def gelu_back(values, grad):
    density = jnp.exp(-0.5 * values * values) * (2 * np.pi) ** -0.5
    return grad * (normal_share(values) + values * density)


def normalised(values):
    centred = values - jnp.mean(values, -1, keepdims=True)
    scale = lax.rsqrt(jnp.mean(centred * centred, -1, keepdims=True) + 1e-06)
    return centred * scale, scale


def norm_back(grad, gain, unit, scale):
    inner = grad * gain
    return scale * (
        inner
        - jnp.mean(inner, -1, keepdims=True)
        - unit * jnp.mean(inner * unit, -1, keepdims=True)
    )


def head_mask():
    shape = (HEADROWS, D)
    return lax.broadcasted_iota(jnp.int32, shape, 0) == (
        lax.broadcasted_iota(jnp.int32, shape, 1) // HDIM
    )


def token_norms(unit, norms, class_normed):
    token = lax.broadcasted_iota(jnp.int32, (TOKENS, D), 0)
    normed = unit * norms[0:1] + norms[1:2]
    return jnp.where(
        token < NPATCH, normed, jnp.where(token == NPATCH, class_normed, 0.0)
    ).astype(BF16)


def forward_kernel(
    plan,
    gathered_ref,
    pixels_ref,
    turn_ref,
    unit_out,
    scale_out,
    probs_ref,
    mixed_ref,
    looked_ref,
    class_ref,
    qkv_out,
    hidden_ref,
    one_ref,
    two_ref,
    bottle_ref,
    middle_ref,
    rows_ref,
    pack_out,
    shards_ref,
    wide_ref,
    place_ref,
    left_ref,
    sums_ref,
    pack_ref,
    unit_ref,
    scale_ref,
    qkv_ref,
    out_sems,
    sems,
):
    shards = Shards(plan, gathered_ref, shards_ref, sems, range(plan.count))
    views = pixels_ref.shape[0]
    temper = HDIM ** (-0.5)
    shards.assemble(0, wide_ref)
    position = wide_ref[PD : PD + TOKENS].astype(F32)
    place_ref[...] = pltpu.roll(position, TOKENS - 1, 0)
    class_place = position[0:1]
    norms = position[NTOK : NTOK + 4]
    class_unit, class_scale = normalised(class_place)
    class_normed = (class_unit * norms[0:1] + norms[1:2]).astype(BF16).astype(F32)
    shards.assemble(1, qkv_ref)
    qkv_copy = pltpu.make_async_copy(qkv_ref, qkv_out, out_sems.at[4])
    qkv_copy.start()
    mask = head_mask()
    query = jnp.broadcast_to(class_normed, (HEADROWS, D)).astype(BF16)
    query = product(query, qkv_ref[:, :D]).astype(BF16).astype(F32)
    by_head = jnp.where(mask, query, 0.0).astype(BF16)
    looked = product_t(by_head, qkv_ref[:, D : 2 * D]).astype(BF16)
    looked_ref[...] = looked

    def copies(v):
        slot = lax.rem(v, 2)
        return (
            pltpu.make_async_copy(unit_ref.at[slot], unit_out.at[v], out_sems.at[slot]),
            pltpu.make_async_copy(scale_ref.at[slot], scale_out.at[v], out_sems.at[2 + slot]),
        )

    def view(v, carry):
        embedded = product(pixels_ref[v], wide_ref[:PD]) + place_ref[...]
        unit, scale = normalised(embedded)

        @pl.when(v >= 2)
        def _():
            for copy in copies(v - 2):
                copy.wait()

        unit_ref[lax.rem(v, 2)] = unit
        scale_ref[lax.rem(v, 2)] = jnp.broadcast_to(scale, (TOKENS, LANES))
        for copy in copies(v):
            copy.start()
        normed = token_norms(unit, norms, class_normed)
        scores = product_t(looked, normed) * temper
        token = lax.broadcasted_iota(jnp.int32, scores.shape, 1)
        scores = jnp.where(token < NTOK, scores, -1e30)
        top = jnp.max(scores, -1, keepdims=True)
        top = top + jnp.log(jnp.sum(jnp.exp(scores - top), -1, keepdims=True))
        head = lax.broadcasted_iota(jnp.int32, scores.shape, 0)
        probs = jnp.where(head < HEADS, jnp.exp(scores - top), 0.0)
        probs_ref[v] = probs
        mixed_ref[v] = product(probs.astype(BF16), normed).astype(BF16)
        return carry

    lax.fori_loop(0, views, view, 0, unroll=4)
    mixed = mixed_ref[...].reshape(views * HEADROWS, D)
    valued = product(mixed, qkv_ref[:, 2 * D :]).reshape(views, HEADROWS, D)
    attended = jnp.sum(jnp.where(mask[None], valued, 0.0), 1).astype(BF16)
    pack_ref[:, :D] = attended.astype(F32)
    shards.times(2, 0, pack_ref[:, :D], left_ref, sums_ref)
    middle = class_place + sums_ref[...]
    unit, scale = normalised(middle)
    middle_ref[0], middle_ref[1] = unit, jnp.broadcast_to(scale, (views, D))
    normed = (unit * norms[2:3] + norms[3:4]).astype(BF16)
    pack_ref[:, D : 2 * D] = normed.astype(F32)
    shards.times(3, 0, pack_ref[:, D : 2 * D], left_ref, hidden_ref)
    act = activate(hidden_ref[...]).astype(BF16)
    pack_ref[:, 2 * D : 2 * D + F] = act.astype(F32)
    shards.times(4, 0, act.astype(F32), left_ref, sums_ref)
    unit, scale = normalised(middle + sums_ref[...])
    middle_ref[2], middle_ref[3] = unit, jnp.broadcast_to(scale, (views, D))
    final = jnp.concatenate(
        [shards.eight(4, F // 8, tile // 2, tile % 2) for tile in range(D // LANES)], 1
    )
    cls = (unit * final[0:1] + final[1:2]).astype(BF16)
    place = 2 * D + F
    pack_ref[:, place : place + D] = cls.astype(F32)
    shards.times(5, 0, cls.astype(F32), left_ref, one_ref)
    first = activate(one_ref[...]).astype(BF16)
    pack_ref[:, place + D : AHEAD] = first.astype(F32)
    shards.times(5, D, first.astype(F32), left_ref, two_ref)
    second = activate(two_ref[...]).astype(BF16)
    shards.times(6, 0, second.astype(F32), left_ref, bottle_ref)
    bottle = bottle_ref[...]
    scale = lax.rsqrt(jnp.sum(bottle * bottle, -1, keepdims=True) + 1e-06)
    rows = product(turn_ref[...], (bottle * scale).astype(BF16)).astype(BF16)
    rows_ref[...] = jnp.broadcast_to(rows[None], rows_ref.shape)
    mixed = mixed_ref[...].astype(F32)
    for head in range(HEADS):
        pack_out[:, head * D : (head + 1) * D] = mixed[:, head, :].astype(BF16)
    pack_out[:, SECOND:CLASS] = second
    row = lax.broadcasted_iota(jnp.int32, (views, D), 0)
    pack_out[:, CLASS:ROWS] = jnp.where(
        row == 0, class_normed, jnp.where(row == 1, query[0:1], 0.0)
    ).astype(BF16)
    pack_out[:, ROWS : ROWS + AHEAD] = pack_ref[...].astype(BF16)
    pack_out[:, ROWS + AHEAD :] = jnp.zeros((views, pack_out.shape[1] - ROWS - AHEAD), BF16)
    class_ref[...] = jnp.concatenate(
        [
            class_unit,
            class_normed,
            query[0:1],
            jnp.broadcast_to(class_scale, (1, D)),
            norms,
            final,
        ],
        0,
    )
    for v in range(max(0, views - 2), views):
        for copy in copies(v):
            copy.wait()
    qkv_copy.wait()
    shards.finish()


def forward(plan, gathered, pixels, turn):
    views = pixels.shape[0]
    shapes = [
        ((views, TOKENS, D), F32),
        ((views, TOKENS, LANES), F32),
        ((views, HEADROWS, TOKENS), F32),
        ((views, HEADROWS, D), BF16),
        ((HEADROWS, D), BF16),
        ((16, D), F32),
        ((D, 3 * D), BF16),
        ((views, F), F32),
        ((views, H), F32),
        ((views, H), F32),
        ((views, B), F32),
        ((4, views, D), F32),
        ((plan.count, views, B), BF16),
        ((views, ROWS + AHEAD + (max(plan.most_chunks.values()) + 1) * CHUNK), BF16),
    ]
    most, longest = plan.largest()
    return pl.pallas_call(
        functools.partial(forward_kernel, plan),
        out_shape=[jax.ShapeDtypeStruct(shape, dtype) for shape, dtype in shapes],
        in_specs=[pl.BlockSpec(memory_space=pl.ANY)]
        + [pl.BlockSpec(memory_space=pltpu.VMEM)] * 2,
        out_specs=[
            pl.BlockSpec(memory_space=pl.ANY if index in (0, 1, 6) else pltpu.VMEM)
            for index in range(len(shapes))
        ],
        scratch_shapes=[
            pltpu.VMEM((plan.count, plan.buffer // TILE, TILE, LANES), BF16),
            pltpu.VMEM((round_up(PD + NTOK + 4, TILE), D), BF16),
            pltpu.VMEM((TOKENS, D), F32),
            pltpu.VMEM((most, views, longest), F32),
            pltpu.VMEM((views, D), F32),
            pltpu.VMEM((views, AHEAD), F32),
            pltpu.VMEM((2, TOKENS, D), F32),
            pltpu.VMEM((2, TOKENS, LANES), F32),
            pltpu.VMEM((D, 3 * D), BF16),
            pltpu.SemaphoreType.DMA((5,)),
            pltpu.SemaphoreType.DMA((plan.count,)),
        ],
        compiler_params=pltpu.CompilerParams(vmem_limit_bytes=VMEM_LIMIT),
        cost_estimate=pl.CostEstimate(
            flops=60 * 10**9, bytes_accessed=40 * 10**6, transcendentals=10**5
        ),
    )(gathered, pixels, turn)


def proto_kernel(
    start_ref,
    rows_ref,
    columns_ref,
    others_ref,
    center_ref,
    note_ref,
    center_out_ref,
    student_ref,
    teacher_ref,
    sums_ref,
):
    count, groups = rows_ref.shape[1], note_ref.shape[0]
    views = (note_ref.shape[1] - 8 * -(-count // B)) // 3
    logits = product(rows_ref[1], others_ref[...])
    center = center_ref[...]
    center_out_ref[...] = CENTER_MOMENTUM * center + (1.0 - CENTER_MOMENTUM) * jnp.mean(
        logits, 0, keepdims=True
    )
    exp_teacher = jnp.exp((logits - center) / TEACHER_TEMP)
    teacher_ref[...] = exp_teacher
    scaled = product(rows_ref[0], columns_ref[...]) / STUDENT_TEMP
    exp_student = jnp.exp(scaled)
    student_ref[...] = exp_student
    turned = []
    for which, values in enumerate((exp_student, exp_teacher, exp_teacher * scaled)):
        total = jnp.broadcast_to(jnp.sum(values, 1, keepdims=True), (count, LANES))
        turned.append(total.T[0:1])
        if which < 2:
            sums_ref[:, which * LANES : (which + 1) * LANES] = total
    turned = jnp.concatenate(turned + [jnp.zeros((5, count), F32)], 0)
    for step in range(-(-count // B)):
        part = turned[:, step * B : (step + 1) * B]
        lines = slice(3 * views + 8 * step, 3 * views + 8 * (step + 1))
        note_ref[:, lines, : part.shape[1]] = jnp.broadcast_to(part[None], (groups,) + part.shape)
        if part.shape[1] < B:
            note_ref[:, lines, part.shape[1] :] = jnp.zeros((groups, 8, B - part.shape[1]), F32)
    start = pl.multiple_of(start_ref[0], 8)
    band, parts = groups * views, []
    for source in (student_ref, teacher_ref):
        rest = source[pl.ds(start, band), :]
        for _ in range(3):
            parts.append(rest.astype(BF16))
            rest = rest - parts[-1].astype(F32)
    pulls = product_t(jnp.concatenate(parts, 0), columns_ref[...])
    for which in range(2):
        first = 3 * which * band
        total = pulls[first : first + band] + pulls[first + band : first + 2 * band]
        total = total + pulls[first + 2 * band : first + 3 * band]
        note_ref[:, which * views : (which + 1) * views, :] = total.reshape(groups, views, B)
    own = sums_ref[pl.ds(start, groups * views), :]
    note_ref[:, 2 * views : 3 * views, :] = own.reshape(groups, views, B)


def prototypes(start, rows, columns, others, center, groups, views):
    count, width = rows.shape[1], columns.shape[1]
    shapes = [(groups, 3 * views + 8 * -(-count // B), B), (1, width)]
    return pl.pallas_call(
        proto_kernel,
        out_shape=[jax.ShapeDtypeStruct(shape, F32) for shape in shapes],
        in_specs=[pl.BlockSpec(memory_space=pltpu.SMEM)]
        + [pl.BlockSpec(memory_space=pltpu.VMEM)] * 4,
        out_specs=[pl.BlockSpec(memory_space=pltpu.VMEM)] * len(shapes),
        scratch_shapes=[pltpu.VMEM((count, width), F32)] * 2
        + [pltpu.VMEM((count, 2 * LANES), F32)],
        compiler_params=pltpu.CompilerParams(vmem_limit_bytes=32 * 1024 * 1024),
        cost_estimate=pl.CostEstimate(
            flops=3 * 10**9, bytes_accessed=6 * 10**6, transcendentals=10**6
        ),
    )(start, rows, columns, others, center)


def proto_back_kernel(
    start_ref,
    rows_ref,
    columns_ref,
    others_ref,
    center_ref,
    totals_ref,
    table_ref,
    scale_ref,
    grad_ref,
    square_ref,
    work_ref,
):
    count = rows_ref.shape[1]
    totals = jnp.broadcast_to(totals_ref[0:2][:, None, :], (2, 8, count))
    student, teacher = (totals[which].T[:, :1] for which in range(2))
    logits = product(rows_ref[1], others_ref[...])
    targets = jnp.exp((logits - center_ref[...]) / TEACHER_TEMP) / teacher
    scaled = product(rows_ref[0], columns_ref[...]) / STUDENT_TEMP
    grad = (jnp.exp(scaled) / student - targets) / STUDENT_TEMP
    parts, rest = [], grad
    for _ in range(3):
        parts.append(rest.astype(BF16))
        rest = rest - parts[-1].astype(F32)
    turned = rows_ref[0].astype(F32).T.astype(BF16)
    work_ref[...] = product(jnp.concatenate([turned] * 3, 1), jnp.concatenate(parts, 0))
    scale = scale_ref[...]
    inner = jnp.sum(work_ref[...] * table_ref[...], 0, keepdims=True)
    start = pl.multiple_of(start_ref[0], 8)
    lines = pl.ds(start, grad_ref.shape[0])
    grad = work_ref[lines, :] * scale - table_ref[lines, :] * (scale * scale * scale * inner)
    grad_ref[...] = grad
    square_ref[...] = jnp.broadcast_to(jnp.sum(grad * grad, keepdims=True), square_ref.shape)


def prototypes_back(start, depth, *values):
    count, width = values[0].shape[1], values[1].shape[1]
    shapes = [(depth, width), (8, LANES)]
    return pl.pallas_call(
        proto_back_kernel,
        out_shape=[jax.ShapeDtypeStruct(shape, F32) for shape in shapes],
        in_specs=[pl.BlockSpec(memory_space=pltpu.SMEM)]
        + [pl.BlockSpec(memory_space=pltpu.VMEM)] * len(values),
        out_specs=[pl.BlockSpec(memory_space=pltpu.VMEM)] * len(shapes),
        scratch_shapes=[pltpu.VMEM((B, width), F32)],
        compiler_params=pltpu.CompilerParams(vmem_limit_bytes=32 * 1024 * 1024),
        cost_estimate=pl.CostEstimate(
            flops=3 * 10**9, bytes_accessed=6 * 10**6, transcendentals=10**6
        ),
    )(start, *values)


def rows_back_kernel(
    plan,
    low_ref,
    gathered_ref,
    note_ref,
    class_ref,
    hidden_ref,
    one_ref,
    two_ref,
    bottle_ref,
    middle_ref,
    pack_ref,
    stream_ref,
    extra_ref,
    shards_ref,
    left_ref,
    values_ref,
    wide_ref,
    sems,
):
    used = {block[0] for blocks in plan.blocks[2:] for block in blocks}
    shards = Shards(plan, gathered_ref, shards_ref, sems, sorted(used, reverse=True))
    work = (values_ref, left_ref, wide_ref)
    norms, final = class_ref[4:8], class_ref[8:10]

    views = bottle_ref.shape[0]
    note = jnp.sum(note_ref[...], 0)
    sums = note[2 * views : 3 * views]
    student, teacher = sums[:, :1], sums[:, LANES : LANES + 1]
    grad_rows = (note[:views] / student - note[views : 2 * views] / teacher) / STUDENT_TEMP
    grad_rows = jnp.where(low_ref[0] == 0, 0.0, grad_rows).astype(BF16).astype(F32)
    bottle = bottle_ref[...]
    scale = lax.rsqrt(jnp.sum(bottle * bottle, -1, keepdims=True) + 1e-06)
    grad_bottle = (
        grad_rows * scale - bottle * scale**3 * jnp.sum(grad_rows * bottle, -1, keepdims=True)
    ).astype(BF16)
    place = 2 * D + F
    pack_ref[:, place : place + B] = grad_bottle
    grad_two = shards.back(6, 0, H, grad_bottle.astype(F32), *work)
    grad_two = gelu_back(two_ref[...], grad_two).astype(BF16)
    pack_ref[:, place + B : place + B + H] = grad_two
    grad_one = shards.back(5, D, H, grad_two.astype(F32), *work)
    grad_one = gelu_back(one_ref[...], grad_one).astype(BF16)
    pack_ref[:, place + B + H : place + B + 2 * H] = grad_one
    grad_cls = shards.back(5, 0, D, grad_one.astype(F32), *work)
    unit, scale = middle_ref[2], middle_ref[3]
    gain_last = jnp.sum(grad_cls * unit, 0, keepdims=True)
    shift_last = jnp.sum(grad_cls, 0, keepdims=True)
    grad_stream = norm_back(grad_cls, final[0:1], unit, scale)
    grad_branch = grad_stream.astype(BF16)
    pack_ref[:, D + F : 2 * D + F] = grad_branch
    grad_hidden = shards.back(4, 0, F, grad_branch.astype(F32), *work)
    grad_hidden = gelu_back(hidden_ref[...], grad_hidden).astype(BF16)
    pack_ref[:, D : D + F] = grad_hidden
    grad_normed = shards.back(3, 0, D, grad_hidden.astype(F32), *work)
    unit, scale = middle_ref[0], middle_ref[1]
    extra_ref[...] = jnp.concatenate(
        [
            jnp.sum(grad_normed * unit, 0, keepdims=True),
            jnp.sum(grad_normed, 0, keepdims=True),
            gain_last,
            shift_last,
            jnp.zeros((4, D), F32),
        ],
        0,
    )
    grad_middle = grad_stream + norm_back(grad_normed, norms[2:3], unit, scale)
    stream_ref[...] = grad_middle
    grad_mixed = grad_middle.astype(BF16)
    pack_ref[:, :D] = grad_mixed
    grad_att = shards.back(2, 0, D, grad_mixed.astype(F32), *work).astype(BF16)
    pack_ref[:, place + B + 2 * H : place + B + 2 * H + D] = grad_att
    shards.finish()


def rows_back(plan, low, gathered, note, kept):
    views = kept[-1].shape[1]
    shapes = [((views, 3 * D + F + B + 2 * H), BF16), ((views, D), F32), ((8, D), F32)]
    most, longest = plan.largest()
    return pl.pallas_call(
        functools.partial(rows_back_kernel, plan),
        out_shape=[jax.ShapeDtypeStruct(shape, dtype) for shape, dtype in shapes],
        in_specs=[pl.BlockSpec(memory_space=pltpu.SMEM), pl.BlockSpec(memory_space=pl.ANY)]
        + [pl.BlockSpec(memory_space=pltpu.VMEM)] * (1 + len(kept)),
        out_specs=[pl.BlockSpec(memory_space=pltpu.VMEM)] * len(shapes),
        scratch_shapes=[
            pltpu.VMEM((plan.count, plan.buffer // TILE, TILE, LANES), BF16),
            pltpu.VMEM((most, views, longest), F32),
            pltpu.VMEM((views, F), F32),
            pltpu.VMEM((views, F + 2 * LANES), F32),
            pltpu.SemaphoreType.DMA((plan.count,)),
        ],
        compiler_params=pltpu.CompilerParams(vmem_limit_bytes=40 * 1024 * 1024),
        cost_estimate=pl.CostEstimate(
            flops=30 * 10**9, bytes_accessed=30 * 10**6, transcendentals=10**5
        ),
    )(low, gathered, note, *kept)


def tokens_back_kernel(
    odd_ref,
    behind_ref,
    stream_ref,
    ends_ref,
    unit_ref,
    scale_ref,
    probs_ref,
    looked_ref,
    class_ref,
    qkv_ref,
    pixels_ref,
    first_ref,
    second_ref,
    kept_ref,
    sent_ref,
    patch_ref,
    place_ref,
    reach_ref,
    back_ref,
    mixed_ref,
    rows_ref,
):
    v = pl.program_id(0)
    views = stream_ref.shape[0]
    temper = HDIM ** (-0.5)
    norms = class_ref[4:8]
    class_unit, class_normed, class_scale = (class_ref[row : row + 1] for row in (0, 1, 3))

    @pl.when(v == 0)
    def _():
        place = 2 * D + F + B + 2 * H
        grad_att = behind_ref[:, place : place + D].astype(F32)
        spread = jnp.where(head_mask()[None], grad_att[:, None, :], 0.0).astype(BF16)
        back = product_t(spread.reshape(views * HEADROWS, D), qkv_ref[:, 2 * D :])
        back_ref[...] = back.astype(BF16).reshape(views, HEADROWS, D)
        patch_ref[...] = jnp.zeros(patch_ref.shape, F32)
        place_ref[...] = jnp.zeros(place_ref.shape, F32)
        reach_ref[...] = jnp.zeros(reach_ref.shape, F32)
        rows_ref[...] = jnp.zeros(rows_ref.shape, F32)

    unit = unit_ref[0]
    scale = scale_ref[0][:, :1]
    normed = token_norms(unit, norms, class_normed)
    back = back_ref[v]
    probs = probs_ref[0]
    grad_probs = product_t(back, normed)
    delta = jnp.sum(probs * grad_probs, -1, keepdims=True)
    grad_scores = (probs * (grad_probs - delta)).astype(BF16)
    reach = product(grad_scores, normed) * temper
    mixed_ref[v] = reach.astype(BF16)
    reach_ref[...] += reach
    left = jnp.concatenate([grad_scores.astype(F32), probs.astype(BF16).astype(F32)], 0)
    looked = (looked_ref[...].astype(F32) * temper).astype(BF16)
    grad = product(left.T.astype(BF16), jnp.concatenate([looked, back], 0))
    row = lax.broadcasted_iota(jnp.int32, (8, D), 0)
    rows_ref[0] += jnp.where(row == v, grad[NPATCH : NPATCH + 1], 0.0)
    token = lax.broadcasted_iota(jnp.int32, (TOKENS, D), 0)
    grad = jnp.where(token < NPATCH, grad, 0.0)
    rows_ref[1, 0:1] += jnp.sum(grad * unit, 0, keepdims=True)
    rows_ref[2, 0:1] += jnp.sum(grad, 0, keepdims=True)
    stream = norm_back(grad, norms[0:1], unit, scale)
    place_ref[...] += stream
    patch_ref[...] += product(pixels_ref[0], stream.astype(BF16))

    @pl.when(v == views - 1)
    def _():
        keyed = product(mixed_ref[...].reshape(views * HEADROWS, D), qkv_ref[:, D : 2 * D])
        keyed = jnp.where(head_mask()[None], keyed.reshape(views, HEADROWS, D), 0.0)
        grad_query = jnp.sum(keyed, 1).astype(BF16)
        class_row = rows_ref[0][:views] + product_t(grad_query, qkv_ref[:, :D])
        class_stream = norm_back(class_row, norms[0:1], class_unit, class_scale)
        class_stream = class_stream + stream_ref[...]
        ends = [
            (0, jnp.sum(class_stream, 0, keepdims=True)),
            (NTOK, rows_ref[1, 0:1] + jnp.sum(class_row * class_unit, 0, keepdims=True)),
            (NTOK + 1, rows_ref[2, 0:1] + jnp.sum(class_row, 0, keepdims=True)),
            (NTOK + 2, ends_ref[0:1]),
            (NTOK + 3, ends_ref[1:2]),
        ]
        tail = pltpu.roll(place_ref[...], 1, 0)
        for row, value in ends:
            tail = jnp.where(token == row, value, tail)
        upper = 2 * SET - 8
        rest = jnp.zeros((2 * SET - (PD - upper) - TOKENS, D), F32)
        query_row = lax.broadcasted_iota(jnp.int32, (8, D), 0) == 0
        total = jnp.sum(grad_query.astype(F32), 0, keepdims=True)
        shared = [reach_ref[...], jnp.where(query_row, total, pltpu.roll(ends_ref[...], 7, 0))]
        shared = jnp.concatenate(shared + [jnp.zeros((SHARED - HEADROWS - 8, D), F32)], 0)
        kept_ref[2 * SET :] = shared
        sent_ref[2 * SET :] = shared.astype(BF16)
        last = jnp.concatenate([patch_ref[upper:], tail, rest], 0)

        @pl.when(odd_ref[0] == 0)
        def _():
            kept_ref[: 2 * SET] = patch_ref[: 2 * SET]
            sent_ref[: 2 * SET] = last.astype(BF16)

        @pl.when(odd_ref[0] != 0)
        def _():
            kept_ref[: 2 * SET] = last
            sent_ref[: 2 * SET] = patch_ref[: 2 * SET].astype(BF16)


def tokens_back(odd, behind, grad_middle, ends, kept, pixels, *before):
    views = grad_middle.shape[0]

    def whole(values):
        return pl.BlockSpec(values.shape, lambda v: (0,) * values.ndim)

    def by_view(values):
        return pl.BlockSpec((1,) + values.shape[1:], lambda v: (v,) + (0,) * (values.ndim - 1))

    unit, scale, probs, looked, classes, qkv_w = kept
    shape = (2 * SET + SHARED, D)
    return pl.pallas_call(
        tokens_back_kernel,
        grid=(views,),
        out_shape=[jax.ShapeDtypeStruct(shape, F32), jax.ShapeDtypeStruct(shape, BF16)],
        in_specs=[
            pl.BlockSpec(memory_space=pltpu.SMEM),
            whole(behind),
            whole(grad_middle),
            whole(ends),
            by_view(unit),
            by_view(scale),
            by_view(probs),
            whole(looked),
            whole(classes),
            whole(qkv_w),
            by_view(pixels),
        ]
        + [pl.BlockSpec(memory_space=pl.ANY)] * len(before),
        out_specs=[pl.BlockSpec(shape, lambda v: (0, 0))] * 2,
        scratch_shapes=[
            pltpu.VMEM((PD, D), F32),
            pltpu.VMEM((TOKENS, D), F32),
            pltpu.VMEM((HEADROWS, D), F32),
            pltpu.VMEM((views, HEADROWS, D), BF16),
            pltpu.VMEM((views, HEADROWS, D), BF16),
            pltpu.VMEM((3, 8, D), F32),
        ],
        compiler_params=pltpu.CompilerParams(vmem_limit_bytes=60 * 1024 * 1024),
        cost_estimate=pl.CostEstimate(
            flops=15 * 10**9, bytes_accessed=15 * 10**6, transcendentals=10**5
        ),
    )(odd, behind, grad_middle, ends, unit, scale, probs, looked, classes, qkv_w, pixels, *before)


def early_kernel(
    plan,
    most,
    tab_ref,
    common_hbm,
    behind_hbm,
    rest_ref,
    *refs,
):
    line_out, square_ref, common_ref, behind_ref, class_ref, line_ref, sem, class_sem = refs[-8:]
    slab = (plan.most_chunks[1] + 1) * CHUNK
    class_copy = pltpu.make_async_copy(
        common_hbm.at[pl.ds(0, TILE), pl.ds(CLASS, D)], class_ref, class_sem
    )
    class_copy.start()
    line_ref[pl.ds(0, plan.used), :] = jnp.zeros((plan.used, LANES), F32)

    def fetch(source, target, column, size):
        which = 0 if target is common_ref else 1
        copy = pltpu.make_async_copy(
            source.at[:, pl.ds(column, size)], target.at[:, pl.ds(0, size)], sem.at[which]
        )
        copy.start()
        return copy

    def turned(lane):
        start = pl.multiple_of(lane // LANES * LANES, LANES)
        both = common_ref[:, pl.ds(start, 2 * LANES)].astype(F32)
        both = pltpu.roll(both, lax.rem(2 * LANES - (lane - start), 2 * LANES), 1)
        return both[:, :LANES].T.astype(BF16)

    def store(goal, width, tile, block):
        line_ref[pl.ds(goal + tile, block.shape[0], stride=width), :] = block

    for part in range(most):
        kind, base, chunks, row0 = (tab_ref[1 + 4 * part + i] for i in range(4))
        for index, (lane, column) in SPANS.items():
            cols = PIECES[index][2]
            width = cols // LANES
            size = (plan.most_chunks[index] + 1) * CHUNK

            @pl.when(kind == index)
            def _(lane=lane, column=column, cols=cols, width=width, size=size):
                skew = lax.rem(row0, LANES)
                place = pl.multiple_of(ROWS + lane + row0 - skew, LANES)
                copies = [
                    fetch(common_hbm, common_ref, place, size),
                    fetch(behind_hbm, behind_ref, column, cols),
                ]
                for copy in copies:
                    copy.wait()

                def move(step, carry):
                    goal = base + step * (CHUNK * width)
                    block = product(turned(skew + step * CHUNK), behind_ref[:, :cols])
                    for tile in range(width):
                        store(goal, width, tile, block[:, tile * LANES : (tile + 1) * LANES])
                    return carry

                lax.fori_loop(0, chunks, move, 0)

        @pl.when(kind == 8)
        def _():
            copies = [
                fetch(behind_hbm, behind_ref, 2 * D + F, B),
                fetch(common_hbm, common_ref, SECOND, H + D),
            ]
            for copy in copies:
                copy.wait()

            def move(step, carry):
                for own in range(2):
                    place = 2 * step + own
                    block = product(turned(row0 + place * CHUNK), behind_ref[:, :B])
                    for tile in range(B // LANES):
                        piece = block[:, tile * LANES : (tile + 1) * LANES]
                        store(base + place * (CHUNK * B // LANES), B // LANES, tile, piece)
                return carry

            lax.fori_loop(0, (chunks + 1) // 2, move, 0)

        @pl.when(kind == 5)
        def _():
            for tile in range(D // LANES):
                store(base, D // LANES, tile, jnp.zeros((8, LANES), F32))

        @pl.when(kind == 1)
        def _():
            skew = lax.rem(row0, LANES)
            first = pl.multiple_of(row0 - skew, LANES)
            copies = [fetch(behind_hbm, behind_ref, ATT_COLUMN, D)]
            for head in range(HEADS):
                copies.append(
                    pltpu.make_async_copy(
                        common_hbm.at[:, pl.ds(pl.multiple_of(head * D + first, LANES), slab)],
                        common_ref.at[:, pl.ds(head * slab, slab)],
                        sem.at[2 + head],
                    )
                )
                copies[-1].start()
            for copy in copies:
                copy.wait()

            def move(step, carry):
                width = 3 * D // LANES
                goal = base + step * (CHUNK * width)
                side = lax.broadcasted_iota(jnp.int32, (CHUNK, LANES), 1)
                for pair in range(HEADS // 2):
                    right = behind_ref[:, pair * LANES : (pair + 1) * LANES]
                    lane = 2 * pair * slab + skew + step * CHUNK
                    left, other = (product(turned(lane + slab * head), right) for head in range(2))
                    block = jnp.where(side < HDIM, left, other)
                    store(goal, width, 2 * D // LANES + pair, block)
                return carry

            lax.fori_loop(0, chunks, move, 0)

    shift = tab_ref[0]
    place = lax.broadcasted_iota(jnp.int32, (8, LANES), 0) * LANES
    place = place + lax.broadcasted_iota(jnp.int32, (8, LANES), 1)
    head = line_ref[FRONT : FRONT + 8, :]
    line_ref[FRONT : FRONT + 8, :] = jnp.where(place >= shift, head, 0.0)
    end = shift + plan.size
    block = pl.multiple_of(end // (8 * LANES) * 8, 8)
    lines = pl.ds(pl.multiple_of(FRONT + block, 8), 8)
    line_ref[lines, :] = jnp.where(place + block * LANES < end, line_ref[lines, :], 0.0)

    def clear(step, carry):
        start = pl.multiple_of(FRONT + block + 8 * step, 8)
        line_ref[pl.ds(start, 8), :] = jnp.zeros((8, LANES), F32)
        return carry

    lax.fori_loop(1, (plan.lines + 8 - block) // 8, clear, 0)

    def square(step, total):
        start = pl.multiple_of(FRONT + step * STEPS, 8)
        part = line_ref[pl.ds(start, STEPS), :]
        return total + part * part

    total = lax.fori_loop(
        0, plan.steps, square, jnp.zeros((STEPS, LANES), F32), unroll=steps_at_once(plan.steps)
    )
    line_copy = pltpu.make_async_copy(line_ref.at[pl.ds(0, plan.used)], line_out, sem.at[0])
    line_copy.start()
    total = jnp.sum(total, keepdims=True) + rest_ref[0:1, 0:1]
    class_copy.wait()
    if len(refs) > 8:
        holds, twice = (tab_ref[1 + 4 * most + which] for which in range(2))
        rows = jnp.sum(refs[0][...] * refs[0][...], 1, keepdims=True)
        place = lax.broadcasted_iota(jnp.int32, (SET, 1), 0)
        pieces = jnp.sum(jnp.where((place < 8) & (twice != 0), 0.0, rows[:SET]), keepdims=True)
        classes = class_ref[...].astype(F32)
        by_head = jnp.where(head_mask(), classes[1:2], 0.0)
        by_head = jnp.sum(by_head * by_head, 1, keepdims=True)
        normed = jnp.sum(classes[0:1] * classes[0:1], 1, keepdims=True)
        outer = jnp.sum(rows[SET : SET + HEADROWS] * by_head, keepdims=True)
        outer = outer + rows[SET + HEADROWS : SET + HEADROWS + 1] * normed
        outer = outer + rows[SET + HEADROWS + 1 : SET + HEADROWS + 2]
        outer = outer + rows[SET + HEADROWS + 2 : SET + HEADROWS + 3]
        total = total + jnp.where(holds != 0, pieces + outer / plan.groups, 0.0)
    square_ref[...] = jnp.broadcast_to(total[None], square_ref.shape)
    line_copy.wait()


def early_gradient(plan, table, common, behind, *values):
    return pl.pallas_call(
        functools.partial(early_kernel, plan, (table.shape[0] - 3) // 4),
        out_shape=[
            jax.ShapeDtypeStruct((plan.used, LANES), F32),
            jax.ShapeDtypeStruct((plan.count, 1, LANES), F32),
        ],
        in_specs=[
            pl.BlockSpec(memory_space=pltpu.SMEM),
            pl.BlockSpec(memory_space=pl.ANY),
            pl.BlockSpec(memory_space=pl.ANY),
        ]
        + [pl.BlockSpec(memory_space=pltpu.VMEM)] * len(values),
        out_specs=[
            pl.BlockSpec(memory_space=pl.ANY),
            pl.BlockSpec(memory_space=pltpu.VMEM),
        ],
        scratch_shapes=[
            pltpu.VMEM((common.shape[0], plan.fetched), BF16),
            pltpu.VMEM((behind.shape[0], F), BF16),
            pltpu.VMEM((TILE, D), BF16),
            pltpu.VMEM((plan.grad_scratch, LANES), F32),
            pltpu.SemaphoreType.DMA((2 + HEADS,)),
            pltpu.SemaphoreType.DMA,
        ],
        compiler_params=pltpu.CompilerParams(vmem_limit_bytes=60 * 1024 * 1024),
        cost_estimate=pl.CostEstimate(
            flops=10 * 10**9, bytes_accessed=10 * 10**6, transcendentals=0
        ),
    )(table, common, behind, *values)


def late_kernel(
    plan,
    most,
    tab_ref,
    lines_ref,
    wide_ref,
    left_ref,
    right_ref,
    ends_ref,
    out_ref,
    line_ref,
    sem,
):
    copy = pltpu.make_async_copy(lines_ref, line_ref.at[pl.ds(0, plan.used)], sem)
    copy.start()
    copy.wait()

    def add(goal, width, tile, block):
        lines = pl.ds(goal + tile, CHUNK, stride=width)
        line_ref[lines, :] = line_ref[lines, :] + block

    for part in range(most):
        kind, base, chunks, row0 = (tab_ref[1 + 4 * part + i] for i in range(4))

        @pl.when(kind == 0)
        def _():
            def move(step, carry):
                width = D // LANES
                rows = pl.ds(pl.multiple_of(row0 + step * CHUNK, 8), CHUNK)
                for tile in range(width):
                    block = wide_ref[rows, tile * LANES : (tile + 1) * LANES]
                    add(base + step * (CHUNK * width), width, tile, block)
                return carry

            lax.fori_loop(0, chunks, move, 0)

        @pl.when(kind == 1)
        def _():
            def move(step, carry):
                width = 3 * D // LANES
                rows = pl.ds(pl.multiple_of(row0 + step * CHUNK, 8), CHUNK)
                block = jnp.dot(
                    left_ref[rows, :],
                    right_ref[...],
                    precision=PRECISE,
                    preferred_element_type=F32,
                )
                for tile in range(2 * D // LANES):
                    piece = block[:, tile * LANES : (tile + 1) * LANES]
                    add(base + step * (CHUNK * width), width, tile, piece)
                return carry

            lax.fori_loop(0, chunks, move, 0)

        @pl.when(kind == 5)
        def _():
            width = D // LANES
            for tile in range(width):
                lines = pl.ds(base + tile, 8, stride=width)
                block = ends_ref[:, tile * LANES : (tile + 1) * LANES]
                line_ref[lines, :] = line_ref[lines, :] + block

    shift = tab_ref[0]
    turn = lax.rem(LANES - shift, LANES)
    lane = lax.broadcasted_iota(jnp.int32, (STEPS + 8, LANES), 1)

    def align(step, carry):
        start = pl.multiple_of(step * STEPS, 8)
        lines = pl.ds(pl.multiple_of(FRONT + start, 8), STEPS + 8)
        here = pltpu.roll(line_ref[lines, :], turn, 1)
        below = pltpu.roll(here, STEPS + 7, 0)
        both = jnp.where(lane < LANES - shift, here, below)
        out_ref[pl.ds(start, STEPS), :] = both[:STEPS]
        return carry

    lax.fori_loop(0, plan.steps, align, 0, unroll=steps_at_once(plan.steps))


def late_gradient(plan, table, lines, *values):
    return pl.pallas_call(
        functools.partial(late_kernel, plan, (table.shape[0] - 3) // 4),
        out_shape=jax.ShapeDtypeStruct((plan.lines, LANES), F32),
        in_specs=[pl.BlockSpec(memory_space=pltpu.SMEM), pl.BlockSpec(memory_space=pl.ANY)]
        + [pl.BlockSpec(memory_space=pltpu.VMEM)] * len(values),
        out_specs=pl.BlockSpec(memory_space=pltpu.VMEM),
        scratch_shapes=[
            pltpu.VMEM((plan.grad_scratch, LANES), F32),
            pltpu.SemaphoreType.DMA,
        ],
        compiler_params=pltpu.CompilerParams(vmem_limit_bytes=24 * 1024 * 1024),
    )(table, lines, *values).reshape(-1)[: plan.size]


def adam_update(weight, grad, first, second, rate):
    first = BETA_FIRST * first + (1.0 - BETA_FIRST) * grad
    second = BETA_SECOND * second + (1.0 - BETA_SECOND) * grad * grad
    stepped = (
        first
        / (1.0 - BETA_FIRST**STEP)
        / (jnp.sqrt(second / (1.0 - BETA_SECOND**STEP)) + ADAM_EPSILON)
    )
    return (weight - rate * (stepped + WEIGHT_DECAY * weight), first, second)


def per_device(
    plan,
    params,
    first_moment,
    second_moment,
    teacher,
    protos,
    proto_first,
    proto_second,
    teacher_protos,
    center,
    patches,
    partner,
):
    reps, groups = lax.axis_size("rep"), lax.axis_size("grp")
    count, half = reps * groups, reps * groups // 2
    rep, grp = lax.axis_index("rep"), lax.axis_index("grp")
    device = rep * groups + grp
    low = rep % 2 == 0
    place = rep // 2 * groups + grp
    halves = [
        [r * groups + g for r in range(parity, reps, 2) for g in range(groups)] for parity in (0, 1)
    ]
    swap = [(r, r ^ 1) for r in range(reps)]
    own_views = patches.shape[0]
    views = 2 * own_views

    def trade(values):
        return lax.ppermute(values, "rep", swap)

    def trade_low(values):
        return jnp.where(low, values, trade(values))

    def in_order(values):
        other = trade(values)
        return jnp.where(low, values, other), jnp.where(low, other, values)

    pairs = [list(range(parity, reps, 2)) for parity in (0, 1)]
    lines = reps // 2
    table = jnp.asarray(plan.lay_table)[device]
    given = lay_out(plan, table, jnp.where(low, teacher, params))
    later, given = lax.optimization_barrier(((params, teacher, protos, teacher_protos), given))
    given = trade(given)
    tables = jnp.stack(later[2:]).astype(BF16)
    around = [tables]
    for step in range(2, reps, 2):
        around.append(lax.ppermute(tables, "rep", [(r, (r + step) % reps) for r in range(reps)]))

    kept = lay_out(plan, table, jnp.where(low, later[0], later[1]))
    given, around = lax.optimization_barrier((given, around))
    shards = jnp.stack([jnp.where(low, kept, given), jnp.where(low, given, kept)])
    gathered = lax.all_gather(shards, BOTH, axis=0, axis_index_groups=halves)
    gathered = gathered.reshape(half, 2, -1, TILE, LANES)
    patches, partner, given = lax.optimization_barrier((patches, partner, given))
    pixels = jnp.concatenate(in_order(patches), 0)
    pixels = jnp.pad(pixels, ((0, 0), (0, TOKENS - NPATCH), (0, 0)))
    around = jnp.concatenate([jnp.stack(around[::-1])] * 2)
    around = lax.dynamic_slice_in_dim(around, lines - 1 - rep // 2, lines, 0)
    tables = jnp.stack(in_order(around))
    tables = tables.transpose(2, 1, 0, 3, 4).reshape(2, B, -1).astype(F32)
    places = in_order(partner.astype(F32))

    def columns_of(values):
        scale = lax.rsqrt(jnp.sum(values * values, 0, keepdims=True) + 1e-06)
        return (values * scale).astype(BF16), scale

    columns, column_scale = columns_of(tables[0])
    teacher_columns = columns_of(tables[1])[0]

    here = jnp.arange(views)
    source = jnp.concatenate([places[0], places[1] + own_views]).astype(jnp.int32)
    source = jnp.where(low, here, source)
    turn = (source[:, None] == here[None, :]).astype(BF16)

    turn, columns, teacher_columns = lax.optimization_barrier((turn, columns, teacher_columns))
    kept = forward(plan, gathered, pixels, turn)
    unit, scale, probs, _, looked, classes, qkv_w = kept[:7]
    all_rows, common = lax.all_to_all(kept[12], BOTH, 0, 0), kept[13]

    def gather_rows(values):
        return lax.all_gather(values, BOTH, axis=0, axis_index_groups=halves).reshape(
            half * views, -1
        )

    other = trade(common)

    all_rows = all_rows.reshape(reps // 2, 2, -1, B).transpose(1, 0, 2, 3).reshape(2, -1, B)
    start = (rep // 2 * groups * views).astype(jnp.int32)[None]
    note, new_center = prototypes(
        start, all_rows, columns, teacher_columns, center[None], groups, views
    )
    note, other = lax.optimization_barrier((note, other))
    common = gather_rows(jnp.where(low, common, other))
    new_center = new_center[0]
    note = lax.all_to_all(note, "grp", 0, 0)
    totals = jnp.sum(note[:, 3 * views :], 0)
    totals = totals.reshape(-1, 8, B).transpose(1, 0, 2).reshape(8, -1)[:, : half * views]
    loss_value = jnp.sum(jnp.log(totals[0]) - totals[2] / totals[1])
    depth = protos.shape[0]
    grad_protos, proto_squares = prototypes_back(
        (rep * depth).astype(jnp.int32)[None],
        depth,
        all_rows,
        columns,
        teacher_columns,
        center[None],
        totals,
        tables[0],
        column_scale,
    )
    behind, grad_middle, ends = rows_back(
        plan, low.astype(jnp.int32)[None], gathered, note, (classes,) + tuple(kept[7:12])
    )
    odd, far = grp % 2 == 1, grp // 2 % 2 == 1
    behind_rows = trade_low(behind)
    kept_rows, sent_rows = tokens_back(
        odd.astype(jnp.int32)[None],
        behind,
        grad_middle,
        ends,
        (unit, scale, probs, looked, classes, qkv_w),
        pixels.transpose(0, 2, 1),
        behind_rows,
        grad_protos,
    )

    def across(bit, values):
        return lax.ppermute(values, "grp", [(g, g ^ bit) for g in range(groups)])

    partial = kept_rows + across(1, sent_rows).astype(F32)
    first, second = partial[:SET], partial[SET : 2 * SET]
    shared = partial[2 * SET :]
    other = jnp.concatenate([jnp.where(far, first, second), shared], 0).astype(BF16)
    partial = jnp.concatenate([jnp.where(far, second, first), shared], 0)
    partial = partial + across(2, other).astype(F32)
    behind_rows, common, partial = lax.optimization_barrier((behind_rows, common, partial))
    behind_rows = gather_rows(behind_rows)
    if plan.near:
        step = 1
        while step < lines:
            hops = [(r, r - 2 * step) for r in range(reps) if r // 2 % (2 * step) == step]
            partial = partial + lax.ppermute(partial.astype(BF16), "rep", hops).astype(F32)
            step *= 2
    else:
        depth = partial.shape[0] // lines
        partial = lax.all_to_all(
            partial.astype(BF16).reshape(lines, depth, D), "rep", 0, 0, axis_index_groups=pairs
        )
        partial = jnp.sum(partial.astype(F32), 0)
    class_rows = common[:2, CLASS:ROWS].astype(F32)
    class_normed, query = class_rows[0:1], class_rows[1:2]
    by_head = jnp.where(head_mask()[:HEADS], query, 0.0)
    values = (proto_squares, partial)
    if not plan.near:
        twice = odd & ~far & (jnp.arange(SET) < 8)
        weights = jnp.concatenate(
            [
                jnp.where(twice, 0.0, 1.0),
                jnp.sum(by_head * by_head, 1) / groups,
                jnp.zeros((HEADROWS - HEADS,), F32),
                jnp.sum(class_normed * class_normed)[None] / groups,
                jnp.full((2,), 1.0 / groups, F32),
                jnp.zeros((SHARED - HEADROWS - 3,), F32),
            ]
        )
        weights = lax.dynamic_slice_in_dim(weights, rep // 2 * depth, depth)
        pieces = jnp.sum(weights * jnp.sum(partial * partial, 1))
        values = (proto_squares + jnp.where(low, pieces, 0.0),)
    early, squares = early_gradient(
        plan, jnp.asarray(plan.grad_table)[device], common, behind_rows, *values
    )
    summed = partial.astype(BF16)
    if not plan.near:
        summed = lax.all_to_all(
            jnp.broadcast_to(summed[None], (lines, depth, D)), "rep", 0, 0, axis_index_groups=pairs
        ).reshape(-1, D)
    shared, summed = summed[SET:], summed[:SET]
    other, squares = lax.optimization_barrier((across(2, summed), squares))
    squares = lax.all_to_all(squares, BOTH, 0, 0)
    grad_norm = jnp.sqrt(jnp.sum(squares[:, 0, 0]))
    factor = jnp.minimum(1.0, CLIP_NORM / (grad_norm + 1e-06))
    summed = jnp.concatenate([jnp.where(far, other, summed), jnp.where(far, summed, other)], 0)
    if plan.all_sets:
        other = across(1, summed)
        summed = jnp.concatenate([jnp.where(odd, other, summed), jnp.where(odd, summed, other)], 0)
    if plan.odd_owner:
        summed = trade_low(summed)
    wide_grad = jnp.pad(summed.astype(F32), ((0, CHUNK), (0, 0)))

    ends = shared[HEADROWS + 1 : HEADROWS + 3]
    shared = trade_low(shared).astype(F32)
    if plan.near:
        for owner in plan.final_reps:
            moved = lax.ppermute(ends, "rep", [(0, owner)]) if owner else ends
            ends = jnp.where(rep == owner, moved, ends)
        ends = ends.astype(F32)
    else:
        ends = shared[HEADROWS + 1 : HEADROWS + 3]
    ends = jnp.pad(ends, ((0, 6), (0, 0)))
    sum_query, reach = shared[HEADROWS : HEADROWS + 1], shared[:HEADS]
    left = jnp.concatenate([class_normed, reach, jnp.zeros((LANES - 1 - HEADS, D), F32)], 0)
    left = jnp.pad(left.T, ((0, CHUNK), (0, 0)))
    right = jnp.concatenate(
        [
            jnp.pad(sum_query, ((0, 0), (0, D))),
            jnp.pad(by_head, ((0, 0), (D, 0))),
            jnp.zeros((LANES - 1 - HEADS, 2 * D), F32),
        ],
        0,
    )
    grad_flat = late_gradient(
        plan, jnp.asarray(plan.late_table)[device], early, wide_grad, left, right, ends
    )
    new_params, new_first, new_second = adam_update(
        params, grad_flat * factor, first_moment, second_moment, LEARNING_RATE
    )
    new_protos, new_proto_first, new_proto_second = adam_update(
        protos, grad_protos * factor, proto_first, proto_second, PROTO_RATE
    )
    new_teacher = TEACHER_MOMENTUM * teacher + (1.0 - TEACHER_MOMENTUM) * new_params
    new_teacher_protos = TEACHER_MOMENTUM * teacher_protos + (1.0 - TEACHER_MOMENTUM) * new_protos
    return (
        new_params,
        new_first,
        new_second,
        new_teacher,
        new_protos,
        new_proto_first,
        new_proto_second,
        new_teacher_protos,
        new_center,
        loss_value,
        grad_norm,
    )


def solution(mesh):
    placed = (
        P(BOTH),
        P(BOTH),
        P(BOTH),
        P(BOTH),
        P("rep", "grp"),
        P("rep", "grp"),
        P("rep", "grp"),
        P("rep", "grp"),
        P("grp"),
        P(BOTH, None, None),
        P(BOTH),
    )
    plan = Plan(mesh.shape["rep"], mesh.shape["grp"])
    return jax.shard_map(
        functools.partial(per_device, plan),
        mesh=mesh,
        in_specs=placed,
        out_specs=placed[:9] + (P(), P()),
        check_vma=False,
    )
```
